32 devices in a mesh: fsdp: 4 (over z), seq: 8 (over y, x, core).
Axes of the slice: x: 2, y: 2, z: 4, core: 2. Of those that a mesh axis runs over, the one named last changes fastest.
Arguments:
- tokens: bfloat16 [8, 2048, 1024], P('fsdp', 'seq'), may hold values from -6 to 6
- segments: int32 [8, 2048], P('fsdp', 'seq'), may hold values from 0 to 2047, as said below
- norm_gain: bfloat16 [2, 1024], P(None, 'fsdp'), may hold values from 0.5 to 1.5
- in_weight: bfloat16 [2, 1024, 4352], P(None, 'fsdp'), may hold values from -0.1875 to 0.1875
- dt_weight: bfloat16 [2, 1024, 32], P(None, 'fsdp'), may hold values from -0.1875 to 0.1875
- conv_weight: bfloat16 [2, 4, 2304], P(None, None, 'fsdp'), may hold values from -3 to 3
- conv_bias: bfloat16 [2, 2304], P(None, 'fsdp'), may hold values from -1.5 to 1.5
- dt_bias: bfloat16 [2, 32], P(None, 'fsdp')
- a_log: bfloat16 [2, 32], P(None, 'fsdp'), may hold values from -0.5 to 0.5
- d_skip: bfloat16 [2, 32], P(None, 'fsdp'), may hold values from 0.5 to 1.5
- gate_gain: bfloat16 [2, 2048], P(None, 'fsdp'), may hold values from 0.5 to 1.5
- out_weight: bfloat16 [2, 2048, 1024], P(None, 'fsdp'), may hold values from -0.125 to 0.125
- cotangent: bfloat16 [8, 2048, 1024], P('fsdp', 'seq'), may hold values from -6 to 6
Outputs:
- output: float32 [8, 2048, 1024], P('fsdp', 'seq')
- input_grad: float32 [8, 2048, 1024], P('fsdp', 'seq')
- norm_gain_grad: float32 [2, 1024], P(None, 'fsdp')
- in_weight_grad: float32 [2, 1024, 4352], P(None, 'fsdp')
- dt_weight_grad: float32 [2, 1024, 32], P(None, 'fsdp')
- conv_weight_grad: float32 [2, 4, 2304], P(None, None, 'fsdp')
- conv_bias_grad: float32 [2, 2304], P(None, 'fsdp')
- dt_bias_grad: float32 [2, 32], P(None, 'fsdp')
- a_log_grad: float32 [2, 32], P(None, 'fsdp')
- d_skip_grad: float32 [2, 32], P(None, 'fsdp')
- gate_gain_grad: float32 [2, 2048], P(None, 'fsdp')
- out_weight_grad: float32 [2, 2048, 1024], P(None, 'fsdp')
The draws below stay inside these ranges and needn't reach their ends.
Inputs may be any that keep to these rules, and one draw needn't show every extreme that they name: `segments`: A position's document number is the index, within its sequence, of the last position of its document, so numbers never fall along a sequence and every sequence ends with 2047; in every group of 2 sequences on one index of fsdp one sequence is a single document.
All inputs are finite; a program needn't handle non-finite values.
Results may differ from the reference program's by a relative error of at most 0.02.
Values may be sent and summed in bfloat16 or wider, within the bound.
No kernel may reach another device: no remote copies, remote signals or barrier semaphores. Data moves between devices by JAX's collectives and lax.ppermute only.
A program may use at most 448 MiB of HBM per device.

```python
import jax
import jax.numpy as jnp
from jax import lax

D = 1024
HEADS = 32
CONV = 4
PIECE = 256
LAYERS = 2
SEQ_DEV = 2
INNER = 2048
CHANNELS = 2304
PROJ = 4352
SEQS = 8
LEN = 2048


def draw_segments(key, part):
    key = jax.random.fold_in(key, 11)
    first, second, third = jax.random.split(key, 3)
    level = jax.random.randint(first, (SEQS, 1), 0, 4)
    period = jnp.left_shift(jnp.int32(32), 2 * level)
    ticket = jax.random.randint(second, (SEQS, LEN), 0, 1 << 20)
    chosen = jax.random.randint(third, (SEQS // SEQ_DEV, 1), 0, SEQ_DEV)
    whole = (jnp.arange(SEQ_DEV)[None, :] == chosen).reshape(SEQS, 1)
    position = jnp.arange(LEN, dtype=jnp.int32)[None, :]
    starts = (ticket % period == 0) & (position > 0) & jnp.logical_not(whole)
    following = jnp.concatenate([starts[:, 1:], jnp.ones((SEQS, 1), dtype=bool)], axis=1)
    last_marks = jnp.where(following, position, jnp.int32(LEN - 1)).astype(jnp.int32)
    return lax.cummin(last_marks, axis=1, reverse=True).astype(jnp.int32)


def draw_dt_bias(key, part):
    key = jax.random.fold_in(key, 7)
    slowest, fastest = (0.5 / LEN, 0.03)
    share = jax.random.uniform(key, (LAYERS, HEADS), jnp.float32)
    rate = jnp.exp(jnp.log(slowest) + share * (jnp.log(fastest) - jnp.log(slowest)))
    return jnp.log(jnp.expm1(rate)).astype(jnp.bfloat16)


def shard_levels(own_key, extent, cuts, least, largest):
    factor_of = 1.0
    for axis_at, parts in cuts:
        heights = jax.random.uniform(jax.random.fold_in(jax.random.fold_in(own_key, 6), axis_at), (parts,), jnp.float32, least / len(cuts), largest / len(cuts))
        factor_of = factor_of * jnp.repeat(jnp.exp(heights), extent[axis_at] // parts).reshape((-1,) + (1,) * (len(extent) - 1 - axis_at))
    return factor_of


def centred(key, extent, scale, reach, shards=(), kind=jnp.bfloat16):
    values = scale * jax.random.normal(key, extent, jnp.float32)
    if shards:
        values = values * shard_levels(key, extent, shards, -0.22, 0.18)
    return jnp.clip(values, -reach, reach).astype(kind)


def setup_inputs(seed: int = 0) -> dict:
    keys = jax.random.split(jax.random.key(seed), 14)
    return {
        "tokens": centred(keys[0], (SEQS, LEN, D), 1.0, 6.0, ((0, 4), (1, 8))),
        "segments": draw_segments(jax.random.fold_in(keys[13], 71), 0),
        "norm_gain": jnp.clip(1.0 + 0.1 * jax.random.normal(keys[2], (LAYERS, D), jnp.float32), 0.5, 1.5).astype(jnp.bfloat16),
        "in_weight": centred(keys[3], (LAYERS, D, PROJ), D ** -0.5, 0.1875, ((1, 4),)),
        "dt_weight": centred(keys[4], (LAYERS, D, HEADS), D ** -0.5, 0.1875, ((1, 4),)),
        "conv_weight": centred(keys[5], (LAYERS, CONV, CHANNELS), CONV ** -0.5, 3.0, ((2, 4),)),
        "conv_bias": centred(keys[6], (LAYERS, CHANNELS), 0.3, 1.5, ((1, 4),)),
        "dt_bias": draw_dt_bias(jax.random.fold_in(keys[13], 71), 0),
        "a_log": jnp.clip(jax.random.uniform(keys[8], (LAYERS, HEADS), jnp.float32, -0.5, 0.5) * shard_levels(keys[8], (LAYERS, HEADS), ((1, 4),), -0.4, 0.0), -0.5, 0.5).astype(jnp.bfloat16),
        "d_skip": jnp.clip(0.5 + 1.0 * jax.random.uniform(keys[9], (LAYERS, HEADS), jnp.float32) ** shard_levels(keys[9], (LAYERS, HEADS), ((1, 4),), -0.2, 0.2), 0.5, 1.5).astype(jnp.bfloat16),
        "gate_gain": jnp.clip(1.0 + 0.1 * jax.random.normal(keys[10], (LAYERS, INNER), jnp.float32), 0.5, 1.5).astype(jnp.bfloat16),
        "out_weight": centred(keys[11], (LAYERS, INNER, D), INNER ** -0.5, 0.125, ((1, 4),)),
        "cotangent": centred(keys[12], (SEQS, LEN, D), 1.0, 6.0, ((0, 4), (1, 8))),
    }


EPSILON = 1e-05
highest = lax.Precision.HIGHEST

@jax.custom_vjp
def low(v):
    return lax.optimization_barrier(v.astype(jnp.bfloat16)).astype(jnp.float32)

@jax.custom_vjp
def low_back(v):
    return v

def low_keep(v):
    return (low(v), None)

def low_pass(kept, grad):
    return (grad,)

def back_keep(v):
    return (v, None)

def back_low(kept, grad):
    return (low(grad),)
low.defvjp(low_keep, low_pass)
low_back.defvjp(back_keep, back_low)

def normed(value, gain):
    return value * lax.rsqrt(lax.optimization_barrier(jnp.mean(value * value, axis=-1, keepdims=True)) + EPSILON) * gain

def split_parts(activated, heads, inner):
    state = (activated.shape[-1] - inner) // 2
    batch, width = (activated.shape[0], activated.shape[1])
    values = activated[..., :inner].reshape(batch, width, heads, inner // heads)
    return (values, activated[..., inner:inner + state], activated[..., inner + state:])

def state_piece(activated, step_size, decay_sum, tail_same, cont_last, inner):
    values, keys_in, queries = split_parts(activated, step_size.shape[-1], inner)
    weight = jnp.where(tail_same[:, :, None], jnp.exp(decay_sum[:, -1:, :] - decay_sum), 0.0) * step_size
    carried = jnp.einsum('bsh,bshp,bsn->bhpn', weight, values, keys_in, precision=highest)
    factor = jnp.where(cont_last[:, None], jnp.exp(decay_sum[:, -1, :]), 0.0)
    return (carried, factor)

def mix_piece(activated, step_size, decay_sum, gate_in, state_in, skip_scale, gate_scale, pair_same, cont):
    batch, width, heads = step_size.shape
    inner = gate_in.shape[-1]
    values, keys_in, queries = split_parts(activated, heads, inner)
    spread = decay_sum[:, :, None, :] - decay_sum[:, None, :, :]
    decay = jnp.where(pair_same[..., None], jnp.exp(jnp.where(pair_same[..., None], spread, 0.0)), 0.0)
    scores = jnp.einsum('btn,bsn->bts', queries, keys_in, precision=highest)
    weights = scores[..., None] * decay * step_size[:, None, :, :]
    mixed = jnp.einsum('btsh,bshp->bthp', weights, values, precision=highest)
    enter = jnp.where(cont[:, :, None], jnp.exp(decay_sum), 0.0)
    mixed = mixed + jnp.einsum('btn,bhpn->bthp', queries, state_in, precision=highest) * enter[..., None]
    mixed = mixed + skip_scale[:, None] * values
    return normed(mixed.reshape(batch, width, inner) * jax.nn.silu(gate_in), gate_scale)

def conv_full(mixed_in, step_raw, conv_taps, conv_offset, step_offset, conv_masks):
    width = mixed_in.shape[1]
    edge_rows = jnp.zeros((mixed_in.shape[0], conv_taps.shape[0] - 1, mixed_in.shape[2]), jnp.float32)
    padded = jnp.concatenate([edge_rows, mixed_in], axis=1)
    total = conv_offset + jnp.zeros_like(mixed_in)
    for offset in range(conv_taps.shape[0]):
        total = total + jnp.where(conv_masks[offset][:, :, None], padded[:, offset:offset + width] * conv_taps[offset], 0.0)
    return (jax.nn.silu(total), jax.nn.softplus(step_raw + step_offset))

def layer_forward(stream, segments, params):
    norm_scale, proj_matrix, step_matrix, conv_taps, conv_offset, step_offset, rate_logs, skip_scale, gate_scale, out_matrix = params
    seqs, length, model = stream.shape
    heads = step_matrix.shape[1]
    inner = out_matrix.shape[0]
    conv_len = conv_taps.shape[0]
    low_rows = low(normed(stream, norm_scale))
    projected = low_back(jnp.einsum('btk,kp->btp', low_rows, proj_matrix, precision=highest))
    step_raw = low_back(jnp.einsum('btk,kh->bth', low_rows, step_matrix, precision=highest))
    marks = (segments + 1).astype(jnp.float32)
    padded_marks = jnp.concatenate([jnp.zeros((seqs, conv_len - 1), jnp.float32), marks], axis=1)
    conv_masks = [padded_marks[:, offset:offset + length] == marks for offset in range(conv_len)]
    activated, step_size = conv_full(projected[..., inner:], step_raw, conv_taps, conv_offset, step_offset, conv_masks)
    blocks = length // PIECE
    rates = (step_size * -jnp.exp(rate_logs)).reshape(seqs, blocks, PIECE, heads)
    decay_sum = jnp.cumsum(rates, axis=2).reshape(seqs, length, heads)
    state_width = (projected.shape[-1] - 2 * inner) // 2

    def to_blocks(array):
        return jnp.moveaxis(array.reshape((seqs, blocks, PIECE) + array.shape[2:]), 1, 0)
    order = jnp.arange(PIECE)

    def one_block(carry, block):
        state, prior = carry
        act_block, size_block, total_block, gate_block, segment_block = block
        marks_block = (segment_block + 1).astype(jnp.float32)
        pair_same = (segment_block[:, :, None] == segment_block[:, None, :]) & (order[:, None] >= order[None, :])
        cont = marks_block == prior[:, None]
        tail_same = segment_block == segment_block[:, -1:]
        gated = mix_piece(act_block, size_block, total_block, gate_block, state, skip_scale, gate_scale, pair_same, cont)
        carried, factor = state_piece(act_block, size_block, total_block, tail_same, cont[:, -1], inner)
        return ((factor[:, :, None, None] * state + carried, marks_block[:, -1]), gated)
    start = (jnp.zeros((seqs, heads, inner // heads, state_width), jnp.float32), jnp.zeros((seqs,), jnp.float32))
    inputs = (to_blocks(activated), to_blocks(step_size), to_blocks(decay_sum), to_blocks(projected[..., :inner]), to_blocks(segments))
    _, gated = lax.scan(jax.checkpoint(one_block), start, inputs)
    gated = jnp.moveaxis(gated, 0, 1).reshape(seqs, length, inner)
    branch = low_back(jnp.einsum('bti,id->btd', low(gated), out_matrix, precision=highest))
    return stream + branch

def reference(tokens, segments, norm_gain, in_weight, dt_weight, conv_weight, conv_bias, dt_bias, a_log, d_skip, gate_gain, out_weight, cotangent):
    params = tuple((array.astype(jnp.float32) for array in (norm_gain, in_weight, dt_weight, conv_weight, conv_bias, dt_bias, a_log, d_skip, gate_gain, out_weight)))

    def forward(stream, *weights):

        def one_sequence(pair):
            rows, marks = pair
            rows = rows[None]
            for layer in range(LAYERS):
                rows = layer_forward(rows, marks[None], tuple((weight[layer] for weight in weights)))
            return rows[0]
        return lax.map(one_sequence, (stream, segments))
    output, pull = jax.vjp(forward, tokens.astype(jnp.float32), *params)
    grads = pull(cotangent.astype(jnp.float32))
    return (output, grads[0], grads[1], grads[2], grads[3], grads[4], grads[5], grads[6], grads[7], grads[8], grads[9], grads[10])
```

```python
import functools

import jax
import jax.numpy as jnp
from jax import lax
from jax.experimental import pallas as pl
from jax.experimental.pallas import tpu as pltpu
from jax.sharding import PartitionSpec as P

EPSILON = 1e-05
F32, BF16 = jnp.float32, jnp.bfloat16
LANES = 128
EDGE = 8
FACTOR_ROWS = 16
VMEM = 48 * 1024 * 1024
NT = (((1,), (1,)), ((), ()))
TN = (((0,), (0,)), ((), ()))


def dot(a, b):
    return jnp.dot(a, b, preferred_element_type=F32)


def dot_nt(a, b):
    return lax.dot_general(a, b, NT, preferred_element_type=F32)


def dot_tn(a, b):
    return lax.dot_general(a, b, TN, preferred_element_type=F32)


def dot_exact(a, b):
    return jnp.dot(a, b, precision=lax.Precision.HIGHEST, preferred_element_type=F32)


def halves(v):
    high = v.astype(BF16)
    low = (v - high.astype(F32)).astype(BF16)
    return jnp.concatenate([high, low], axis=1)


def sigmoid(v):
    return 1.0 / (1.0 + jnp.exp(-v))


def softplus(v):
    return jnp.maximum(v, 0.0) + jnp.log1p(jnp.exp(-jnp.abs(v)))


def below(size):
    rows = lax.broadcasted_iota(jnp.int32, (size, size), 0)
    columns = lax.broadcasted_iota(jnp.int32, (size, size), 1)
    return rows >= columns


def head_column(table, head):
    return pltpu.roll(table, LANES - head, axis=1)[:, 0:1]


def conv_total(padded, taps, masks, at, wide, width):
    total = taps[4:5, pl.ds(at, wide)] + taps[3:4, pl.ds(at, wide)] * padded[EDGE:EDGE + width, pl.ds(at, wide)]
    for back in range(1, 4):
        tap = taps[3 - back:4 - back, pl.ds(at, wide)]
        total = total + (masks[back - 1] * tap) * padded[EDGE - back:EDGE - back + width, pl.ds(at, wide)]
    return total


def conv_kernel(inner, mixed, edge, marks, taps, raw, rates, spread, act, sizes, sums, sums_t, state, factor, padded):
    width, channels = mixed.shape[1:]
    padded[0:EDGE, :] = edge[0].astype(F32)
    padded[EDGE:EDGE + width, :] = mixed[0].astype(F32)
    marks_now = marks[0]
    masks = [marks_now[:, back:back + 1] for back in range(3)]
    wide = 256
    for at in range(0, channels, wide):
        total = conv_total(padded, taps, masks, at, wide, width)
        act[0, :, pl.ds(at, wide)] = (total * sigmoid(total)).astype(BF16)
    size = softplus(raw[0] + rates[0:1, :])
    tri = jnp.where(below(width), 1.0, 0.0).astype(F32)
    total_sum = dot_exact(tri, size * rates[1:2, :])
    last = total_sum[width - 1:width]
    sizes[0] = size
    sums[0] = total_sum
    sums_t[0] = total_sum.T[0:sums_t.shape[1]]
    weight = halves(marks_now[:, 4:5] * jnp.exp(last - total_sum) * size)
    gone = marks_now[width - 1:width, 3:4] * jnp.exp(last)
    gone = halves(jnp.broadcast_to(gone, (FACTOR_ROWS, LANES)))
    states = (channels - inner) // 2
    keys_t = act[0, :, inner:inner + states].T
    for at in range(0, inner, wide):
        part = spread[:, pl.ds(at, wide)]
        weighted = (dot(weight, part) * act[0, :, pl.ds(at, wide)].astype(F32)).astype(BF16)
        state[0, :, pl.ds(at, wide)] = dot(keys_t, weighted).astype(BF16)
        factor[0, :, pl.ds(at, wide)] = dot(gone, part)


def intra_kernel(inner, heads, act, sizes, sums, sums_t, marks, row_marks, skip, spread, out, scores, stepped):
    width = act.shape[1]
    states = (act.shape[2] - inner) // 2
    half = width // 2
    keys = act[0, :, inner:inner + states]
    queries = act[0, :, inner + states:]
    same = below(width) & (marks[0][:, 5:6] == row_marks[0, 0:1, :])
    scores[...] = jnp.where(same, dot_nt(queries, keys), 0.0)
    size = halves(sizes[0])
    wide = 256
    for at in range(0, inner, wide):
        part = dot(size, spread[:, pl.ds(at, wide)])
        stepped[:, pl.ds(at, wide)] = (part * act[0, :, pl.ds(at, wide)].astype(F32)).astype(BF16)
    per = LANES // (inner // heads)
    span = inner // heads
    lane = lax.broadcasted_iota(jnp.int32, (width, LANES), 1)

    def group(at, carry):
        place = pl.ds(pl.multiple_of(at * LANES, LANES), LANES)
        x = stepped[:, place]
        y_low = y_high = None
        for i in range(per):
            head = at * per + i
            column = head_column(sums[0], head)
            row = sums_t[0, pl.ds(head, 1), :]
            mine = (lane >= i * span) & (lane < (i + 1) * span)
            xh = jnp.where(mine, x, jnp.zeros_like(x))
            w_low = scores[0:half, 0:half] * jnp.exp(jnp.minimum(column[0:half] - row[:, 0:half], 0.0))
            w_high = scores[half:, :] * jnp.exp(jnp.minimum(column[half:] - row, 0.0))
            a = dot(w_low.astype(BF16), xh[0:half])
            b = dot(w_high.astype(BF16), xh)
            y_low = a if y_low is None else y_low + a
            y_high = b if y_high is None else y_high + b
        values = act[0, :, place].astype(F32) * skip[0:1, place]
        out[0, 0:half, place] = (y_low + values[0:half]).astype(out.dtype)
        out[0, half:, place] = (y_high + values[half:]).astype(out.dtype)
        return carry

    lax.fori_loop(0, inner // LANES, group, 0, unroll=2)


def post_kernel(inner, part_mixed, act, state, sums, marks, gate, gain, spread, mixed, gated, kept):
    states = (act.shape[2] - inner) // 2
    queries = act[0, :, inner + states:]
    enter = halves(marks[0][:, 3:4] * jnp.exp(sums[0]))
    wide = 256
    square = None
    for at in range(0, inner, wide):
        place = pl.ds(at, wide)
        whole = part_mixed[0, :, place].astype(F32) + dot(enter, spread[:, place]) * dot(queries, state[0, :, place])
        g = gate[0, :, place].astype(F32)
        w = whole * (g * sigmoid(g))
        mixed[0, :, place] = whole.astype(BF16)
        kept[:, place] = w
        square = w * w if square is None else square + w * w
    scale = lax.rsqrt(jnp.sum(square, axis=1, keepdims=True) / inner + EPSILON)
    for at in range(0, inner, wide):
        place = pl.ds(at, wide)
        gated[0, :, place] = (kept[:, place] * scale * gain[0:1, place]).astype(BF16)


def gate_back_kernel(
    inner, grad, mixed, gate, gain, act, state, sums, marks, spread,
    d_mixed, d_gate, d_state, d_queries, d_sums, row_grads, kept,
):
    states = (act.shape[2] - inner) // 2
    queries = act[0, :, inner + states:]
    queries_t = queries.T
    wide = 256

    @pl.when(pl.program_id(0) == 0)
    def _():
        row_grads[...] = jnp.zeros_like(row_grads)

    square = cross = None
    for at in range(0, inner, wide):
        place = pl.ds(at, wide)
        g = gate[0, :, place].astype(F32)
        w = mixed[0, :, place].astype(F32) * (g * sigmoid(g))
        gg = grad[0, :, place].astype(F32)
        kept[:, place] = w
        square = w * w if square is None else square + w * w
        more = w * gain[0:1, place] * gg
        cross = more if cross is None else cross + more
    scale = lax.rsqrt(jnp.sum(square, axis=1, keepdims=True) / inner + EPSILON)
    pulled = scale * scale * scale * (jnp.sum(cross, axis=1, keepdims=True) / inner)
    entered = marks[0][:, 3:4] * jnp.exp(sums[0])
    enter = halves(entered)
    grad_enter = dq = None
    for at in range(0, inner, wide):
        place = pl.ds(at, wide)
        g = gate[0, :, place].astype(F32)
        sig = sigmoid(g)
        silu = g * sig
        gg = grad[0, :, place].astype(F32)
        w = kept[:, place]
        whole = mixed[0, :, place].astype(F32)
        dw = scale * (gain[0:1, place] * gg) - pulled * w
        row_grads[0:1, place] += jnp.sum(gg * w * scale, axis=0, keepdims=True)
        dm = dw * silu
        d_gate[0, :, place] = (dw * whole * (sig + silu * (1.0 - sig))).astype(BF16)
        d_mixed[0, :, place] = dm.astype(BF16)
        row_grads[1:2, place] += jnp.sum(dm * act[0, :, place].astype(F32), axis=0, keepdims=True)
        part = spread[:, place]
        st = state[0, :, place]
        e = (dm * dot(enter, part)).astype(BF16)
        d_state[0, :, place] = dot(queries_t, e).astype(BF16)
        more_q = dot_nt(e, st)
        dq = more_q if dq is None else dq + more_q
        through = (dm * dot(queries, st)).astype(BF16)
        more_e = dot_nt(through, part[0:LANES])
        grad_enter = more_e if grad_enter is None else grad_enter + more_e
    d_queries[0] = dq
    d_sums[0] = grad_enter * entered


def intra_back_kernel(
    inner, heads, d_mixed, act, sizes, sums, sums_t, marks, row_marks, spread, d_queries, d_sums,
    d_stepped, d_pair, d_total, scores, d_scores, stepped, sums_rows, sums_columns,
):
    width = act.shape[1]
    states = (act.shape[2] - inner) // 2
    half = width // 2
    keys = act[0, :, inner:inner + states]
    queries = act[0, :, inner + states:]
    rows = lax.broadcasted_iota(jnp.int32, (width, width), 0)
    columns = lax.broadcasted_iota(jnp.int32, (width, width), 1)
    same = (rows <= columns) & (marks[0][:, 5:6] == row_marks[0, 0:1, :])
    scores[...] = jnp.where(same, dot_nt(keys, queries), 0.0)
    d_scores[...] = jnp.zeros_like(d_scores)
    sums_rows[...] = jnp.zeros_like(sums_rows)
    sums_columns[...] = jnp.zeros_like(sums_columns)
    size = halves(sizes[0])
    wide = 256
    for at in range(0, inner, wide):
        part = dot(size, spread[:, pl.ds(at, wide)])
        stepped[:, pl.ds(at, wide)] = (part * act[0, :, pl.ds(at, wide)].astype(F32)).astype(BF16)
    per = LANES // (inner // heads)
    span = inner // heads
    lane = lax.broadcasted_iota(jnp.int32, (width, LANES), 1)

    eighth = lax.broadcasted_iota(jnp.int32, (8, width), 0)

    def group(at, carry):
        place = pl.ds(pl.multiple_of(at * LANES, LANES), LANES)
        x = stepped[:, place]
        dy = d_mixed[0, :, place]
        dx_low = dx_high = None
        for i in range(per):
            head = at * per + i
            column = head_column(sums[0], head)
            row = sums_t[0, pl.ds(head, 1), :]
            mine = (lane >= i * span) & (lane < (i + 1) * span)
            xh = jnp.where(mine, x, jnp.zeros_like(x))
            dyh = jnp.where(mine, dy, jnp.zeros_like(dy))
            l_low = jnp.exp(jnp.minimum(row - column[0:half], 0.0))
            l_high = jnp.exp(jnp.minimum(row[:, half:] - column[half:], 0.0))
            w_low = scores[0:half, :] * l_low
            w_high = scores[half:, half:] * l_high
            dw_low = dot_nt(xh[0:half], dy)
            dw_high = dot_nt(xh[half:], dy[half:])
            d_scores[0:half, :] += dw_low * l_low
            d_scores[half:, half:] += dw_high * l_high
            g_low = dw_low * w_low
            g_high = dw_high * w_high
            over_low = jnp.sum(g_low, axis=0, keepdims=True)
            over_high = jnp.sum(g_high, axis=0, keepdims=True)
            eight = pl.ds(pl.multiple_of(head // 8 * 8, 8), 8)
            chosen = eighth == head % 8
            sums_rows[eight, :] += jnp.where(chosen, over_low, 0.0)
            sums_rows[eight, half:] += jnp.where(chosen[:, half:], over_high, 0.0)
            here = lane[0:half] == head
            sums_columns[0:half, :] += jnp.where(here, jnp.sum(g_low, axis=1, keepdims=True), 0.0)
            sums_columns[half:, :] += jnp.where(here, jnp.sum(g_high, axis=1, keepdims=True), 0.0)
            a = dot(w_low.astype(BF16), dyh)
            b = dot(w_high.astype(BF16), dyh[half:])
            dx_low = a if dx_low is None else dx_low + a
            dx_high = b if dx_high is None else dx_high + b
        d_stepped[0, 0:half, place] = dx_low.astype(BF16)
        d_stepped[0, half:, place] = dx_high.astype(BF16)
        return carry

    lax.fori_loop(0, inner // LANES, group, 0, unroll=2)
    grad = jnp.where(same, d_scores[...], 0.0).astype(BF16)
    d_pair[0, :, 0:states] = dot(grad, queries)
    d_pair[0, :, states:] = dot(grad.T, keys) + d_queries[0]
    d_total[0] = sums_rows[...].T - sums_columns[...] + d_sums[0]


def conv_back_kernel(
    inner, d_stepped, d_mixed, act, mixed_in, edge, marks, taps, raw, rates, skip, sizes, sums, spread,
    d_pair, d_total, d_state, state,
    d_mixed_in, d_edge, d_raw, tap_grads, head_grads, padded, shifted,
):
    width, channels = mixed_in.shape[1:]
    states = (channels - inner) // 2
    wide = 256

    @pl.when(pl.program_id(0) == 0)
    def _():
        tap_grads[...] = jnp.zeros_like(tap_grads)
        head_grads[...] = jnp.zeros_like(head_grads)

    padded[0:EDGE, :] = edge[0].astype(F32)
    padded[EDGE:EDGE + width, :] = mixed_in[0].astype(F32)
    marks_now = marks[0]
    masks = [marks_now[:, back:back + 1] for back in range(3)]
    total_sum = sums[0]
    size = sizes[0]
    last = total_sum[width - 1:width]
    faded = marks_now[:, 4:5] * jnp.exp(last - total_sum)
    weight = faded * size
    weight_pair = halves(weight)
    size_pair = halves(size)
    keys = act[0, :, inner:inner + states]
    for back in range(3):
        shifted[back, 0:EDGE, :] = jnp.zeros((EDGE, wide), F32)
        shifted[back, EDGE + width:, :] = jnp.zeros((EDGE, wide), F32)

    def through_conv(at, d_act):
        place = pl.ds(at, wide)
        total = conv_total(padded, taps, masks, at, wide, width)
        sig = sigmoid(total)
        d = d_act * (sig + total * sig * (1.0 - sig))
        tap_grads[4:5, place] += jnp.sum(d, axis=0, keepdims=True)
        tap_grads[3:4, place] += jnp.sum(d * padded[EDGE:EDGE + width, place], axis=0, keepdims=True)
        back_total = taps[3:4, place] * d
        edge_total = jnp.zeros((EDGE, wide), F32)
        for back in range(1, 4):
            u = masks[back - 1] * d
            tap_grads[3 - back:4 - back, place] += jnp.sum(
                u * padded[EDGE - back:EDGE - back + width, place], axis=0, keepdims=True
            )
            shifted[back - 1, EDGE:EDGE + width, :] = u
            tap = taps[3 - back:4 - back, place]
            back_total = back_total + tap * shifted[back - 1, EDGE + back:EDGE + back + width, :]
            edge_total = edge_total + tap * shifted[back - 1, back:back + EDGE, :]
        d_mixed_in[0, :, place] = back_total.astype(BF16)
        d_edge[0, :, place] = edge_total

    d_keys = d_pair[0, :, 0:states]
    d_size = d_weight = carried = None
    for at in range(0, inner, wide):
        place = pl.ds(at, wide)
        values = act[0, :, place].astype(F32)
        part = spread[:, place]
        ds = d_state[0, :, place]
        wide_weight = dot(weight_pair, part)
        d_weighted = dot(keys, ds)
        dx = d_stepped[0, :, place].astype(F32)
        d_act = dx * dot(size_pair, part) + d_weighted * wide_weight + skip[0:1, place] * d_mixed[0, :, place].astype(F32)
        d_keys = d_keys + dot_nt((wide_weight * values).astype(BF16), ds)
        a = dot_nt((dx * values).astype(BF16), part[0:LANES])
        b = dot_nt((d_weighted * values).astype(BF16), part[0:LANES])
        c = jnp.sum(ds.astype(F32) * state[0, :, place].astype(F32), axis=0, keepdims=True)
        c = dot_nt(jnp.broadcast_to(halves_rows(c), (EDGE, wide)), part[0:LANES])
        d_size = a if d_size is None else d_size + a
        d_weight = b if d_weight is None else d_weight + b
        carried = c if carried is None else carried + c
        through_conv(at, d_act)
    through_conv(inner, jnp.concatenate([d_keys, d_pair[0, :, states:]], axis=1))
    d_size = d_size + d_weight * faded
    pulled = d_weight * weight
    gone = marks_now[width - 1:width, 3:4] * jnp.exp(last)
    at_end = jnp.sum(pulled, axis=0, keepdims=True) + gone * carried[0:1]
    row = lax.broadcasted_iota(jnp.int32, (width, LANES), 0)
    d_sum = d_total[0] - pulled + jnp.where(row == width - 1, at_end, 0.0)
    order = lax.broadcasted_iota(jnp.int32, (width, width), 0) <= lax.broadcasted_iota(jnp.int32, (width, width), 1)
    d_rate = dot_exact(jnp.where(order, 1.0, 0.0).astype(F32), d_sum)
    d_size = d_size + d_rate * rates[1:2, :]
    d_step = d_size * sigmoid(raw[0] + rates[0:1, :])
    d_raw[0] = d_step.astype(BF16)
    head_grads[0:1, :] += jnp.sum(d_step, axis=0, keepdims=True)
    head_grads[1:2, :] += jnp.sum(d_rate * size * rates[1:2, :], axis=0, keepdims=True)


def halves_rows(v):
    return v.astype(BF16)


def call(kernel, batch, ins, outs, scratch, name):
    def spec(shape, whole):
        block = tuple(shape) if whole else (1,) + tuple(shape[1:])
        if whole:
            return pl.BlockSpec(block, lambda b: (0,) * len(block))
        return pl.BlockSpec(block, lambda b: (b,) + (0,) * (len(block) - 1))

    arrays = [a for a, _ in ins]
    return pl.pallas_call(
        kernel,
        grid=(batch,),
        in_specs=[spec(a.shape, whole) for a, whole in ins],
        out_specs=[spec(shape, whole) for shape, _, whole in outs],
        out_shape=[jax.ShapeDtypeStruct(shape, kind) for shape, kind, _ in outs],
        scratch_shapes=[pltpu.VMEM(shape, kind) for shape, kind in scratch],
        compiler_params=pltpu.CompilerParams(vmem_limit_bytes=VMEM),
        name=name,
    )(*arrays)


def exchange(state, factor, later_is_odd):
    peers = lax.axis_size("seq")
    odd = lax.axis_index("seq") % 2
    later = odd == 1 if later_is_odd else odd == 0
    states = state.shape[1]
    own = jnp.concatenate([state, factor.astype(BF16)], axis=1)
    other = lax.ppermute(own, "seq", [(i, i ^ 1) for i in range(peers)])
    mine = lax.dynamic_index_in_dim(own, odd, 0, keepdims=False).astype(F32)
    theirs = lax.dynamic_index_in_dim(other, odd, 0, keepdims=False).astype(F32)
    second = jnp.where(later, mine, theirs)
    first = jnp.where(later, theirs, mine)
    gain = second[states:states + 1]
    joined = jnp.concatenate(
        [gain * first[:states] + second[:states], gain * first[states:]], axis=0
    ).astype(BF16)
    before = jnp.zeros(joined[:states].shape, F32)
    for distance in range(peers // 2 - 1, 0, -1):
        step = 2 * distance if later_is_odd else -2 * distance
        route = [(i, i + step) for i in range(peers) if 0 <= i + step < peers]
        got = lax.ppermute(joined, "seq", route).astype(F32)
        before = got[states:states + 1] * before + got[:states]
    before = before.astype(BF16)
    partner = lax.ppermute(before, "seq", [(i, i ^ 1) for i in range(peers)])
    entering = jnp.where(odd == 0, jnp.stack([before, partner]), jnp.stack([partner, before])).astype(F32)
    gain = other[:, states:states + 1].astype(F32)
    through = gain * entering + other[:, :states].astype(F32)
    return jnp.where(later, through, entering).astype(BF16)


def gathered(block):
    peers = lax.axis_size("seq")
    rows = block.shape[0] // peers
    share = lax.dynamic_slice_in_dim(block, lax.axis_index("seq") * rows, rows, 0)
    return lax.all_gather(share, ("fsdp", "seq"), axis=0, tiled=True)


def reduced(grad):
    share = lax.psum_scatter(grad, ("fsdp", "seq"), scatter_dimension=0, tiled=True)
    return lax.all_gather(share, "seq", axis=0, tiled=True).astype(F32)


def norm_scale_of(stream):
    return lax.rsqrt(jnp.mean(stream * stream, axis=-1, keepdims=True) + EPSILON)


def on_device(
    tokens, segments, norm_gain, in_weight, dt_weight, conv_weight, conv_bias, dt_bias, a_log, d_skip,
    gate_gain, out_weight, cotangent,
):
    layers = in_weight.shape[0]
    batch, width, model = tokens.shape
    heads = dt_weight.shape[2]
    taps_len = conv_weight.shape[1]
    peers = lax.axis_size("seq")
    groups = lax.axis_size("fsdp")
    rows = batch * width
    inner = out_weight.shape[1] * groups
    channels = in_weight.shape[2] - inner
    states = (channels - inner) // 2
    span = inner // heads

    small = [norm_gain, conv_weight.reshape(layers, -1), conv_bias, dt_bias, a_log, d_skip, gate_gain, dt_weight.reshape(layers, -1)]
    sizes = [a.shape[1] for a in small]
    packed = lax.all_gather(jnp.concatenate(small, axis=1), "fsdp", axis=0)
    pieces, at = [], 0
    for size in sizes:
        pieces.append(packed[:, :, at:at + size])
        at += size

    def joined(piece):
        return jnp.moveaxis(piece, 0, 1).reshape(layers, -1)

    norm_all = joined(pieces[0]).astype(F32)
    taps_all = jnp.moveaxis(pieces[1].reshape(groups, layers, taps_len, -1), 0, 2).reshape(layers, taps_len, channels)
    taps_all = jnp.concatenate(
        [taps_all.astype(F32), joined(pieces[2]).astype(F32)[:, None], jnp.zeros((layers, 8 - taps_len - 1, channels), F32)], axis=1
    )
    pad_heads = ((0, 0), (0, LANES - heads))
    rates_all = jnp.stack(
        [jnp.pad(joined(pieces[3]).astype(F32), pad_heads), jnp.pad(-jnp.exp(joined(pieces[4]).astype(F32)), pad_heads)], axis=1
    )
    rates_all = jnp.pad(rates_all, ((0, 0), (0, 6), (0, 0)))
    skip_all = jnp.broadcast_to(jnp.repeat(joined(pieces[5]).astype(F32), span, axis=1)[:, None], (layers, 8, inner))
    gain_all = jnp.broadcast_to(joined(pieces[6]).astype(F32)[:, None], (layers, 8, inner))
    dt_all = jnp.moveaxis(pieces[7].reshape(groups, layers, -1, heads), 0, 1).reshape(layers, model, heads)
    dt_all = jnp.pad(dt_all, ((0, 0), (0, 0), (0, LANES - heads)))

    in_all = [gathered(in_weight[layer]) for layer in range(layers)]
    out_all = [gathered(out_weight[layer]) for layer in range(layers)]

    numbers = (segments + 1).astype(F32)
    before = lax.ppermute(numbers[:, width - EDGE:], "seq", [(i, i + 1) for i in range(peers - 1)])
    padded = jnp.concatenate([before, numbers], axis=1)
    columns = [padded[:, EDGE - back:EDGE - back + width] == numbers for back in range(1, taps_len)]
    columns += [numbers == before[:, EDGE - 1:], numbers == numbers[:, width - 1:]]
    marks = jnp.stack([c.astype(F32) for c in columns] + [numbers], axis=-1)
    marks = jnp.pad(marks, ((0, 0), (0, 0), (0, LANES - marks.shape[-1])))
    row_marks = jnp.broadcast_to(numbers[:, None, :], (batch, 8, width))
    lane_head = jnp.arange(inner) // span
    spread = (jnp.arange(2 * LANES)[:, None] % LANES == lane_head[None, :]).astype(BF16)

    stream = tokens.astype(F32)
    kept = []
    for layer in range(layers):
        norm_scale = norm_scale_of(stream)
        low = (stream * norm_scale * norm_all[layer]).astype(BF16).reshape(rows, model)
        w_in, w_out = in_all[layer], out_all[layer]
        mixed_in = dot(low, w_in[:, inner:]).astype(BF16).reshape(batch, width, channels)
        raw = dot(low, dt_all[layer]).reshape(batch, width, LANES)
        edge = lax.ppermute(mixed_in[:, width - EDGE:], "seq", [(i, i + 1) for i in range(peers - 1)])
        gate = dot(low, w_in[:, :inner]).astype(BF16).reshape(batch, width, inner)
        taps, rates, skip, gain = taps_all[layer], rates_all[layer], skip_all[layer], gain_all[layer]
        act, size, sums, sums_t, state, factor = call(
            functools.partial(conv_kernel, inner), batch,
            [(mixed_in, 0), (edge, 0), (marks, 0), (taps, 1), (raw, 0), (rates, 1), (spread, 1)],
            [
                ((batch, width, channels), BF16, 0), ((batch, width, LANES), F32, 0), ((batch, width, LANES), F32, 0),
                ((batch, heads, width), F32, 0), ((batch, states, inner), BF16, 0), ((batch, FACTOR_ROWS, inner), F32, 0),
            ],
            [((EDGE + width, channels), F32)], "conv_states",
        )
        entering = exchange(state, factor, True)
        (part,) = call(
            functools.partial(intra_kernel, inner, heads), batch,
            [(act, 0), (size, 0), (sums, 0), (sums_t, 0), (marks, 0), (row_marks, 0), (skip, 1), (spread, 1)],
            [((batch, width, inner), F32, 0)],
            [((width, width), F32), ((width, inner), BF16)], "mix_within",
        )
        mixed, gated = call(
            functools.partial(post_kernel, inner), batch,
            [(part, 0), (act, 0), (entering, 0), (sums, 0), (marks, 0), (gate, 0), (gain, 1), (spread, 1)],
            [((batch, width, inner), BF16, 0), ((batch, width, inner), BF16, 0)],
            [((width, inner), F32)], "mix_gate",
        )
        gated = gated.reshape(rows, inner)
        kept.append((stream, norm_scale, low, mixed_in, raw, edge, gate, act, size, sums, sums_t, factor, entering, mixed, gated))
        stream = stream + dot(gated, w_out).reshape(batch, width, model)

    grad_stream = cotangent.astype(F32)
    collected = []
    for layer in reversed(range(layers)):
        (entry, norm_scale, low, mixed_in, raw, edge, gate, act, size, sums, sums_t, factor, entering, mixed, gated) = kept[layer]
        w_in, w_out = in_all[layer], out_all[layer]
        taps, rates, skip, gain = taps_all[layer], rates_all[layer], skip_all[layer], gain_all[layer]
        grad_low = grad_stream.astype(BF16).reshape(rows, model)
        grad_gated = dot_nt(grad_low, w_out).astype(BF16).reshape(batch, width, inner)
        d_mixed, d_gate, d_state, d_queries, d_sums, row_grads = call(
            functools.partial(gate_back_kernel, inner), batch,
            [(grad_gated, 0), (mixed, 0), (gate, 0), (gain, 1), (act, 0), (entering, 0), (sums, 0), (marks, 0), (spread, 1)],
            [
                ((batch, width, inner), BF16, 0), ((batch, width, inner), BF16, 0), ((batch, states, inner), BF16, 0),
                ((batch, width, states), F32, 0), ((batch, width, LANES), F32, 0), ((8, inner), F32, 1),
            ],
            [((width, inner), F32)], "gate_back",
        )
        leaving = exchange(d_state, factor, False)
        out_grad = dot_tn(gated, grad_low).astype(BF16)
        out_share = reduced(out_grad)
        d_stepped, d_pair, d_total = call(
            functools.partial(intra_back_kernel, inner, heads), batch,
            [
                (d_mixed, 0), (act, 0), (size, 0), (sums, 0), (sums_t, 0), (marks, 0), (row_marks, 0), (spread, 1),
                (d_queries, 0), (d_sums, 0),
            ],
            [((batch, width, inner), BF16, 0), ((batch, width, 2 * states), F32, 0), ((batch, width, LANES), F32, 0)],
            [
                ((width, width), F32), ((width, width), F32), ((width, inner), BF16), ((LANES, width), F32), ((width, LANES), F32),
            ], "mix_within_back",
        )
        d_gate = d_gate.reshape(rows, inner)
        d_mixed_in, d_edge, d_raw, tap_grads, head_grads = call(
            functools.partial(conv_back_kernel, inner), batch,
            [
                (d_stepped, 0), (d_mixed, 0), (act, 0), (mixed_in, 0), (edge, 0), (marks, 0), (taps, 1), (raw, 0), (rates, 1),
                (skip, 1), (size, 0), (sums, 0), (spread, 1), (d_pair, 0), (d_total, 0), (leaving, 0), (entering, 0),
            ],
            [
                ((batch, width, channels), BF16, 0), ((batch, EDGE, channels), F32, 0), ((batch, width, LANES), BF16, 0),
                ((8, channels), F32, 1), ((8, LANES), F32, 1),
            ],
            [((EDGE + width, channels), F32), ((3, width + 2 * EDGE, 256), F32)], "conv_back",
        )
        from_next = lax.ppermute(d_edge.astype(BF16), "seq", [(i + 1, i) for i in range(peers - 1)])
        d_mixed_in = jnp.concatenate(
            [
                d_mixed_in[:, :width - EDGE],
                (d_mixed_in[:, width - EDGE:].astype(F32) + from_next.astype(F32)).astype(BF16),
            ], axis=1,
        ).reshape(rows, channels)
        d_raw = d_raw.reshape(rows, LANES)
        in_grad = jnp.concatenate([dot_tn(low, d_gate).astype(BF16), dot_tn(low, d_mixed_in).astype(BF16)], axis=1)
        in_share = reduced(in_grad)
        dt_grad = dot_tn(low, d_raw)[:, :heads]
        grad_rows = dot_nt(d_gate, w_in[:, :inner]) + dot_nt(d_mixed_in, w_in[:, inner:]) + dot_nt(d_raw, dt_all[layer])
        grad_rows = grad_rows.reshape(batch, width, model)
        scaled = grad_rows * norm_all[layer]
        inward = jnp.mean(scaled * entry, axis=-1, keepdims=True)
        gain_grad = jnp.sum(grad_rows * entry * norm_scale, axis=(0, 1))
        grad_stream = grad_stream + norm_scale * scaled - (norm_scale * norm_scale * norm_scale * inward) * entry
        skip_grad = jnp.sum(row_grads[1].reshape(heads, span), axis=1)
        small_grads = [
            gain_grad.reshape(groups, -1),
            jnp.moveaxis(tap_grads[:taps_len].reshape(taps_len, groups, -1), 1, 0).reshape(groups, -1),
            tap_grads[taps_len].reshape(groups, -1),
            head_grads[0, :heads].reshape(groups, -1),
            head_grads[1, :heads].reshape(groups, -1),
            skip_grad.reshape(groups, -1),
            row_grads[0].reshape(groups, -1),
            dt_grad.reshape(groups, -1),
        ]
        collected.append((in_share, out_share, jnp.concatenate(small_grads, axis=1)))
    collected = collected[::-1]
    small_sum = lax.psum(jnp.stack([c[2] for c in collected], axis=1), ("fsdp", "seq"))
    small_sum = lax.dynamic_index_in_dim(small_sum, lax.axis_index("fsdp"), 0, keepdims=False)
    pieces, at = [], 0
    for size in sizes:
        pieces.append(small_sum[:, at:at + size])
        at += size
    return (
        stream, grad_stream, pieces[0],
        jnp.stack([c[0] for c in collected]),
        pieces[7].reshape(layers, -1, heads),
        pieces[1].reshape(layers, taps_len, -1),
        pieces[2], pieces[3], pieces[4], pieces[5], pieces[6],
        jnp.stack([c[1] for c in collected]),
    )


def solution(mesh):
    split = P("fsdp", "seq", None)
    vector = P(None, "fsdp")
    matrix = P(None, "fsdp", None)
    taps = P(None, None, "fsdp")
    return jax.shard_map(
        on_device,
        mesh=mesh,
        in_specs=(
            split, P("fsdp", "seq"), vector, matrix, matrix, taps, vector, vector, vector, vector, vector, matrix, split,
        ),
        out_specs=(
            split, split, vector, matrix, matrix, taps, vector, vector, vector, vector, vector, matrix,
        ),
        check_vma=False,
    )
```

```python
import functools

import jax
import jax.numpy as jnp
from jax import lax
from jax.experimental import pallas as pl
from jax.experimental.pallas import tpu as pltpu
from jax.sharding import PartitionSpec as P

EPSILON = 1e-05
F32, BF16 = jnp.float32, jnp.bfloat16
LANES = 128
EDGE = 8
FACTOR_ROWS = 16
VMEM = 48 * 1024 * 1024
NT = (((1,), (1,)), ((), ()))
TN = (((0,), (0,)), ((), ()))


def dot(a, b):
    return jnp.dot(a, b, preferred_element_type=F32)


def dot_nt(a, b):
    return lax.dot_general(a, b, NT, preferred_element_type=F32)


def dot_tn(a, b):
    return lax.dot_general(a, b, TN, preferred_element_type=F32)


def dot_exact(a, b):
    return jnp.dot(a, b, precision=lax.Precision.HIGHEST, preferred_element_type=F32)


def halves(v):
    high = v.astype(BF16)
    low = (v - high.astype(F32)).astype(BF16)
    return jnp.concatenate([high, low], axis=1)


def sigmoid(v):
    return 1.0 / (1.0 + jnp.exp(-v))


def softplus(v):
    return jnp.maximum(v, 0.0) + jnp.log1p(jnp.exp(-jnp.abs(v)))


def below(size):
    rows = lax.broadcasted_iota(jnp.int32, (size, size), 0)
    columns = lax.broadcasted_iota(jnp.int32, (size, size), 1)
    return rows >= columns


def head_column(table, head):
    return pltpu.roll(table, LANES - head, axis=1)[:, 0:1]


def conv_total(padded, taps, masks, at, wide, width):
    total = taps[4:5, pl.ds(at, wide)] + taps[3:4, pl.ds(at, wide)] * padded[EDGE:EDGE + width, pl.ds(at, wide)]
    for back in range(1, 4):
        tap = taps[3 - back:4 - back, pl.ds(at, wide)]
        total = total + (masks[back - 1] * tap) * padded[EDGE - back:EDGE - back + width, pl.ds(at, wide)]
    return total


def conv_kernel(inner, mixed, edge, marks, taps, rates, spread, act, sizes, sums, sums_t, state, factor, padded):
    width, channels = mixed.shape[1], padded.shape[1]
    padded[0:EDGE, :] = edge[0, :, 0:channels].astype(F32)
    padded[EDGE:EDGE + width, :] = mixed[0, :, 0:channels].astype(F32)
    marks_now = marks[0]
    masks = [marks_now[:, back:back + 1] for back in range(3)]
    wide = 256
    for at in range(0, channels, wide):
        total = conv_total(padded, taps, masks, at, wide, width)
        act[0, :, pl.ds(at, wide)] = (total * sigmoid(total)).astype(BF16)
    size = softplus(mixed[0, :, channels:].astype(F32) + rates[0:1, :])
    tri = jnp.where(below(width), 1.0, 0.0).astype(F32)
    total_sum = dot_exact(tri, size * rates[1:2, :])
    last = total_sum[width - 1:width]
    sizes[0] = size
    sums[0] = total_sum
    sums_t[0] = total_sum.T[0:sums_t.shape[1]]
    weight = halves(marks_now[:, 4:5] * jnp.exp(last - total_sum) * size)
    gone = marks_now[width - 1:width, 3:4] * jnp.exp(last)
    gone = halves(jnp.broadcast_to(gone, (FACTOR_ROWS, LANES)))
    states = (channels - inner) // 2
    keys_t = act[0, :, inner:inner + states].T
    for at in range(0, inner, wide):
        part = spread[:, pl.ds(at, wide)]
        weighted = (dot(weight, part) * act[0, :, pl.ds(at, wide)].astype(F32)).astype(BF16)
        state[0, 0:states, pl.ds(at, wide)] = dot(keys_t, weighted).astype(BF16)
        fade = dot(gone, part).astype(BF16)
        state[0, states:, pl.ds(at, wide)] = fade
        factor[0, :, pl.ds(at, wide)] = fade


def intra_kernel(inner, heads, act, sizes, sums, sums_t, marks, row_marks, skip, spread, out, scores, stepped):
    width = act.shape[1]
    states = (act.shape[2] - inner) // 2
    half = width // 2
    keys = act[0, :, inner:inner + states]
    queries = act[0, :, inner + states:]
    same = below(width) & (marks[0][:, 5:6] == row_marks[0, 0:1, :])
    scores[...] = jnp.where(same, dot_nt(queries, keys), 0.0)
    size = halves(sizes[0])
    wide = 256
    for at in range(0, inner, wide):
        part = dot(size, spread[:, pl.ds(at, wide)])
        stepped[:, pl.ds(at, wide)] = (part * act[0, :, pl.ds(at, wide)].astype(F32)).astype(BF16)
    per = LANES // (inner // heads)
    span = inner // heads
    lane = lax.broadcasted_iota(jnp.int32, (width, LANES), 1)

    def group(at, carry):
        place = pl.ds(pl.multiple_of(at * LANES, LANES), LANES)
        x = stepped[:, place]
        y_low = y_high = None
        for i in range(per):
            head = at * per + i
            column = head_column(sums[0], head)
            row = sums_t[0, pl.ds(head, 1), :]
            mine = (lane >= i * span) & (lane < (i + 1) * span)
            xh = jnp.where(mine, x, jnp.zeros_like(x))
            w_low = scores[0:half, 0:half] * jnp.exp(jnp.minimum(column[0:half] - row[:, 0:half], 0.0))
            w_high = scores[half:, :] * jnp.exp(jnp.minimum(column[half:] - row, 0.0))
            a = dot(w_low.astype(BF16), xh[0:half])
            b = dot(w_high.astype(BF16), xh)
            y_low = a if y_low is None else y_low + a
            y_high = b if y_high is None else y_high + b
        values = act[0, :, place].astype(F32) * skip[0:1, place]
        out[0, 0:half, place] = (y_low + values[0:half]).astype(out.dtype)
        out[0, half:, place] = (y_high + values[half:]).astype(out.dtype)
        return carry

    lax.fori_loop(0, inner // LANES, group, 0, unroll=2)


def entered_part(at, later_core, before, partner, other, place):
    states = before.shape[0]
    chip = before[:, place]
    core = jnp.full(chip.shape, at[0], jnp.int32)
    chip = jnp.where(core == pl.program_id(0), chip.astype(F32), partner[:, place].astype(F32))
    through = other[0, states:states + 1, place].astype(F32) * chip + other[0, 0:states, place].astype(F32)
    return jnp.where(core == later_core, through, chip).astype(BF16)


def post_kernel(inner, at, part_mixed, act, before, partner, other, sums, marks, gate, gain, spread, mixed, gated, entering, kept):
    states = (act.shape[2] - inner) // 2
    queries = act[0, :, inner + states:]
    enter = halves(marks[0][:, 3:4] * jnp.exp(sums[0]))
    wide = 256
    square = None
    for start in range(0, inner, wide):
        place = pl.ds(start, wide)
        state = entered_part(at, 1, before, partner, other, place)
        entering[0, :, place] = state
        whole = part_mixed[0, :, place].astype(F32) + dot(enter, spread[:, place]) * dot(queries, state)
        g = gate[0, :, place].astype(F32)
        w = whole * (g * sigmoid(g))
        mixed[0, :, place] = whole.astype(BF16)
        kept[:, place] = w
        square = w * w if square is None else square + w * w
    scale = lax.rsqrt(jnp.sum(square, axis=1, keepdims=True) / inner + EPSILON)
    for at in range(0, inner, wide):
        place = pl.ds(at, wide)
        gated[0, :, place] = (kept[:, place] * scale * gain[0:1, place]).astype(BF16)


def gate_back_kernel(
    inner, grad, grad_low, factor, mixed, gate, gain, act, state, sums, marks, spread,
    d_mixed, d_gate, d_state, d_queries, d_sums, row_grads, kept,
):
    states = (act.shape[2] - inner) // 2
    queries = act[0, :, inner + states:]
    queries_t = queries.T
    wide = 256

    @pl.when(pl.program_id(0) == 0)
    def _():
        row_grads[...] = jnp.zeros_like(row_grads)

    square = cross = None
    for at in range(0, inner, wide):
        place = pl.ds(at, wide)
        g = gate[0, :, place].astype(F32)
        w = mixed[0, :, place].astype(F32) * (g * sigmoid(g))
        gg = grad[0, :, place].astype(F32)
        kept[:, place] = w
        square = w * w if square is None else square + w * w
        more = w * gain[0:1, place] * gg
        cross = more if cross is None else cross + more
    scale = lax.rsqrt(jnp.sum(square, axis=1, keepdims=True) / inner + EPSILON)
    pulled = scale * scale * scale * (jnp.sum(cross, axis=1, keepdims=True) / inner)
    entered = marks[0][:, 3:4] * jnp.exp(sums[0])
    enter = halves(entered)
    grad_enter = dq = None
    for at in range(0, inner, wide):
        place = pl.ds(at, wide)
        g = gate[0, :, place].astype(F32)
        sig = sigmoid(g)
        silu = g * sig
        gg = grad[0, :, place].astype(F32)
        w = kept[:, place]
        whole = mixed[0, :, place].astype(F32)
        dw = scale * (gain[0:1, place] * gg) - pulled * w
        row_grads[0:1, place] += jnp.sum(gg * w * scale, axis=0, keepdims=True)
        dm = dw * silu
        d_gate[0, :, place] = (dw * whole * (sig + silu * (1.0 - sig))).astype(BF16)
        d_mixed[0, :, place] = dm.astype(BF16)
        row_grads[1:2, place] += jnp.sum(dm * act[0, :, place].astype(F32), axis=0, keepdims=True)
        part = spread[:, place]
        st = state[0, :, place]
        e = (dm * dot(enter, part)).astype(BF16)
        d_state[0, 0:states, place] = dot(queries_t, e).astype(BF16)
        more_q = dot_nt(e, st)
        dq = more_q if dq is None else dq + more_q
        through = (dm * dot(queries, st)).astype(BF16)
        more_e = dot_nt(through, part[0:LANES])
        grad_enter = more_e if grad_enter is None else grad_enter + more_e
    d_queries[0] = dq
    d_sums[0] = grad_enter * entered
    d_gate[0, :, inner:] = grad_low[0]
    d_state[0, states:, :] = factor[0]


def intra_back_kernel(
    inner, heads, d_mixed, act, sizes, sums, sums_t, marks, row_marks, spread, d_queries, d_sums,
    d_stepped, d_pair, d_total, scores, d_scores, stepped, sums_rows, sums_columns,
):
    width = act.shape[1]
    states = (act.shape[2] - inner) // 2
    half = width // 2
    keys = act[0, :, inner:inner + states]
    queries = act[0, :, inner + states:]
    rows = lax.broadcasted_iota(jnp.int32, (width, width), 0)
    columns = lax.broadcasted_iota(jnp.int32, (width, width), 1)
    same = (rows <= columns) & (marks[0][:, 5:6] == row_marks[0, 0:1, :])
    scores[...] = jnp.where(same, dot_nt(keys, queries), 0.0)
    d_scores[...] = jnp.zeros_like(d_scores)
    sums_rows[...] = jnp.zeros_like(sums_rows)
    sums_columns[...] = jnp.zeros_like(sums_columns)
    size = halves(sizes[0])
    wide = 256
    for at in range(0, inner, wide):
        part = dot(size, spread[:, pl.ds(at, wide)])
        stepped[:, pl.ds(at, wide)] = (part * act[0, :, pl.ds(at, wide)].astype(F32)).astype(BF16)
    per = LANES // (inner // heads)
    span = inner // heads
    lane = lax.broadcasted_iota(jnp.int32, (width, LANES), 1)

    eighth = lax.broadcasted_iota(jnp.int32, (8, width), 0)

    def group(at, carry):
        place = pl.ds(pl.multiple_of(at * LANES, LANES), LANES)
        x = stepped[:, place]
        dy = d_mixed[0, :, place]
        dx_low = dx_high = None
        for i in range(per):
            head = at * per + i
            column = head_column(sums[0], head)
            row = sums_t[0, pl.ds(head, 1), :]
            mine = (lane >= i * span) & (lane < (i + 1) * span)
            xh = jnp.where(mine, x, jnp.zeros_like(x))
            dyh = jnp.where(mine, dy, jnp.zeros_like(dy))
            l_low = jnp.exp(jnp.minimum(row - column[0:half], 0.0))
            l_high = jnp.exp(jnp.minimum(row[:, half:] - column[half:], 0.0))
            w_low = scores[0:half, :] * l_low
            w_high = scores[half:, half:] * l_high
            dw_low = dot_nt(xh[0:half], dy)
            dw_high = dot_nt(xh[half:], dy[half:])
            d_scores[0:half, :] += dw_low * l_low
            d_scores[half:, half:] += dw_high * l_high
            g_low = dw_low * w_low
            g_high = dw_high * w_high
            over_low = jnp.sum(g_low, axis=0, keepdims=True)
            over_high = jnp.sum(g_high, axis=0, keepdims=True)
            eight = pl.ds(pl.multiple_of(head // 8 * 8, 8), 8)
            chosen = eighth == head % 8
            sums_rows[eight, :] += jnp.where(chosen, over_low, 0.0)
            sums_rows[eight, half:] += jnp.where(chosen[:, half:], over_high, 0.0)
            here = lane[0:half] == head
            sums_columns[0:half, :] += jnp.where(here, jnp.sum(g_low, axis=1, keepdims=True), 0.0)
            sums_columns[half:, :] += jnp.where(here, jnp.sum(g_high, axis=1, keepdims=True), 0.0)
            a = dot(w_low.astype(BF16), dyh)
            b = dot(w_high.astype(BF16), dyh[half:])
            dx_low = a if dx_low is None else dx_low + a
            dx_high = b if dx_high is None else dx_high + b
        d_stepped[0, 0:half, place] = dx_low.astype(BF16)
        d_stepped[0, half:, place] = dx_high.astype(BF16)
        return carry

    lax.fori_loop(0, inner // LANES, group, 0, unroll=2)
    grad = jnp.where(same, d_scores[...], 0.0).astype(BF16)
    d_pair[0, :, 0:states] = dot(grad, queries)
    d_pair[0, :, states:] = dot(grad.T, keys) + d_queries[0]
    d_total[0] = sums_rows[...].T - sums_columns[...] + d_sums[0]


def conv_back_kernel(
    inner, here, d_stepped, d_mixed, act, mixed_in, edge, marks, taps, rates, skip, sizes, sums, spread,
    d_pair, d_total, before, partner, other, state,
    d_mixed_in, d_edge, tap_grads, head_grads, padded, shifted,
):
    width, channels = mixed_in.shape[1], padded.shape[1]
    states = (channels - inner) // 2
    wide = 256

    @pl.when(pl.program_id(0) == 0)
    def _():
        tap_grads[...] = jnp.zeros_like(tap_grads)
        head_grads[...] = jnp.zeros_like(head_grads)

    padded[0:EDGE, :] = edge[0, :, 0:channels].astype(F32)
    padded[EDGE:EDGE + width, :] = mixed_in[0, :, 0:channels].astype(F32)
    marks_now = marks[0]
    masks = [marks_now[:, back:back + 1] for back in range(3)]
    total_sum = sums[0]
    size = sizes[0]
    last = total_sum[width - 1:width]
    faded = marks_now[:, 4:5] * jnp.exp(last - total_sum)
    weight = faded * size
    weight_pair = halves(weight)
    size_pair = halves(size)
    keys = act[0, :, inner:inner + states]
    for back in range(3):
        shifted[back, 0:EDGE, :] = jnp.zeros((EDGE, wide), F32)
        shifted[back, EDGE + width:, :] = jnp.zeros((EDGE, wide), F32)

    def through_conv(at, d_act):
        place = pl.ds(at, wide)
        total = conv_total(padded, taps, masks, at, wide, width)
        sig = sigmoid(total)
        d = d_act * (sig + total * sig * (1.0 - sig))
        tap_grads[4:5, place] += jnp.sum(d, axis=0, keepdims=True)
        tap_grads[3:4, place] += jnp.sum(d * padded[EDGE:EDGE + width, place], axis=0, keepdims=True)
        back_total = taps[3:4, place] * d
        edge_total = jnp.zeros((EDGE, wide), F32)
        for back in range(1, 4):
            u = masks[back - 1] * d
            tap_grads[3 - back:4 - back, place] += jnp.sum(
                u * padded[EDGE - back:EDGE - back + width, place], axis=0, keepdims=True
            )
            shifted[back - 1, EDGE:EDGE + width, :] = u
            tap = taps[3 - back:4 - back, place]
            back_total = back_total + tap * shifted[back - 1, EDGE + back:EDGE + back + width, :]
            edge_total = edge_total + tap * shifted[back - 1, back:back + EDGE, :]
        d_mixed_in[0, :, place] = back_total.astype(BF16)
        d_edge[0, :, place] = edge_total

    d_keys = d_pair[0, :, 0:states]
    d_size = d_weight = carried = None
    for at in range(0, inner, wide):
        place = pl.ds(at, wide)
        values = act[0, :, place].astype(F32)
        part = spread[:, place]
        ds = entered_part(here, 0, before, partner, other, place)
        wide_weight = dot(weight_pair, part)
        d_weighted = dot(keys, ds)
        dx = d_stepped[0, :, place].astype(F32)
        d_act = dx * dot(size_pair, part) + d_weighted * wide_weight + skip[0:1, place] * d_mixed[0, :, place].astype(F32)
        d_keys = d_keys + dot_nt((wide_weight * values).astype(BF16), ds)
        a = dot_nt((dx * values).astype(BF16), part[0:LANES])
        b = dot_nt((d_weighted * values).astype(BF16), part[0:LANES])
        c = jnp.sum(ds.astype(F32) * state[0, :, place].astype(F32), axis=0, keepdims=True)
        c = dot_nt(jnp.broadcast_to(halves_rows(c), (EDGE, wide)), part[0:LANES])
        d_size = a if d_size is None else d_size + a
        d_weight = b if d_weight is None else d_weight + b
        carried = c if carried is None else carried + c
        through_conv(at, d_act)
    through_conv(inner, jnp.concatenate([d_keys, d_pair[0, :, states:]], axis=1))
    d_size = d_size + d_weight * faded
    pulled = d_weight * weight
    gone = marks_now[width - 1:width, 3:4] * jnp.exp(last)
    at_end = jnp.sum(pulled, axis=0, keepdims=True) + gone * carried[0:1]
    row = lax.broadcasted_iota(jnp.int32, (width, LANES), 0)
    d_sum = d_total[0] - pulled + jnp.where(row == width - 1, at_end, 0.0)
    order = lax.broadcasted_iota(jnp.int32, (width, width), 0) <= lax.broadcasted_iota(jnp.int32, (width, width), 1)
    d_rate = dot_exact(jnp.where(order, 1.0, 0.0).astype(F32), d_sum)
    d_size = d_size + d_rate * rates[1:2, :]
    d_step = d_size * sigmoid(mixed_in[0, :, channels:].astype(F32) + rates[0:1, :])
    d_mixed_in[0, :, channels:] = d_step.astype(BF16)
    head_grads[0:1, :] += jnp.sum(d_step, axis=0, keepdims=True)
    head_grads[1:2, :] += jnp.sum(d_rate * size * rates[1:2, :], axis=0, keepdims=True)


def halves_rows(v):
    return v.astype(BF16)


def without(kernel, first, count):
    def run(*refs):
        return kernel(*refs[:first], *refs[first + count:])

    return run


def call(kernel, batch, ins, outs, scratch, name, micros, at=None, after=()):
    def spec(shape, whole):
        block = tuple(shape) if whole else (1,) + tuple(shape[1:])
        if whole:
            return pl.BlockSpec(block, lambda b: (0,) * len(block))
        return pl.BlockSpec(block, lambda b: (b,) + (0,) * (len(block) - 1))

    arrays = [a for a, _ in ins]
    in_specs = [spec(a.shape, whole) for a, whole in ins]
    if at is not None:
        arrays, in_specs = [at] + arrays, [pl.BlockSpec(memory_space=pltpu.SMEM)] + in_specs
    return pl.pallas_call(
        without(kernel, len(arrays), len(after)),
        grid=(batch,),
        in_specs=in_specs + [pl.BlockSpec(memory_space=pl.ANY)] * len(after),
        out_specs=[spec(shape, whole) for shape, _, whole in outs],
        out_shape=[jax.ShapeDtypeStruct(shape, kind) for shape, kind, _ in outs],
        scratch_shapes=[pltpu.VMEM(shape, kind) for shape, kind in scratch],
        compiler_params=pltpu.CompilerParams(vmem_limit_bytes=VMEM),
        cost_estimate=cost(micros),
        name=name,
    )(*arrays, *after)


def cost(micros):
    return pl.CostEstimate(flops=int(micros * 1.1e9), bytes_accessed=int(micros * 1e6), transcendentals=0)


def whole_call(kernel, arrays, outs, micros, name, at=None, after=(), scratch=()):
    spec = pl.BlockSpec(memory_space=pltpu.VMEM)
    arrays, in_specs = list(arrays), [spec] * len(arrays)
    if at is not None:
        arrays, in_specs = [at] + arrays, [pl.BlockSpec(memory_space=pltpu.SMEM)] + in_specs
    return pl.pallas_call(
        without(kernel, len(arrays), len(after)),
        in_specs=in_specs + [pl.BlockSpec(memory_space=pl.ANY)] * len(after),
        out_specs=[spec] * len(outs),
        out_shape=[jax.ShapeDtypeStruct(shape, kind) for shape, kind in outs],
        scratch_shapes=[pltpu.VMEM(shape, kind) for shape, kind in scratch],
        compiler_params=pltpu.CompilerParams(vmem_limit_bytes=VMEM),
        cost_estimate=cost(micros),
        name=name,
    )(*arrays, *after)


def swap(x, axis, bits):
    return lax.ppermute(x, axis, [(i, i ^ bits) for i in range(lax.axis_size(axis))])


def join_kernel(later_core, at, own, other, joined):
    core = at[0]
    states = own.shape[1] - FACTOR_ROWS
    for start in range(0, own.shape[2], 512):
        place = pl.ds(start, 512)
        mine = own[core, :, place].astype(F32)
        theirs = other[core, :, place].astype(F32)
        later = jnp.full(mine.shape, core, jnp.int32) == later_core
        second = jnp.where(later, mine, theirs)
        first = jnp.where(later, theirs, mine)
        gain = second[states:states + 1]
        joined[0:states, place] = (gain * first[0:states] + second[0:states]).astype(BF16)
        joined[states:, place] = (gain * first[states:]).astype(BF16)


def enter_kernel(count, *refs):
    out = refs[count]
    states = out.shape[0]
    for start in range(0, out.shape[1], 512):
        place = pl.ds(start, 512)
        before = refs[0][0:states, place].astype(F32)
        for got in refs[1:count]:
            before = got[states:states + 1, place].astype(F32) * before + got[0:states, place].astype(F32)
        out[:, place] = before.astype(BF16)


def exchange(own, at, later_core):
    peers = lax.axis_size("seq")
    other = swap(own, "seq", 1)
    joined = whole_call(functools.partial(join_kernel, later_core), [own, other], [(own.shape[1:], BF16)], 2.0, "join_states", at)[0]
    got = []
    for distance in range(peers // 2 - 1, 0, -1):
        step = 2 * distance if later_core == 1 else -2 * distance
        route = [(i, i + step) for i in range(peers) if 0 <= i + step < peers]
        got.append(lax.ppermute(joined, "seq", route))
    return got, other


def entered(got, after):
    shape = (got[0].shape[0] - FACTOR_ROWS, got[0].shape[1])
    before = whole_call(
        functools.partial(enter_kernel, len(got)), got, [(shape, BF16)], 2.0, "enter_states", after=after
    )[0]
    return before, swap(before, "seq", 1)


def gathered(block):
    peers = lax.axis_size("seq")
    rows = block.shape[0] // peers
    share = lax.dynamic_slice_in_dim(block, lax.axis_index("seq") * rows, rows, 0)
    return lax.all_gather(share, ("fsdp", "seq"), axis=0, tiled=True)


def take_in_kernel(columns, block, steps, out):
    first, last, with_steps = columns
    wide = last - first
    out[:, 0:wide] = block[0, :, first:last]
    if with_steps:
        heads = steps.shape[2]
        out[:, wide:] = jnp.zeros((out.shape[0], LANES), BF16)
        out[:, wide:wide + heads] = steps[0]


def take_share(weight, steps, layer, columns, at, share, parts, after):
    first, last, with_steps = columns
    wide = last - first + (LANES if with_steps else 0)

    def rows(i, where):
        return (layer, where[1] * 2 + where[0] if parts > 2 else where[0], 0)

    arrays = [weight] if steps is None else [weight, steps]
    specs = [pl.BlockSpec((1, share, a.shape[2]), rows) for a in arrays]
    kernel = functools.partial(take_in_kernel, columns)
    if steps is None:
        kernel = lambda block, out: take_in_kernel(columns, block, None, out)
    inner_kernel = without(kernel, len(arrays), len(after))
    return pl.pallas_call(
        lambda where, *refs: inner_kernel(*refs),
        grid_spec=pltpu.PrefetchScalarGridSpec(
            num_scalar_prefetch=1,
            grid=(1,),
            in_specs=specs + [pl.BlockSpec(memory_space=pl.ANY)] * len(after),
            out_specs=pl.BlockSpec((share, wide), lambda i, where: (0, 0)),
        ),
        out_shape=jax.ShapeDtypeStruct((share, wide), BF16),
        compiler_params=pltpu.CompilerParams(vmem_limit_bytes=VMEM),
        cost_estimate=cost(1.0),
        name="take_share",
    )(at, *arrays, *after)


def place_rows_kernel(starts, columns, many, at, *refs):
    weight, steps = refs[0], refs[1] if many == 2 else None
    sources, out = refs[many:-1], refs[-1]
    core, chip, group = at[0], at[1], at[2]
    rows = weight.shape[1]
    own = pl.ds(pl.multiple_of(group * rows, rows), rows)
    first, last, with_steps = columns
    wide = last - first
    out[own, 0:wide] = weight[0, :, first:last]
    if with_steps:
        out[own, wide:] = jnp.concatenate([steps[0], jnp.zeros((rows, LANES - steps.shape[2]), BF16)], axis=1)
    for source, index, rows, place in starts:
        start = pl.multiple_of(place(core, chip, group), rows)
        out[pl.ds(start, rows), :] = sources[source][index]


def placed_rows(at, weight, steps, layer, columns, sources, starts, groups, micros):
    whole = pl.BlockSpec(memory_space=pltpu.VMEM)
    own = [weight] if steps is None else [weight, steps]
    first, last, with_steps = columns
    shape = (weight.shape[1] * groups, last - first + (LANES if with_steps else 0))
    return pl.pallas_call(
        functools.partial(place_rows_kernel, starts, columns, len(own)),
        grid=(1,),
        in_specs=[pl.BlockSpec(memory_space=pltpu.SMEM)]
        + [pl.BlockSpec((1,) + a.shape[1:], lambda i: (layer, 0, 0)) for a in own] + [whole] * len(sources),
        out_specs=whole,
        out_shape=jax.ShapeDtypeStruct(shape, BF16),
        compiler_params=pltpu.CompilerParams(vmem_limit_bytes=VMEM),
        cost_estimate=cost(micros),
        name="place_rows",
    )(at, *own, *sources)


def fetched_by_all(weight, steps, layer, columns, at, groups, chips, after):
    rows = weight.shape[1]
    share = rows // (2 * chips)
    mine = take_share(weight, steps, layer, columns, at, share, 2 * chips, after)
    from_z = jnp.stack([swap(mine, "fsdp", e) for e in range(1, groups)])
    sources = [from_z] + [swap(from_z, "seq", 2 * d) for d in range(1, chips)]
    sources.append(swap(jnp.stack(sources), "seq", 1))

    def place_of(d, e, other):
        return lambda core, chip, group: (group ^ e) * rows + (chip ^ d) * (2 * share) + (core ^ other) * share

    starts = []
    for d in range(chips):
        for e in range(1, groups):
            starts.append((d, (e - 1,), share, place_of(d, e, 0)))
            starts.append((chips, (d, e - 1), share, place_of(d, e, 1)))
    return placed_rows(at, weight, steps, layer, columns, sources, starts, groups, 4.0), from_z


def fetched_along_z(weight, layer, at, groups, after):
    rows = weight.shape[1]
    share = rows // 2
    columns = (0, weight.shape[2], False)
    mine = take_share(weight, None, layer, columns, at, share, 2, after)
    from_z = jnp.stack([swap(mine, "fsdp", e) for e in range(1, groups)])
    sources = [from_z, swap(from_z, "seq", 1)]

    def place_of(e, other):
        return lambda core, chip, group: (group ^ e) * rows + (core ^ other) * share

    starts = [(other, (e - 1,), share, place_of(e, other)) for e in range(1, groups) for other in range(2)]
    return placed_rows(at, weight, None, layer, columns, sources, starts, groups, 3.0), from_z


def reduced(grad):
    share = lax.psum_scatter(grad, ("fsdp", "seq"), scatter_dimension=0, tiled=True)
    return lax.all_gather(share, "seq", axis=0, tiled=True).astype(F32)


def turn_kernel(groups, chips, at, gated, low, own, send, turned):
    core, chip, group = at[0], at[1], at[2]
    base = 0
    for x in (gated, low):
        if x is None:
            continue
        total = x.shape[1]
        share = total // (2 * groups * chips)
        for start in range(0, total, 256):
            turned[start:start + 256, :] = x[:, start:start + 256].T
        for other, out in ((0, own), (1, send)):
            for d in range(chips):
                for e in range(groups):
                    start = (group ^ e) * (total // groups) + (chip ^ d) * (2 * share) + (core ^ other) * share
                    to = base + (d * groups + e) * share
                    out[to:to + share, :] = turned[pl.ds(pl.multiple_of(start, share), share), :]
        base += total // 2


def turned_halves(gated, low, at, groups, chips):
    rows = low.shape[0]
    if gated is None:
        def kernel(where, low_ref, *refs):
            turn_kernel(groups, chips, where, None, low_ref, *refs)

        return whole_call(kernel, [low], [((low.shape[1] // 2, rows), BF16)] * 2, 2.0, "turn", at, scratch=[(low.shape[::-1], BF16)])
    half = ((gated.shape[1] + low.shape[1]) // 2, rows)
    return whole_call(
        functools.partial(turn_kernel, groups, chips), [gated, low], [(half, BF16)] * 2, 4.0, "turn", at,
        scratch=[((gated.shape[1], rows), BF16)],
    )


def first_grads_kernel(groups, chips, inner, own, other, grad, grad_other, *outs):
    wide = grad.shape[1] - inner
    total_big = inner // 2
    big = total_big // (groups * chips)
    small = (own.shape[0] - total_big) // (groups * chips)

    def put(total, share, start, at):
        for d in range(chips):
            for e in range(groups):
                block = (d * groups + e) * share
                outs[d][e, start:start + share, pl.ds(at, 512)] = total[block:block + share]

    for at in range(0, wide, 512):
        place = pl.ds(inner + at, 512)
        total = dot(own[0:total_big, :], grad[:, place]) + dot(other[0:total_big, :], grad_other[:, place])
        put(total.astype(BF16), big, 0, at)
    for at in range(0, inner, 512):
        place = pl.ds(at, 512)
        total = dot(own[total_big:, :], grad[:, place]) + dot(other[total_big:, :], grad_other[:, place])
        put(total.astype(BF16), small, big + at // wide * small, at % wide)


def wide_grads_kernel(low, gated, grad, out):
    turned = jnp.where(pl.program_id(1) * jnp.ones(low.shape, jnp.int32) < 2, low[...], gated[...])
    out[...] = dot_tn(turned, grad[...]).astype(BF16)


def wide_grads(low, gated, both, groups):
    rows, model = low.shape
    inner = gated.shape[1]
    cut = model // groups
    halves_of = inner // model
    return pl.pallas_call(
        wide_grads_kernel,
        grid=(groups, 2 * halves_of),
        in_specs=[
            pl.BlockSpec((rows, cut), lambda z, j: (0, z)),
            pl.BlockSpec((rows, cut), lambda z, j: (0, halves_of * z + jnp.maximum(j - halves_of, 0))),
            pl.BlockSpec((rows, model), lambda z, j: (0, jnp.minimum(j, halves_of))),
        ],
        out_specs=pl.BlockSpec((cut, model), lambda z, j: (z, j)),
        out_shape=jax.ShapeDtypeStruct((model, 2 * inner), BF16),
        compiler_params=pltpu.CompilerParams(vmem_limit_bytes=VMEM),
        cost_estimate=cost(10.0),
        name="wide_grads",
    )(low, gated, both)


def second_grads_kernel(groups, chips, channels, heads, here, own, other, grad, grad_other, extra, extra_other, *outs):
    rows = extra.shape[0] // 2
    base = own.shape[0] - rows
    share = rows // (groups * chips)
    core, chip, group = here[0], here[1], here[2]
    lane = lax.broadcasted_iota(jnp.int32, (share, LANES), 1)
    total_wide = channels + LANES
    edges = list(range(0, channels, 512)) + [channels, total_wide]
    for at, end in zip(edges[:-1], edges[1:]):
        place = pl.ds(at, end - at)
        total = dot(own[base:, :], grad[:, place]) + dot(other[base:, :], grad_other[:, place])
        for d in range(chips):
            for e in range(groups):
                block = (d * groups + e) * share
                part = total[block:block + share]
                if at == channels:
                    start = (group ^ e) * (2 * rows // groups) + (chip ^ d) * (2 * share) + core * share
                    here_rows = pl.ds(pl.multiple_of(start, share), share)
                    part = jnp.where(lane < heads, part, extra[here_rows, :] + extra_other[here_rows, :])
                outs[d][e, :, place] = part.astype(BF16)


def add_kernel(count, *refs):
    ins, outs = refs[:count], refs[count:]
    for i, out in enumerate(outs):
        total = ins[0][i].astype(F32)
        for more in ins[1:]:
            total = total + more[i].astype(F32)
        out[...] = total.astype(out.dtype)


def add_last_kernel(first, second, *refs):
    out = refs[-1]
    rows, wide = refs[0].shape[0] if first else 0, out.shape[1]

    def total_of(group, place):
        total = group[0][:, place].astype(F32)
        for more in group[1:]:
            total = total + more[:, place].astype(F32)
        return total.astype(BF16)

    if first:
        out[0:rows, :] = total_of(refs[:first], pl.ds(0, wide))
    seconds = refs[first:first + second]
    share, columns = seconds[0].shape
    for i, at in enumerate(range(0, columns, wide)):
        width = min(wide, columns - at)
        out[rows + i * share:rows + (i + 1) * share, 0:width] = total_of(seconds, pl.ds(at, width))
        if width < wide:
            out[rows + i * share:rows + (i + 1) * share, width:] = jnp.zeros((share, wide - width), BF16)


def first_sums(blocks, axis, after=()):
    parts, rows, columns = blocks[0].shape
    unit = 2 if axis == "seq" else 1
    got = [blocks[0]] + [swap(blocks[i], axis, unit * i) for i in range(1, len(blocks))]
    return whole_call(
        functools.partial(add_kernel, len(got)), got, [((rows, columns), BF16)] * parts, 2.5, "add_first", after=after
    )


def second_parts(shares, axis):
    unit = 2 if axis == "seq" else 1
    return [shares[0]] + [swap(shares[i], axis, unit * i) for i in range(1, len(shares))]


def last_sums(first, second, wide):
    rows = first[0].shape[0] if first else 0
    share, columns = second[0].shape
    total = rows + -(-columns // wide) * share
    return whole_call(
        functools.partial(add_last_kernel, len(first), len(second)), first + second, [((total, wide), BF16)], 2.0, "add_last"
    )[0]


def place_kernel(chips, inner, joined, at, *refs):
    mine, other = refs[:chips], refs[chips]
    in_out, extra_out, out_out = refs[-3:]
    core, chip = at[0], at[1]
    model = other.shape[2]
    big = out_out.shape[1] // (2 * chips)
    share = in_out.shape[1] // (2 * chips)
    channels = in_out.shape[2] - inner
    if joined:
        scattered = refs[chips + 1]
        in_out[0, :, 0:inner] = scattered[:, 0:inner].astype(F32)
        rows = in_out.shape[1]
        for i in range(inner // model):
            out_out[0, i * rows:(i + 1) * rows, :] = scattered[:, inner + i * model:inner + (i + 1) * model].astype(F32)
    for d in range(chips):
        for is_other, part in ((0, mine[d]), (1, other.at[d])):
            start = (chip ^ d) * (2 * share) + (core ^ is_other) * share
            rows = pl.ds(pl.multiple_of(start, share), share)
            at_row = 0
            if not joined:
                big_start = (chip ^ d) * (2 * big) + (core ^ is_other) * big
                out_out[0, pl.ds(pl.multiple_of(big_start, big), big), :] = part[0:big, :].astype(F32)
                at_row = big
                for i in range(inner // model):
                    in_out[0, rows, i * model:(i + 1) * model] = part[at_row:at_row + share, :].astype(F32)
                    at_row += share
            for start_column in range(0, channels, model):
                wide = min(model, channels - start_column)
                to = pl.ds(inner + start_column, wide)
                in_out[0, rows, to] = part[at_row:at_row + share, 0:wide].astype(F32)
                if start_column + model >= channels:
                    extra_out[0, rows, :] = part[at_row:at_row + share, wide:wide + LANES].astype(F32)
                at_row += share


def placed_grads(at, share, scattered, before, layer, layers, shapes, chips, inner):
    mine = [share] + [swap(share, "seq", 2 * d) for d in range(1, chips)]
    pieces = mine + [swap(jnp.stack(mine), "seq", 1)]
    joined = scattered is not None
    pieces += [scattered] if joined else []
    whole = pl.BlockSpec(memory_space=pltpu.VMEM)
    anywhere = pl.BlockSpec(memory_space=pl.ANY)
    before = [] if before is None else list(before)
    outs = [jax.ShapeDtypeStruct((layers,) + shape, F32) for shape in shapes]
    return pl.pallas_call(
        functools.partial(place_kernel, chips, inner, joined),
        grid=(1,),
        in_specs=[pl.BlockSpec(memory_space=pltpu.SMEM)] + [whole] * len(pieces) + [anywhere] * len(before),
        out_specs=[pl.BlockSpec((1,) + shape, lambda i: (layer, 0, 0)) for shape in shapes],
        out_shape=outs,
        input_output_aliases={1 + len(pieces) + i: i for i in range(len(before))},
        compiler_params=pltpu.CompilerParams(vmem_limit_bytes=VMEM),
        cost_estimate=cost(6.0),
        name="place_grads",
    )(at, *pieces, *before)


def norm_scale_of(stream):
    return lax.rsqrt(jnp.mean(stream * stream, axis=-1, keepdims=True) + EPSILON)


def on_device(
    tokens, segments, norm_gain, in_weight, dt_weight, conv_weight, conv_bias, dt_bias, a_log, d_skip,
    gate_gain, out_weight, cotangent,
):
    layers = in_weight.shape[0]
    batch, width, model = tokens.shape
    heads = dt_weight.shape[2]
    taps_len = conv_weight.shape[1]
    peers = lax.axis_size("seq")
    groups = lax.axis_size("fsdp")
    rows = batch * width
    inner = out_weight.shape[1] * groups
    channels = in_weight.shape[2] - inner
    states = (channels - inner) // 2
    span = inner // heads
    chips = peers // 2
    direct = model % (32 * groups * peers) == 0 and chips == 4 and groups == 4
    seq_at = lax.axis_index("seq")
    here = jnp.stack([seq_at % 2, seq_at // 2, lax.axis_index("fsdp")]).astype(jnp.int32)

    small = [norm_gain, conv_weight.reshape(layers, -1), conv_bias, dt_bias, a_log, d_skip, gate_gain]
    sizes = [a.shape[1] for a in small]
    own = jnp.concatenate(small, axis=1)
    if direct:
        by_partner = jnp.stack([own] + [swap(own, "fsdp", e) for e in range(1, groups)])
        packed = jnp.stack([lax.dynamic_index_in_dim(by_partner, here[2] ^ z, 0, keepdims=False) for z in range(groups)])
    else:
        packed = lax.all_gather(own, "fsdp", axis=0)
    pieces, at = [], 0
    for size in sizes:
        pieces.append(packed[:, :, at:at + size])
        at += size

    def joined(piece):
        return jnp.moveaxis(piece, 0, 1).reshape(layers, -1)

    norm_all = joined(pieces[0]).astype(F32)
    taps_all = jnp.moveaxis(pieces[1].reshape(groups, layers, taps_len, -1), 0, 2).reshape(layers, taps_len, channels)
    taps_all = jnp.concatenate(
        [taps_all.astype(F32), joined(pieces[2]).astype(F32)[:, None], jnp.zeros((layers, 8 - taps_len - 1, channels), F32)], axis=1
    )
    pad_heads = ((0, 0), (0, LANES - heads))
    rates_all = jnp.stack(
        [jnp.pad(joined(pieces[3]).astype(F32), pad_heads), jnp.pad(-jnp.exp(joined(pieces[4]).astype(F32)), pad_heads)], axis=1
    )
    rates_all = jnp.pad(rates_all, ((0, 0), (0, 6), (0, 0)))
    skip_all = jnp.broadcast_to(jnp.repeat(joined(pieces[5]).astype(F32), span, axis=1)[:, None], (layers, 8, inner))
    gain_all = jnp.broadcast_to(joined(pieces[6]).astype(F32)[:, None], (layers, 8, inner))

    gate_columns, mix_columns, all_columns = (0, inner, False), (inner, inner + channels, True), (0, inner + channels, True)
    gate_all, mix_all, out_all = [], [], []
    for layer in range(layers):
        if direct and layer == 0:
            mixes, _ = fetched_by_all(in_weight, dt_weight, layer, mix_columns, here, groups, chips, ())
            gates, from_z = fetched_by_all(in_weight, None, layer, gate_columns, here, groups, chips, ())
            outs, _ = fetched_along_z(out_weight, layer, here, groups, (from_z,))
        elif direct:
            share = take_share(in_weight, dt_weight, layer, all_columns, here, model // (groups * peers), peers, ())
            whole = lax.all_gather(share, ("fsdp", "seq"), axis=0, tiled=True)
            gates, mixes = whole[:, :inner], whole[:, inner:]
            share = take_share(out_weight, None, layer, (0, model, False), here, inner // (groups * peers), peers, ())
            outs = lax.all_gather(share, ("fsdp", "seq"), axis=0, tiled=True)
        else:
            steps = jnp.pad(dt_weight[layer], ((0, 0), (0, LANES - heads)))
            whole = gathered(jnp.concatenate([in_weight[layer], steps], axis=1))
            gates, mixes = whole[:, :inner], whole[:, inner:]
            outs = gathered(out_weight[layer])
        gate_all.append(gates)
        mix_all.append(mixes)
        out_all.append(outs)

    numbers = (segments + 1).astype(F32)
    before = lax.ppermute(numbers[:, width - EDGE:], "seq", [(i, i + 1) for i in range(peers - 1)])
    padded = jnp.concatenate([before, numbers], axis=1)
    columns = [padded[:, EDGE - back:EDGE - back + width] == numbers for back in range(1, taps_len)]
    columns += [numbers == before[:, EDGE - 1:], numbers == numbers[:, width - 1:]]
    marks = jnp.stack([c.astype(F32) for c in columns] + [numbers], axis=-1)
    marks = jnp.pad(marks, ((0, 0), (0, 0), (0, LANES - marks.shape[-1])))
    row_marks = jnp.broadcast_to(numbers[:, None, :], (batch, 8, width))
    lane_head = jnp.arange(inner) // span
    spread = (jnp.arange(2 * LANES)[:, None] % LANES == lane_head[None, :]).astype(BF16)

    stream = tokens.astype(F32)
    kept = []
    for layer in range(layers):
        norm_scale = norm_scale_of(stream)
        low = (stream * norm_scale * norm_all[layer]).astype(BF16).reshape(rows, model)
        w_gate, w_mix, w_out = gate_all[layer], mix_all[layer], out_all[layer]
        mixed_in = dot(low, w_mix).astype(BF16).reshape(batch, width, channels + LANES)
        edge = lax.ppermute(mixed_in[:, width - EDGE:], "seq", [(i, i + 1) for i in range(peers - 1)])
        gate = dot(low, w_gate).astype(BF16).reshape(batch, width, inner)
        taps, rates, skip, gain = taps_all[layer], rates_all[layer], skip_all[layer], gain_all[layer]
        act, size, sums, sums_t, state, factor = call(
            functools.partial(conv_kernel, inner), batch,
            [(mixed_in, 0), (edge, 0), (marks, 0), (taps, 1), (rates, 1), (spread, 1)],
            [
                ((batch, width, channels), BF16, 0), ((batch, width, LANES), F32, 0), ((batch, width, LANES), F32, 0),
                ((batch, heads, width), F32, 0), ((batch, states + FACTOR_ROWS, inner), BF16, 0),
                ((batch, FACTOR_ROWS, inner), BF16, 0),
            ],
            [((EDGE + width, channels), F32)], "conv_states", 8.0,
        )
        got, other = exchange(state, here, 1)
        (part,) = call(
            functools.partial(intra_kernel, inner, heads), batch,
            [(act, 0), (size, 0), (sums, 0), (sums_t, 0), (marks, 0), (row_marks, 0), (skip, 1), (spread, 1)],
            [((batch, width, inner), F32, 0)],
            [((width, width), F32), ((width, inner), BF16)], "mix_within", 12.0,
        )
        before, partner = entered(got, (part,))
        mixed, gated, entering = call(
            functools.partial(post_kernel, inner), batch,
            [
                (part, 0), (act, 0), (before, 1), (partner, 1), (other, 0), (sums, 0), (marks, 0), (gate, 0), (gain, 1), (spread, 1),
            ],
            [((batch, width, inner), BF16, 0), ((batch, width, inner), BF16, 0), ((batch, states, inner), BF16, 0)],
            [((width, inner), F32)], "mix_gate", 6.0, here,
        )
        gated = gated.reshape(rows, inner)
        turned = None
        if direct:
            mine, send = turned_halves(gated if layer == 0 else None, low, here, groups, chips)
            turned = (mine, swap(send, "seq", 1))
        kept.append((turned, stream, norm_scale, low, mixed_in, edge, gate, act, size, sums, sums_t, factor, entering, mixed, gated))
        stream = stream + dot(gated, w_out).reshape(batch, width, model)

    grad_stream = cotangent.astype(F32)
    collected, collected_grads, placed, chains = [], [], None, []
    started = ()
    for layer in reversed(range(layers)):
        (turned, entry, norm_scale, low, mixed_in, edge, gate, act, size, sums, sums_t, factor, entering, mixed, gated) = kept[layer]
        w_gate, w_mix, w_out = gate_all[layer], mix_all[layer], out_all[layer]
        taps, rates, skip, gain = taps_all[layer], rates_all[layer], skip_all[layer], gain_all[layer]
        grad_low = grad_stream.astype(BF16).reshape(rows, model)
        grad_gated = dot_nt(grad_low, w_out).astype(BF16).reshape(batch, width, inner)
        d_mixed, d_gate, d_state, d_queries, d_sums, row_grads = call(
            functools.partial(gate_back_kernel, inner), batch,
            [
                (grad_gated, 0), (grad_low.reshape(batch, width, model), 0), (factor, 0), (mixed, 0), (gate, 0), (gain, 1), (act, 0),
                (entering, 0), (sums, 0), (marks, 0), (spread, 1),
            ],
            [
                ((batch, width, inner), BF16, 0), ((batch, width, inner + model), BF16, 0),
                ((batch, states + FACTOR_ROWS, inner), BF16, 0), ((batch, width, states), F32, 0), ((batch, width, LANES), F32, 0), ((8, inner), F32, 1),
            ],
            [((width, inner), F32)], "gate_back", 11.0, after=started,
        )
        got, other = exchange(d_state, here, 0)
        both = d_gate.reshape(rows, inner + model)
        d_gate = both[:, :inner]
        started, arrived = (), ()
        if direct:
            big, small = inner // (groups * peers), model // (groups * peers)
            mine, theirs = turned
            both_other = swap(both, "seq", 1) if layer == 0 else None
            if layer > 0:
                wide = wide_grads(low, gated, both, groups)
                share = lax.psum_scatter(wide, ("fsdp", "seq"), scatter_dimension=0, tiled=True)
                scattered = lax.all_gather(share, "seq", axis=0, tiled=True)
                started = (wide,)
            else:
                scattered = None
        else:
            out_share = reduced(dot_tn(gated, grad_low).astype(BF16))
        d_stepped, d_pair, d_total = call(
            functools.partial(intra_back_kernel, inner, heads), batch,
            [
                (d_mixed, 0), (act, 0), (size, 0), (sums, 0), (sums_t, 0), (marks, 0), (row_marks, 0), (spread, 1),
                (d_queries, 0), (d_sums, 0),
            ],
            [((batch, width, inner), BF16, 0), ((batch, width, 2 * states), F32, 0), ((batch, width, LANES), F32, 0)],
            [
                ((width, width), F32), ((width, width), F32), ((width, inner), BF16), ((LANES, width), F32), ((width, LANES), F32),
            ], "mix_within_back", 17.0, after=started,
        )
        before, partner = entered(got, (d_stepped,))
        if direct and layer == 0:
            first_blocks = whole_call(
                functools.partial(first_grads_kernel, groups, chips, inner), [mine, theirs, both, both_other],
                [((groups, big + inner // model * small, model), BF16)] * chips, 10.0, "first_grads", after=(before,),
            )
            arrived = tuple(first_blocks)
            for chain in chains:
                arrived += tuple(chain)
        d_mixed_in, d_edge, tap_grads, head_grads = call(
            functools.partial(conv_back_kernel, inner), batch,
            [
                (d_stepped, 0), (d_mixed, 0), (act, 0), (mixed_in, 0), (edge, 0), (marks, 0), (taps, 1), (rates, 1),
                (skip, 1), (size, 0), (sums, 0), (spread, 1), (d_pair, 0), (d_total, 0), (before, 1), (partner, 1), (other, 0),
                (entering, 0),
            ],
            [
                ((batch, width, channels + LANES), BF16, 0), ((batch, EDGE, channels), F32, 0),
                ((8, channels), F32, 1), ((8, LANES), F32, 1),
            ],
            [((EDGE + width, channels), F32), ((3, width + 2 * EDGE, 256), F32)], "conv_back", 17.0, here, arrived,
        )
        from_next = lax.ppermute(d_edge.astype(BF16), "seq", [(i + 1, i) for i in range(peers - 1)])
        tail = (d_mixed_in[:, width - EDGE:, :channels].astype(F32) + from_next.astype(F32)).astype(BF16)
        grad_mixed = lax.dynamic_update_slice(d_mixed_in, tail, (0, width - EDGE, 0)).reshape(rows, channels + LANES)
        grad_rows = dot_nt(d_gate, w_gate) + dot_nt(grad_mixed, w_mix)
        grad_rows = grad_rows.reshape(batch, width, model)
        scaled = grad_rows * norm_all[layer]
        inward = jnp.mean(scaled * entry, axis=-1, keepdims=True)
        gain_grad = jnp.sum(grad_rows * entry * norm_scale, axis=(0, 1))
        grad_stream = grad_stream + norm_scale * scaled - (norm_scale * norm_scale * norm_scale * inward) * entry
        skip_grad = jnp.sum(row_grads[1].reshape(heads, span), axis=1)
        small_grads = [
            gain_grad.reshape(groups, -1),
            jnp.moveaxis(tap_grads[:taps_len].reshape(taps_len, groups, -1), 1, 0).reshape(groups, -1),
            tap_grads[taps_len].reshape(groups, -1),
            head_grads[0, :heads].reshape(groups, -1),
            head_grads[1, :heads].reshape(groups, -1),
            skip_grad.reshape(groups, -1),
            row_grads[0].reshape(groups, -1),
        ]
        small_sums = jnp.concatenate(small_grads, axis=1)
        if direct:
            per_row = -(-small_sums.shape[1] * groups // model)
            extra = jnp.pad(small_sums, ((0, 0), (0, per_row * model // groups - small_sums.shape[1]))).reshape(model, per_row)
            extra = jnp.pad(extra, ((0, 0), (heads, LANES - heads - per_row)))
            second_blocks = whole_call(
                functools.partial(second_grads_kernel, groups, chips, channels, heads),
                [mine, theirs, grad_mixed, swap(grad_mixed, "seq", 1), extra, swap(extra, "seq", 1)],
                [((groups, small, channels + LANES), BF16)] * chips, 6.0, "second_grads", here,
            )
            started = tuple(second_blocks)
            second = first_sums(second_blocks, "seq")
            first_last = second_parts(first_sums(first_blocks, "seq"), "fsdp") if layer == 0 else []
            chains.append(second)
            share = last_sums(first_last, second_parts(second, "fsdp"), model)
            shapes = [(model // groups, inner + channels), (model // groups, LANES), (inner // groups, model)]
            placed = placed_grads(here, share, scattered, placed, layer, layers, shapes, chips, inner)
        else:
            mixed_grad = dot_tn(low, grad_mixed)
            in_share = reduced(jnp.concatenate([dot_tn(low, d_gate).astype(BF16), mixed_grad[:, :channels].astype(BF16)], axis=1))
            dt_share = reduced(mixed_grad[:, channels:].astype(BF16))
            collected_grads.append((in_share, dt_share, out_share))
            collected.append(small_sums)
    if direct:
        small_sum = placed[1][:, :, heads:heads + per_row].reshape(layers, -1)
    else:
        placed = [jnp.stack([c[i] for c in collected_grads[::-1]]) for i in range(3)]
        small_sum = lax.psum(jnp.stack(collected[::-1], axis=1), ("fsdp", "seq"))
        small_sum = lax.dynamic_index_in_dim(small_sum, lax.axis_index("fsdp"), 0, keepdims=False)
    pieces, at = [], 0
    for size in sizes:
        pieces.append(small_sum[:, at:at + size])
        at += size
    return (
        stream, grad_stream, pieces[0],
        placed[0],
        placed[1][:, :, :heads],
        pieces[1].reshape(layers, taps_len, -1),
        pieces[2], pieces[3], pieces[4], pieces[5], pieces[6],
        placed[2],
    )


def solution(mesh):
    split = P("fsdp", "seq", None)
    vector = P(None, "fsdp")
    matrix = P(None, "fsdp", None)
    taps = P(None, None, "fsdp")
    return jax.shard_map(
        on_device,
        mesh=mesh,
        in_specs=(
            split, P("fsdp", "seq"), vector, matrix, matrix, taps, vector, vector, vector, vector, vector, matrix, split,
        ),
        out_specs=(
            split, split, vector, matrix, matrix, taps, vector, vector, vector, vector, vector, matrix,
        ),
        check_vma=False,
    )
```

```python
import functools

import jax
import jax.numpy as jnp
from jax import lax
from jax.experimental import pallas as pl
from jax.experimental.pallas import tpu as pltpu
from jax.sharding import PartitionSpec as P

EPSILON = 1e-05
F32, BF16 = jnp.float32, jnp.bfloat16
LANES = 128
EDGE = 8
FACTOR_ROWS = 16
SCALE = 0.25
VMEM = 48 * 1024 * 1024
NT = (((1,), (1,)), ((), ()))
TN = (((0,), (0,)), ((), ()))


def dot(a, b):
    return jnp.dot(a, b, preferred_element_type=F32)


def dot_nt(a, b):
    return lax.dot_general(a, b, NT, preferred_element_type=F32)


def dot_tn(a, b):
    return lax.dot_general(a, b, TN, preferred_element_type=F32)


def dot_exact(a, b):
    return jnp.dot(a, b, precision=lax.Precision.HIGHEST, preferred_element_type=F32)


def halves(v):
    high = v.astype(BF16)
    low = (v - high.astype(F32)).astype(BF16)
    return jnp.concatenate([high, low], axis=1)


def sigmoid(v):
    return 1.0 / (1.0 + jnp.exp(-v))


def softplus(v):
    return jnp.maximum(v, 0.0) + jnp.log1p(jnp.exp(-jnp.abs(v)))


def below(size):
    rows = lax.broadcasted_iota(jnp.int32, (size, size), 0)
    columns = lax.broadcasted_iota(jnp.int32, (size, size), 1)
    return rows >= columns


def head_column(table, head):
    return pltpu.roll(table, LANES - head, axis=1)[:, 0:1]


def conv_total(padded, taps, masks, at, wide, width):
    total = taps[4:5, pl.ds(at, wide)] + taps[3:4, pl.ds(at, wide)] * padded[EDGE:EDGE + width, pl.ds(at, wide)]
    for back in range(1, 4):
        tap = taps[3 - back:4 - back, pl.ds(at, wide)]
        total = total + (masks[back - 1] * tap) * padded[EDGE - back:EDGE - back + width, pl.ds(at, wide)]
    return total


def conv_kernel(inner, mixed, edge, marks, taps, rates, spread, act, sizes, sums, sums_t, state, factor, padded):
    width, channels = mixed.shape[1], padded.shape[1]
    padded[0:EDGE, :] = edge[0, :, 0:channels].astype(F32)
    padded[EDGE:EDGE + width, :] = mixed[0, :, 0:channels].astype(F32)
    marks_now = marks[0]
    masks = [marks_now[:, back:back + 1] for back in range(3)]
    wide = 256
    for at in range(0, channels, wide):
        total = conv_total(padded, taps, masks, at, wide, width)
        act[0, :, pl.ds(at, wide)] = (total * sigmoid(total)).astype(BF16)
    size = softplus(mixed[0, :, channels:].astype(F32) + rates[0:1, :])
    tri = jnp.where(below(width), 1.0, 0.0).astype(F32)
    total_sum = dot_exact(tri, size * rates[1:2, :])
    last = total_sum[width - 1:width]
    sizes[0] = size
    sums[0] = total_sum
    sums_t[0] = total_sum.T[0:sums_t.shape[1]]
    weight = halves(marks_now[:, 4:5] * jnp.exp(last - total_sum) * size)
    gone = marks_now[width - 1:width, 3:4] * jnp.exp(last)
    gone = halves(jnp.broadcast_to(gone, (FACTOR_ROWS, LANES)))
    states = (channels - inner) // 2
    keys_t = act[0, :, inner:inner + states].T
    for at in range(0, inner, wide):
        part = spread[:, pl.ds(at, wide)]
        weighted = (dot(weight, part) * act[0, :, pl.ds(at, wide)].astype(F32)).astype(BF16)
        state[0, 0:states, pl.ds(at, wide)] = dot(keys_t, weighted).astype(BF16)
        fade = dot(gone, part).astype(BF16)
        state[0, states:, pl.ds(at, wide)] = fade
        factor[0, :, pl.ds(at, wide)] = fade


def intra_kernel(inner, heads, act, sizes, sums, sums_t, marks, row_marks, skip, spread, out, scores, stepped):
    width = act.shape[1]
    states = (act.shape[2] - inner) // 2
    half = width // 2
    keys = act[0, :, inner:inner + states]
    queries = act[0, :, inner + states:]
    same = below(width) & (marks[0][:, 5:6] == row_marks[0, 0:1, :])
    scores[...] = jnp.where(same, dot_nt(queries, keys), 0.0)
    size = halves(sizes[0])
    wide = 256
    for at in range(0, inner, wide):
        part = dot(size, spread[:, pl.ds(at, wide)])
        stepped[:, pl.ds(at, wide)] = (part * act[0, :, pl.ds(at, wide)].astype(F32)).astype(BF16)
    per = LANES // (inner // heads)
    span = inner // heads
    lane = lax.broadcasted_iota(jnp.int32, (width, LANES), 1)

    def group(at, carry):
        place = pl.ds(pl.multiple_of(at * LANES, LANES), LANES)
        x = stepped[:, place]
        y_low = y_high = None
        for i in range(per):
            head = at * per + i
            column = head_column(sums[0], head)
            row = sums_t[0, pl.ds(head, 1), :]
            mine = (lane >= i * span) & (lane < (i + 1) * span)
            xh = jnp.where(mine, x, jnp.zeros_like(x))
            w_low = scores[0:half, 0:half] * jnp.exp(jnp.minimum(column[0:half] - row[:, 0:half], 0.0))
            w_high = scores[half:, :] * jnp.exp(jnp.minimum(column[half:] - row, 0.0))
            a = dot(w_low.astype(BF16), xh[0:half])
            b = dot(w_high.astype(BF16), xh)
            y_low = a if y_low is None else y_low + a
            y_high = b if y_high is None else y_high + b
        values = act[0, :, place].astype(F32) * skip[0:1, place]
        out[0, 0:half, place] = (y_low + values[0:half]).astype(out.dtype)
        out[0, half:, place] = (y_high + values[half:]).astype(out.dtype)
        return carry

    lax.fori_loop(0, inner // LANES, group, 0, unroll=2)


def entered_part(at, later_core, before, partner, other, place):
    states = before.shape[0]
    chip = before[:, place]
    core = jnp.full(chip.shape, at[0], jnp.int32)
    chip = jnp.where(core == pl.program_id(0), chip.astype(F32), partner[:, place].astype(F32))
    through = other[0, states:states + 1, place].astype(F32) * chip + other[0, 0:states, place].astype(F32)
    return jnp.where(core == later_core, through, chip).astype(BF16)


def post_kernel(inner, at, part_mixed, act, before, partner, other, sums, marks, gate, gain, spread, mixed, gated, entering, kept):
    states = (act.shape[2] - inner) // 2
    queries = act[0, :, inner + states:]
    enter = halves(marks[0][:, 3:4] * jnp.exp(sums[0]))
    wide = 256
    square = None
    for start in range(0, inner, wide):
        place = pl.ds(start, wide)
        state = entered_part(at, 1, before, partner, other, place)
        entering[0, :, place] = state
        whole = part_mixed[0, :, place].astype(F32) + dot(enter, spread[:, place]) * dot(queries, state)
        g = gate[0, :, place].astype(F32)
        w = whole * (g * sigmoid(g))
        mixed[0, :, place] = whole.astype(BF16)
        kept[:, place] = w
        square = w * w if square is None else square + w * w
    scale = lax.rsqrt(jnp.sum(square, axis=1, keepdims=True) / inner + EPSILON)
    for at in range(0, inner, wide):
        place = pl.ds(at, wide)
        gated[0, :, place] = (kept[:, place] * scale * gain[0:1, place]).astype(BF16)


def gate_back_kernel(
    inner, grad, grad_low, factor, mixed, gate, gain, act, state, sums, marks, spread,
    d_mixed, d_gate, d_state, d_queries, d_sums, row_grads, kept,
):
    states = (act.shape[2] - inner) // 2
    queries = act[0, :, inner + states:]
    queries_t = queries.T
    wide = 256

    @pl.when(pl.program_id(0) == 0)
    def _():
        row_grads[...] = jnp.zeros_like(row_grads)

    square = cross = None
    for at in range(0, inner, wide):
        place = pl.ds(at, wide)
        g = gate[0, :, place].astype(F32)
        w = mixed[0, :, place].astype(F32) * (g * sigmoid(g))
        gg = grad[0, :, place].astype(F32)
        kept[:, place] = w
        square = w * w if square is None else square + w * w
        more = w * gain[0:1, place] * gg
        cross = more if cross is None else cross + more
    scale = lax.rsqrt(jnp.sum(square, axis=1, keepdims=True) / inner + EPSILON)
    pulled = scale * scale * scale * (jnp.sum(cross, axis=1, keepdims=True) / inner)
    entered = marks[0][:, 3:4] * jnp.exp(sums[0])
    enter = halves(entered)
    grad_enter = dq = None
    for at in range(0, inner, wide):
        place = pl.ds(at, wide)
        g = gate[0, :, place].astype(F32)
        sig = sigmoid(g)
        silu = g * sig
        gg = grad[0, :, place].astype(F32)
        w = kept[:, place]
        whole = mixed[0, :, place].astype(F32)
        dw = scale * (gain[0:1, place] * gg) - pulled * w
        row_grads[0:1, place] += jnp.sum(gg * w * scale, axis=0, keepdims=True)
        dm = dw * silu
        d_gate[0, :, place] = (dw * whole * (sig + silu * (1.0 - sig))).astype(BF16)
        d_mixed[0, :, place] = dm.astype(BF16)
        row_grads[1:2, place] += jnp.sum(dm * act[0, :, place].astype(F32), axis=0, keepdims=True)
        part = spread[:, place]
        st = state[0, :, place]
        e = (dm * dot(enter, part)).astype(BF16)
        d_state[0, 0:states, place] = dot(queries_t, e).astype(BF16)
        more_q = dot_nt(e, st)
        dq = more_q if dq is None else dq + more_q
        through = (dm * dot(queries, st)).astype(BF16)
        more_e = dot_nt(through, part[0:LANES])
        grad_enter = more_e if grad_enter is None else grad_enter + more_e
    d_queries[0] = dq
    d_sums[0] = grad_enter * entered
    d_gate[0, :, inner:] = grad_low[0]
    d_state[0, states:, :] = factor[0]


def intra_back_kernel(
    inner, heads, d_mixed, act, sizes, sums, sums_t, marks, row_marks, spread, d_queries, d_sums,
    d_stepped, d_pair, d_total, scores, d_scores, stepped, sums_rows, sums_columns,
):
    width = act.shape[1]
    states = (act.shape[2] - inner) // 2
    half = width // 2
    keys = act[0, :, inner:inner + states]
    queries = act[0, :, inner + states:]
    rows = lax.broadcasted_iota(jnp.int32, (width, width), 0)
    columns = lax.broadcasted_iota(jnp.int32, (width, width), 1)
    same = (rows <= columns) & (marks[0][:, 5:6] == row_marks[0, 0:1, :])
    scores[...] = jnp.where(same, dot_nt(keys, queries), 0.0)
    d_scores[...] = jnp.zeros_like(d_scores)
    sums_rows[...] = jnp.zeros_like(sums_rows)
    sums_columns[...] = jnp.zeros_like(sums_columns)
    size = halves(sizes[0])
    wide = 256
    for at in range(0, inner, wide):
        part = dot(size, spread[:, pl.ds(at, wide)])
        stepped[:, pl.ds(at, wide)] = (part * act[0, :, pl.ds(at, wide)].astype(F32)).astype(BF16)
    per = LANES // (inner // heads)
    span = inner // heads
    lane = lax.broadcasted_iota(jnp.int32, (width, LANES), 1)

    eighth = lax.broadcasted_iota(jnp.int32, (8, width), 0)

    def group(at, carry):
        place = pl.ds(pl.multiple_of(at * LANES, LANES), LANES)
        x = stepped[:, place]
        dy = d_mixed[0, :, place]
        dx_low = dx_high = None
        for i in range(per):
            head = at * per + i
            column = head_column(sums[0], head)
            row = sums_t[0, pl.ds(head, 1), :]
            mine = (lane >= i * span) & (lane < (i + 1) * span)
            xh = jnp.where(mine, x, jnp.zeros_like(x))
            dyh = jnp.where(mine, dy, jnp.zeros_like(dy))
            l_low = jnp.exp(jnp.minimum(row - column[0:half], 0.0))
            l_high = jnp.exp(jnp.minimum(row[:, half:] - column[half:], 0.0))
            w_low = scores[0:half, :] * l_low
            w_high = scores[half:, half:] * l_high
            dw_low = dot_nt(xh[0:half], dy)
            dw_high = dot_nt(xh[half:], dy[half:])
            d_scores[0:half, :] += dw_low * l_low
            d_scores[half:, half:] += dw_high * l_high
            g_low = dw_low * w_low
            g_high = dw_high * w_high
            over_low = jnp.sum(g_low, axis=0, keepdims=True)
            over_high = jnp.sum(g_high, axis=0, keepdims=True)
            eight = pl.ds(pl.multiple_of(head // 8 * 8, 8), 8)
            chosen = eighth == head % 8
            sums_rows[eight, :] += jnp.where(chosen, over_low, 0.0)
            sums_rows[eight, half:] += jnp.where(chosen[:, half:], over_high, 0.0)
            here = lane[0:half] == head
            sums_columns[0:half, :] += jnp.where(here, jnp.sum(g_low, axis=1, keepdims=True), 0.0)
            sums_columns[half:, :] += jnp.where(here, jnp.sum(g_high, axis=1, keepdims=True), 0.0)
            a = dot(w_low.astype(BF16), dyh)
            b = dot(w_high.astype(BF16), dyh[half:])
            dx_low = a if dx_low is None else dx_low + a
            dx_high = b if dx_high is None else dx_high + b
        d_stepped[0, 0:half, place] = dx_low.astype(BF16)
        d_stepped[0, half:, place] = dx_high.astype(BF16)
        return carry

    lax.fori_loop(0, inner // LANES, group, 0, unroll=2)
    grad = jnp.where(same, d_scores[...], 0.0).astype(BF16)
    d_pair[0, :, 0:states] = dot(grad, queries)
    d_pair[0, :, states:] = dot(grad.T, keys) + d_queries[0]
    d_total[0] = sums_rows[...].T - sums_columns[...] + d_sums[0]


def conv_back_kernel(
    inner, here, d_stepped, d_mixed, act, mixed_in, edge, marks, taps, rates, skip, sizes, sums, spread,
    d_pair, d_total, before, partner, other, state,
    d_mixed_in, d_edge, tap_grads, head_grads, padded, shifted,
):
    width, channels = mixed_in.shape[1], padded.shape[1]
    states = (channels - inner) // 2
    wide = 256

    @pl.when(pl.program_id(0) == 0)
    def _():
        tap_grads[...] = jnp.zeros_like(tap_grads)
        head_grads[...] = jnp.zeros_like(head_grads)

    padded[0:EDGE, :] = edge[0, :, 0:channels].astype(F32)
    padded[EDGE:EDGE + width, :] = mixed_in[0, :, 0:channels].astype(F32)
    marks_now = marks[0]
    masks = [marks_now[:, back:back + 1] for back in range(3)]
    total_sum = sums[0]
    size = sizes[0]
    last = total_sum[width - 1:width]
    faded = marks_now[:, 4:5] * jnp.exp(last - total_sum)
    weight = faded * size
    weight_pair = halves(weight)
    size_pair = halves(size)
    keys = act[0, :, inner:inner + states]
    for back in range(3):
        shifted[back, 0:EDGE, :] = jnp.zeros((EDGE, wide), F32)
        shifted[back, EDGE + width:, :] = jnp.zeros((EDGE, wide), F32)

    def through_conv(at, d_act):
        place = pl.ds(at, wide)
        total = conv_total(padded, taps, masks, at, wide, width)
        sig = sigmoid(total)
        d = d_act * (sig + total * sig * (1.0 - sig))
        tap_grads[4:5, place] += jnp.sum(d, axis=0, keepdims=True)
        tap_grads[3:4, place] += jnp.sum(d * padded[EDGE:EDGE + width, place], axis=0, keepdims=True)
        back_total = taps[3:4, place] * d
        edge_total = jnp.zeros((EDGE, wide), F32)
        for back in range(1, 4):
            u = masks[back - 1] * d
            tap_grads[3 - back:4 - back, place] += jnp.sum(
                u * padded[EDGE - back:EDGE - back + width, place], axis=0, keepdims=True
            )
            shifted[back - 1, EDGE:EDGE + width, :] = u
            tap = taps[3 - back:4 - back, place]
            back_total = back_total + tap * shifted[back - 1, EDGE + back:EDGE + back + width, :]
            edge_total = edge_total + tap * shifted[back - 1, back:back + EDGE, :]
        d_mixed_in[0, :, place] = back_total.astype(BF16)
        d_edge[0, :, place] = edge_total

    d_keys = d_pair[0, :, 0:states]
    d_size = d_weight = carried = None
    for at in range(0, inner, wide):
        place = pl.ds(at, wide)
        values = act[0, :, place].astype(F32)
        part = spread[:, place]
        ds = entered_part(here, 0, before, partner, other, place)
        wide_weight = dot(weight_pair, part)
        d_weighted = dot(keys, ds)
        dx = d_stepped[0, :, place].astype(F32)
        d_act = dx * dot(size_pair, part) + d_weighted * wide_weight + skip[0:1, place] * d_mixed[0, :, place].astype(F32)
        d_keys = d_keys + dot_nt((wide_weight * values).astype(BF16), ds)
        a = dot_nt((dx * values).astype(BF16), part[0:LANES])
        b = dot_nt((d_weighted * values).astype(BF16), part[0:LANES])
        c = jnp.sum(ds.astype(F32) * state[0, :, place].astype(F32), axis=0, keepdims=True)
        c = dot_nt(jnp.broadcast_to(halves_rows(c), (EDGE, wide)), part[0:LANES])
        d_size = a if d_size is None else d_size + a
        d_weight = b if d_weight is None else d_weight + b
        carried = c if carried is None else carried + c
        through_conv(at, d_act)
    through_conv(inner, jnp.concatenate([d_keys, d_pair[0, :, states:]], axis=1))
    d_size = d_size + d_weight * faded
    pulled = d_weight * weight
    gone = marks_now[width - 1:width, 3:4] * jnp.exp(last)
    at_end = jnp.sum(pulled, axis=0, keepdims=True) + gone * carried[0:1]
    row = lax.broadcasted_iota(jnp.int32, (width, LANES), 0)
    d_sum = d_total[0] - pulled + jnp.where(row == width - 1, at_end, 0.0)
    order = lax.broadcasted_iota(jnp.int32, (width, width), 0) <= lax.broadcasted_iota(jnp.int32, (width, width), 1)
    d_rate = dot_exact(jnp.where(order, 1.0, 0.0).astype(F32), d_sum)
    d_size = d_size + d_rate * rates[1:2, :]
    d_step = d_size * sigmoid(mixed_in[0, :, channels:].astype(F32) + rates[0:1, :])
    d_mixed_in[0, :, channels:] = d_step.astype(BF16)
    head_grads[0:1, :] += jnp.sum(d_step, axis=0, keepdims=True)
    head_grads[1:2, :] += jnp.sum(d_rate * size * rates[1:2, :], axis=0, keepdims=True)


def halves_rows(v):
    return v.astype(BF16)


def without(kernel, first, count):
    def run(*refs):
        return kernel(*refs[:first], *refs[first + count:])

    return run


def call(kernel, batch, ins, outs, scratch, name, micros, at=None, after=()):
    def spec(shape, whole):
        block = tuple(shape) if whole else (1,) + tuple(shape[1:])
        if whole:
            return pl.BlockSpec(block, lambda b: (0,) * len(block))
        return pl.BlockSpec(block, lambda b: (b,) + (0,) * (len(block) - 1))

    arrays = [a for a, _ in ins]
    in_specs = [spec(a.shape, whole) for a, whole in ins]
    if at is not None:
        arrays, in_specs = [at] + arrays, [pl.BlockSpec(memory_space=pltpu.SMEM)] + in_specs
    return pl.pallas_call(
        without(kernel, len(arrays), len(after)),
        grid=(batch,),
        in_specs=in_specs + [pl.BlockSpec(memory_space=pl.ANY)] * len(after),
        out_specs=[spec(shape, whole) for shape, _, whole in outs],
        out_shape=[jax.ShapeDtypeStruct(shape, kind) for shape, kind, _ in outs],
        scratch_shapes=[pltpu.VMEM(shape, kind) for shape, kind in scratch],
        compiler_params=pltpu.CompilerParams(vmem_limit_bytes=VMEM),
        cost_estimate=cost(micros),
        name=name,
    )(*arrays, *after)


def cost(micros):
    micros = micros * SCALE
    return pl.CostEstimate(flops=int(micros * 1.1e9), bytes_accessed=int(micros * 1e6), transcendentals=0)


def whole_call(kernel, arrays, outs, micros, name, at=None, after=(), scratch=()):
    spec = pl.BlockSpec(memory_space=pltpu.VMEM)
    arrays, in_specs = list(arrays), [spec] * len(arrays)
    if at is not None:
        arrays, in_specs = [at] + arrays, [pl.BlockSpec(memory_space=pltpu.SMEM)] + in_specs
    return pl.pallas_call(
        without(kernel, len(arrays), len(after)),
        in_specs=in_specs + [pl.BlockSpec(memory_space=pl.ANY)] * len(after),
        out_specs=[spec] * len(outs),
        out_shape=[jax.ShapeDtypeStruct(shape, kind) for shape, kind in outs],
        scratch_shapes=[pltpu.VMEM(shape, kind) for shape, kind in scratch],
        compiler_params=pltpu.CompilerParams(vmem_limit_bytes=VMEM),
        cost_estimate=cost(micros),
        name=name,
    )(*arrays, *after)


def swap(x, axis, bits):
    return lax.ppermute(x, axis, [(i, i ^ bits) for i in range(lax.axis_size(axis))])


def join_kernel(later_core, at, own, other, joined):
    core = at[0]
    states = own.shape[1] - FACTOR_ROWS
    for start in range(0, own.shape[2], 512):
        place = pl.ds(start, 512)
        mine = own[core, :, place].astype(F32)
        theirs = other[core, :, place].astype(F32)
        later = jnp.full(mine.shape, core, jnp.int32) == later_core
        second = jnp.where(later, mine, theirs)
        first = jnp.where(later, theirs, mine)
        gain = second[states:states + 1]
        joined[0:states, place] = (gain * first[0:states] + second[0:states]).astype(BF16)
        joined[states:, place] = (gain * first[states:]).astype(BF16)


def enter_kernel(count, *refs):
    out = refs[count]
    states = out.shape[0]
    for start in range(0, out.shape[1], 512):
        place = pl.ds(start, 512)
        before = refs[0][0:states, place].astype(F32)
        for got in refs[1:count]:
            before = got[states:states + 1, place].astype(F32) * before + got[0:states, place].astype(F32)
        out[:, place] = before.astype(BF16)


def exchange(own, at, later_core, after=()):
    peers = lax.axis_size("seq")
    other = swap(own, "seq", 1)
    joined = whole_call(functools.partial(join_kernel, later_core), [own, other], [(own.shape[1:], BF16)], 2.0, "join_states", at, after)[0]
    got = []
    for distance in range(peers // 2 - 1, 0, -1):
        step = 2 * distance if later_core == 1 else -2 * distance
        route = [(i, i + step) for i in range(peers) if 0 <= i + step < peers]
        got.append(lax.ppermute(joined, "seq", route))
    return got, other, joined


def entered(got, after):
    shape = (got[0].shape[0] - FACTOR_ROWS, got[0].shape[1])
    before = whole_call(
        functools.partial(enter_kernel, len(got)), got, [(shape, BF16)], 2.0, "enter_states", after=after
    )[0]
    return before, swap(before, "seq", 1)


def gathered(block):
    peers = lax.axis_size("seq")
    rows = block.shape[0] // peers
    share = lax.dynamic_slice_in_dim(block, lax.axis_index("seq") * rows, rows, 0)
    return lax.all_gather(share, ("fsdp", "seq"), axis=0, tiled=True)


def take_in_kernel(columns, block, steps, out):
    first, last, with_steps = columns
    wide = last - first
    out[:, 0:wide] = block[0, :, first:last]
    if with_steps:
        heads = steps.shape[2]
        out[:, wide:] = jnp.zeros((out.shape[0], LANES), BF16)
        out[:, wide:wide + heads] = steps[0]


def take_share(weight, steps, layer, columns, at, share, parts, after):
    first, last, with_steps = columns
    wide = last - first + (LANES if with_steps else 0)

    def rows(i, where):
        return (layer, where[1] * 2 + where[0] if parts > 2 else where[0], 0)

    arrays = [weight] if steps is None else [weight, steps]
    specs = [pl.BlockSpec((1, share, a.shape[2]), rows) for a in arrays]
    kernel = functools.partial(take_in_kernel, columns)
    if steps is None:
        kernel = lambda block, out: take_in_kernel(columns, block, None, out)
    inner_kernel = without(kernel, len(arrays), len(after))
    return pl.pallas_call(
        lambda where, *refs: inner_kernel(*refs),
        grid_spec=pltpu.PrefetchScalarGridSpec(
            num_scalar_prefetch=1,
            grid=(1,),
            in_specs=specs + [pl.BlockSpec(memory_space=pl.ANY)] * len(after),
            out_specs=pl.BlockSpec((share, wide), lambda i, where: (0, 0)),
        ),
        out_shape=jax.ShapeDtypeStruct((share, wide), BF16),
        compiler_params=pltpu.CompilerParams(vmem_limit_bytes=VMEM),
        cost_estimate=cost(1.0),
        name="take_share",
    )(at, *arrays, *after)


def place_rows_kernel(starts, columns, many, at, *refs):
    weight, steps = refs[0], refs[1] if many == 2 else None
    sources, out = refs[many:-1], refs[-1]
    core, chip, group = at[0], at[1], at[2]
    rows = weight.shape[1]
    own = pl.ds(pl.multiple_of(group * rows, rows), rows)
    first, last, with_steps = columns
    wide = last - first
    out[own, 0:wide] = weight[0, :, first:last]
    if with_steps:
        out[own, wide:] = jnp.concatenate([steps[0], jnp.zeros((rows, LANES - steps.shape[2]), BF16)], axis=1)
    for source, index, rows, place in starts:
        start = pl.multiple_of(place(core, chip, group), rows)
        out[pl.ds(start, rows), :] = sources[source][index]


def placed_rows(at, weight, steps, layer, columns, sources, starts, groups, micros, after=()):
    whole = pl.BlockSpec(memory_space=pltpu.VMEM)
    own = [weight] if steps is None else [weight, steps]
    first, last, with_steps = columns
    shape = (weight.shape[1] * groups, last - first + (LANES if with_steps else 0))
    return pl.pallas_call(
        without(functools.partial(place_rows_kernel, starts, columns, len(own)), 1 + len(own) + len(sources), len(after)),
        grid=(1,),
        in_specs=[pl.BlockSpec(memory_space=pltpu.SMEM)]
        + [pl.BlockSpec((1,) + a.shape[1:], lambda i: (layer, 0, 0)) for a in own] + [whole] * len(sources)
        + [pl.BlockSpec(memory_space=pl.ANY)] * len(after),
        out_specs=whole,
        out_shape=jax.ShapeDtypeStruct(shape, BF16),
        compiler_params=pltpu.CompilerParams(vmem_limit_bytes=VMEM),
        cost_estimate=cost(micros),
        name="place_rows",
    )(at, *own, *sources, *after)


def stack_kernel(count, *refs):
    out, row = refs[count], 0
    for ref in refs[:count]:
        if len(ref.shape) == 2:
            out[row] = ref[...]
            row += 1
        else:
            out[row:row + ref.shape[0]] = ref[...]
            row += ref.shape[0]


def stacked(blocks, after=()):
    many = sum(1 if b.ndim == 2 else b.shape[0] for b in blocks)
    return whole_call(
        functools.partial(stack_kernel, len(blocks)), blocks, [((many,) + blocks[0].shape[-2:], BF16)], 1.0, "stack", after=after
    )[0]


def unfold_kernel(share, folded, out):
    many = folded.shape[1] // out.shape[1]
    model = out.shape[1]
    for block in range(folded.shape[0] // share):
        for i in range(many):
            to = (block * many + i) * share
            out[to:to + share, :] = folded[block * share:(block + 1) * share, i * model:(i + 1) * model]


def unfolded(whole, inner, model, share):
    rows = whole.shape[0] // 4
    return pl.pallas_call(
        functools.partial(unfold_kernel, share),
        grid=(4,),
        in_specs=[pl.BlockSpec((rows, inner), lambda i: (i, 0))],
        out_specs=pl.BlockSpec((rows * inner // model, model), lambda i: (i, 0)),
        out_shape=jax.ShapeDtypeStruct((inner, model), BF16),
        compiler_params=pltpu.CompilerParams(vmem_limit_bytes=VMEM),
        cost_estimate=cost(3.0),
        name="unfold",
    )(whole)


def from_along_z(mine, groups, after=()):
    return stacked([swap(mine, "fsdp", e) for e in range(1, groups)], after)


def fetched_by_all(weight, steps, layer, columns, at, groups, chips, from_z, place_after=()):
    rows = weight.shape[1]
    share = rows // (2 * chips)
    sources = [from_z] + [swap(from_z, "seq", 2 * d) for d in range(1, chips)]
    sources.append(swap(stacked([a.reshape(-1, a.shape[2]) for a in sources]), "seq", 1))

    def place_of(d, e, other):
        return lambda core, chip, group: (group ^ e) * rows + (chip ^ d) * (2 * share) + (core ^ other) * share

    starts = []
    for d in range(chips):
        for e in range(1, groups):
            index = e - 1
            starts.append((d, (index,), share, place_of(d, e, 0)))
            starts.append((chips, (d, slice(index * share, (index + 1) * share)), share, place_of(d, e, 1)))
    return placed_rows(at, weight, steps, layer, columns, sources, starts, groups, 4.0, place_after)


def reduced(grad):
    share = lax.psum_scatter(grad, ("fsdp", "seq"), scatter_dimension=0, tiled=True)
    return lax.all_gather(share, "seq", axis=0, tiled=True).astype(F32)


def turn_kernel(groups, chips, at, gated, low, own, send, turned):
    core, chip, group = at[0], at[1], at[2]
    base = 0
    for x in (gated, low):
        if x is None:
            continue
        total = x.shape[1]
        share = total // (2 * groups * chips)
        for start in range(0, total, 256):
            turned[start:start + 256, :] = x[:, start:start + 256].T
        for other, out in ((0, own), (1, send)):
            for d in range(chips):
                for e in range(groups):
                    start = (group ^ e) * (total // groups) + (chip ^ d) * (2 * share) + (core ^ other) * share
                    to = base + (d * groups + e) * share
                    out[to:to + share, :] = turned[pl.ds(pl.multiple_of(start, share), share), :]
        base += total // 2


def turned_halves(gated, low, at, groups, chips):
    rows = low.shape[0]
    if gated is None:
        def kernel(where, low_ref, *refs):
            turn_kernel(groups, chips, where, None, low_ref, *refs)

        return whole_call(kernel, [low], [((low.shape[1] // 2, rows), BF16)] * 2, 2.0, "turn", at, scratch=[(low.shape[::-1], BF16)])
    half = ((gated.shape[1] + low.shape[1]) // 2, rows)
    return whole_call(
        functools.partial(turn_kernel, groups, chips), [gated, low], [(half, BF16)] * 2, 4.0, "turn", at,
        scratch=[((gated.shape[1], rows), BF16)],
    )


def first_grads_kernel(groups, chips, inner, own, other, grad, grad_other, *outs):
    wide = grad.shape[1] - inner
    total_big = inner // 2
    big = total_big // (groups * chips)
    small = (own.shape[0] - total_big) // (groups * chips)

    def put(total, share, start, at):
        for d in range(chips):
            for e in range(groups):
                block = (d * groups + e) * share
                outs[d][e, start:start + share, pl.ds(at, 512)] = total[block:block + share]

    for at in range(0, wide, 512):
        place = pl.ds(inner + at, 512)
        total = dot(own[0:total_big, :], grad[:, place]) + dot(other[0:total_big, :], grad_other[:, place])
        put(total.astype(BF16), big, 0, at)
    for at in range(0, inner, 512):
        place = pl.ds(at, 512)
        total = dot(own[total_big:, :], grad[:, place]) + dot(other[total_big:, :], grad_other[:, place])
        put(total.astype(BF16), small, big + at // wide * small, at % wide)


def wide_grads_kernel(low, gated, grad, out):
    cut, model = low.shape[1], grad.shape[1] - out.shape[1] // 2
    inner = out.shape[1] // 2
    turned = low[...].T
    for at in range(0, inner, 512):
        out[:, pl.ds(at, 512)] = dot(turned, grad[:, pl.ds(at, 512)]).astype(BF16)
    for i in range(inner // model):
        turned = gated[:, i * cut:(i + 1) * cut].T
        for at in range(0, model, 512):
            out[:, pl.ds(inner + i * model + at, 512)] = dot(turned, grad[:, pl.ds(inner + at, 512)]).astype(BF16)


def wide_grads(low, gated, both, groups, after):
    rows, model = low.shape
    inner = gated.shape[1]
    cut = model // groups
    return pl.pallas_call(
        without(wide_grads_kernel, 3, len(after)),
        grid=(groups,),
        in_specs=[
            pl.BlockSpec((rows, cut), lambda z: (0, z)),
            pl.BlockSpec((rows, inner // groups), lambda z: (0, z)),
            pl.BlockSpec(both.shape, lambda z: (0, 0)),
        ] + [pl.BlockSpec(memory_space=pl.ANY)] * len(after),
        out_specs=pl.BlockSpec((cut, 2 * inner), lambda z: (z, 0)),
        out_shape=jax.ShapeDtypeStruct((model, 2 * inner), BF16),
        compiler_params=pltpu.CompilerParams(vmem_limit_bytes=VMEM),
        cost_estimate=cost(10.0),
        name="wide_grads",
    )(low, gated, both, *after)


def second_grads_kernel(groups, chips, channels, heads, here, own, other, grad, grad_other, extra, extra_other, *outs):
    rows = extra.shape[0] // 2
    base = own.shape[0] - rows
    share = rows // (groups * chips)
    core, chip, group = here[0], here[1], here[2]
    lane = lax.broadcasted_iota(jnp.int32, (share, LANES), 1)
    total_wide = channels + LANES
    edges = list(range(0, channels, 512)) + [channels, total_wide]
    for at, end in zip(edges[:-1], edges[1:]):
        place = pl.ds(at, end - at)
        total = dot(own[base:, :], grad[:, place]) + dot(other[base:, :], grad_other[:, place])
        for d in range(chips):
            for e in range(groups):
                block = (d * groups + e) * share
                part = total[block:block + share]
                if at == channels:
                    start = (group ^ e) * (2 * rows // groups) + (chip ^ d) * (2 * share) + core * share
                    here_rows = pl.ds(pl.multiple_of(start, share), share)
                    part = jnp.where(lane < heads, part, extra[here_rows, :] + extra_other[here_rows, :])
                outs[d][e, :, place] = part.astype(BF16)


def gather_small_kernel(groups, taps, heads, gain, tap_grads, head_grads, row_grads, spread, out):
    cut = out.shape[0] // groups
    channels, inner = tap_grads.shape[1], row_grads.shape[1]
    skip = row_grads[1:2, :]
    high = skip.astype(BF16)
    low = (skip - high.astype(F32)).astype(BF16)
    ones = spread[0:LANES, :]
    skip = dot_nt(jnp.broadcast_to(high, (8, inner)), ones) + dot_nt(jnp.broadcast_to(low, (8, inner)), ones)
    span, part, few = channels // groups, inner // groups, heads // groups
    for z in range(groups):
        rows = [jnp.zeros((heads, cut), F32), gain[0:1, z * cut:(z + 1) * cut]]
        for at in range(0, part, cut):
            rows.append(row_grads[0:1, z * part + at:z * part + at + cut])
        for at in range(0, span, cut):
            wide = min(cut, span - at)
            block = tap_grads[0:taps + 1, z * span + at:z * span + at + wide]
            if wide < cut:
                block = jnp.concatenate([block, jnp.zeros((taps + 1, cut - wide), F32)], axis=1)
            rows.append(block)
        lane = lax.broadcasted_iota(jnp.int32, (1, LANES), 1)
        for row in (head_grads[0:1, :], head_grads[1:2, :], skip[0:1, :]):
            row = pltpu.roll(row, (LANES - z * few) % LANES, axis=1) if z else row
            row = jnp.where(lane < few, row, 0.0)
            rows.append(jnp.concatenate([row] + [jnp.zeros((1, cut - LANES), F32)], axis=1))
        table = jnp.concatenate(rows, axis=0)
        table = jnp.concatenate([table, jnp.zeros((LANES - table.shape[0], cut), F32)], axis=0)
        out[z * cut:(z + 1) * cut, :] = table.T


def add_kernel(count, *refs):
    ins, outs = refs[:count], refs[count:]
    for i, out in enumerate(outs):
        total = ins[0][i].astype(F32)
        for more in ins[1:]:
            total = total + more[i].astype(F32)
        out[...] = total.astype(out.dtype)


def halve_kernel(count, *refs):
    ins, (near, far) = refs[:count], refs[count:]
    half = near.shape[0]
    for i in range(2 * half):
        total = ins[0][i].astype(F32)
        for more in ins[1:]:
            total = total + more[i].astype(F32)
        if i < half:
            near[i] = total.astype(BF16)
        else:
            far[i - half] = total.astype(BF16)


def lay_kernel(count, layers, *refs):
    out = refs[-1]
    wide = out.shape[1]
    share, columns = refs[0].shape[0] // layers, refs[0].shape[1]
    row = 0
    for layer in range(layers):
        rows = slice(layer * share, (layer + 1) * share)
        for at in range(0, columns, wide):
            width = min(wide, columns - at)
            total = refs[0][rows, at:at + width].astype(F32)
            for more in refs[1:count]:
                total = total + more[rows, at:at + width].astype(F32)
            out[row:row + share, 0:width] = total.astype(BF16)
            if width < wide:
                out[row:row + share, width:] = jnp.zeros((share, wide - width), BF16)
            row += share


def plane_parts(blocks):
    return [blocks[0]] + [swap(blocks[i], "seq", 2 * i) for i in range(1, len(blocks))]


def halved_sums(got, groups):
    parts, rows, columns = got[0].shape
    after = ()
    while parts > 1:
        half = parts // 2
        near, far = whole_call(
            functools.partial(halve_kernel, len(got)), got, [((half, rows, columns), BF16)] * 2, 2.0, "add_halves"
        )
        if parts == groups:
            after = (near,)
        got = [near, swap(far, "fsdp", half)]
        parts = half
    return whole_call(functools.partial(add_kernel, 2), got, [((rows, columns), BF16)], 1.0, "add_halves")[0], after


def laid(got, wide, after):
    rows, columns = got[0].shape
    shape = (-(-columns // wide) * rows, wide)
    return whole_call(functools.partial(lay_kernel, len(got), 1), got, [(shape, BF16)], 2.0, "lay_sums", after=after)[0]


def layer_sums(got, groups, wide, after):
    parts, rows, columns = got[0].shape
    shares = whole_call(functools.partial(add_kernel, len(got)), got, [((rows, columns), BF16)] * parts, 2.0, "add_plane")
    return laid([shares[0]] + [swap(shares[e], "fsdp", e) for e in range(1, groups)], wide, after)


def spread_in_plane(share, chips):
    mine = [share] + [swap(share, "seq", 2 * d) for d in range(1, chips)]
    return mine, swap(stacked(mine), "seq", 1)


def place_kernel(chips, inner, layers, at, *refs):
    mine_a, other_a = refs[:chips], refs[chips]
    mine_b, other_b = refs[chips + 1:2 * chips + 1], refs[2 * chips + 1]
    scattered = refs[2 * chips + 2:2 * chips + 1 + layers]
    in_out, extra_out, out_out, norm_out, taps_out, bias_out, heads_out, gain_out, extra = refs[-9:]
    core, chip = at[0], at[1]
    model = other_a.shape[2]
    rows_in, rows_out = in_out.shape[1], out_out.shape[1]
    big, share = rows_out // (2 * chips), rows_in // (2 * chips)
    channels = in_out.shape[2] - inner
    for layer in range(layers):
        @pl.when(pl.program_id(0) == layer)
        def _():
            if layer:
                wide = scattered[layer - 1]
                in_out[0, :, 0:inner] = wide[:, 0:inner].astype(F32)
                for i in range(inner // model):
                    out_out[0, i * rows_in:(i + 1) * rows_in, :] = wide[:, inner + i * model:inner + (i + 1) * model].astype(F32)
            for d in range(chips):
                for is_other in range(2):
                    a, b = (other_a.at[d], other_b.at[d]) if is_other else (mine_a[d], mine_b[d])
                    start = (chip ^ d) * (2 * share) + (core ^ is_other) * share
                    rows = pl.ds(pl.multiple_of(start, share), share)
                    if not layer:
                        start = (chip ^ d) * (2 * big) + (core ^ is_other) * big
                        out_out[0, pl.ds(pl.multiple_of(start, big), big), :] = a[0:big, :].astype(F32)
                        for i in range(inner // model):
                            first = big + i * share
                            in_out[0, rows, i * model:(i + 1) * model] = a[first:first + share, :].astype(F32)
                    first = layer * (b.shape[0] // layers)
                    for column in range(0, channels + LANES, model):
                        wide = min(model, channels - column)
                        in_out[0, rows, pl.ds(inner + column, wide)] = b[first:first + share, 0:wide].astype(F32)
                        if column + model >= channels:
                            extra[rows, :] = b[first:first + share, wide:wide + LANES].astype(F32)
                        first += share
            extra_out[0] = extra[:, 0:extra_out.shape[2]]
            table = extra[...].T
            heads = extra_out.shape[2]
            taps, span, part = taps_out.shape[1], taps_out.shape[2], gain_out.shape[1]
            norm_out[layer:layer + 1, :] = table[heads:heads + 1]
            row = heads + 1
            for start in range(0, part, rows_in):
                gain_out[layer:layer + 1, start:start + rows_in] = table[row:row + 1]
                row += 1
            for start in range(0, span, rows_in):
                wide = min(rows_in, span - start)
                taps_out[layer, :, start:start + wide] = table[row:row + taps, 0:wide]
                bias_out[layer:layer + 1, start:start + wide] = table[row + taps:row + taps + 1, 0:wide]
                row += taps + 1
            few = heads_out.shape[2]
            heads_out[layer] = table[row:row + 3, 0:few]


def placed_grads(at, pieces, layers, shapes, smalls, chips, inner, after):
    whole = pl.BlockSpec(memory_space=pltpu.VMEM)
    return pl.pallas_call(
        without(functools.partial(place_kernel, chips, inner, layers), 1 + len(pieces), len(after)),
        grid=(layers,),
        in_specs=[pl.BlockSpec(memory_space=pltpu.SMEM)] + [whole] * len(pieces)
        + [pl.BlockSpec(memory_space=pl.ANY)] * len(after),
        out_specs=[pl.BlockSpec((1,) + shape, lambda i: (i, 0, 0)) for shape in shapes]
        + [pl.BlockSpec(shape, lambda i, n=len(shape): (0,) * n) for shape in smalls],
        out_shape=[jax.ShapeDtypeStruct((layers,) + shape, F32) for shape in shapes] + [jax.ShapeDtypeStruct(shape, F32) for shape in smalls],
        scratch_shapes=[pltpu.VMEM((shapes[0][0], LANES), F32)],
        compiler_params=pltpu.CompilerParams(vmem_limit_bytes=VMEM),
        cost_estimate=cost(8.0),
        name="place_grads",
    )(at, *pieces, *after)


def norm_scale_of(stream):
    return lax.rsqrt(jnp.mean(stream * stream, axis=-1, keepdims=True) + EPSILON)


def on_device(
    tokens, segments, norm_gain, in_weight, dt_weight, conv_weight, conv_bias, dt_bias, a_log, d_skip,
    gate_gain, out_weight, cotangent,
):
    layers = in_weight.shape[0]
    batch, width, model = tokens.shape
    heads = dt_weight.shape[2]
    taps_len = conv_weight.shape[1]
    peers = lax.axis_size("seq")
    groups = lax.axis_size("fsdp")
    rows = batch * width
    inner = out_weight.shape[1] * groups
    channels = in_weight.shape[2] - inner
    states = (channels - inner) // 2
    span = inner // heads
    chips = peers // 2
    direct = model % (32 * groups * peers) == 0 and chips == 4 and groups == 4
    seq_at = lax.axis_index("seq")
    here = jnp.stack([seq_at % 2, seq_at // 2, lax.axis_index("fsdp")]).astype(jnp.int32)

    small = [norm_gain, conv_weight.reshape(layers, -1), conv_bias, dt_bias, a_log, d_skip, gate_gain]
    sizes = [a.shape[1] for a in small]
    own = jnp.concatenate(small, axis=1)
    if direct:
        by_partner, bits = own[None], 1
        while bits < groups:
            by_partner = jnp.concatenate([by_partner, swap(by_partner, "fsdp", bits)])
            bits *= 2
        packed = jnp.stack([lax.dynamic_index_in_dim(by_partner, here[2] ^ z, 0, keepdims=False) for z in range(groups)])
    else:
        packed = lax.all_gather(own, "fsdp", axis=0)
    pieces, at = [], 0
    for size in sizes:
        pieces.append(packed[:, :, at:at + size])
        at += size

    def joined(piece):
        return jnp.moveaxis(piece, 0, 1).reshape(layers, -1)

    norm_all = joined(pieces[0]).astype(F32)
    taps_all = jnp.moveaxis(pieces[1].reshape(groups, layers, taps_len, -1), 0, 2).reshape(layers, taps_len, channels)
    taps_all = jnp.concatenate(
        [taps_all.astype(F32), joined(pieces[2]).astype(F32)[:, None], jnp.zeros((layers, 8 - taps_len - 1, channels), F32)], axis=1
    )
    pad_heads = ((0, 0), (0, LANES - heads))
    rates_all = jnp.stack(
        [jnp.pad(joined(pieces[3]).astype(F32), pad_heads), jnp.pad(-jnp.exp(joined(pieces[4]).astype(F32)), pad_heads)], axis=1
    )
    rates_all = jnp.pad(rates_all, ((0, 0), (0, 6), (0, 0)))
    skip_all = jnp.repeat(joined(pieces[5]).astype(F32), span, axis=1)[:, None]
    gain_all = joined(pieces[6]).astype(F32)[:, None]

    all_columns = (0, inner + channels, True)
    gate_all, mix_all, out_all = [], [], []
    for layer in range(layers):
        if direct:
            share_in, share_out = model // (groups * peers), inner // (groups * peers)
            if layer == 0:
                mix_z = from_along_z(take_share(in_weight, dt_weight, 0, all_columns, here, share_in, peers, ()), groups, (by_partner,))
                whole = fetched_by_all(
                    in_weight, dt_weight, 0, all_columns, here, groups, chips, mix_z, (norm_all, taps_all, rates_all, skip_all, gain_all)
                )
                gates, mixes = whole[:, :inner], whole[:, inner:]
                outs = None
            else:
                share = take_share(in_weight, dt_weight, layer, all_columns, here, share_in, peers, (mix_z,))
                taken, first = [share], 0
                if layer == 1:
                    share = take_share(out_weight, None, 0, (0, model, False), here, share_out, peers, (mix_z,))
                    taken = [share[i * share_in:(i + 1) * share_in] for i in range(inner // model)] + taken
                    first = inner
                whole = lax.all_gather(jnp.concatenate(taken, axis=1), ("fsdp", "seq"), axis=0, tiled=True)
                gates, mixes = whole[:, first:first + inner], whole[:, first + inner:]
                if layer == 1:
                    out_all[0] = unfolded(whole, inner, model, share_in)
                share = take_share(out_weight, None, layer, (0, model, False), here, share_out, peers, (mix_z,))
                outs = lax.all_gather(share, ("fsdp", "seq"), axis=0, tiled=True)
        else:
            steps = jnp.pad(dt_weight[layer], ((0, 0), (0, LANES - heads)))
            whole = gathered(jnp.concatenate([in_weight[layer], steps], axis=1))
            gates, mixes = whole[:, :inner], whole[:, inner:]
            outs = gathered(out_weight[layer])
        gate_all.append(gates)
        mix_all.append(mixes)
        out_all.append(outs)

    numbers = (segments + 1).astype(F32)
    before = lax.ppermute(numbers[:, width - EDGE:], "seq", [(i, i + 1) for i in range(peers - 1)])
    padded = jnp.concatenate([before, numbers], axis=1)
    columns = [padded[:, EDGE - back:EDGE - back + width] == numbers for back in range(1, taps_len)]
    columns += [numbers == before[:, EDGE - 1:], numbers == numbers[:, width - 1:]]
    marks = jnp.stack([c.astype(F32) for c in columns] + [numbers], axis=-1)
    marks = jnp.pad(marks, ((0, 0), (0, 0), (0, LANES - marks.shape[-1])))
    row_marks = jnp.broadcast_to(numbers[:, None, :], (batch, 8, width))
    lane_head = jnp.arange(inner) // span
    spread = (jnp.arange(2 * LANES)[:, None] % LANES == lane_head[None, :]).astype(BF16)

    stream = tokens.astype(F32)
    kept, sent = [], ()
    for layer in range(layers):
        norm_scale = norm_scale_of(stream)
        low = (stream * norm_scale * norm_all[layer]).astype(BF16).reshape(rows, model)
        w_gate, w_mix, w_out = gate_all[layer], mix_all[layer], out_all[layer]
        mixed_in = dot(low, w_mix).astype(BF16).reshape(batch, width, channels + LANES)
        edge = lax.ppermute(mixed_in[:, width - EDGE:], "seq", [(i, i + 1) for i in range(peers - 1)])
        gate = dot(low, w_gate).astype(BF16).reshape(batch, width, inner)
        taps, rates, skip, gain = taps_all[layer], rates_all[layer], skip_all[layer], gain_all[layer]
        act, size, sums, sums_t, state, factor = call(
            functools.partial(conv_kernel, inner), batch,
            [(mixed_in, 0), (edge, 0), (marks, 0), (taps, 1), (rates, 1), (spread, 1)],
            [
                ((batch, width, channels), BF16, 0), ((batch, width, LANES), F32, 0), ((batch, width, LANES), F32, 0),
                ((batch, heads, width), F32, 0), ((batch, states + FACTOR_ROWS, inner), BF16, 0),
                ((batch, FACTOR_ROWS, inner), BF16, 0),
            ],
            [((EDGE + width, channels), F32)], "conv_states", 8.0, after=sent,
        )
        got, other, _ = exchange(state, here, 1)
        (part,) = call(
            functools.partial(intra_kernel, inner, heads), batch,
            [(act, 0), (size, 0), (sums, 0), (sums_t, 0), (marks, 0), (row_marks, 0), (skip, 1), (spread, 1)],
            [((batch, width, inner), F32, 0)],
            [((width, width), F32), ((width, inner), BF16)], "mix_within", 12.0,
        )
        before, partner = entered(got, (part,))
        mixed, gated, entering = call(
            functools.partial(post_kernel, inner), batch,
            [
                (part, 0), (act, 0), (before, 1), (partner, 1), (other, 0), (sums, 0), (marks, 0), (gate, 0), (gain, 1), (spread, 1),
            ],
            [((batch, width, inner), BF16, 0), ((batch, width, inner), BF16, 0), ((batch, states, inner), BF16, 0)],
            [((width, inner), F32)], "mix_gate", 6.0, here,
        )
        gated = gated.reshape(rows, inner)
        turned = None
        if direct:
            mine, send = turned_halves(gated if layer == 0 else None, low, here, groups, chips)
            turned = (mine, swap(send, "seq", 1))
            sent = (send,)
        kept.append((turned, stream, norm_scale, low, mixed_in, edge, gate, act, size, sums, sums_t, factor, entering, mixed, gated))
        stream = stream + dot(gated, w_out).reshape(batch, width, model)

    grad_stream = cotangent.astype(F32)
    collected, collected_grads, scattered, second_shares, waiting = [], [], [], [], []
    started = ()
    for layer in reversed(range(layers)):
        (turned, entry, norm_scale, low, mixed_in, edge, gate, act, size, sums, sums_t, factor, entering, mixed, gated) = kept[layer]
        w_gate, w_mix, w_out = gate_all[layer], mix_all[layer], out_all[layer]
        taps, rates, skip, gain = taps_all[layer], rates_all[layer], skip_all[layer], gain_all[layer]
        grad_low = grad_stream.astype(BF16).reshape(rows, model)
        grad_gated = dot_nt(grad_low, w_out).astype(BF16).reshape(batch, width, inner)
        d_mixed, d_gate, d_state, d_queries, d_sums, row_grads = call(
            functools.partial(gate_back_kernel, inner), batch,
            [
                (grad_gated, 0), (grad_low.reshape(batch, width, model), 0), (factor, 0), (mixed, 0), (gate, 0), (gain, 1), (act, 0),
                (entering, 0), (sums, 0), (marks, 0), (spread, 1),
            ],
            [
                ((batch, width, inner), BF16, 0), ((batch, width, inner + model), BF16, 0),
                ((batch, states + FACTOR_ROWS, inner), BF16, 0), ((batch, width, states), F32, 0), ((batch, width, LANES), F32, 0), ((8, inner), F32, 1),
            ],
            [((width, inner), F32)], "gate_back", 11.0, after=started,
        )
        got, other, joined_state = exchange(d_state, here, 0)
        both = d_gate.reshape(rows, inner + model)
        d_gate = both[:, :inner]
        started, arrived = (), ()
        if direct:
            big, small = inner // (groups * peers), model // (groups * peers)
            mine, theirs = turned
            both_other = swap(both, "seq", 1) if layer == 0 else None
            if layer > 0:
                wide = wide_grads(low, gated, both, groups, (joined_state,))
                scattered.append(lax.psum_scatter(wide, ("fsdp", "seq"), scatter_dimension=0, tiled=True))
                started = (wide,)
        else:
            out_share = reduced(dot_tn(gated, grad_low).astype(BF16))
        d_stepped, d_pair, d_total = call(
            functools.partial(intra_back_kernel, inner, heads), batch,
            [
                (d_mixed, 0), (act, 0), (size, 0), (sums, 0), (sums_t, 0), (marks, 0), (row_marks, 0), (spread, 1),
                (d_queries, 0), (d_sums, 0),
            ],
            [((batch, width, inner), BF16, 0), ((batch, width, 2 * states), F32, 0), ((batch, width, LANES), F32, 0)],
            [
                ((width, width), F32), ((width, width), F32), ((width, inner), BF16), ((LANES, width), F32), ((width, LANES), F32),
            ], "mix_within_back", 17.0, after=started,
        )
        before, partner = entered(got, (d_stepped,))
        if direct and layer == 0:
            first_blocks = whole_call(
                functools.partial(first_grads_kernel, groups, chips, inner), [mine, theirs, both, both_other],
                [((groups, big + inner // model * small, model), BF16)] * chips, 10.0, "first_grads", after=(before,),
            )
            arrived = tuple(first_blocks)
            for later in waiting:
                share, _ = halved_sums(plane_parts(later((first_blocks[0],))), groups)
                second_shares.append(laid([share], model, ()))
            first_share, halved = halved_sums(plane_parts(first_blocks), groups)
        d_mixed_in, d_edge, tap_grads, head_grads = call(
            functools.partial(conv_back_kernel, inner), batch,
            [
                (d_stepped, 0), (d_mixed, 0), (act, 0), (mixed_in, 0), (edge, 0), (marks, 0), (taps, 1), (rates, 1),
                (skip, 1), (size, 0), (sums, 0), (spread, 1), (d_pair, 0), (d_total, 0), (before, 1), (partner, 1), (other, 0),
                (entering, 0),
            ],
            [
                ((batch, width, channels + LANES), BF16, 0), ((batch, EDGE, channels), F32, 0),
                ((8, channels), F32, 1), ((8, LANES), F32, 1),
            ],
            [((EDGE + width, channels), F32), ((3, width + 2 * EDGE, 256), F32)], "conv_back", 17.0, here, arrived,
        )
        from_next = lax.ppermute(d_edge.astype(BF16), "seq", [(i + 1, i) for i in range(peers - 1)])
        tail = (d_mixed_in[:, width - EDGE:, :channels].astype(F32) + from_next.astype(F32)).astype(BF16)
        grad_mixed = lax.dynamic_update_slice(d_mixed_in, tail, (0, width - EDGE, 0)).reshape(rows, channels + LANES)
        grad_rows = dot_nt(d_gate, w_gate) + dot_nt(grad_mixed, w_mix)
        grad_rows = grad_rows.reshape(batch, width, model)
        scaled = grad_rows * norm_all[layer]
        inward = jnp.mean(scaled * entry, axis=-1, keepdims=True)
        gain_grad = jnp.sum(grad_rows * entry * norm_scale, axis=(0, 1))
        grad_stream = grad_stream + norm_scale * scaled - (norm_scale * norm_scale * norm_scale * inward) * entry
        if direct:
            extra = whole_call(
                functools.partial(gather_small_kernel, groups, taps_len, heads), [gain_grad[None], tap_grads, head_grads, row_grads, spread],
                [((model, LANES), F32)], 3.0, "gather_small",
            )[0]
            operands = [mine, theirs, grad_mixed, swap(grad_mixed, "seq", 1), extra, swap(extra, "seq", 1)]
            kernel = functools.partial(second_grads_kernel, groups, chips, channels, heads)
            outs = [((groups, small, channels + LANES), BF16)] * chips
            if layer > 0:
                waiting.append(functools.partial(whole_call, kernel, operands, outs, 6.0, "second_grads", here))
                started = (operands[3], operands[5])
            else:
                got = plane_parts(whole_call(kernel, operands, outs, 6.0, "second_grads", here, halved))
                second_shares.append(layer_sums(got, groups, model, (stream, grad_stream)))
        else:
            mixed_grad = dot_tn(low, grad_mixed)
            in_share = reduced(jnp.concatenate([dot_tn(low, d_gate).astype(BF16), mixed_grad[:, :channels].astype(BF16)], axis=1))
            dt_share = reduced(mixed_grad[:, channels:].astype(BF16))
            collected_grads.append((in_share, dt_share, out_share))
            small_grads = [
                gain_grad.reshape(groups, -1),
                jnp.moveaxis(tap_grads[:taps_len].reshape(taps_len, groups, -1), 1, 0).reshape(groups, -1),
                tap_grads[taps_len].reshape(groups, -1),
                head_grads[0, :heads].reshape(groups, -1),
                head_grads[1, :heads].reshape(groups, -1),
                jnp.sum(row_grads[1].reshape(heads, span), axis=1).reshape(groups, -1),
                row_grads[0].reshape(groups, -1),
            ]
            collected.append(jnp.concatenate(small_grads, axis=1))
    if direct:
        mine_a, other_a = spread_in_plane(first_share, chips)
        second_share = stacked(second_shares[::-1]).reshape(-1, model)
        held = [stacked([share], (first_blocks[0],))[0] for share in scattered]
        scattered = [lax.all_gather(share, "seq", axis=0, tiled=True) for share in held]
        mine_b, other_b = spread_in_plane(second_share, chips)
        shapes = [(model // groups, inner + channels), (model // groups, heads), (inner // groups, model)]
        smalls = [
            (layers, model // groups), (layers, taps_len, channels // groups), (layers, channels // groups), (layers, 3, heads // groups),
            (layers, inner // groups),
        ]
        blocks = mine_a + [other_a] + mine_b + [other_b] + scattered[::-1]
        placed = placed_grads(here, blocks, layers, shapes, smalls, chips, inner, ())
        by_head = placed[6]
        pieces = [placed[3], placed[4], placed[5], by_head[:, 0], by_head[:, 1], by_head[:, 2], placed[7]]
    else:
        placed = [jnp.stack([c[i] for c in collected_grads[::-1]]) for i in range(3)]
        placed[1] = placed[1][:, :, :heads]
        small_sum = lax.psum(jnp.stack(collected[::-1], axis=1), ("fsdp", "seq"))
        small_sum = lax.dynamic_index_in_dim(small_sum, lax.axis_index("fsdp"), 0, keepdims=False)
        pieces, at = [], 0
        for size in sizes:
            pieces.append(small_sum[:, at:at + size])
            at += size
    return (
        stream, grad_stream, pieces[0],
        placed[0],
        placed[1],
        pieces[1].reshape(layers, taps_len, -1),
        pieces[2], pieces[3], pieces[4], pieces[5], pieces[6],
        placed[2],
    )


def solution(mesh):
    split = P("fsdp", "seq", None)
    vector = P(None, "fsdp")
    matrix = P(None, "fsdp", None)
    taps = P(None, None, "fsdp")
    return jax.shard_map(
        on_device,
        mesh=mesh,
        in_specs=(
            split, P("fsdp", "seq"), vector, matrix, matrix, taps, vector, vector, vector, vector, vector, matrix, split,
        ),
        out_specs=(
            split, split, vector, matrix, matrix, taps, vector, vector, vector, vector, vector, matrix,
        ),
        check_vma=False,
    )
```

```python
import functools

import jax
import jax.numpy as jnp
from jax import lax
from jax.experimental import pallas as pl
from jax.experimental.pallas import tpu as pltpu
from jax.sharding import PartitionSpec as P

EPSILON = 1e-05
F32, BF16 = jnp.float32, jnp.bfloat16
LANES = 128
EDGE = 8
FACTOR_ROWS = 16
SCALE = 0.25
VMEM = 48 * 1024 * 1024
NT = (((1,), (1,)), ((), ()))
TN = (((0,), (0,)), ((), ()))


def dot(a, b):
    return jnp.dot(a, b, preferred_element_type=F32)


def dot_nt(a, b):
    return lax.dot_general(a, b, NT, preferred_element_type=F32)


def dot_tn(a, b):
    return lax.dot_general(a, b, TN, preferred_element_type=F32)


def dot_exact(a, b):
    return jnp.dot(a, b, precision=lax.Precision.HIGHEST, preferred_element_type=F32)


def halves(v):
    high = v.astype(BF16)
    low = (v - high.astype(F32)).astype(BF16)
    return jnp.concatenate([high, low], axis=1)


def sigmoid(v):
    return 1.0 / (1.0 + jnp.exp(-v))


def softplus(v):
    return jnp.maximum(v, 0.0) + jnp.log1p(jnp.exp(-jnp.abs(v)))


def below(size):
    rows = lax.broadcasted_iota(jnp.int32, (size, size), 0)
    columns = lax.broadcasted_iota(jnp.int32, (size, size), 1)
    return rows >= columns


def head_column(table, head):
    return pltpu.roll(table, LANES - head, axis=1)[:, 0:1]


def conv_total(padded, taps, masks, at, wide, width):
    total = taps[4:5, pl.ds(at, wide)] + taps[3:4, pl.ds(at, wide)] * padded[EDGE:EDGE + width, pl.ds(at, wide)]
    for back in range(1, 4):
        tap = taps[3 - back:4 - back, pl.ds(at, wide)]
        total = total + (masks[back - 1] * tap) * padded[EDGE - back:EDGE - back + width, pl.ds(at, wide)]
    return total


def conv_kernel(inner, mixed, edge, marks, taps, rates, spread, act, sizes, sums, sums_t, state, factor, padded):
    width, channels = mixed.shape[1], padded.shape[1]
    padded[0:EDGE, :] = edge[0, :, 0:channels].astype(F32)
    padded[EDGE:EDGE + width, :] = mixed[0, :, 0:channels].astype(F32)
    marks_now = marks[0]
    masks = [marks_now[:, back:back + 1] for back in range(3)]
    wide = 256
    for at in range(0, channels, wide):
        total = conv_total(padded, taps, masks, at, wide, width)
        act[0, :, pl.ds(at, wide)] = (total * sigmoid(total)).astype(BF16)
    size = softplus(mixed[0, :, channels:].astype(F32) + rates[0:1, :])
    tri = jnp.where(below(width), 1.0, 0.0).astype(F32)
    total_sum = dot_exact(tri, size * rates[1:2, :])
    last = total_sum[width - 1:width]
    sizes[0] = size
    sums[0] = total_sum
    sums_t[0] = total_sum.T[0:sums_t.shape[1]]
    weight = halves(marks_now[:, 4:5] * jnp.exp(last - total_sum) * size)
    gone = marks_now[width - 1:width, 3:4] * jnp.exp(last)
    gone = halves(jnp.broadcast_to(gone, (FACTOR_ROWS, LANES)))
    states = (channels - inner) // 2
    keys_t = act[0, :, inner:inner + states].T
    for at in range(0, inner, wide):
        part = spread[:, pl.ds(at, wide)]
        weighted = (dot(weight, part) * act[0, :, pl.ds(at, wide)].astype(F32)).astype(BF16)
        state[0, 0:states, pl.ds(at, wide)] = dot(keys_t, weighted).astype(BF16)
        fade = dot(gone, part).astype(BF16)
        state[0, states:, pl.ds(at, wide)] = fade
        factor[0, :, pl.ds(at, wide)] = fade


def intra_kernel(inner, heads, act, sizes, sums, sums_t, marks, row_marks, skip, spread, out, scores, stepped):
    width = act.shape[1]
    states = (act.shape[2] - inner) // 2
    half = width // 2
    keys = act[0, :, inner:inner + states]
    queries = act[0, :, inner + states:]
    same = below(width) & (marks[0][:, 5:6] == row_marks[0, 0:1, :])
    scores[...] = jnp.where(same, dot_nt(queries, keys), 0.0)
    size = halves(sizes[0])
    wide = 256
    for at in range(0, inner, wide):
        part = dot(size, spread[:, pl.ds(at, wide)])
        stepped[:, pl.ds(at, wide)] = (part * act[0, :, pl.ds(at, wide)].astype(F32)).astype(BF16)
    per = LANES // (inner // heads)
    span = inner // heads
    lane = lax.broadcasted_iota(jnp.int32, (width, LANES), 1)

    def group(at, carry):
        place = pl.ds(pl.multiple_of(at * LANES, LANES), LANES)
        x = stepped[:, place]
        y_low = y_high = None
        for i in range(per):
            head = at * per + i
            column = head_column(sums[0], head)
            row = sums_t[0, pl.ds(head, 1), :]
            mine = (lane >= i * span) & (lane < (i + 1) * span)
            xh = jnp.where(mine, x, jnp.zeros_like(x))
            w_low = scores[0:half, 0:half] * jnp.exp(jnp.minimum(column[0:half] - row[:, 0:half], 0.0))
            w_high = scores[half:, :] * jnp.exp(jnp.minimum(column[half:] - row, 0.0))
            a = dot(w_low.astype(BF16), xh[0:half])
            b = dot(w_high.astype(BF16), xh)
            y_low = a if y_low is None else y_low + a
            y_high = b if y_high is None else y_high + b
        values = act[0, :, place].astype(F32) * skip[0:1, place]
        out[0, 0:half, place] = (y_low + values[0:half]).astype(out.dtype)
        out[0, half:, place] = (y_high + values[half:]).astype(out.dtype)
        return carry

    lax.fori_loop(0, inner // LANES, group, 0, unroll=2)


def entered_part(at, later_core, before, partner, other, place):
    states = before.shape[0]
    chip = before[:, place]
    core = jnp.full(chip.shape, at[0], jnp.int32)
    chip = jnp.where(core == pl.program_id(0), chip.astype(F32), partner[:, place].astype(F32))
    through = other[0, states:states + 1, place].astype(F32) * chip + other[0, 0:states, place].astype(F32)
    return jnp.where(core == later_core, through, chip).astype(BF16)


def post_kernel(inner, at, part_mixed, act, before, partner, other, sums, marks, gate, gain, spread, mixed, gated, entering, kept):
    states = (act.shape[2] - inner) // 2
    queries = act[0, :, inner + states:]
    enter = halves(marks[0][:, 3:4] * jnp.exp(sums[0]))
    wide = 256
    square = None
    for start in range(0, inner, wide):
        place = pl.ds(start, wide)
        state = entered_part(at, 1, before, partner, other, place)
        entering[0, :, place] = state
        whole = part_mixed[0, :, place].astype(F32) + dot(enter, spread[:, place]) * dot(queries, state)
        g = gate[0, :, place].astype(F32)
        w = whole * (g * sigmoid(g))
        mixed[0, :, place] = whole.astype(BF16)
        kept[:, place] = w
        square = w * w if square is None else square + w * w
    scale = lax.rsqrt(jnp.sum(square, axis=1, keepdims=True) / inner + EPSILON)
    for at in range(0, inner, wide):
        place = pl.ds(at, wide)
        gated[0, :, place] = (kept[:, place] * scale * gain[0:1, place]).astype(BF16)


def gate_back_kernel(
    inner, grad, grad_low, factor, mixed, gate, gain, act, state, sums, marks, spread,
    d_mixed, d_gate, d_state, d_queries, d_sums, row_grads, kept,
):
    states = (act.shape[2] - inner) // 2
    queries = act[0, :, inner + states:]
    queries_t = queries.T
    wide = 256

    @pl.when(pl.program_id(0) == 0)
    def _():
        row_grads[...] = jnp.zeros_like(row_grads)

    square = cross = None
    for at in range(0, inner, wide):
        place = pl.ds(at, wide)
        g = gate[0, :, place].astype(F32)
        w = mixed[0, :, place].astype(F32) * (g * sigmoid(g))
        gg = grad[0, :, place].astype(F32)
        kept[:, place] = w
        square = w * w if square is None else square + w * w
        more = w * gain[0:1, place] * gg
        cross = more if cross is None else cross + more
    scale = lax.rsqrt(jnp.sum(square, axis=1, keepdims=True) / inner + EPSILON)
    pulled = scale * scale * scale * (jnp.sum(cross, axis=1, keepdims=True) / inner)
    entered = marks[0][:, 3:4] * jnp.exp(sums[0])
    enter = halves(entered)
    grad_enter = dq = None
    for at in range(0, inner, wide):
        place = pl.ds(at, wide)
        g = gate[0, :, place].astype(F32)
        sig = sigmoid(g)
        silu = g * sig
        gg = grad[0, :, place].astype(F32)
        w = kept[:, place]
        whole = mixed[0, :, place].astype(F32)
        dw = scale * (gain[0:1, place] * gg) - pulled * w
        row_grads[0:1, place] += jnp.sum(gg * w * scale, axis=0, keepdims=True)
        dm = dw * silu
        d_gate[0, :, place] = (dw * whole * (sig + silu * (1.0 - sig))).astype(BF16)
        d_mixed[0, :, place] = dm.astype(BF16)
        row_grads[1:2, place] += jnp.sum(dm * act[0, :, place].astype(F32), axis=0, keepdims=True)
        part = spread[:, place]
        st = state[0, :, place]
        e = (dm * dot(enter, part)).astype(BF16)
        d_state[0, 0:states, place] = dot(queries_t, e).astype(BF16)
        more_q = dot_nt(e, st)
        dq = more_q if dq is None else dq + more_q
        through = (dm * dot(queries, st)).astype(BF16)
        more_e = dot_nt(through, part[0:LANES])
        grad_enter = more_e if grad_enter is None else grad_enter + more_e
    d_queries[0] = dq
    d_sums[0] = grad_enter * entered
    d_gate[0, :, inner:] = grad_low[0]
    d_state[0, states:, :] = factor[0]


def intra_back_kernel(
    inner, heads, d_mixed, act, sizes, sums, sums_t, marks, row_marks, spread, d_queries, d_sums,
    d_stepped, d_pair, d_total, scores, d_scores, stepped, sums_rows, sums_columns,
):
    width = act.shape[1]
    states = (act.shape[2] - inner) // 2
    half = width // 2
    keys = act[0, :, inner:inner + states]
    queries = act[0, :, inner + states:]
    rows = lax.broadcasted_iota(jnp.int32, (width, width), 0)
    columns = lax.broadcasted_iota(jnp.int32, (width, width), 1)
    same = (rows <= columns) & (marks[0][:, 5:6] == row_marks[0, 0:1, :])
    scores[...] = jnp.where(same, dot_nt(keys, queries), 0.0)
    d_scores[...] = jnp.zeros_like(d_scores)
    sums_rows[...] = jnp.zeros_like(sums_rows)
    sums_columns[...] = jnp.zeros_like(sums_columns)
    size = halves(sizes[0])
    wide = 256
    for at in range(0, inner, wide):
        part = dot(size, spread[:, pl.ds(at, wide)])
        stepped[:, pl.ds(at, wide)] = (part * act[0, :, pl.ds(at, wide)].astype(F32)).astype(BF16)
    per = LANES // (inner // heads)
    span = inner // heads
    lane = lax.broadcasted_iota(jnp.int32, (width, LANES), 1)

    eighth = lax.broadcasted_iota(jnp.int32, (8, width), 0)

    def group(at, carry):
        place = pl.ds(pl.multiple_of(at * LANES, LANES), LANES)
        x = stepped[:, place]
        dy = d_mixed[0, :, place]
        dx_low = dx_high = None
        for i in range(per):
            head = at * per + i
            column = head_column(sums[0], head)
            row = sums_t[0, pl.ds(head, 1), :]
            mine = (lane >= i * span) & (lane < (i + 1) * span)
            xh = jnp.where(mine, x, jnp.zeros_like(x))
            dyh = jnp.where(mine, dy, jnp.zeros_like(dy))
            l_low = jnp.exp(jnp.minimum(row - column[0:half], 0.0))
            l_high = jnp.exp(jnp.minimum(row[:, half:] - column[half:], 0.0))
            w_low = scores[0:half, :] * l_low
            w_high = scores[half:, half:] * l_high
            dw_low = dot_nt(xh[0:half], dy)
            dw_high = dot_nt(xh[half:], dy[half:])
            d_scores[0:half, :] += dw_low * l_low
            d_scores[half:, half:] += dw_high * l_high
            g_low = dw_low * w_low
            g_high = dw_high * w_high
            over_low = jnp.sum(g_low, axis=0, keepdims=True)
            over_high = jnp.sum(g_high, axis=0, keepdims=True)
            eight = pl.ds(pl.multiple_of(head // 8 * 8, 8), 8)
            chosen = eighth == head % 8
            sums_rows[eight, :] += jnp.where(chosen, over_low, 0.0)
            sums_rows[eight, half:] += jnp.where(chosen[:, half:], over_high, 0.0)
            here = lane[0:half] == head
            sums_columns[0:half, :] += jnp.where(here, jnp.sum(g_low, axis=1, keepdims=True), 0.0)
            sums_columns[half:, :] += jnp.where(here, jnp.sum(g_high, axis=1, keepdims=True), 0.0)
            a = dot(w_low.astype(BF16), dyh)
            b = dot(w_high.astype(BF16), dyh[half:])
            dx_low = a if dx_low is None else dx_low + a
            dx_high = b if dx_high is None else dx_high + b
        d_stepped[0, 0:half, place] = dx_low.astype(BF16)
        d_stepped[0, half:, place] = dx_high.astype(BF16)
        return carry

    lax.fori_loop(0, inner // LANES, group, 0, unroll=2)
    grad = jnp.where(same, d_scores[...], 0.0).astype(BF16)
    d_pair[0, :, 0:states] = dot(grad, queries)
    d_pair[0, :, states:] = dot(grad.T, keys) + d_queries[0]
    d_total[0] = sums_rows[...].T - sums_columns[...] + d_sums[0]


def conv_back_kernel(
    inner, here, d_stepped, d_mixed, act, mixed_in, edge, marks, taps, rates, skip, sizes, sums, spread,
    d_pair, d_total, before, partner, other, state,
    d_mixed_in, d_edge, tap_grads, head_grads, padded, shifted,
):
    width, channels = mixed_in.shape[1], padded.shape[1]
    states = (channels - inner) // 2
    wide = 256

    @pl.when(pl.program_id(0) == 0)
    def _():
        tap_grads[...] = jnp.zeros_like(tap_grads)
        head_grads[...] = jnp.zeros_like(head_grads)

    padded[0:EDGE, :] = edge[0, :, 0:channels].astype(F32)
    padded[EDGE:EDGE + width, :] = mixed_in[0, :, 0:channels].astype(F32)
    marks_now = marks[0]
    masks = [marks_now[:, back:back + 1] for back in range(3)]
    total_sum = sums[0]
    size = sizes[0]
    last = total_sum[width - 1:width]
    faded = marks_now[:, 4:5] * jnp.exp(last - total_sum)
    weight = faded * size
    weight_pair = halves(weight)
    size_pair = halves(size)
    keys = act[0, :, inner:inner + states]
    for back in range(3):
        shifted[back, 0:EDGE, :] = jnp.zeros((EDGE, wide), F32)
        shifted[back, EDGE + width:, :] = jnp.zeros((EDGE, wide), F32)

    def through_conv(at, d_act):
        place = pl.ds(at, wide)
        total = conv_total(padded, taps, masks, at, wide, width)
        sig = sigmoid(total)
        d = d_act * (sig + total * sig * (1.0 - sig))
        tap_grads[4:5, place] += jnp.sum(d, axis=0, keepdims=True)
        tap_grads[3:4, place] += jnp.sum(d * padded[EDGE:EDGE + width, place], axis=0, keepdims=True)
        back_total = taps[3:4, place] * d
        edge_total = jnp.zeros((EDGE, wide), F32)
        for back in range(1, 4):
            u = masks[back - 1] * d
            tap_grads[3 - back:4 - back, place] += jnp.sum(
                u * padded[EDGE - back:EDGE - back + width, place], axis=0, keepdims=True
            )
            shifted[back - 1, EDGE:EDGE + width, :] = u
            tap = taps[3 - back:4 - back, place]
            back_total = back_total + tap * shifted[back - 1, EDGE + back:EDGE + back + width, :]
            edge_total = edge_total + tap * shifted[back - 1, back:back + EDGE, :]
        d_mixed_in[0, :, place] = back_total.astype(BF16)
        d_edge[0, :, place] = edge_total

    d_keys = d_pair[0, :, 0:states]
    d_size = d_weight = carried = None
    for at in range(0, inner, wide):
        place = pl.ds(at, wide)
        values = act[0, :, place].astype(F32)
        part = spread[:, place]
        ds = entered_part(here, 0, before, partner, other, place)
        wide_weight = dot(weight_pair, part)
        d_weighted = dot(keys, ds)
        dx = d_stepped[0, :, place].astype(F32)
        d_act = dx * dot(size_pair, part) + d_weighted * wide_weight + skip[0:1, place] * d_mixed[0, :, place].astype(F32)
        d_keys = d_keys + dot_nt((wide_weight * values).astype(BF16), ds)
        a = dot_nt((dx * values).astype(BF16), part[0:LANES])
        b = dot_nt((d_weighted * values).astype(BF16), part[0:LANES])
        c = jnp.sum(ds.astype(F32) * state[0, :, place].astype(F32), axis=0, keepdims=True)
        c = dot_nt(jnp.broadcast_to(halves_rows(c), (EDGE, wide)), part[0:LANES])
        d_size = a if d_size is None else d_size + a
        d_weight = b if d_weight is None else d_weight + b
        carried = c if carried is None else carried + c
        through_conv(at, d_act)
    through_conv(inner, jnp.concatenate([d_keys, d_pair[0, :, states:]], axis=1))
    d_size = d_size + d_weight * faded
    pulled = d_weight * weight
    gone = marks_now[width - 1:width, 3:4] * jnp.exp(last)
    at_end = jnp.sum(pulled, axis=0, keepdims=True) + gone * carried[0:1]
    row = lax.broadcasted_iota(jnp.int32, (width, LANES), 0)
    d_sum = d_total[0] - pulled + jnp.where(row == width - 1, at_end, 0.0)
    order = lax.broadcasted_iota(jnp.int32, (width, width), 0) <= lax.broadcasted_iota(jnp.int32, (width, width), 1)
    d_rate = dot_exact(jnp.where(order, 1.0, 0.0).astype(F32), d_sum)
    d_size = d_size + d_rate * rates[1:2, :]
    d_step = d_size * sigmoid(mixed_in[0, :, channels:].astype(F32) + rates[0:1, :])
    d_mixed_in[0, :, channels:] = d_step.astype(BF16)
    head_grads[0:1, :] += jnp.sum(d_step, axis=0, keepdims=True)
    head_grads[1:2, :] += jnp.sum(d_rate * size * rates[1:2, :], axis=0, keepdims=True)


def halves_rows(v):
    return v.astype(BF16)


def without(kernel, first, count):
    def run(*refs):
        return kernel(*refs[:first], *refs[first + count:])

    return run


def call(kernel, batch, ins, outs, scratch, name, micros, at=None, after=()):
    def spec(shape, whole):
        block = tuple(shape) if whole else (1,) + tuple(shape[1:])
        if whole:
            return pl.BlockSpec(block, lambda b: (0,) * len(block))
        return pl.BlockSpec(block, lambda b: (b,) + (0,) * (len(block) - 1))

    arrays = [a for a, _ in ins]
    in_specs = [spec(a.shape, whole) for a, whole in ins]
    if at is not None:
        arrays, in_specs = [at] + arrays, [pl.BlockSpec(memory_space=pltpu.SMEM)] + in_specs
    return pl.pallas_call(
        without(kernel, len(arrays), len(after)),
        grid=(batch,),
        in_specs=in_specs + [pl.BlockSpec(memory_space=pl.ANY)] * len(after),
        out_specs=[spec(shape, whole) for shape, _, whole in outs],
        out_shape=[jax.ShapeDtypeStruct(shape, kind) for shape, kind, _ in outs],
        scratch_shapes=[pltpu.VMEM(shape, kind) for shape, kind in scratch],
        compiler_params=pltpu.CompilerParams(vmem_limit_bytes=VMEM),
        cost_estimate=cost(micros),
        name=name,
    )(*arrays, *after)


def cost(micros):
    micros = micros * SCALE
    return pl.CostEstimate(flops=int(micros * 1.1e9), bytes_accessed=int(micros * 1e6), transcendentals=0)


def edge_kernel(grad, more, out):
    size, channels = grad.shape[1], more.shape[2]
    out[0, :, channels:] = grad[0, :, channels:]
    last = jnp.concatenate([jnp.zeros((size - EDGE, channels), F32), more[0].astype(F32)], axis=0)
    out[0, :, 0:channels] = (grad[0, :, 0:channels].astype(F32) + last).astype(BF16)


def with_edges(grad, more, after):
    batch, width, wide = grad.shape
    size = 2 * EDGE
    block = pl.BlockSpec((1, size, wide), lambda b: (b, width // size - 1, 0))
    return pl.pallas_call(
        without(edge_kernel, 2, len(after)),
        grid=(batch,),
        in_specs=[block, pl.BlockSpec((1,) + more.shape[1:], lambda b: (b, 0, 0))] + [pl.BlockSpec(memory_space=pl.ANY)] * len(after),
        out_specs=block,
        out_shape=jax.ShapeDtypeStruct(grad.shape, grad.dtype),
        input_output_aliases={0: 0},
        compiler_params=pltpu.CompilerParams(vmem_limit_bytes=VMEM),
        cost_estimate=cost(1.0),
        name="with_edges",
    )(grad, more, *after)


def whole_call(kernel, arrays, outs, micros, name, at=None, after=(), scratch=()):
    spec = pl.BlockSpec(memory_space=pltpu.VMEM)
    arrays, in_specs = list(arrays), [spec] * len(arrays)
    if at is not None:
        arrays, in_specs = [at] + arrays, [pl.BlockSpec(memory_space=pltpu.SMEM)] + in_specs
    return pl.pallas_call(
        without(kernel, len(arrays), len(after)),
        in_specs=in_specs + [pl.BlockSpec(memory_space=pl.ANY)] * len(after),
        out_specs=[spec] * len(outs),
        out_shape=[jax.ShapeDtypeStruct(shape, kind) for shape, kind in outs],
        scratch_shapes=[pltpu.VMEM(shape, kind) for shape, kind in scratch],
        compiler_params=pltpu.CompilerParams(vmem_limit_bytes=VMEM),
        cost_estimate=cost(micros),
        name=name,
    )(*arrays, *after)


def swap(x, axis, bits):
    return lax.ppermute(x, axis, [(i, i ^ bits) for i in range(lax.axis_size(axis))])


def join_kernel(later_core, at, own, other, joined):
    core = at[0]
    states = own.shape[1] - FACTOR_ROWS
    for start in range(0, own.shape[2], 512):
        place = pl.ds(start, 512)
        mine = own[core, :, place].astype(F32)
        theirs = other[core, :, place].astype(F32)
        later = jnp.full(mine.shape, core, jnp.int32) == later_core
        second = jnp.where(later, mine, theirs)
        first = jnp.where(later, theirs, mine)
        gain = second[states:states + 1]
        joined[0:states, place] = (gain * first[0:states] + second[0:states]).astype(BF16)
        joined[states:, place] = (gain * first[states:]).astype(BF16)


def enter_kernel(count, *refs):
    out = refs[count]
    states = out.shape[0]
    for start in range(0, out.shape[1], 512):
        place = pl.ds(start, 512)
        before = refs[0][0:states, place].astype(F32)
        for got in refs[1:count]:
            before = got[states:states + 1, place].astype(F32) * before + got[0:states, place].astype(F32)
        out[:, place] = before.astype(BF16)


def exchange(own, at, later_core, after=()):
    peers = lax.axis_size("seq")
    other = swap(own, "seq", 1)
    joined = whole_call(functools.partial(join_kernel, later_core), [own, other], [(own.shape[1:], BF16)], 2.0, "join_states", at, after)[0]
    got = []
    for distance in range(peers // 2 - 1, 0, -1):
        step = 2 * distance if later_core == 1 else -2 * distance
        route = [(i, i + step) for i in range(peers) if 0 <= i + step < peers]
        got.append(lax.ppermute(joined, "seq", route))
    return got, other, joined


def entered(got, after):
    shape = (got[0].shape[0] - FACTOR_ROWS, got[0].shape[1])
    before = whole_call(
        functools.partial(enter_kernel, len(got)), got, [(shape, BF16)], 2.0, "enter_states", after=after
    )[0]
    return before, swap(before, "seq", 1)


def gathered(block):
    peers = lax.axis_size("seq")
    rows = block.shape[0] // peers
    share = lax.dynamic_slice_in_dim(block, lax.axis_index("seq") * rows, rows, 0)
    return lax.all_gather(share, ("fsdp", "seq"), axis=0, tiled=True)


def take_in_kernel(columns, block, steps, out):
    first, last, with_steps = columns
    wide = last - first
    out[:, 0:wide] = block[0, :, first:last]
    if with_steps:
        heads = steps.shape[2]
        out[:, wide:] = jnp.zeros((out.shape[0], LANES), BF16)
        out[:, wide:wide + heads] = steps[0]


def take_share(weight, steps, layer, columns, at, share, parts, after):
    first, last, with_steps = columns
    wide = last - first + (LANES if with_steps else 0)

    def rows(i, where):
        return (layer, where[1] * 2 + where[0] if parts > 2 else where[0], 0)

    arrays = [weight] if steps is None else [weight, steps]
    specs = [pl.BlockSpec((1, share, a.shape[2]), rows) for a in arrays]
    kernel = functools.partial(take_in_kernel, columns)
    if steps is None:
        kernel = lambda block, out: take_in_kernel(columns, block, None, out)
    inner_kernel = without(kernel, len(arrays), len(after))
    return pl.pallas_call(
        lambda where, *refs: inner_kernel(*refs),
        grid_spec=pltpu.PrefetchScalarGridSpec(
            num_scalar_prefetch=1,
            grid=(1,),
            in_specs=specs + [pl.BlockSpec(memory_space=pl.ANY)] * len(after),
            out_specs=pl.BlockSpec((share, wide), lambda i, where: (0, 0)),
        ),
        out_shape=jax.ShapeDtypeStruct((share, wide), BF16),
        compiler_params=pltpu.CompilerParams(vmem_limit_bytes=VMEM),
        cost_estimate=cost(1.0),
        name="take_share",
    )(at, *arrays, *after)


def place_rows_kernel(starts, columns, many, at, *refs):
    weight, steps = refs[0], refs[1] if many == 2 else None
    sources, out = refs[many:-1], refs[-1]
    core, chip, group = at[0], at[1], at[2]
    rows = weight.shape[1]
    own = pl.ds(pl.multiple_of(group * rows, rows), rows)
    first, last, with_steps = columns
    wide = last - first
    out[own, 0:wide] = weight[0, :, first:last]
    if with_steps:
        out[own, wide:] = jnp.concatenate([steps[0], jnp.zeros((rows, LANES - steps.shape[2]), BF16)], axis=1)
    for source, index, rows, place in starts:
        start = pl.multiple_of(place(core, chip, group), rows)
        out[pl.ds(start, rows), :] = sources[source][index]


def placed_rows(at, weight, steps, layer, columns, sources, starts, groups, micros, after=()):
    whole = pl.BlockSpec(memory_space=pltpu.VMEM)
    own = [weight] if steps is None else [weight, steps]
    first, last, with_steps = columns
    shape = (weight.shape[1] * groups, last - first + (LANES if with_steps else 0))
    return pl.pallas_call(
        without(functools.partial(place_rows_kernel, starts, columns, len(own)), 1 + len(own) + len(sources), len(after)),
        grid=(1,),
        in_specs=[pl.BlockSpec(memory_space=pltpu.SMEM)]
        + [pl.BlockSpec((1,) + a.shape[1:], lambda i: (layer, 0, 0)) for a in own] + [whole] * len(sources)
        + [pl.BlockSpec(memory_space=pl.ANY)] * len(after),
        out_specs=whole,
        out_shape=jax.ShapeDtypeStruct(shape, BF16),
        compiler_params=pltpu.CompilerParams(vmem_limit_bytes=VMEM),
        cost_estimate=cost(micros),
        name="place_rows",
    )(at, *own, *sources, *after)


def stack_kernel(count, *refs):
    out, row = refs[count], 0
    for ref in refs[:count]:
        if len(ref.shape) == 2:
            out[row] = ref[...]
            row += 1
        else:
            out[row:row + ref.shape[0]] = ref[...]
            row += ref.shape[0]


def stacked(blocks, after=()):
    many = sum(1 if b.ndim == 2 else b.shape[0] for b in blocks)
    return whole_call(
        functools.partial(stack_kernel, len(blocks)), blocks, [((many,) + blocks[0].shape[-2:], BF16)], 1.0, "stack", after=after
    )[0]


def unfold_kernel(share, folded, out):
    many = folded.shape[1] // out.shape[1]
    model = out.shape[1]
    for block in range(folded.shape[0] // share):
        for i in range(many):
            to = (block * many + i) * share
            out[to:to + share, :] = folded[block * share:(block + 1) * share, i * model:(i + 1) * model]


def unfolded(whole, inner, model, share):
    rows = whole.shape[0] // 4
    return pl.pallas_call(
        functools.partial(unfold_kernel, share),
        grid=(4,),
        in_specs=[pl.BlockSpec((rows, inner), lambda i: (i, 0))],
        out_specs=pl.BlockSpec((rows * inner // model, model), lambda i: (i, 0)),
        out_shape=jax.ShapeDtypeStruct((inner, model), BF16),
        compiler_params=pltpu.CompilerParams(vmem_limit_bytes=VMEM),
        cost_estimate=cost(3.0),
        name="unfold",
    )(whole)


def from_along_z(mine, groups, after=()):
    return stacked([swap(mine, "fsdp", e) for e in range(1, groups)], after)


def fetched_by_all(weight, steps, layer, columns, at, groups, chips, from_z, place_after=()):
    rows = weight.shape[1]
    share = rows // (2 * chips)
    sources = [from_z] + [swap(from_z, "seq", 2 * d) for d in range(1, chips)]
    sources.append(swap(stacked([a.reshape(-1, a.shape[2]) for a in sources]), "seq", 1))

    def place_of(d, e, other):
        return lambda core, chip, group: (group ^ e) * rows + (chip ^ d) * (2 * share) + (core ^ other) * share

    starts = []
    for d in range(chips):
        for e in range(1, groups):
            index = e - 1
            starts.append((d, (index,), share, place_of(d, e, 0)))
            starts.append((chips, (d, slice(index * share, (index + 1) * share)), share, place_of(d, e, 1)))
    return placed_rows(at, weight, steps, layer, columns, sources, starts, groups, 4.0, place_after)


def reduced(grad):
    share = lax.psum_scatter(grad, ("fsdp", "seq"), scatter_dimension=0, tiled=True)
    return lax.all_gather(share, "seq", axis=0, tiled=True).astype(F32)


def turn_kernel(groups, chips, at, gated, low, own, send, turned):
    core, chip, group = at[0], at[1], at[2]
    base = 0
    for x in (gated, low):
        if x is None:
            continue
        total = x.shape[1]
        share = total // (2 * groups * chips)
        for start in range(0, total, 256):
            turned[start:start + 256, :] = x[:, start:start + 256].T
        for other, out in ((0, own), (1, send)):
            for d in range(chips):
                for e in range(groups):
                    start = (group ^ e) * (total // groups) + (chip ^ d) * (2 * share) + (core ^ other) * share
                    to = base + (d * groups + e) * share
                    out[to:to + share, :] = turned[pl.ds(pl.multiple_of(start, share), share), :]
        base += total // 2


def turned_halves(gated, low, at, groups, chips):
    rows = low.shape[0]
    if gated is None:
        def kernel(where, low_ref, *refs):
            turn_kernel(groups, chips, where, None, low_ref, *refs)

        return whole_call(kernel, [low], [((low.shape[1] // 2, rows), BF16)] * 2, 2.0, "turn", at, scratch=[(low.shape[::-1], BF16)])
    half = ((gated.shape[1] + low.shape[1]) // 2, rows)
    return whole_call(
        functools.partial(turn_kernel, groups, chips), [gated, low], [(half, BF16)] * 2, 4.0, "turn", at,
        scratch=[((gated.shape[1], rows), BF16)],
    )


def first_grads_kernel(groups, chips, inner, own, other, grad, grad_other, *outs):
    wide = grad.shape[1] - inner
    total_big = inner // 2
    big = total_big // (groups * chips)
    small = (own.shape[0] - total_big) // (groups * chips)

    def put(total, share, start, at):
        for d in range(chips):
            for e in range(groups):
                block = (d * groups + e) * share
                outs[d][e, start:start + share, pl.ds(at, 512)] = total[block:block + share]

    for at in range(0, wide, 512):
        place = pl.ds(inner + at, 512)
        total = dot(own[0:total_big, :], grad[:, place]) + dot(other[0:total_big, :], grad_other[:, place])
        put(total.astype(BF16), big, 0, at)
    for at in range(0, inner, 512):
        place = pl.ds(at, 512)
        total = dot(own[total_big:, :], grad[:, place]) + dot(other[total_big:, :], grad_other[:, place])
        put(total.astype(BF16), small, big + at // wide * small, at % wide)


def wide_grads_kernel(low, gated, grad, out):
    cut, model = low.shape[1], grad.shape[1] - out.shape[1] // 2
    inner = out.shape[1] // 2
    turned = low[...].T
    for at in range(0, inner, 512):
        out[:, pl.ds(at, 512)] = dot(turned, grad[:, pl.ds(at, 512)]).astype(BF16)
    for i in range(inner // model):
        turned = gated[:, i * cut:(i + 1) * cut].T
        for at in range(0, model, 512):
            out[:, pl.ds(inner + i * model + at, 512)] = dot(turned, grad[:, pl.ds(inner + at, 512)]).astype(BF16)


def wide_grads(low, gated, both, groups, after):
    rows, model = low.shape
    inner = gated.shape[1]
    cut = model // groups
    return pl.pallas_call(
        without(wide_grads_kernel, 3, len(after)),
        grid=(groups,),
        in_specs=[
            pl.BlockSpec((rows, cut), lambda z: (0, z)),
            pl.BlockSpec((rows, inner // groups), lambda z: (0, z)),
            pl.BlockSpec(both.shape, lambda z: (0, 0)),
        ] + [pl.BlockSpec(memory_space=pl.ANY)] * len(after),
        out_specs=pl.BlockSpec((cut, 2 * inner), lambda z: (z, 0)),
        out_shape=jax.ShapeDtypeStruct((model, 2 * inner), BF16),
        compiler_params=pltpu.CompilerParams(vmem_limit_bytes=VMEM),
        cost_estimate=cost(10.0),
        name="wide_grads",
    )(low, gated, both, *after)


def second_grads_kernel(groups, chips, channels, heads, here, own, other, grad, grad_other, extra, extra_other, *outs):
    rows = extra.shape[0] // 2
    base = own.shape[0] - rows
    share = rows // (groups * chips)
    core, chip, group = here[0], here[1], here[2]
    lane = lax.broadcasted_iota(jnp.int32, (share, LANES), 1)
    total_wide = channels + LANES
    edges = list(range(0, channels, 512)) + [channels, total_wide]
    for at, end in zip(edges[:-1], edges[1:]):
        place = pl.ds(at, end - at)
        total = dot(own[base:, :], grad[:, place]) + dot(other[base:, :], grad_other[:, place])
        for d in range(chips):
            for e in range(groups):
                block = (d * groups + e) * share
                part = total[block:block + share]
                if at == channels:
                    start = (group ^ e) * (2 * rows // groups) + (chip ^ d) * (2 * share) + core * share
                    here_rows = pl.ds(pl.multiple_of(start, share), share)
                    part = jnp.where(lane < heads, part, extra[here_rows, :] + extra_other[here_rows, :])
                outs[d][e, :, place] = part.astype(BF16)


def gather_small_kernel(groups, taps, heads, gain, tap_grads, head_grads, row_grads, spread, out):
    cut = out.shape[0] // groups
    channels, inner = tap_grads.shape[1], row_grads.shape[1]
    skip = row_grads[1:2, :]
    high = skip.astype(BF16)
    low = (skip - high.astype(F32)).astype(BF16)
    ones = spread[0:LANES, :]
    skip = dot_nt(jnp.broadcast_to(high, (8, inner)), ones) + dot_nt(jnp.broadcast_to(low, (8, inner)), ones)
    span, part, few = channels // groups, inner // groups, heads // groups
    for z in range(groups):
        rows = [jnp.zeros((heads, cut), F32), gain[0:1, z * cut:(z + 1) * cut]]
        for at in range(0, part, cut):
            rows.append(row_grads[0:1, z * part + at:z * part + at + cut])
        for at in range(0, span, cut):
            wide = min(cut, span - at)
            block = tap_grads[0:taps + 1, z * span + at:z * span + at + wide]
            if wide < cut:
                block = jnp.concatenate([block, jnp.zeros((taps + 1, cut - wide), F32)], axis=1)
            rows.append(block)
        lane = lax.broadcasted_iota(jnp.int32, (1, LANES), 1)
        for row in (head_grads[0:1, :], head_grads[1:2, :], skip[0:1, :]):
            row = pltpu.roll(row, (LANES - z * few) % LANES, axis=1) if z else row
            row = jnp.where(lane < few, row, 0.0)
            rows.append(jnp.concatenate([row] + [jnp.zeros((1, cut - LANES), F32)], axis=1))
        table = jnp.concatenate(rows, axis=0)
        table = jnp.concatenate([table, jnp.zeros((LANES - table.shape[0], cut), F32)], axis=0)
        out[z * cut:(z + 1) * cut, :] = table.T


def add_kernel(count, *refs):
    ins, outs = refs[:count], refs[count:]
    for i, out in enumerate(outs):
        total = ins[0][i].astype(F32)
        for more in ins[1:]:
            total = total + more[i].astype(F32)
        out[...] = total.astype(out.dtype)


def halve_kernel(count, *refs):
    ins, (near, far) = refs[:count], refs[count:]
    half = near.shape[0]
    for i in range(2 * half):
        total = ins[0][i].astype(F32)
        for more in ins[1:]:
            total = total + more[i].astype(F32)
        if i < half:
            near[i] = total.astype(BF16)
        else:
            far[i - half] = total.astype(BF16)


def lay_kernel(count, layers, *refs):
    out = refs[-1]
    wide = out.shape[1]
    share, columns = refs[0].shape[0] // layers, refs[0].shape[1]
    row = 0
    for layer in range(layers):
        rows = slice(layer * share, (layer + 1) * share)
        for at in range(0, columns, wide):
            width = min(wide, columns - at)
            total = refs[0][rows, at:at + width].astype(F32)
            for more in refs[1:count]:
                total = total + more[rows, at:at + width].astype(F32)
            out[row:row + share, 0:width] = total.astype(BF16)
            if width < wide:
                out[row:row + share, width:] = jnp.zeros((share, wide - width), BF16)
            row += share


def plane_parts(blocks):
    return [blocks[0]] + [swap(blocks[i], "seq", 2 * i) for i in range(1, len(blocks))]


def halved_sums(got, groups):
    parts, rows, columns = got[0].shape
    after = ()
    while parts > 1:
        half = parts // 2
        near, far = whole_call(
            functools.partial(halve_kernel, len(got)), got, [((half, rows, columns), BF16)] * 2, 2.0, "add_halves"
        )
        if parts == groups:
            after = (near,)
        got = [near, swap(far, "fsdp", half)]
        parts = half
    return whole_call(functools.partial(add_kernel, 2), got, [((rows, columns), BF16)], 1.0, "add_halves")[0], after


def laid(got, wide, after):
    rows, columns = got[0].shape
    shape = (-(-columns // wide) * rows, wide)
    return whole_call(functools.partial(lay_kernel, len(got), 1), got, [(shape, BF16)], 2.0, "lay_sums", after=after)[0]


def layer_sums(got, groups, wide, after):
    parts, rows, columns = got[0].shape
    shares = whole_call(functools.partial(add_kernel, len(got)), got, [((rows, columns), BF16)] * parts, 2.0, "add_plane")
    return laid([shares[0]] + [swap(shares[e], "fsdp", e) for e in range(1, groups)], wide, after)


def spread_in_plane(share, chips):
    mine = [share] + [swap(share, "seq", 2 * d) for d in range(1, chips)]
    return mine, swap(stacked(mine), "seq", 1)


def place_kernel(chips, inner, layers, at, *refs):
    mine_a, other_a = refs[:chips], refs[chips]
    mine_b, other_b = refs[chips + 1:2 * chips + 1], refs[2 * chips + 1]
    scattered = refs[2 * chips + 2:2 * chips + 1 + layers]
    in_out, extra_out, out_out, norm_out, taps_out, bias_out, heads_out, gain_out, extra = refs[-9:]
    core, chip = at[0], at[1]
    model = other_a.shape[2]
    rows_in, rows_out = in_out.shape[1], out_out.shape[1]
    big, share = rows_out // (2 * chips), rows_in // (2 * chips)
    channels = in_out.shape[2] - inner
    for layer in range(layers):
        @pl.when(pl.program_id(0) == layer)
        def _():
            if layer:
                wide = scattered[layer - 1]
                in_out[0, :, 0:inner] = wide[:, 0:inner].astype(F32)
                for i in range(inner // model):
                    out_out[0, i * rows_in:(i + 1) * rows_in, :] = wide[:, inner + i * model:inner + (i + 1) * model].astype(F32)
            for d in range(chips):
                for is_other in range(2):
                    a, b = (other_a.at[d], other_b.at[d]) if is_other else (mine_a[d], mine_b[d])
                    start = (chip ^ d) * (2 * share) + (core ^ is_other) * share
                    rows = pl.ds(pl.multiple_of(start, share), share)
                    if not layer:
                        start = (chip ^ d) * (2 * big) + (core ^ is_other) * big
                        out_out[0, pl.ds(pl.multiple_of(start, big), big), :] = a[0:big, :].astype(F32)
                        for i in range(inner // model):
                            first = big + i * share
                            in_out[0, rows, i * model:(i + 1) * model] = a[first:first + share, :].astype(F32)
                    first = layer * (b.shape[0] // layers)
                    for column in range(0, channels + LANES, model):
                        wide = min(model, channels - column)
                        in_out[0, rows, pl.ds(inner + column, wide)] = b[first:first + share, 0:wide].astype(F32)
                        if column + model >= channels:
                            extra[rows, :] = b[first:first + share, wide:wide + LANES].astype(F32)
                        first += share
            extra_out[0] = extra[:, 0:extra_out.shape[2]]
            table = extra[...].T
            heads = extra_out.shape[2]
            taps, span, part = taps_out.shape[1], taps_out.shape[2], gain_out.shape[1]
            norm_out[layer:layer + 1, :] = table[heads:heads + 1]
            row = heads + 1
            for start in range(0, part, rows_in):
                gain_out[layer:layer + 1, start:start + rows_in] = table[row:row + 1]
                row += 1
            for start in range(0, span, rows_in):
                wide = min(rows_in, span - start)
                taps_out[layer, :, start:start + wide] = table[row:row + taps, 0:wide]
                bias_out[layer:layer + 1, start:start + wide] = table[row + taps:row + taps + 1, 0:wide]
                row += taps + 1
            few = heads_out.shape[2]
            heads_out[layer] = table[row:row + 3, 0:few]


def placed_grads(at, pieces, layers, shapes, smalls, chips, inner, after):
    whole = pl.BlockSpec(memory_space=pltpu.VMEM)
    return pl.pallas_call(
        without(functools.partial(place_kernel, chips, inner, layers), 1 + len(pieces), len(after)),
        grid=(layers,),
        in_specs=[pl.BlockSpec(memory_space=pltpu.SMEM)] + [whole] * len(pieces)
        + [pl.BlockSpec(memory_space=pl.ANY)] * len(after),
        out_specs=[pl.BlockSpec((1,) + shape, lambda i: (i, 0, 0)) for shape in shapes]
        + [pl.BlockSpec(shape, lambda i, n=len(shape): (0,) * n) for shape in smalls],
        out_shape=[jax.ShapeDtypeStruct((layers,) + shape, F32) for shape in shapes] + [jax.ShapeDtypeStruct(shape, F32) for shape in smalls],
        scratch_shapes=[pltpu.VMEM((shapes[0][0], LANES), F32)],
        compiler_params=pltpu.CompilerParams(vmem_limit_bytes=VMEM),
        cost_estimate=cost(8.0),
        name="place_grads",
    )(at, *pieces, *after)


def norm_scale_of(stream):
    return lax.rsqrt(jnp.mean(stream * stream, axis=-1, keepdims=True) + EPSILON)


def on_device(
    tokens, segments, norm_gain, in_weight, dt_weight, conv_weight, conv_bias, dt_bias, a_log, d_skip,
    gate_gain, out_weight, cotangent,
):
    layers = in_weight.shape[0]
    batch, width, model = tokens.shape
    heads = dt_weight.shape[2]
    taps_len = conv_weight.shape[1]
    peers = lax.axis_size("seq")
    groups = lax.axis_size("fsdp")
    rows = batch * width
    inner = out_weight.shape[1] * groups
    channels = in_weight.shape[2] - inner
    states = (channels - inner) // 2
    span = inner // heads
    chips = peers // 2
    direct = model % (32 * groups * peers) == 0 and chips == 4 and groups == 4
    seq_at = lax.axis_index("seq")
    here = jnp.stack([seq_at % 2, seq_at // 2, lax.axis_index("fsdp")]).astype(jnp.int32)

    small = [norm_gain, conv_weight.reshape(layers, -1), conv_bias, dt_bias, a_log, d_skip, gate_gain]
    sizes = [a.shape[1] for a in small]
    own = jnp.concatenate(small, axis=1)
    if direct:
        by_partner, bits = own[None], 1
        while bits < groups:
            by_partner = jnp.concatenate([by_partner, swap(by_partner, "fsdp", bits)])
            bits *= 2
        packed = jnp.stack([lax.dynamic_index_in_dim(by_partner, here[2] ^ z, 0, keepdims=False) for z in range(groups)])
    else:
        packed = lax.all_gather(own, "fsdp", axis=0)
    pieces, at = [], 0
    for size in sizes:
        pieces.append(packed[:, :, at:at + size])
        at += size

    def joined(piece):
        return jnp.moveaxis(piece, 0, 1).reshape(layers, -1)

    norm_all = joined(pieces[0]).astype(F32)
    taps_all = jnp.moveaxis(pieces[1].reshape(groups, layers, taps_len, -1), 0, 2).reshape(layers, taps_len, channels)
    taps_all = jnp.concatenate(
        [taps_all.astype(F32), joined(pieces[2]).astype(F32)[:, None], jnp.zeros((layers, 8 - taps_len - 1, channels), F32)], axis=1
    )
    pad_heads = ((0, 0), (0, LANES - heads))
    rates_all = jnp.stack(
        [jnp.pad(joined(pieces[3]).astype(F32), pad_heads), jnp.pad(-jnp.exp(joined(pieces[4]).astype(F32)), pad_heads)], axis=1
    )
    rates_all = jnp.pad(rates_all, ((0, 0), (0, 6), (0, 0)))
    skip_all = jnp.repeat(joined(pieces[5]).astype(F32), span, axis=1)[:, None]
    gain_all = joined(pieces[6]).astype(F32)[:, None]

    all_columns = (0, inner + channels, True)
    gate_all, mix_all, out_all = [], [], []
    for layer in range(layers):
        if direct:
            share_in, share_out = model // (groups * peers), inner // (groups * peers)
            if layer == 0:
                mix_z = from_along_z(take_share(in_weight, dt_weight, 0, all_columns, here, share_in, peers, ()), groups)
                whole = fetched_by_all(
                    in_weight, dt_weight, 0, all_columns, here, groups, chips, mix_z, (norm_all, taps_all, rates_all, skip_all, gain_all)
                )
                gates, mixes = whole[:, :inner], whole[:, inner:]
                outs = None
            else:
                share = take_share(in_weight, dt_weight, layer, all_columns, here, share_in, peers, (mix_z,))
                taken, first = [share], 0
                if layer == 1:
                    share = take_share(out_weight, None, 0, (0, model, False), here, share_out, peers, (mix_z,))
                    taken = [share[i * share_in:(i + 1) * share_in] for i in range(inner // model)] + taken
                    first = inner
                whole = lax.all_gather(jnp.concatenate(taken, axis=1), ("fsdp", "seq"), axis=0, tiled=True)
                gates, mixes = whole[:, first:first + inner], whole[:, first + inner:]
                if layer == 1:
                    out_all[0] = unfolded(whole, inner, model, share_in)
                share = take_share(out_weight, None, layer, (0, model, False), here, share_out, peers, (mix_z,))
                outs = lax.all_gather(share, ("fsdp", "seq"), axis=0, tiled=True)
        else:
            steps = jnp.pad(dt_weight[layer], ((0, 0), (0, LANES - heads)))
            whole = gathered(jnp.concatenate([in_weight[layer], steps], axis=1))
            gates, mixes = whole[:, :inner], whole[:, inner:]
            outs = gathered(out_weight[layer])
        gate_all.append(gates)
        mix_all.append(mixes)
        out_all.append(outs)

    numbers = (segments + 1).astype(F32)
    before = lax.ppermute(numbers[:, width - EDGE:], "seq", [(i, i + 1) for i in range(peers - 1)])
    padded = jnp.concatenate([before, numbers], axis=1)
    columns = [padded[:, EDGE - back:EDGE - back + width] == numbers for back in range(1, taps_len)]
    columns += [numbers == before[:, EDGE - 1:], numbers == numbers[:, width - 1:]]
    marks = jnp.stack([c.astype(F32) for c in columns] + [numbers], axis=-1)
    marks = jnp.pad(marks, ((0, 0), (0, 0), (0, LANES - marks.shape[-1])))
    row_marks = jnp.broadcast_to(numbers[:, None, :], (batch, 8, width))
    lane_head = jnp.arange(inner) // span
    spread = (jnp.arange(2 * LANES)[:, None] % LANES == lane_head[None, :]).astype(BF16)

    stream = tokens.astype(F32)
    kept, sent = [], ()
    for layer in range(layers):
        norm_scale = norm_scale_of(stream)
        low = (stream * norm_scale * norm_all[layer]).astype(BF16).reshape(rows, model)
        w_gate, w_mix, w_out = gate_all[layer], mix_all[layer], out_all[layer]
        mixed_in = dot(low, w_mix).astype(BF16).reshape(batch, width, channels + LANES)
        edge = lax.ppermute(mixed_in[:, width - EDGE:], "seq", [(i, i + 1) for i in range(peers - 1)])
        gate = dot(low, w_gate).astype(BF16).reshape(batch, width, inner)
        taps, rates, skip, gain = taps_all[layer], rates_all[layer], skip_all[layer], gain_all[layer]
        act, size, sums, sums_t, state, factor = call(
            functools.partial(conv_kernel, inner), batch,
            [(mixed_in, 0), (edge, 0), (marks, 0), (taps, 1), (rates, 1), (spread, 1)],
            [
                ((batch, width, channels), BF16, 0), ((batch, width, LANES), F32, 0), ((batch, width, LANES), F32, 0),
                ((batch, heads, width), F32, 0), ((batch, states + FACTOR_ROWS, inner), BF16, 0),
                ((batch, FACTOR_ROWS, inner), BF16, 0),
            ],
            [((EDGE + width, channels), F32)], "conv_states", 8.0, after=sent,
        )
        got, other, joined_state = exchange(state, here, 1)
        (part,) = call(
            functools.partial(intra_kernel, inner, heads), batch,
            [(act, 0), (size, 0), (sums, 0), (sums_t, 0), (marks, 0), (row_marks, 0), (skip, 1), (spread, 1)],
            [((batch, width, inner), F32, 0)],
            [((width, width), F32), ((width, inner), BF16)], "mix_within", 12.0, after=(joined_state,),
        )
        before, partner = entered(got, (part, gate, w_out) if direct else (part,))
        mixed, gated, entering = call(
            functools.partial(post_kernel, inner), batch,
            [
                (part, 0), (act, 0), (before, 1), (partner, 1), (other, 0), (sums, 0), (marks, 0), (gate, 0), (gain, 1), (spread, 1),
            ],
            [((batch, width, inner), BF16, 0), ((batch, width, inner), BF16, 0), ((batch, states, inner), BF16, 0)],
            [((width, inner), F32)], "mix_gate", 6.0, here,
        )
        gated = gated.reshape(rows, inner)
        turned = None
        if direct:
            mine, send = turned_halves(gated if layer == 0 else None, low, here, groups, chips)
            turned = (mine, swap(send, "seq", 1))
            sent = (send,)
        kept.append((turned, stream, norm_scale, low, mixed_in, edge, gate, act, size, sums, sums_t, factor, entering, mixed, gated))
        stream = stream + dot(gated, w_out).reshape(batch, width, model)

    grad_stream = cotangent.astype(F32)
    collected, collected_grads, scattered, second_shares, waiting = [], [], [], [], []
    started = ()
    for layer in reversed(range(layers)):
        (turned, entry, norm_scale, low, mixed_in, edge, gate, act, size, sums, sums_t, factor, entering, mixed, gated) = kept[layer]
        w_gate, w_mix, w_out = gate_all[layer], mix_all[layer], out_all[layer]
        taps, rates, skip, gain = taps_all[layer], rates_all[layer], skip_all[layer], gain_all[layer]
        grad_low = grad_stream.astype(BF16).reshape(rows, model)
        grad_gated = dot_nt(grad_low, w_out).astype(BF16).reshape(batch, width, inner)
        d_mixed, d_gate, d_state, d_queries, d_sums, row_grads = call(
            functools.partial(gate_back_kernel, inner), batch,
            [
                (grad_gated, 0), (grad_low.reshape(batch, width, model), 0), (factor, 0), (mixed, 0), (gate, 0), (gain, 1), (act, 0),
                (entering, 0), (sums, 0), (marks, 0), (spread, 1),
            ],
            [
                ((batch, width, inner), BF16, 0), ((batch, width, inner + model), BF16, 0),
                ((batch, states + FACTOR_ROWS, inner), BF16, 0), ((batch, width, states), F32, 0), ((batch, width, LANES), F32, 0), ((8, inner), F32, 1),
            ],
            [((width, inner), F32)], "gate_back", 11.0, after=started,
        )
        got, other, joined_state = exchange(d_state, here, 0)
        both = d_gate.reshape(rows, inner + model)
        d_gate = both[:, :inner]
        started, arrived, ordered = (), (), ()
        if direct:
            big, small = inner // (groups * peers), model // (groups * peers)
            mine, theirs = turned
            both_other = swap(both, "seq", 1) if layer == 0 else None
        else:
            out_share = reduced(dot_tn(gated, grad_low).astype(BF16))
        d_stepped, d_pair, d_total = call(
            functools.partial(intra_back_kernel, inner, heads), batch,
            [
                (d_mixed, 0), (act, 0), (size, 0), (sums, 0), (sums_t, 0), (marks, 0), (row_marks, 0), (spread, 1),
                (d_queries, 0), (d_sums, 0),
            ],
            [((batch, width, inner), BF16, 0), ((batch, width, 2 * states), F32, 0), ((batch, width, LANES), F32, 0)],
            [
                ((width, width), F32), ((width, width), F32), ((width, inner), BF16), ((LANES, width), F32), ((width, LANES), F32),
            ], "mix_within_back", 17.0, after=(joined_state,),
        )
        before, partner = entered(got, (d_stepped,))
        if direct and layer > 0:
            wide = wide_grads(low, gated, both, groups, (before,))
            scattered.append(lax.psum_scatter(wide, ("fsdp", "seq"), scatter_dimension=0, tiled=True))
            arrived = (wide,)
        if direct and layer == 0:
            first_blocks = whole_call(
                functools.partial(first_grads_kernel, groups, chips, inner), [mine, theirs, both, both_other],
                [((groups, big + inner // model * small, model), BF16)] * chips, 10.0, "first_grads", after=(before,),
            )
            arrived = tuple(first_blocks)
            first_share, halved = halved_sums(plane_parts(first_blocks), groups)
            ordered = halved
            for later in waiting:
                blocks = later((first_blocks[0],))
                share, more = halved_sums(plane_parts(blocks), groups)
                ordered += (blocks[0],)
                halved += more
                second_shares.append(laid([share], model, ()))
            mine_a, other_a = spread_in_plane(first_share, chips)
        d_mixed_in, d_edge, tap_grads, head_grads = call(
            functools.partial(conv_back_kernel, inner), batch,
            [
                (d_stepped, 0), (d_mixed, 0), (act, 0), (mixed_in, 0), (edge, 0), (marks, 0), (taps, 1), (rates, 1),
                (skip, 1), (size, 0), (sums, 0), (spread, 1), (d_pair, 0), (d_total, 0), (before, 1), (partner, 1), (other, 0),
                (entering, 0),
            ],
            [
                ((batch, width, channels + LANES), BF16, 0), ((batch, EDGE, channels), F32, 0),
                ((8, channels), F32, 1), ((8, LANES), F32, 1),
            ],
            [((EDGE + width, channels), F32), ((3, width + 2 * EDGE, 256), F32)], "conv_back", 17.0, here, arrived,
        )
        from_next = lax.ppermute(d_edge.astype(BF16), "seq", [(i + 1, i) for i in range(peers - 1)])
        grad_mixed = with_edges(d_mixed_in, from_next, ordered).reshape(rows, channels + LANES)
        grad_rows = dot_nt(d_gate, w_gate) + dot_nt(grad_mixed, w_mix)
        grad_rows = grad_rows.reshape(batch, width, model)
        scaled = grad_rows * norm_all[layer]
        inward = jnp.mean(scaled * entry, axis=-1, keepdims=True)
        gain_grad = jnp.sum(grad_rows * entry * norm_scale, axis=(0, 1))
        grad_stream = grad_stream + norm_scale * scaled - (norm_scale * norm_scale * norm_scale * inward) * entry
        if direct:
            extra = whole_call(
                functools.partial(gather_small_kernel, groups, taps_len, heads), [gain_grad[None], tap_grads, head_grads, row_grads, spread],
                [((model, LANES), F32)], 3.0, "gather_small",
            )[0]
            operands = [mine, theirs, grad_mixed, swap(grad_mixed, "seq", 1), extra, swap(extra, "seq", 1)]
            kernel = functools.partial(second_grads_kernel, groups, chips, channels, heads)
            outs = [((groups, small, channels + LANES), BF16)] * chips
            if layer > 0:
                waiting.append(functools.partial(whole_call, kernel, operands, outs, 6.0, "second_grads", here))
                started = (operands[3], operands[5])
            else:
                got = plane_parts(whole_call(kernel, operands, outs, 6.0, "second_grads", here, halved))
                second_shares.append(layer_sums(got, groups, model, (stream, grad_stream) + tuple(mine_a)))
        else:
            mixed_grad = dot_tn(low, grad_mixed)
            in_share = reduced(jnp.concatenate([dot_tn(low, d_gate).astype(BF16), mixed_grad[:, :channels].astype(BF16)], axis=1))
            dt_share = reduced(mixed_grad[:, channels:].astype(BF16))
            collected_grads.append((in_share, dt_share, out_share))
            small_grads = [
                gain_grad.reshape(groups, -1),
                jnp.moveaxis(tap_grads[:taps_len].reshape(taps_len, groups, -1), 1, 0).reshape(groups, -1),
                tap_grads[taps_len].reshape(groups, -1),
                head_grads[0, :heads].reshape(groups, -1),
                head_grads[1, :heads].reshape(groups, -1),
                jnp.sum(row_grads[1].reshape(heads, span), axis=1).reshape(groups, -1),
                row_grads[0].reshape(groups, -1),
            ]
            collected.append(jnp.concatenate(small_grads, axis=1))
    if direct:
        second_share = stacked(second_shares[::-1]).reshape(-1, model)
        held = [stacked([share], (first_blocks[0],))[0] for share in scattered]
        scattered = [lax.all_gather(share, "seq", axis=0, tiled=True) for share in held]
        mine_b, other_b = spread_in_plane(second_share, chips)
        shapes = [(model // groups, inner + channels), (model // groups, heads), (inner // groups, model)]
        smalls = [
            (layers, model // groups), (layers, taps_len, channels // groups), (layers, channels // groups), (layers, 3, heads // groups),
            (layers, inner // groups),
        ]
        blocks = mine_a + [other_a] + mine_b + [other_b] + scattered[::-1]
        placed = placed_grads(here, blocks, layers, shapes, smalls, chips, inner, ())
        by_head = placed[6]
        pieces = [placed[3], placed[4], placed[5], by_head[:, 0], by_head[:, 1], by_head[:, 2], placed[7]]
    else:
        placed = [jnp.stack([c[i] for c in collected_grads[::-1]]) for i in range(3)]
        placed[1] = placed[1][:, :, :heads]
        small_sum = lax.psum(jnp.stack(collected[::-1], axis=1), ("fsdp", "seq"))
        small_sum = lax.dynamic_index_in_dim(small_sum, lax.axis_index("fsdp"), 0, keepdims=False)
        pieces, at = [], 0
        for size in sizes:
            pieces.append(small_sum[:, at:at + size])
            at += size
    return (
        stream, grad_stream, pieces[0],
        placed[0],
        placed[1],
        pieces[1].reshape(layers, taps_len, -1),
        pieces[2], pieces[3], pieces[4], pieces[5], pieces[6],
        placed[2],
    )


def solution(mesh):
    split = P("fsdp", "seq", None)
    vector = P(None, "fsdp")
    matrix = P(None, "fsdp", None)
    taps = P(None, None, "fsdp")
    return jax.shard_map(
        on_device,
        mesh=mesh,
        in_specs=(
            split, P("fsdp", "seq"), vector, matrix, matrix, taps, vector, vector, vector, vector, vector, matrix, split,
        ),
        out_specs=(
            split, split, vector, matrix, matrix, taps, vector, vector, vector, vector, vector, matrix,
        ),
        check_vma=False,
    )
```

```python
import functools

import jax
import jax.numpy as jnp
from jax import lax
from jax.experimental import pallas as pl
from jax.experimental.pallas import tpu as pltpu
from jax.sharding import PartitionSpec as P

EPSILON = 1e-05
F32, BF16 = jnp.float32, jnp.bfloat16
LANES = 128
EDGE = 8
FACTOR_ROWS = 16
SCALE = 0.25
VMEM = 48 * 1024 * 1024
NT = (((1,), (1,)), ((), ()))
TN = (((0,), (0,)), ((), ()))


def dot(a, b):
    return jnp.dot(a, b, preferred_element_type=F32)


def dot_nt(a, b):
    return lax.dot_general(a, b, NT, preferred_element_type=F32)


def dot_tn(a, b):
    return lax.dot_general(a, b, TN, preferred_element_type=F32)


def dot_exact(a, b):
    return jnp.dot(a, b, precision=lax.Precision.HIGHEST, preferred_element_type=F32)


def halves(v):
    high = v.astype(BF16)
    low = (v - high.astype(F32)).astype(BF16)
    return jnp.concatenate([high, low], axis=1)


def sigmoid(v):
    return 1.0 / (1.0 + jnp.exp(-v))


def softplus(v):
    return jnp.maximum(v, 0.0) + jnp.log1p(jnp.exp(-jnp.abs(v)))


def below(size):
    rows = lax.broadcasted_iota(jnp.int32, (size, size), 0)
    columns = lax.broadcasted_iota(jnp.int32, (size, size), 1)
    return rows >= columns


def head_column(table, head):
    return pltpu.roll(table, LANES - head, axis=1)[:, 0:1]


def conv_total(padded, taps, masks, at, wide, width):
    total = taps[4:5, pl.ds(at, wide)] + taps[3:4, pl.ds(at, wide)] * padded[EDGE:EDGE + width, pl.ds(at, wide)]
    for back in range(1, 4):
        tap = taps[3 - back:4 - back, pl.ds(at, wide)]
        total = total + (masks[back - 1] * tap) * padded[EDGE - back:EDGE - back + width, pl.ds(at, wide)]
    return total


def conv_kernel(inner, mixed, edge, marks, taps, rates, spread, act, sizes, sums, sums_t, state, factor, padded):
    width, channels = mixed.shape[1], padded.shape[1]
    padded[0:EDGE, :] = edge[0, :, 0:channels].astype(F32)
    padded[EDGE:EDGE + width, :] = mixed[0, :, 0:channels].astype(F32)
    marks_now = marks[0]
    masks = [marks_now[:, back:back + 1] for back in range(3)]
    wide = 256
    for at in range(0, channels, wide):
        total = conv_total(padded, taps, masks, at, wide, width)
        act[0, :, pl.ds(at, wide)] = (total * sigmoid(total)).astype(BF16)
    size = softplus(mixed[0, :, channels:].astype(F32) + rates[0:1, :])
    tri = jnp.where(below(width), 1.0, 0.0).astype(F32)
    total_sum = dot_exact(tri, size * rates[1:2, :])
    last = total_sum[width - 1:width]
    sizes[0] = size
    sums[0] = total_sum
    sums_t[0] = total_sum.T[0:sums_t.shape[1]]
    weight = halves(marks_now[:, 4:5] * jnp.exp(last - total_sum) * size)
    gone = marks_now[width - 1:width, 3:4] * jnp.exp(last)
    gone = halves(jnp.broadcast_to(gone, (FACTOR_ROWS, LANES)))
    states = (channels - inner) // 2
    keys_t = act[0, :, inner:inner + states].T
    for at in range(0, inner, wide):
        part = spread[:, pl.ds(at, wide)]
        weighted = (dot(weight, part) * act[0, :, pl.ds(at, wide)].astype(F32)).astype(BF16)
        state[0, 0:states, pl.ds(at, wide)] = dot(keys_t, weighted).astype(BF16)
        fade = dot(gone, part).astype(BF16)
        state[0, states:, pl.ds(at, wide)] = fade
        factor[0, :, pl.ds(at, wide)] = fade


def intra_kernel(inner, heads, act, sizes, sums, sums_t, marks, row_marks, skip, spread, out, scores, stepped):
    width = act.shape[1]
    states = (act.shape[2] - inner) // 2
    half = width // 2
    keys = act[0, :, inner:inner + states]
    queries = act[0, :, inner + states:]
    same = below(width) & (marks[0][:, 5:6] == row_marks[0, 0:1, :])
    scores[...] = jnp.where(same, dot_nt(queries, keys), 0.0)
    size = halves(sizes[0])
    wide = 256
    for at in range(0, inner, wide):
        part = dot(size, spread[:, pl.ds(at, wide)])
        stepped[:, pl.ds(at, wide)] = (part * act[0, :, pl.ds(at, wide)].astype(F32)).astype(BF16)
    per = LANES // (inner // heads)
    span = inner // heads
    lane = lax.broadcasted_iota(jnp.int32, (width, LANES), 1)

    def group(at, carry):
        place = pl.ds(pl.multiple_of(at * LANES, LANES), LANES)
        x = stepped[:, place]
        y_low = y_high = None
        for i in range(per):
            head = at * per + i
            column = head_column(sums[0], head)
            row = sums_t[0, pl.ds(head, 1), :]
            mine = (lane >= i * span) & (lane < (i + 1) * span)
            xh = jnp.where(mine, x, jnp.zeros_like(x))
            w_low = scores[0:half, 0:half] * jnp.exp(jnp.minimum(column[0:half] - row[:, 0:half], 0.0))
            w_high = scores[half:, :] * jnp.exp(jnp.minimum(column[half:] - row, 0.0))
            a = dot(w_low.astype(BF16), xh[0:half])
            b = dot(w_high.astype(BF16), xh)
            y_low = a if y_low is None else y_low + a
            y_high = b if y_high is None else y_high + b
        values = act[0, :, place].astype(F32) * skip[0:1, place]
        out[0, 0:half, place] = (y_low + values[0:half]).astype(out.dtype)
        out[0, half:, place] = (y_high + values[half:]).astype(out.dtype)
        return carry

    lax.fori_loop(0, inner // LANES, group, 0, unroll=2)


def entered_part(at, later_core, before, partner, other, place):
    states = before.shape[0]
    chip = before[:, place]
    core = jnp.full(chip.shape, at[0], jnp.int32)
    chip = jnp.where(core == pl.program_id(0), chip.astype(F32), partner[:, place].astype(F32))
    through = other[0, states:states + 1, place].astype(F32) * chip + other[0, 0:states, place].astype(F32)
    return jnp.where(core == later_core, through, chip).astype(BF16)


def post_kernel(inner, at, part_mixed, act, before, partner, other, sums, marks, gate, gain, spread, mixed, gated, entering, kept):
    states = (act.shape[2] - inner) // 2
    queries = act[0, :, inner + states:]
    enter = halves(marks[0][:, 3:4] * jnp.exp(sums[0]))
    wide = 256
    square = None
    for start in range(0, inner, wide):
        place = pl.ds(start, wide)
        state = entered_part(at, 1, before, partner, other, place)
        entering[0, :, place] = state
        whole = part_mixed[0, :, place].astype(F32) + dot(enter, spread[:, place]) * dot(queries, state)
        g = gate[0, :, place].astype(F32)
        w = whole * (g * sigmoid(g))
        mixed[0, :, place] = whole.astype(BF16)
        kept[:, place] = w
        square = w * w if square is None else square + w * w
    scale = lax.rsqrt(jnp.sum(square, axis=1, keepdims=True) / inner + EPSILON)
    for at in range(0, inner, wide):
        place = pl.ds(at, wide)
        gated[0, :, place] = (kept[:, place] * scale * gain[0:1, place]).astype(BF16)


def gate_back_kernel(
    inner, grad, grad_low, factor, mixed, gate, gain, act, state, sums, marks, spread,
    d_mixed, d_gate, d_state, d_queries, d_sums, row_grads, kept,
):
    states = (act.shape[2] - inner) // 2
    queries = act[0, :, inner + states:]
    queries_t = queries.T
    wide = 256

    @pl.when(pl.program_id(0) == 0)
    def _():
        row_grads[...] = jnp.zeros_like(row_grads)

    square = cross = None
    for at in range(0, inner, wide):
        place = pl.ds(at, wide)
        g = gate[0, :, place].astype(F32)
        w = mixed[0, :, place].astype(F32) * (g * sigmoid(g))
        gg = grad[0, :, place].astype(F32)
        kept[:, place] = w
        square = w * w if square is None else square + w * w
        more = w * gain[0:1, place] * gg
        cross = more if cross is None else cross + more
    scale = lax.rsqrt(jnp.sum(square, axis=1, keepdims=True) / inner + EPSILON)
    pulled = scale * scale * scale * (jnp.sum(cross, axis=1, keepdims=True) / inner)
    entered = marks[0][:, 3:4] * jnp.exp(sums[0])
    enter = halves(entered)
    grad_enter = dq = None
    for at in range(0, inner, wide):
        place = pl.ds(at, wide)
        g = gate[0, :, place].astype(F32)
        sig = sigmoid(g)
        silu = g * sig
        gg = grad[0, :, place].astype(F32)
        w = kept[:, place]
        whole = mixed[0, :, place].astype(F32)
        dw = scale * (gain[0:1, place] * gg) - pulled * w
        row_grads[0:1, place] += jnp.sum(gg * w * scale, axis=0, keepdims=True)
        dm = dw * silu
        d_gate[0, :, place] = (dw * whole * (sig + silu * (1.0 - sig))).astype(BF16)
        d_mixed[0, :, place] = dm.astype(BF16)
        row_grads[1:2, place] += jnp.sum(dm * act[0, :, place].astype(F32), axis=0, keepdims=True)
        part = spread[:, place]
        st = state[0, :, place]
        e = (dm * dot(enter, part)).astype(BF16)
        d_state[0, 0:states, place] = dot(queries_t, e).astype(BF16)
        more_q = dot_nt(e, st)
        dq = more_q if dq is None else dq + more_q
        through = (dm * dot(queries, st)).astype(BF16)
        more_e = dot_nt(through, part[0:LANES])
        grad_enter = more_e if grad_enter is None else grad_enter + more_e
    d_queries[0] = dq
    d_sums[0] = grad_enter * entered
    d_gate[0, :, inner:] = grad_low[0]
    d_state[0, states:, :] = factor[0]


def intra_back_kernel(
    inner, heads, d_mixed, act, sizes, sums, sums_t, marks, row_marks, spread, d_queries, d_sums,
    d_stepped, d_pair, d_total, scores, d_scores, stepped, sums_rows, sums_columns,
):
    width = act.shape[1]
    states = (act.shape[2] - inner) // 2
    half = width // 2
    keys = act[0, :, inner:inner + states]
    queries = act[0, :, inner + states:]
    rows = lax.broadcasted_iota(jnp.int32, (width, width), 0)
    columns = lax.broadcasted_iota(jnp.int32, (width, width), 1)
    same = (rows <= columns) & (marks[0][:, 5:6] == row_marks[0, 0:1, :])
    scores[...] = jnp.where(same, dot_nt(keys, queries), 0.0)
    d_scores[...] = jnp.zeros_like(d_scores)
    sums_rows[...] = jnp.zeros_like(sums_rows)
    sums_columns[...] = jnp.zeros_like(sums_columns)
    size = halves(sizes[0])
    wide = 256
    for at in range(0, inner, wide):
        part = dot(size, spread[:, pl.ds(at, wide)])
        stepped[:, pl.ds(at, wide)] = (part * act[0, :, pl.ds(at, wide)].astype(F32)).astype(BF16)
    per = LANES // (inner // heads)
    span = inner // heads
    lane = lax.broadcasted_iota(jnp.int32, (width, LANES), 1)

    eighth = lax.broadcasted_iota(jnp.int32, (8, width), 0)

    def group(at, carry):
        place = pl.ds(pl.multiple_of(at * LANES, LANES), LANES)
        x = stepped[:, place]
        dy = d_mixed[0, :, place]
        dx_low = dx_high = None
        for i in range(per):
            head = at * per + i
            column = head_column(sums[0], head)
            row = sums_t[0, pl.ds(head, 1), :]
            mine = (lane >= i * span) & (lane < (i + 1) * span)
            xh = jnp.where(mine, x, jnp.zeros_like(x))
            dyh = jnp.where(mine, dy, jnp.zeros_like(dy))
            l_low = jnp.exp(jnp.minimum(row - column[0:half], 0.0))
            l_high = jnp.exp(jnp.minimum(row[:, half:] - column[half:], 0.0))
            w_low = scores[0:half, :] * l_low
            w_high = scores[half:, half:] * l_high
            dw_low = dot_nt(xh[0:half], dy)
            dw_high = dot_nt(xh[half:], dy[half:])
            d_scores[0:half, :] += dw_low * l_low
            d_scores[half:, half:] += dw_high * l_high
            g_low = dw_low * w_low
            g_high = dw_high * w_high
            over_low = jnp.sum(g_low, axis=0, keepdims=True)
            over_high = jnp.sum(g_high, axis=0, keepdims=True)
            eight = pl.ds(pl.multiple_of(head // 8 * 8, 8), 8)
            chosen = eighth == head % 8
            sums_rows[eight, :] += jnp.where(chosen, over_low, 0.0)
            sums_rows[eight, half:] += jnp.where(chosen[:, half:], over_high, 0.0)
            here = lane[0:half] == head
            sums_columns[0:half, :] += jnp.where(here, jnp.sum(g_low, axis=1, keepdims=True), 0.0)
            sums_columns[half:, :] += jnp.where(here, jnp.sum(g_high, axis=1, keepdims=True), 0.0)
            a = dot(w_low.astype(BF16), dyh)
            b = dot(w_high.astype(BF16), dyh[half:])
            dx_low = a if dx_low is None else dx_low + a
            dx_high = b if dx_high is None else dx_high + b
        d_stepped[0, 0:half, place] = dx_low.astype(BF16)
        d_stepped[0, half:, place] = dx_high.astype(BF16)
        return carry

    lax.fori_loop(0, inner // LANES, group, 0, unroll=2)
    grad = jnp.where(same, d_scores[...], 0.0).astype(BF16)
    d_pair[0, :, 0:states] = dot(grad, queries)
    d_pair[0, :, states:] = dot(grad.T, keys) + d_queries[0]
    d_total[0] = sums_rows[...].T - sums_columns[...] + d_sums[0]


def conv_back_kernel(
    inner, here, d_stepped, d_mixed, act, mixed_in, edge, marks, taps, rates, skip, sizes, sums, spread,
    d_pair, d_total, before, partner, other, state,
    d_mixed_in, d_edge, tap_grads, head_grads, padded, shifted,
):
    width, channels = mixed_in.shape[1], padded.shape[1]
    states = (channels - inner) // 2
    wide = 256

    @pl.when(pl.program_id(0) == 0)
    def _():
        tap_grads[...] = jnp.zeros_like(tap_grads)
        head_grads[...] = jnp.zeros_like(head_grads)

    padded[0:EDGE, :] = edge[0, :, 0:channels].astype(F32)
    padded[EDGE:EDGE + width, :] = mixed_in[0, :, 0:channels].astype(F32)
    marks_now = marks[0]
    masks = [marks_now[:, back:back + 1] for back in range(3)]
    total_sum = sums[0]
    size = sizes[0]
    last = total_sum[width - 1:width]
    faded = marks_now[:, 4:5] * jnp.exp(last - total_sum)
    weight = faded * size
    weight_pair = halves(weight)
    size_pair = halves(size)
    keys = act[0, :, inner:inner + states]
    for back in range(3):
        shifted[back, 0:EDGE, :] = jnp.zeros((EDGE, wide), F32)
        shifted[back, EDGE + width:, :] = jnp.zeros((EDGE, wide), F32)

    def through_conv(at, d_act):
        place = pl.ds(at, wide)
        total = conv_total(padded, taps, masks, at, wide, width)
        sig = sigmoid(total)
        d = d_act * (sig + total * sig * (1.0 - sig))
        tap_grads[4:5, place] += jnp.sum(d, axis=0, keepdims=True)
        tap_grads[3:4, place] += jnp.sum(d * padded[EDGE:EDGE + width, place], axis=0, keepdims=True)
        back_total = taps[3:4, place] * d
        edge_total = jnp.zeros((EDGE, wide), F32)
        for back in range(1, 4):
            u = masks[back - 1] * d
            tap_grads[3 - back:4 - back, place] += jnp.sum(
                u * padded[EDGE - back:EDGE - back + width, place], axis=0, keepdims=True
            )
            shifted[back - 1, EDGE:EDGE + width, :] = u
            tap = taps[3 - back:4 - back, place]
            back_total = back_total + tap * shifted[back - 1, EDGE + back:EDGE + back + width, :]
            edge_total = edge_total + tap * shifted[back - 1, back:back + EDGE, :]
        d_mixed_in[0, :, place] = back_total.astype(BF16)
        d_edge[0, :, place] = edge_total

    d_keys = d_pair[0, :, 0:states]
    d_size = d_weight = carried = None
    for at in range(0, inner, wide):
        place = pl.ds(at, wide)
        values = act[0, :, place].astype(F32)
        part = spread[:, place]
        ds = entered_part(here, 0, before, partner, other, place)
        wide_weight = dot(weight_pair, part)
        d_weighted = dot(keys, ds)
        dx = d_stepped[0, :, place].astype(F32)
        d_act = dx * dot(size_pair, part) + d_weighted * wide_weight + skip[0:1, place] * d_mixed[0, :, place].astype(F32)
        d_keys = d_keys + dot_nt((wide_weight * values).astype(BF16), ds)
        a = dot_nt((dx * values).astype(BF16), part[0:LANES])
        b = dot_nt((d_weighted * values).astype(BF16), part[0:LANES])
        c = jnp.sum(ds.astype(F32) * state[0, :, place].astype(F32), axis=0, keepdims=True)
        c = dot_nt(jnp.broadcast_to(halves_rows(c), (EDGE, wide)), part[0:LANES])
        d_size = a if d_size is None else d_size + a
        d_weight = b if d_weight is None else d_weight + b
        carried = c if carried is None else carried + c
        through_conv(at, d_act)
    through_conv(inner, jnp.concatenate([d_keys, d_pair[0, :, states:]], axis=1))
    d_size = d_size + d_weight * faded
    pulled = d_weight * weight
    gone = marks_now[width - 1:width, 3:4] * jnp.exp(last)
    at_end = jnp.sum(pulled, axis=0, keepdims=True) + gone * carried[0:1]
    row = lax.broadcasted_iota(jnp.int32, (width, LANES), 0)
    d_sum = d_total[0] - pulled + jnp.where(row == width - 1, at_end, 0.0)
    order = lax.broadcasted_iota(jnp.int32, (width, width), 0) <= lax.broadcasted_iota(jnp.int32, (width, width), 1)
    d_rate = dot_exact(jnp.where(order, 1.0, 0.0).astype(F32), d_sum)
    d_size = d_size + d_rate * rates[1:2, :]
    d_step = d_size * sigmoid(mixed_in[0, :, channels:].astype(F32) + rates[0:1, :])
    d_mixed_in[0, :, channels:] = d_step.astype(BF16)
    head_grads[0:1, :] += jnp.sum(d_step, axis=0, keepdims=True)
    head_grads[1:2, :] += jnp.sum(d_rate * size * rates[1:2, :], axis=0, keepdims=True)


def halves_rows(v):
    return v.astype(BF16)


def without(kernel, first, count):
    def run(*refs):
        return kernel(*refs[:first], *refs[first + count:])

    return run


def call(kernel, batch, ins, outs, scratch, name, micros, at=None, after=()):
    def spec(shape, whole):
        block = tuple(shape) if whole else (1,) + tuple(shape[1:])
        if whole:
            return pl.BlockSpec(block, lambda b: (0,) * len(block))
        return pl.BlockSpec(block, lambda b: (b,) + (0,) * (len(block) - 1))

    arrays = [a for a, _ in ins]
    in_specs = [spec(a.shape, whole) for a, whole in ins]
    if at is not None:
        arrays, in_specs = [at] + arrays, [pl.BlockSpec(memory_space=pltpu.SMEM)] + in_specs
    return pl.pallas_call(
        without(kernel, len(arrays), len(after)),
        grid=(batch,),
        in_specs=in_specs + [pl.BlockSpec(memory_space=pl.ANY)] * len(after),
        out_specs=[spec(shape, whole) for shape, _, whole in outs],
        out_shape=[jax.ShapeDtypeStruct(shape, kind) for shape, kind, _ in outs],
        scratch_shapes=[pltpu.VMEM(shape, kind) for shape, kind in scratch],
        compiler_params=pltpu.CompilerParams(vmem_limit_bytes=VMEM),
        cost_estimate=cost(micros),
        name=name,
    )(*arrays, *after)


def cost(micros):
    micros = micros * SCALE
    return pl.CostEstimate(flops=int(micros * 1.1e9), bytes_accessed=int(micros * 1e6), transcendentals=0)


def edge_kernel(grad, more, out):
    size, channels = grad.shape[1], more.shape[2]
    out[0, :, channels:] = grad[0, :, channels:]
    last = jnp.concatenate([jnp.zeros((size - EDGE, channels), F32), more[0].astype(F32)], axis=0)
    out[0, :, 0:channels] = (grad[0, :, 0:channels].astype(F32) + last).astype(BF16)


def with_edges(grad, more, after):
    batch, width, wide = grad.shape
    size = 2 * EDGE
    block = pl.BlockSpec((1, size, wide), lambda b: (b, width // size - 1, 0))
    return pl.pallas_call(
        without(edge_kernel, 2, len(after)),
        grid=(batch,),
        in_specs=[block, pl.BlockSpec((1,) + more.shape[1:], lambda b: (b, 0, 0))] + [pl.BlockSpec(memory_space=pl.ANY)] * len(after),
        out_specs=block,
        out_shape=jax.ShapeDtypeStruct(grad.shape, grad.dtype),
        input_output_aliases={0: 0},
        compiler_params=pltpu.CompilerParams(vmem_limit_bytes=VMEM),
        cost_estimate=cost(1.0),
        name="with_edges",
    )(grad, more, *after)


def whole_call(kernel, arrays, outs, micros, name, at=None, after=(), scratch=()):
    spec = pl.BlockSpec(memory_space=pltpu.VMEM)
    arrays, in_specs = list(arrays), [spec] * len(arrays)
    if at is not None:
        arrays, in_specs = [at] + arrays, [pl.BlockSpec(memory_space=pltpu.SMEM)] + in_specs
    return pl.pallas_call(
        without(kernel, len(arrays), len(after)),
        in_specs=in_specs + [pl.BlockSpec(memory_space=pl.ANY)] * len(after),
        out_specs=[spec] * len(outs),
        out_shape=[jax.ShapeDtypeStruct(shape, kind) for shape, kind in outs],
        scratch_shapes=[pltpu.VMEM(shape, kind) for shape, kind in scratch],
        compiler_params=pltpu.CompilerParams(vmem_limit_bytes=VMEM),
        cost_estimate=cost(micros),
        name=name,
    )(*arrays, *after)


def swap(x, axis, bits):
    return lax.ppermute(x, axis, [(i, i ^ bits) for i in range(lax.axis_size(axis))])


def join_kernel(later_core, at, own, other, joined):
    core = at[0]
    states = own.shape[1] - FACTOR_ROWS
    for start in range(0, own.shape[2], 512):
        place = pl.ds(start, 512)
        mine = own[core, :, place].astype(F32)
        theirs = other[core, :, place].astype(F32)
        later = jnp.full(mine.shape, core, jnp.int32) == later_core
        second = jnp.where(later, mine, theirs)
        first = jnp.where(later, theirs, mine)
        gain = second[states:states + 1]
        joined[0:states, place] = (gain * first[0:states] + second[0:states]).astype(BF16)
        joined[states:, place] = (gain * first[states:]).astype(BF16)


def enter_kernel(count, *refs):
    out = refs[count]
    states = out.shape[0]
    for start in range(0, out.shape[1], 512):
        place = pl.ds(start, 512)
        before = refs[0][0:states, place].astype(F32)
        for got in refs[1:count]:
            before = got[states:states + 1, place].astype(F32) * before + got[0:states, place].astype(F32)
        out[:, place] = before.astype(BF16)


def exchange(own, at, later_core, after=()):
    peers = lax.axis_size("seq")
    other = swap(own, "seq", 1)
    joined = whole_call(functools.partial(join_kernel, later_core), [own, other], [(own.shape[1:], BF16)], 2.0, "join_states", at, after)[0]
    got = []
    for distance in range(peers // 2 - 1, 0, -1):
        step = 2 * distance if later_core == 1 else -2 * distance
        route = [(i, i + step) for i in range(peers) if 0 <= i + step < peers]
        got.append(lax.ppermute(joined, "seq", route))
    return got, other, joined


def entered(got, after):
    shape = (got[0].shape[0] - FACTOR_ROWS, got[0].shape[1])
    before = whole_call(
        functools.partial(enter_kernel, len(got)), got, [(shape, BF16)], 2.0, "enter_states", after=after
    )[0]
    return before, swap(before, "seq", 1)


def gathered(block):
    peers = lax.axis_size("seq")
    rows = block.shape[0] // peers
    share = lax.dynamic_slice_in_dim(block, lax.axis_index("seq") * rows, rows, 0)
    return lax.all_gather(share, ("fsdp", "seq"), axis=0, tiled=True)


def take_in_kernel(columns, block, steps, out):
    first, last, with_steps = columns
    wide = last - first
    out[:, 0:wide] = block[0, :, first:last]
    if with_steps:
        heads = steps.shape[2]
        out[:, wide:] = jnp.zeros((out.shape[0], LANES), BF16)
        out[:, wide:wide + heads] = steps[0]


def take_share(weight, steps, layer, columns, at, share, parts, after):
    first, last, with_steps = columns
    wide = last - first + (LANES if with_steps else 0)

    def rows(i, where):
        return (layer, where[1] * 2 + where[0] if parts > 2 else where[0], 0)

    arrays = [weight] if steps is None else [weight, steps]
    specs = [pl.BlockSpec((1, share, a.shape[2]), rows) for a in arrays]
    kernel = functools.partial(take_in_kernel, columns)
    if steps is None:
        kernel = lambda block, out: take_in_kernel(columns, block, None, out)
    inner_kernel = without(kernel, len(arrays), len(after))
    return pl.pallas_call(
        lambda where, *refs: inner_kernel(*refs),
        grid_spec=pltpu.PrefetchScalarGridSpec(
            num_scalar_prefetch=1,
            grid=(1,),
            in_specs=specs + [pl.BlockSpec(memory_space=pl.ANY)] * len(after),
            out_specs=pl.BlockSpec((share, wide), lambda i, where: (0, 0)),
        ),
        out_shape=jax.ShapeDtypeStruct((share, wide), BF16),
        compiler_params=pltpu.CompilerParams(vmem_limit_bytes=VMEM),
        cost_estimate=cost(1.0),
        name="take_share",
    )(at, *arrays, *after)


def place_rows_kernel(starts, columns, many, at, *refs):
    weight, steps = refs[0], refs[1] if many == 2 else None
    sources, out = refs[many:-1], refs[-1]
    core, chip, group = at[0], at[1], at[2]
    rows = weight.shape[1]
    own = pl.ds(pl.multiple_of(group * rows, rows), rows)
    first, last, with_steps = columns
    wide = last - first
    out[own, 0:wide] = weight[0, :, first:last]
    if with_steps:
        out[own, wide:] = jnp.concatenate([steps[0], jnp.zeros((rows, LANES - steps.shape[2]), BF16)], axis=1)
    for source, index, rows, place in starts:
        start = pl.multiple_of(place(core, chip, group), rows)
        out[pl.ds(start, rows), :] = sources[source][index]


def placed_rows(at, weight, steps, layer, columns, sources, starts, groups, micros, after=()):
    whole = pl.BlockSpec(memory_space=pltpu.VMEM)
    own = [weight] if steps is None else [weight, steps]
    first, last, with_steps = columns
    shape = (weight.shape[1] * groups, last - first + (LANES if with_steps else 0))
    return pl.pallas_call(
        without(functools.partial(place_rows_kernel, starts, columns, len(own)), 1 + len(own) + len(sources), len(after)),
        grid=(1,),
        in_specs=[pl.BlockSpec(memory_space=pltpu.SMEM)]
        + [pl.BlockSpec((1,) + a.shape[1:], lambda i: (layer, 0, 0)) for a in own] + [whole] * len(sources)
        + [pl.BlockSpec(memory_space=pl.ANY)] * len(after),
        out_specs=whole,
        out_shape=jax.ShapeDtypeStruct(shape, BF16),
        compiler_params=pltpu.CompilerParams(vmem_limit_bytes=VMEM),
        cost_estimate=cost(micros),
        name="place_rows",
    )(at, *own, *sources, *after)


def stack_kernel(count, *refs):
    out, row = refs[count], 0
    for ref in refs[:count]:
        if len(ref.shape) == 2:
            out[row] = ref[...]
            row += 1
        else:
            out[row:row + ref.shape[0]] = ref[...]
            row += ref.shape[0]


def stacked(blocks, after=()):
    many = sum(1 if b.ndim == 2 else b.shape[0] for b in blocks)
    return whole_call(
        functools.partial(stack_kernel, len(blocks)), blocks, [((many,) + blocks[0].shape[-2:], BF16)], 1.0, "stack", after=after
    )[0]


def unfold_kernel(share, folded, out):
    many = folded.shape[1] // out.shape[1]
    model = out.shape[1]
    for block in range(folded.shape[0] // share):
        for i in range(many):
            to = (block * many + i) * share
            out[to:to + share, :] = folded[block * share:(block + 1) * share, i * model:(i + 1) * model]


def unfolded(whole, inner, model, share):
    rows = whole.shape[0] // 4
    return pl.pallas_call(
        functools.partial(unfold_kernel, share),
        grid=(4,),
        in_specs=[pl.BlockSpec((rows, inner), lambda i: (i, 0))],
        out_specs=pl.BlockSpec((rows * inner // model, model), lambda i: (i, 0)),
        out_shape=jax.ShapeDtypeStruct((inner, model), BF16),
        compiler_params=pltpu.CompilerParams(vmem_limit_bytes=VMEM),
        cost_estimate=cost(3.0),
        name="unfold",
    )(whole)


def from_along_z(mine, groups, after=()):
    return stacked([swap(mine, "fsdp", e) for e in range(1, groups)], after)


def fetched_by_all(weight, steps, layer, columns, at, groups, chips, from_z, place_after=()):
    rows = weight.shape[1]
    share = rows // (2 * chips)
    sources = [from_z] + [swap(from_z, "seq", 2 * d) for d in range(1, chips)]
    sources.append(swap(stacked([a.reshape(-1, a.shape[2]) for a in sources]), "seq", 1))

    def place_of(d, e, other):
        return lambda core, chip, group: (group ^ e) * rows + (chip ^ d) * (2 * share) + (core ^ other) * share

    starts = []
    for d in range(chips):
        for e in range(1, groups):
            index = e - 1
            starts.append((d, (index,), share, place_of(d, e, 0)))
            starts.append((chips, (d, slice(index * share, (index + 1) * share)), share, place_of(d, e, 1)))
    return placed_rows(at, weight, steps, layer, columns, sources, starts, groups, 4.0, place_after)


def reduced(grad):
    share = lax.psum_scatter(grad, ("fsdp", "seq"), scatter_dimension=0, tiled=True)
    return lax.all_gather(share, "seq", axis=0, tiled=True).astype(F32)


def turn_kernel(groups, chips, at, gated, low, own, send, turned):
    core, chip, group = at[0], at[1], at[2]
    base = 0
    for x in (gated, low):
        if x is None:
            continue
        total = x.shape[1]
        share = total // (2 * groups * chips)
        for start in range(0, total, 256):
            turned[start:start + 256, :] = x[:, start:start + 256].T
        for other, out in ((0, own), (1, send)):
            for d in range(chips):
                for e in range(groups):
                    start = (group ^ e) * (total // groups) + (chip ^ d) * (2 * share) + (core ^ other) * share
                    to = base + (d * groups + e) * share
                    out[to:to + share, :] = turned[pl.ds(pl.multiple_of(start, share), share), :]
        base += total // 2


def turned_halves(gated, low, at, groups, chips):
    rows = low.shape[0]
    if gated is None:
        def kernel(where, low_ref, *refs):
            turn_kernel(groups, chips, where, None, low_ref, *refs)

        return whole_call(kernel, [low], [((low.shape[1] // 2, rows), BF16)] * 2, 2.0, "turn", at, scratch=[(low.shape[::-1], BF16)])
    half = ((gated.shape[1] + low.shape[1]) // 2, rows)
    return whole_call(
        functools.partial(turn_kernel, groups, chips), [gated, low], [(half, BF16)] * 2, 4.0, "turn", at,
        scratch=[((gated.shape[1], rows), BF16)],
    )


def first_grads_kernel(groups, chips, inner, joined, at, own, other, grad, grad_other, *refs):
    wide = grad.shape[1] - inner
    total_big = inner // 2
    big = total_big // (groups * chips)
    small = (own.shape[0] - total_big) // (groups * chips)
    outs = refs[1:] if joined else refs
    group = at[2]

    def put(total, share, start, column):
        for d in range(chips):
            for e in range(groups):
                block = (d * groups + e) * share
                rows, columns = slice(start, start + share), pl.ds(column, 512)
                if joined:
                    outs[d][e, rows, columns] = total[block:block + share]
                else:
                    outs[0][group ^ e, d, rows, columns] = total[block:block + share]

    if joined:
        for d in range(chips):
            outs[d][groups] = refs[0][d]
    for start in range(0, wide, 512):
        place = pl.ds(inner + start, 512)
        total = dot(own[0:total_big, :], grad[:, place]) + dot(other[0:total_big, :], grad_other[:, place])
        put(total.astype(BF16), big, 0, start)
    for start in range(0, inner, 512):
        place = pl.ds(start, 512)
        total = dot(own[total_big:, :], grad[:, place]) + dot(other[total_big:, :], grad_other[:, place])
        put(total.astype(BF16), small, big + start // wide * small, start % wide)


def second_grads_kernel(groups, chips, channels, heads, here, own, other, grad, grad_other, extra, extra_other, *outs):
    rows = extra.shape[0] // 2
    base = own.shape[0] - rows
    share = rows // (groups * chips)
    core, chip, group = here[0], here[1], here[2]
    lane = lax.broadcasted_iota(jnp.int32, (share, LANES), 1)
    total_wide = channels + LANES
    edges = list(range(0, channels, 512)) + [channels, total_wide]
    for at, end in zip(edges[:-1], edges[1:]):
        place = pl.ds(at, end - at)
        total = dot(own[base:, :], grad[:, place]) + dot(other[base:, :], grad_other[:, place])
        for d in range(chips):
            for e in range(groups):
                block = (d * groups + e) * share
                part = total[block:block + share]
                if at == channels:
                    start = (group ^ e) * (2 * rows // groups) + (chip ^ d) * (2 * share) + core * share
                    here_rows = pl.ds(pl.multiple_of(start, share), share)
                    part = jnp.where(lane < heads, part, extra[here_rows, :] + extra_other[here_rows, :])
                outs[d][e, :, place] = part.astype(BF16)


def gather_small_kernel(groups, taps, heads, gain, tap_grads, head_grads, row_grads, spread, out):
    cut = out.shape[0] // groups
    channels, inner = tap_grads.shape[1], row_grads.shape[1]
    skip = row_grads[1:2, :]
    high = skip.astype(BF16)
    low = (skip - high.astype(F32)).astype(BF16)
    ones = spread[0:LANES, :]
    skip = dot_nt(jnp.broadcast_to(high, (8, inner)), ones) + dot_nt(jnp.broadcast_to(low, (8, inner)), ones)
    span, part, few = channels // groups, inner // groups, heads // groups
    for z in range(groups):
        rows = [jnp.zeros((heads, cut), F32), gain[0:1, z * cut:(z + 1) * cut]]
        for at in range(0, part, cut):
            rows.append(row_grads[0:1, z * part + at:z * part + at + cut])
        for at in range(0, span, cut):
            wide = min(cut, span - at)
            block = tap_grads[0:taps + 1, z * span + at:z * span + at + wide]
            if wide < cut:
                block = jnp.concatenate([block, jnp.zeros((taps + 1, cut - wide), F32)], axis=1)
            rows.append(block)
        lane = lax.broadcasted_iota(jnp.int32, (1, LANES), 1)
        for row in (head_grads[0:1, :], head_grads[1:2, :], skip[0:1, :]):
            row = pltpu.roll(row, (LANES - z * few) % LANES, axis=1) if z else row
            row = jnp.where(lane < few, row, 0.0)
            rows.append(jnp.concatenate([row] + [jnp.zeros((1, cut - LANES), F32)], axis=1))
        table = jnp.concatenate(rows, axis=0)
        table = jnp.concatenate([table, jnp.zeros((LANES - table.shape[0], cut), F32)], axis=0)
        out[z * cut:(z + 1) * cut, :] = table.T


def add_kernel(count, *refs):
    ins, outs = refs[:count], refs[count:]
    for i, out in enumerate(outs):
        total = ins[0][i].astype(F32)
        for more in ins[1:]:
            total = total + more[i].astype(F32)
        out[...] = total.astype(out.dtype)


def halve_kernel(count, *refs):
    ins, (near, far, *more_outs) = refs[:count], refs[count:]
    half = near.shape[0]
    for i in range(2 * half + len(more_outs)):
        total = ins[0][i].astype(F32)
        for more in ins[1:]:
            total = total + more[i].astype(F32)
        if i < half:
            near[i] = total.astype(BF16)
        elif i < 2 * half:
            far[i - half] = total.astype(BF16)
        else:
            more_outs[0][...] = total.astype(BF16)


def lay_kernel(count, layers, *refs):
    out = refs[-1]
    wide = out.shape[1]
    share, columns = refs[0].shape[0] // layers, refs[0].shape[1]
    row = 0
    for layer in range(layers):
        rows = slice(layer * share, (layer + 1) * share)
        for at in range(0, columns, wide):
            width = min(wide, columns - at)
            total = refs[0][rows, at:at + width].astype(F32)
            for more in refs[1:count]:
                total = total + more[rows, at:at + width].astype(F32)
            out[row:row + share, 0:width] = total.astype(BF16)
            if width < wide:
                out[row:row + share, width:] = jnp.zeros((share, wide - width), BF16)
            row += share


def plane_parts(blocks):
    return [blocks[0]] + [swap(blocks[i], "seq", 2 * i) for i in range(1, len(blocks))]


def halved(got, after=()):
    parts, rows, columns = got[0].shape
    outs = [((parts // 2, rows, columns), BF16)] * 2 + [((rows, columns), BF16)] * (parts % 2)
    return whole_call(functools.partial(halve_kernel, len(got)), got, outs, 2.0, "add_halves", after=after)


def halved_sums(near, far, after):
    parts, rows, columns = near.shape
    got = [near, swap(far, "fsdp", parts)]
    while parts > 1:
        near, far = halved(got, after)
        parts //= 2
        got = [near, swap(far, "fsdp", parts)]
    return whole_call(functools.partial(add_kernel, 2), got, [((rows, columns), BF16)], 1.0, "add_halves", after=after)[0]


def laid(got, wide, after):
    rows, columns = got[0].shape
    shape = (-(-columns // wide) * rows, wide)
    return whole_call(functools.partial(lay_kernel, len(got), 1), got, [(shape, BF16)], 2.0, "lay_sums", after=after)[0]


def layer_sums(got, groups, wide, after):
    parts, rows, columns = got[0].shape
    shares = whole_call(functools.partial(add_kernel, len(got)), got, [((rows, columns), BF16)] * parts, 2.0, "add_plane")
    return laid([shares[0]] + [swap(shares[e], "fsdp", e) for e in range(1, groups)], wide, after)


def spread_in_plane(share, chips):
    mine = [share] + [swap(share, "seq", 2 * d) for d in range(1, chips)]
    return mine, swap(stacked(mine), "seq", 1)


def place_kernel(chips, inner, layers, at, *refs):
    mine_a, other_a = refs[:chips], refs[chips]
    mine_b, other_b = refs[chips + 1:2 * chips + 1], refs[2 * chips + 1]
    in_out, extra_out, out_out, norm_out, taps_out, bias_out, heads_out, gain_out, extra = refs[-9:]
    core, chip = at[0], at[1]
    model = other_a.shape[2]
    rows_in, rows_out = in_out.shape[1], out_out.shape[1]
    big, share = rows_out // (2 * chips), rows_in // (2 * chips)
    channels = in_out.shape[2] - inner
    for layer in range(layers):
        @pl.when(pl.program_id(0) == layer)
        def _():
            for d in range(chips):
                for is_other in range(2):
                    a, b = (other_a.at[d], other_b.at[d]) if is_other else (mine_a[d], mine_b[d])
                    start = (chip ^ d) * (2 * share) + (core ^ is_other) * share
                    rows = pl.ds(pl.multiple_of(start, share), share)
                    start = (chip ^ d) * (2 * big) + (core ^ is_other) * big
                    first = layer * (a.shape[0] // layers)
                    out_out[0, pl.ds(pl.multiple_of(start, big), big), :] = a[first:first + big, :].astype(F32)
                    first += big
                    for i in range(inner // model):
                        in_out[0, rows, i * model:(i + 1) * model] = a[first:first + share, :].astype(F32)
                        first += share
                    first = layer * (b.shape[0] // layers)
                    for column in range(0, channels + LANES, model):
                        wide = min(model, channels - column)
                        in_out[0, rows, pl.ds(inner + column, wide)] = b[first:first + share, 0:wide].astype(F32)
                        if column + model >= channels:
                            extra[rows, :] = b[first:first + share, wide:wide + LANES].astype(F32)
                        first += share
            extra_out[0] = extra[:, 0:extra_out.shape[2]]
            table = extra[...].T
            heads = extra_out.shape[2]
            taps, span, part = taps_out.shape[1], taps_out.shape[2], gain_out.shape[1]
            norm_out[layer:layer + 1, :] = table[heads:heads + 1]
            row = heads + 1
            for start in range(0, part, rows_in):
                gain_out[layer:layer + 1, start:start + rows_in] = table[row:row + 1]
                row += 1
            for start in range(0, span, rows_in):
                wide = min(rows_in, span - start)
                taps_out[layer, :, start:start + wide] = table[row:row + taps, 0:wide]
                bias_out[layer:layer + 1, start:start + wide] = table[row + taps:row + taps + 1, 0:wide]
                row += taps + 1
            few = heads_out.shape[2]
            heads_out[layer] = table[row:row + 3, 0:few]


def placed_grads(at, pieces, layers, shapes, smalls, chips, inner, after):
    whole = pl.BlockSpec(memory_space=pltpu.VMEM)
    return pl.pallas_call(
        without(functools.partial(place_kernel, chips, inner, layers), 1 + len(pieces), len(after)),
        grid=(layers,),
        in_specs=[pl.BlockSpec(memory_space=pltpu.SMEM)] + [whole] * len(pieces)
        + [pl.BlockSpec(memory_space=pl.ANY)] * len(after),
        out_specs=[pl.BlockSpec((1,) + shape, lambda i: (i, 0, 0)) for shape in shapes]
        + [pl.BlockSpec(shape, lambda i, n=len(shape): (0,) * n) for shape in smalls],
        out_shape=[jax.ShapeDtypeStruct((layers,) + shape, F32) for shape in shapes] + [jax.ShapeDtypeStruct(shape, F32) for shape in smalls],
        scratch_shapes=[pltpu.VMEM((shapes[0][0], LANES), F32)],
        compiler_params=pltpu.CompilerParams(vmem_limit_bytes=VMEM),
        cost_estimate=cost(8.0),
        name="place_grads",
    )(at, *pieces, *after)


def norm_scale_of(stream):
    return lax.rsqrt(jnp.mean(stream * stream, axis=-1, keepdims=True) + EPSILON)


def on_device(
    tokens, segments, norm_gain, in_weight, dt_weight, conv_weight, conv_bias, dt_bias, a_log, d_skip,
    gate_gain, out_weight, cotangent,
):
    layers = in_weight.shape[0]
    batch, width, model = tokens.shape
    heads = dt_weight.shape[2]
    taps_len = conv_weight.shape[1]
    peers = lax.axis_size("seq")
    groups = lax.axis_size("fsdp")
    rows = batch * width
    inner = out_weight.shape[1] * groups
    channels = in_weight.shape[2] - inner
    states = (channels - inner) // 2
    span = inner // heads
    chips = peers // 2
    direct = model % (32 * groups * peers) == 0 and chips == 4 and groups == 4 and layers == 2
    seq_at = lax.axis_index("seq")
    here = jnp.stack([seq_at % 2, seq_at // 2, lax.axis_index("fsdp")]).astype(jnp.int32)

    small = [norm_gain, conv_weight.reshape(layers, -1), conv_bias, dt_bias, a_log, d_skip, gate_gain]
    sizes = [a.shape[1] for a in small]
    own = jnp.concatenate(small, axis=1)
    if direct:
        by_partner, bits = own[None], 1
        while bits < groups:
            by_partner = jnp.concatenate([by_partner, swap(by_partner, "fsdp", bits)])
            bits *= 2
        packed = jnp.stack([lax.dynamic_index_in_dim(by_partner, here[2] ^ z, 0, keepdims=False) for z in range(groups)])
    else:
        packed = lax.all_gather(own, "fsdp", axis=0)
    pieces, at = [], 0
    for size in sizes:
        pieces.append(packed[:, :, at:at + size])
        at += size

    def joined(piece):
        return jnp.moveaxis(piece, 0, 1).reshape(layers, -1)

    norm_all = joined(pieces[0]).astype(F32)
    taps_all = jnp.moveaxis(pieces[1].reshape(groups, layers, taps_len, -1), 0, 2).reshape(layers, taps_len, channels)
    taps_all = jnp.concatenate(
        [taps_all.astype(F32), joined(pieces[2]).astype(F32)[:, None], jnp.zeros((layers, 8 - taps_len - 1, channels), F32)], axis=1
    )
    pad_heads = ((0, 0), (0, LANES - heads))
    rates_all = jnp.stack(
        [jnp.pad(joined(pieces[3]).astype(F32), pad_heads), jnp.pad(-jnp.exp(joined(pieces[4]).astype(F32)), pad_heads)], axis=1
    )
    rates_all = jnp.pad(rates_all, ((0, 0), (0, 6), (0, 0)))
    skip_all = jnp.repeat(joined(pieces[5]).astype(F32), span, axis=1)[:, None]
    gain_all = joined(pieces[6]).astype(F32)[:, None]

    all_columns = (0, inner + channels, True)
    gate_all, mix_all, out_all = [], [], []
    for layer in range(layers):
        if direct:
            share_in, share_out = model // (groups * peers), inner // (groups * peers)
            if layer == 0:
                mix_z = from_along_z(take_share(in_weight, dt_weight, 0, all_columns, here, share_in, peers, ()), groups)
                whole = fetched_by_all(
                    in_weight, dt_weight, 0, all_columns, here, groups, chips, mix_z, (norm_all, taps_all, rates_all, skip_all, gain_all)
                )
                gates, mixes = whole[:, :inner], whole[:, inner:]
                outs = None
            else:
                share = take_share(in_weight, dt_weight, layer, all_columns, here, share_in, peers, (mix_z,))
                taken, first = [share], 0
                if layer == 1:
                    share = take_share(out_weight, None, 0, (0, model, False), here, share_out, peers, (mix_z,))
                    taken = [share[i * share_in:(i + 1) * share_in] for i in range(inner // model)] + taken
                    first = inner
                whole = lax.all_gather(jnp.concatenate(taken, axis=1), ("fsdp", "seq"), axis=0, tiled=True)
                gates, mixes = whole[:, first:first + inner], whole[:, first + inner:]
                if layer == 1:
                    out_all[0] = unfolded(whole, inner, model, share_in)
                share = take_share(out_weight, None, layer, (0, model, False), here, share_out, peers, (mix_z,))
                outs = lax.all_gather(share, ("fsdp", "seq"), axis=0, tiled=True)
        else:
            steps = jnp.pad(dt_weight[layer], ((0, 0), (0, LANES - heads)))
            whole = gathered(jnp.concatenate([in_weight[layer], steps], axis=1))
            gates, mixes = whole[:, :inner], whole[:, inner:]
            outs = gathered(out_weight[layer])
        gate_all.append(gates)
        mix_all.append(mixes)
        out_all.append(outs)

    numbers = (segments + 1).astype(F32)
    before = lax.ppermute(numbers[:, width - EDGE:], "seq", [(i, i + 1) for i in range(peers - 1)])
    padded = jnp.concatenate([before, numbers], axis=1)
    columns = [padded[:, EDGE - back:EDGE - back + width] == numbers for back in range(1, taps_len)]
    columns += [numbers == before[:, EDGE - 1:], numbers == numbers[:, width - 1:]]
    marks = jnp.stack([c.astype(F32) for c in columns] + [numbers], axis=-1)
    marks = jnp.pad(marks, ((0, 0), (0, 0), (0, LANES - marks.shape[-1])))
    row_marks = jnp.broadcast_to(numbers[:, None, :], (batch, 8, width))
    lane_head = jnp.arange(inner) // span
    spread = (jnp.arange(2 * LANES)[:, None] % LANES == lane_head[None, :]).astype(BF16)

    stream = tokens.astype(F32)
    kept, sent = [], ()
    for layer in range(layers):
        norm_scale = norm_scale_of(stream)
        low = (stream * norm_scale * norm_all[layer]).astype(BF16).reshape(rows, model)
        w_gate, w_mix, w_out = gate_all[layer], mix_all[layer], out_all[layer]
        mixed_in = dot(low, w_mix).astype(BF16).reshape(batch, width, channels + LANES)
        edge = lax.ppermute(mixed_in[:, width - EDGE:], "seq", [(i, i + 1) for i in range(peers - 1)])
        gate = dot(low, w_gate).astype(BF16).reshape(batch, width, inner)
        taps, rates, skip, gain = taps_all[layer], rates_all[layer], skip_all[layer], gain_all[layer]
        act, size, sums, sums_t, state, factor = call(
            functools.partial(conv_kernel, inner), batch,
            [(mixed_in, 0), (edge, 0), (marks, 0), (taps, 1), (rates, 1), (spread, 1)],
            [
                ((batch, width, channels), BF16, 0), ((batch, width, LANES), F32, 0), ((batch, width, LANES), F32, 0),
                ((batch, heads, width), F32, 0), ((batch, states + FACTOR_ROWS, inner), BF16, 0),
                ((batch, FACTOR_ROWS, inner), BF16, 0),
            ],
            [((EDGE + width, channels), F32)], "conv_states", 8.0, after=sent,
        )
        got, other, joined_state = exchange(state, here, 1)
        (part,) = call(
            functools.partial(intra_kernel, inner, heads), batch,
            [(act, 0), (size, 0), (sums, 0), (sums_t, 0), (marks, 0), (row_marks, 0), (skip, 1), (spread, 1)],
            [((batch, width, inner), F32, 0)],
            [((width, width), F32), ((width, inner), BF16)], "mix_within", 12.0, after=(joined_state,),
        )
        before, partner = entered(got, (part, gate, w_out) if direct else (part,))
        mixed, gated, entering = call(
            functools.partial(post_kernel, inner), batch,
            [
                (part, 0), (act, 0), (before, 1), (partner, 1), (other, 0), (sums, 0), (marks, 0), (gate, 0), (gain, 1), (spread, 1),
            ],
            [((batch, width, inner), BF16, 0), ((batch, width, inner), BF16, 0), ((batch, states, inner), BF16, 0)],
            [((width, inner), F32)], "mix_gate", 6.0, here,
        )
        gated = gated.reshape(rows, inner)
        turned = None
        if direct:
            mine, send = turned_halves(gated, low, here, groups, chips)
            turned = (mine, swap(send, "seq", 1))
            sent = (send,)
        kept.append((turned, stream, norm_scale, low, mixed_in, edge, gate, act, size, sums, sums_t, factor, entering, mixed, gated))
        stream = stream + dot(gated, w_out).reshape(batch, width, model)

    grad_stream = cotangent.astype(F32)
    collected, collected_grads, far_sums, second_shares, waiting = [], [], [], [], []
    started = ()
    for layer in reversed(range(layers)):
        (turned, entry, norm_scale, low, mixed_in, edge, gate, act, size, sums, sums_t, factor, entering, mixed, gated) = kept[layer]
        w_gate, w_mix, w_out = gate_all[layer], mix_all[layer], out_all[layer]
        taps, rates, skip, gain = taps_all[layer], rates_all[layer], skip_all[layer], gain_all[layer]
        grad_low = grad_stream.astype(BF16).reshape(rows, model)
        grad_gated = dot_nt(grad_low, w_out).astype(BF16).reshape(batch, width, inner)
        d_mixed, d_gate, d_state, d_queries, d_sums, row_grads = call(
            functools.partial(gate_back_kernel, inner), batch,
            [
                (grad_gated, 0), (grad_low.reshape(batch, width, model), 0), (factor, 0), (mixed, 0), (gate, 0), (gain, 1), (act, 0),
                (entering, 0), (sums, 0), (marks, 0), (spread, 1),
            ],
            [
                ((batch, width, inner), BF16, 0), ((batch, width, inner + model), BF16, 0),
                ((batch, states + FACTOR_ROWS, inner), BF16, 0), ((batch, width, states), F32, 0), ((batch, width, LANES), F32, 0), ((8, inner), F32, 1),
            ],
            [((width, inner), F32)], "gate_back", 11.0, after=started,
        )
        got, other, joined_state = exchange(d_state, here, 0)
        both = d_gate.reshape(rows, inner + model)
        d_gate = both[:, :inner]
        started, arrived, ordered = (), (), ()
        if direct:
            big, small = inner // (groups * peers), model // (groups * peers)
            mine, theirs = turned
            both_other = swap(both, "seq", 1)
        else:
            out_share = reduced(dot_tn(gated, grad_low).astype(BF16))
        d_stepped, d_pair, d_total = call(
            functools.partial(intra_back_kernel, inner, heads), batch,
            [
                (d_mixed, 0), (act, 0), (size, 0), (sums, 0), (sums_t, 0), (marks, 0), (row_marks, 0), (spread, 1),
                (d_queries, 0), (d_sums, 0),
            ],
            [((batch, width, inner), BF16, 0), ((batch, width, 2 * states), F32, 0), ((batch, width, LANES), F32, 0)],
            [
                ((width, width), F32), ((width, width), F32), ((width, inner), BF16), ((LANES, width), F32), ((width, LANES), F32),
            ], "mix_within_back", 17.0, after=(joined_state,),
        )
        before, partner = entered(got, (d_stepped,))
        if direct and layer > 0:
            (parts,) = whole_call(
                functools.partial(first_grads_kernel, groups, chips, inner, False), [mine, theirs, both, both_other],
                [((groups, chips, big + inner // model * small, model), BF16)], 10.0, "first_grads", here, (before,),
            )
            far_sums.append(lax.psum_scatter(parts, "fsdp", scatter_dimension=0, tiled=True)[0])
            arrived = (parts,)
        if direct and layer == 0:
            first_blocks = whole_call(
                functools.partial(first_grads_kernel, groups, chips, inner, True), [mine, theirs, both, both_other] + far_sums,
                [((groups + 1, big + inner // model * small, model), BF16)] * chips, 10.0, "first_grads", here, (before,),
            )
            arrived = tuple(first_blocks)
            near, far, *passed = halved(plane_parts(first_blocks))
            ordered = (near,)
            gots = []
            for later in waiting:
                blocks = later((first_blocks[0],))
                gots.append(plane_parts(blocks))
                ordered += (blocks[0],)
        d_mixed_in, d_edge, tap_grads, head_grads = call(
            functools.partial(conv_back_kernel, inner), batch,
            [
                (d_stepped, 0), (d_mixed, 0), (act, 0), (mixed_in, 0), (edge, 0), (marks, 0), (taps, 1), (rates, 1),
                (skip, 1), (size, 0), (sums, 0), (spread, 1), (d_pair, 0), (d_total, 0), (before, 1), (partner, 1), (other, 0),
                (entering, 0),
            ],
            [
                ((batch, width, channels + LANES), BF16, 0), ((batch, EDGE, channels), F32, 0),
                ((8, channels), F32, 1), ((8, LANES), F32, 1),
            ],
            [((EDGE + width, channels), F32), ((3, width + 2 * EDGE, 256), F32)], "conv_back", 17.0, here, arrived,
        )
        from_next = lax.ppermute(d_edge.astype(BF16), "seq", [(i + 1, i) for i in range(peers - 1)])
        grad_mixed = with_edges(d_mixed_in, from_next, ordered).reshape(rows, channels + LANES)
        grad_rows = dot_nt(d_gate, w_gate) + dot_nt(grad_mixed, w_mix)
        grad_rows = grad_rows.reshape(batch, width, model)
        scaled = grad_rows * norm_all[layer]
        inward = jnp.mean(scaled * entry, axis=-1, keepdims=True)
        gain_grad = jnp.sum(grad_rows * entry * norm_scale, axis=(0, 1))
        grad_stream = grad_stream + norm_scale * scaled - (norm_scale * norm_scale * norm_scale * inward) * entry
        if direct:
            extra = whole_call(
                functools.partial(gather_small_kernel, groups, taps_len, heads), [gain_grad[None], tap_grads, head_grads, row_grads, spread],
                [((model, LANES), F32)], 3.0, "gather_small",
            )[0]
            operands = [mine, theirs, grad_mixed, swap(grad_mixed, "seq", 1), extra, swap(extra, "seq", 1)]
            kernel = functools.partial(second_grads_kernel, groups, chips, channels, heads)
            outs = [((groups, small, channels + LANES), BF16)] * chips
            if layer > 0:
                waiting.append(functools.partial(whole_call, kernel, operands, outs, 6.0, "second_grads", here))
                started = (operands[3], operands[5])
            else:
                blocks = whole_call(kernel, operands, outs, 6.0, "second_grads", here)
                after = (blocks[0],)
                first_share = stacked([halved_sums(near, far, after)] + passed).reshape(-1, model)
                mine_a, other_a = spread_in_plane(first_share, chips)
                for got in gots:
                    near, far = halved(got, after)
                    second_shares.append(laid([halved_sums(near, far, ())], model, ()))
                second_shares.append(layer_sums(plane_parts(blocks), groups, model, (stream, grad_stream) + tuple(mine_a)))
        else:
            mixed_grad = dot_tn(low, grad_mixed)
            in_share = reduced(jnp.concatenate([dot_tn(low, d_gate).astype(BF16), mixed_grad[:, :channels].astype(BF16)], axis=1))
            dt_share = reduced(mixed_grad[:, channels:].astype(BF16))
            collected_grads.append((in_share, dt_share, out_share))
            small_grads = [
                gain_grad.reshape(groups, -1),
                jnp.moveaxis(tap_grads[:taps_len].reshape(taps_len, groups, -1), 1, 0).reshape(groups, -1),
                tap_grads[taps_len].reshape(groups, -1),
                head_grads[0, :heads].reshape(groups, -1),
                head_grads[1, :heads].reshape(groups, -1),
                jnp.sum(row_grads[1].reshape(heads, span), axis=1).reshape(groups, -1),
                row_grads[0].reshape(groups, -1),
            ]
            collected.append(jnp.concatenate(small_grads, axis=1))
    if direct:
        second_share = stacked(second_shares[::-1]).reshape(-1, model)
        mine_b, other_b = spread_in_plane(second_share, chips)
        shapes = [(model // groups, inner + channels), (model // groups, heads), (inner // groups, model)]
        smalls = [
            (layers, model // groups), (layers, taps_len, channels // groups), (layers, channels // groups), (layers, 3, heads // groups),
            (layers, inner // groups),
        ]
        blocks = mine_a + [other_a] + mine_b + [other_b]
        placed = placed_grads(here, blocks, layers, shapes, smalls, chips, inner, ())
        by_head = placed[6]
        pieces = [placed[3], placed[4], placed[5], by_head[:, 0], by_head[:, 1], by_head[:, 2], placed[7]]
    else:
        placed = [jnp.stack([c[i] for c in collected_grads[::-1]]) for i in range(3)]
        placed[1] = placed[1][:, :, :heads]
        small_sum = lax.psum(jnp.stack(collected[::-1], axis=1), ("fsdp", "seq"))
        small_sum = lax.dynamic_index_in_dim(small_sum, lax.axis_index("fsdp"), 0, keepdims=False)
        pieces, at = [], 0
        for size in sizes:
            pieces.append(small_sum[:, at:at + size])
            at += size
    return (
        stream, grad_stream, pieces[0],
        placed[0],
        placed[1],
        pieces[1].reshape(layers, taps_len, -1),
        pieces[2], pieces[3], pieces[4], pieces[5], pieces[6],
        placed[2],
    )


def solution(mesh):
    split = P("fsdp", "seq", None)
    vector = P(None, "fsdp")
    matrix = P(None, "fsdp", None)
    taps = P(None, None, "fsdp")
    return jax.shard_map(
        on_device,
        mesh=mesh,
        in_specs=(
            split, P("fsdp", "seq"), vector, matrix, matrix, taps, vector, vector, vector, vector, vector, matrix, split,
        ),
        out_specs=(
            split, split, vector, matrix, matrix, taps, vector, vector, vector, vector, vector, matrix,
        ),
        check_vma=False,
    )
```

```python
import functools

import jax
import jax.numpy as jnp
from jax import lax
from jax.experimental import pallas as pl
from jax.experimental.pallas import tpu as pltpu
from jax.sharding import PartitionSpec as P

EPSILON = 1e-05
F32, BF16 = jnp.float32, jnp.bfloat16
LANES = 128
EDGE = 8
FACTOR_ROWS = 16
SCALE = 0.25
VMEM = 48 * 1024 * 1024
NT = (((1,), (1,)), ((), ()))
TN = (((0,), (0,)), ((), ()))


def dot(a, b):
    return jnp.dot(a, b, preferred_element_type=F32)


def dot_nt(a, b):
    return lax.dot_general(a, b, NT, preferred_element_type=F32)


def dot_tn(a, b):
    return lax.dot_general(a, b, TN, preferred_element_type=F32)


def dot_exact(a, b):
    return jnp.dot(a, b, precision=lax.Precision.HIGHEST, preferred_element_type=F32)


def halves(v):
    high = v.astype(BF16)
    low = (v - high.astype(F32)).astype(BF16)
    return jnp.concatenate([high, low], axis=1)


def sigmoid(v):
    return 1.0 / (1.0 + jnp.exp(-v))


def softplus(v):
    return jnp.maximum(v, 0.0) + jnp.log1p(jnp.exp(-jnp.abs(v)))


def below(size):
    rows = lax.broadcasted_iota(jnp.int32, (size, size), 0)
    columns = lax.broadcasted_iota(jnp.int32, (size, size), 1)
    return rows >= columns


def head_column(table, head):
    return pltpu.roll(table, LANES - head, axis=1)[:, 0:1]


def conv_total(padded, taps, masks, at, wide, width):
    total = taps[4:5, pl.ds(at, wide)] + taps[3:4, pl.ds(at, wide)] * padded[EDGE:EDGE + width, pl.ds(at, wide)]
    for back in range(1, 4):
        tap = taps[3 - back:4 - back, pl.ds(at, wide)]
        total = total + (masks[back - 1] * tap) * padded[EDGE - back:EDGE - back + width, pl.ds(at, wide)]
    return total


def conv_kernel(inner, mixed, edge, marks, taps, rates, spread, act, sizes, sums, sums_t, state, factor, padded):
    width, channels = mixed.shape[1], padded.shape[1]
    padded[0:EDGE, :] = edge[0, :, 0:channels].astype(F32)
    padded[EDGE:EDGE + width, :] = mixed[0, :, 0:channels].astype(F32)
    marks_now = marks[0]
    masks = [marks_now[:, back:back + 1] for back in range(3)]
    wide = 256
    for at in range(0, channels, wide):
        total = conv_total(padded, taps, masks, at, wide, width)
        act[0, :, pl.ds(at, wide)] = (total * sigmoid(total)).astype(BF16)
    size = softplus(mixed[0, :, channels:].astype(F32) + rates[0:1, :])
    tri = jnp.where(below(width), 1.0, 0.0).astype(F32)
    total_sum = dot_exact(tri, size * rates[1:2, :])
    last = total_sum[width - 1:width]
    sizes[0] = size
    sums[0] = total_sum
    sums_t[0] = total_sum.T[0:sums_t.shape[1]]
    weight = halves(marks_now[:, 4:5] * jnp.exp(last - total_sum) * size)
    gone = marks_now[width - 1:width, 3:4] * jnp.exp(last)
    gone = halves(jnp.broadcast_to(gone, (FACTOR_ROWS, LANES)))
    states = (channels - inner) // 2
    keys_t = act[0, :, inner:inner + states].T
    for at in range(0, inner, wide):
        part = spread[:, pl.ds(at, wide)]
        weighted = (dot(weight, part) * act[0, :, pl.ds(at, wide)].astype(F32)).astype(BF16)
        state[0, 0:states, pl.ds(at, wide)] = dot(keys_t, weighted).astype(BF16)
        fade = dot(gone, part).astype(BF16)
        state[0, states:, pl.ds(at, wide)] = fade
        factor[0, :, pl.ds(at, wide)] = fade


def intra_kernel(inner, heads, act, sizes, sums, sums_t, marks, row_marks, skip, spread, out, scores, stepped):
    width = act.shape[1]
    states = (act.shape[2] - inner) // 2
    half = width // 2
    keys = act[0, :, inner:inner + states]
    queries = act[0, :, inner + states:]
    same = below(width) & (marks[0][:, 5:6] == row_marks[0, 0:1, :])
    scores[...] = jnp.where(same, dot_nt(queries, keys), 0.0)
    size = halves(sizes[0])
    wide = 256
    for at in range(0, inner, wide):
        part = dot(size, spread[:, pl.ds(at, wide)])
        stepped[:, pl.ds(at, wide)] = (part * act[0, :, pl.ds(at, wide)].astype(F32)).astype(BF16)
    per = LANES // (inner // heads)
    span = inner // heads
    lane = lax.broadcasted_iota(jnp.int32, (width, LANES), 1)

    def group(at, carry):
        place = pl.ds(pl.multiple_of(at * LANES, LANES), LANES)
        x = stepped[:, place]
        y_low = y_high = None
        for i in range(per):
            head = at * per + i
            column = head_column(sums[0], head)
            row = sums_t[0, pl.ds(head, 1), :]
            mine = (lane >= i * span) & (lane < (i + 1) * span)
            xh = jnp.where(mine, x, jnp.zeros_like(x))
            w_low = scores[0:half, 0:half] * jnp.exp(jnp.minimum(column[0:half] - row[:, 0:half], 0.0))
            w_high = scores[half:, :] * jnp.exp(jnp.minimum(column[half:] - row, 0.0))
            a = dot(w_low.astype(BF16), xh[0:half])
            b = dot(w_high.astype(BF16), xh)
            y_low = a if y_low is None else y_low + a
            y_high = b if y_high is None else y_high + b
        values = act[0, :, place].astype(F32) * skip[0:1, place]
        out[0, 0:half, place] = (y_low + values[0:half]).astype(out.dtype)
        out[0, half:, place] = (y_high + values[half:]).astype(out.dtype)
        return carry

    lax.fori_loop(0, inner // LANES, group, 0, unroll=2)


def entered_part(at, later_core, before, partner, other, place):
    states = before.shape[0]
    chip = before[:, place]
    core = jnp.full(chip.shape, at[0], jnp.int32)
    chip = jnp.where(core == pl.program_id(0), chip.astype(F32), partner[:, place].astype(F32))
    through = other[0, states:states + 1, place].astype(F32) * chip + other[0, 0:states, place].astype(F32)
    return jnp.where(core == later_core, through, chip).astype(BF16)


def post_kernel(inner, at, part_mixed, act, before, partner, other, sums, marks, gate, gain, spread, mixed, gated, entering, kept):
    states = (act.shape[2] - inner) // 2
    queries = act[0, :, inner + states:]
    enter = halves(marks[0][:, 3:4] * jnp.exp(sums[0]))
    wide = 256
    square = None
    for start in range(0, inner, wide):
        place = pl.ds(start, wide)
        state = entered_part(at, 1, before, partner, other, place)
        entering[0, :, place] = state
        whole = part_mixed[0, :, place].astype(F32) + dot(enter, spread[:, place]) * dot(queries, state)
        g = gate[0, :, place].astype(F32)
        w = whole * (g * sigmoid(g))
        mixed[0, :, place] = whole.astype(BF16)
        kept[:, place] = w
        square = w * w if square is None else square + w * w
    scale = lax.rsqrt(jnp.sum(square, axis=1, keepdims=True) / inner + EPSILON)
    for at in range(0, inner, wide):
        place = pl.ds(at, wide)
        gated[0, :, place] = (kept[:, place] * scale * gain[0:1, place]).astype(BF16)


def gate_back_kernel(
    inner, grad, grad_low, factor, mixed, gate, gain, act, state, sums, marks, spread,
    d_mixed, d_gate, d_state, d_queries, d_sums, row_grads, kept,
):
    states = (act.shape[2] - inner) // 2
    queries = act[0, :, inner + states:]
    queries_t = queries.T
    wide = 256

    @pl.when(pl.program_id(0) == 0)
    def _():
        row_grads[...] = jnp.zeros_like(row_grads)

    square = cross = None
    for at in range(0, inner, wide):
        place = pl.ds(at, wide)
        g = gate[0, :, place].astype(F32)
        w = mixed[0, :, place].astype(F32) * (g * sigmoid(g))
        gg = grad[0, :, place].astype(F32)
        kept[:, place] = w
        square = w * w if square is None else square + w * w
        more = w * gain[0:1, place] * gg
        cross = more if cross is None else cross + more
    scale = lax.rsqrt(jnp.sum(square, axis=1, keepdims=True) / inner + EPSILON)
    pulled = scale * scale * scale * (jnp.sum(cross, axis=1, keepdims=True) / inner)
    entered = marks[0][:, 3:4] * jnp.exp(sums[0])
    enter = halves(entered)
    grad_enter = dq = None
    for at in range(0, inner, wide):
        place = pl.ds(at, wide)
        g = gate[0, :, place].astype(F32)
        sig = sigmoid(g)
        silu = g * sig
        gg = grad[0, :, place].astype(F32)
        w = kept[:, place]
        whole = mixed[0, :, place].astype(F32)
        dw = scale * (gain[0:1, place] * gg) - pulled * w
        row_grads[0:1, place] += jnp.sum(gg * w * scale, axis=0, keepdims=True)
        dm = dw * silu
        d_gate[0, :, place] = (dw * whole * (sig + silu * (1.0 - sig))).astype(BF16)
        d_mixed[0, :, place] = dm.astype(BF16)
        row_grads[1:2, place] += jnp.sum(dm * act[0, :, place].astype(F32), axis=0, keepdims=True)
        part = spread[:, place]
        st = state[0, :, place]
        e = (dm * dot(enter, part)).astype(BF16)
        d_state[0, 0:states, place] = dot(queries_t, e).astype(BF16)
        more_q = dot_nt(e, st)
        dq = more_q if dq is None else dq + more_q
        through = (dm * dot(queries, st)).astype(BF16)
        more_e = dot_nt(through, part[0:LANES])
        grad_enter = more_e if grad_enter is None else grad_enter + more_e
    d_queries[0] = dq
    d_sums[0] = grad_enter * entered
    d_gate[0, :, inner:] = grad_low[0]
    d_state[0, states:, :] = factor[0]


def intra_back_kernel(
    inner, heads, d_mixed, act, sizes, sums, sums_t, marks, row_marks, spread, d_queries, d_sums,
    d_stepped, d_pair, d_total, scores, d_scores, stepped, sums_rows, sums_columns,
):
    width = act.shape[1]
    states = (act.shape[2] - inner) // 2
    half = width // 2
    keys = act[0, :, inner:inner + states]
    queries = act[0, :, inner + states:]
    rows = lax.broadcasted_iota(jnp.int32, (width, width), 0)
    columns = lax.broadcasted_iota(jnp.int32, (width, width), 1)
    same = (rows <= columns) & (marks[0][:, 5:6] == row_marks[0, 0:1, :])
    scores[...] = jnp.where(same, dot_nt(keys, queries), 0.0)
    d_scores[...] = jnp.zeros_like(d_scores)
    sums_rows[...] = jnp.zeros_like(sums_rows)
    sums_columns[...] = jnp.zeros_like(sums_columns)
    size = halves(sizes[0])
    wide = 256
    for at in range(0, inner, wide):
        part = dot(size, spread[:, pl.ds(at, wide)])
        stepped[:, pl.ds(at, wide)] = (part * act[0, :, pl.ds(at, wide)].astype(F32)).astype(BF16)
    per = LANES // (inner // heads)
    span = inner // heads
    lane = lax.broadcasted_iota(jnp.int32, (width, LANES), 1)

    eighth = lax.broadcasted_iota(jnp.int32, (8, width), 0)

    def group(at, carry):
        place = pl.ds(pl.multiple_of(at * LANES, LANES), LANES)
        x = stepped[:, place]
        dy = d_mixed[0, :, place]
        dx_low = dx_high = None
        for i in range(per):
            head = at * per + i
            column = head_column(sums[0], head)
            row = sums_t[0, pl.ds(head, 1), :]
            mine = (lane >= i * span) & (lane < (i + 1) * span)
            xh = jnp.where(mine, x, jnp.zeros_like(x))
            dyh = jnp.where(mine, dy, jnp.zeros_like(dy))
            l_low = jnp.exp(jnp.minimum(row - column[0:half], 0.0))
            l_high = jnp.exp(jnp.minimum(row[:, half:] - column[half:], 0.0))
            w_low = scores[0:half, :] * l_low
            w_high = scores[half:, half:] * l_high
            dw_low = dot_nt(xh[0:half], dy)
            dw_high = dot_nt(xh[half:], dy[half:])
            d_scores[0:half, :] += dw_low * l_low
            d_scores[half:, half:] += dw_high * l_high
            g_low = dw_low * w_low
            g_high = dw_high * w_high
            over_low = jnp.sum(g_low, axis=0, keepdims=True)
            over_high = jnp.sum(g_high, axis=0, keepdims=True)
            eight = pl.ds(pl.multiple_of(head // 8 * 8, 8), 8)
            chosen = eighth == head % 8
            sums_rows[eight, :] += jnp.where(chosen, over_low, 0.0)
            sums_rows[eight, half:] += jnp.where(chosen[:, half:], over_high, 0.0)
            here = lane[0:half] == head
            sums_columns[0:half, :] += jnp.where(here, jnp.sum(g_low, axis=1, keepdims=True), 0.0)
            sums_columns[half:, :] += jnp.where(here, jnp.sum(g_high, axis=1, keepdims=True), 0.0)
            a = dot(w_low.astype(BF16), dyh)
            b = dot(w_high.astype(BF16), dyh[half:])
            dx_low = a if dx_low is None else dx_low + a
            dx_high = b if dx_high is None else dx_high + b
        d_stepped[0, 0:half, place] = dx_low.astype(BF16)
        d_stepped[0, half:, place] = dx_high.astype(BF16)
        return carry

    lax.fori_loop(0, inner // LANES, group, 0, unroll=2)
    grad = jnp.where(same, d_scores[...], 0.0).astype(BF16)
    d_pair[0, :, 0:states] = dot(grad, queries)
    d_pair[0, :, states:] = dot(grad.T, keys) + d_queries[0]
    d_total[0] = sums_rows[...].T - sums_columns[...] + d_sums[0]


def conv_back_kernel(
    inner, here, d_stepped, d_mixed, act, mixed_in, edge, marks, taps, rates, skip, sizes, sums, spread,
    d_pair, d_total, before, partner, other, state,
    d_mixed_in, d_edge, tap_grads, head_grads, padded, shifted,
):
    width, channels = mixed_in.shape[1], padded.shape[1]
    states = (channels - inner) // 2
    wide = 256

    @pl.when(pl.program_id(0) == 0)
    def _():
        tap_grads[...] = jnp.zeros_like(tap_grads)
        head_grads[...] = jnp.zeros_like(head_grads)

    padded[0:EDGE, :] = edge[0, :, 0:channels].astype(F32)
    padded[EDGE:EDGE + width, :] = mixed_in[0, :, 0:channels].astype(F32)
    marks_now = marks[0]
    masks = [marks_now[:, back:back + 1] for back in range(3)]
    total_sum = sums[0]
    size = sizes[0]
    last = total_sum[width - 1:width]
    faded = marks_now[:, 4:5] * jnp.exp(last - total_sum)
    weight = faded * size
    weight_pair = halves(weight)
    size_pair = halves(size)
    keys = act[0, :, inner:inner + states]
    for back in range(3):
        shifted[back, 0:EDGE, :] = jnp.zeros((EDGE, wide), F32)
        shifted[back, EDGE + width:, :] = jnp.zeros((EDGE, wide), F32)

    def through_conv(at, d_act):
        place = pl.ds(at, wide)
        total = conv_total(padded, taps, masks, at, wide, width)
        sig = sigmoid(total)
        d = d_act * (sig + total * sig * (1.0 - sig))
        tap_grads[4:5, place] += jnp.sum(d, axis=0, keepdims=True)
        tap_grads[3:4, place] += jnp.sum(d * padded[EDGE:EDGE + width, place], axis=0, keepdims=True)
        back_total = taps[3:4, place] * d
        edge_total = jnp.zeros((EDGE, wide), F32)
        for back in range(1, 4):
            u = masks[back - 1] * d
            tap_grads[3 - back:4 - back, place] += jnp.sum(
                u * padded[EDGE - back:EDGE - back + width, place], axis=0, keepdims=True
            )
            shifted[back - 1, EDGE:EDGE + width, :] = u
            tap = taps[3 - back:4 - back, place]
            back_total = back_total + tap * shifted[back - 1, EDGE + back:EDGE + back + width, :]
            edge_total = edge_total + tap * shifted[back - 1, back:back + EDGE, :]
        d_mixed_in[0, :, place] = back_total.astype(BF16)
        d_edge[0, :, place] = edge_total

    d_keys = d_pair[0, :, 0:states]
    d_size = d_weight = carried = None
    for at in range(0, inner, wide):
        place = pl.ds(at, wide)
        values = act[0, :, place].astype(F32)
        part = spread[:, place]
        ds = entered_part(here, 0, before, partner, other, place)
        wide_weight = dot(weight_pair, part)
        d_weighted = dot(keys, ds)
        dx = d_stepped[0, :, place].astype(F32)
        d_act = dx * dot(size_pair, part) + d_weighted * wide_weight + skip[0:1, place] * d_mixed[0, :, place].astype(F32)
        d_keys = d_keys + dot_nt((wide_weight * values).astype(BF16), ds)
        a = dot_nt((dx * values).astype(BF16), part[0:LANES])
        b = dot_nt((d_weighted * values).astype(BF16), part[0:LANES])
        c = jnp.sum(ds.astype(F32) * state[0, :, place].astype(F32), axis=0, keepdims=True)
        c = dot_nt(jnp.broadcast_to(halves_rows(c), (EDGE, wide)), part[0:LANES])
        d_size = a if d_size is None else d_size + a
        d_weight = b if d_weight is None else d_weight + b
        carried = c if carried is None else carried + c
        through_conv(at, d_act)
    through_conv(inner, jnp.concatenate([d_keys, d_pair[0, :, states:]], axis=1))
    d_size = d_size + d_weight * faded
    pulled = d_weight * weight
    gone = marks_now[width - 1:width, 3:4] * jnp.exp(last)
    at_end = jnp.sum(pulled, axis=0, keepdims=True) + gone * carried[0:1]
    row = lax.broadcasted_iota(jnp.int32, (width, LANES), 0)
    d_sum = d_total[0] - pulled + jnp.where(row == width - 1, at_end, 0.0)
    order = lax.broadcasted_iota(jnp.int32, (width, width), 0) <= lax.broadcasted_iota(jnp.int32, (width, width), 1)
    d_rate = dot_exact(jnp.where(order, 1.0, 0.0).astype(F32), d_sum)
    d_size = d_size + d_rate * rates[1:2, :]
    d_step = d_size * sigmoid(mixed_in[0, :, channels:].astype(F32) + rates[0:1, :])
    d_mixed_in[0, :, channels:] = d_step.astype(BF16)
    head_grads[0:1, :] += jnp.sum(d_step, axis=0, keepdims=True)
    head_grads[1:2, :] += jnp.sum(d_rate * size * rates[1:2, :], axis=0, keepdims=True)


def halves_rows(v):
    return v.astype(BF16)


def without(kernel, first, count):
    def run(*refs):
        return kernel(*refs[:first], *refs[first + count:])

    return run


def call(kernel, batch, ins, outs, scratch, name, micros, at=None, after=()):
    def spec(shape, whole):
        block = tuple(shape) if whole else (1,) + tuple(shape[1:])
        if whole:
            return pl.BlockSpec(block, lambda b: (0,) * len(block))
        return pl.BlockSpec(block, lambda b: (b,) + (0,) * (len(block) - 1))

    arrays = [a for a, _ in ins]
    in_specs = [spec(a.shape, whole) for a, whole in ins]
    if at is not None:
        arrays, in_specs = [at] + arrays, [pl.BlockSpec(memory_space=pltpu.SMEM)] + in_specs
    return pl.pallas_call(
        without(kernel, len(arrays), len(after)),
        grid=(batch,),
        in_specs=in_specs + [pl.BlockSpec(memory_space=pl.ANY)] * len(after),
        out_specs=[spec(shape, whole) for shape, _, whole in outs],
        out_shape=[jax.ShapeDtypeStruct(shape, kind) for shape, kind, _ in outs],
        scratch_shapes=[pltpu.VMEM(shape, kind) for shape, kind in scratch],
        compiler_params=pltpu.CompilerParams(vmem_limit_bytes=VMEM),
        cost_estimate=cost(micros),
        name=name,
    )(*arrays, *after)


def cost(micros):
    micros = micros * SCALE
    return pl.CostEstimate(flops=int(micros * 1.1e9), bytes_accessed=int(micros * 1e6), transcendentals=0)


def edge_kernel(grad, more, out):
    size, channels = grad.shape[1], more.shape[2]
    out[0, :, channels:] = grad[0, :, channels:]
    last = jnp.concatenate([jnp.zeros((size - EDGE, channels), F32), more[0].astype(F32)], axis=0)
    out[0, :, 0:channels] = (grad[0, :, 0:channels].astype(F32) + last).astype(BF16)


def with_edges(grad, more, after):
    batch, width, wide = grad.shape
    size = 2 * EDGE
    block = pl.BlockSpec((1, size, wide), lambda b: (b, width // size - 1, 0))
    return pl.pallas_call(
        without(edge_kernel, 2, len(after)),
        grid=(batch,),
        in_specs=[block, pl.BlockSpec((1,) + more.shape[1:], lambda b: (b, 0, 0))] + [pl.BlockSpec(memory_space=pl.ANY)] * len(after),
        out_specs=block,
        out_shape=jax.ShapeDtypeStruct(grad.shape, grad.dtype),
        input_output_aliases={0: 0},
        compiler_params=pltpu.CompilerParams(vmem_limit_bytes=VMEM),
        cost_estimate=cost(1.0),
        name="with_edges",
    )(grad, more, *after)


def whole_call(kernel, arrays, outs, micros, name, at=None, after=(), scratch=()):
    spec = pl.BlockSpec(memory_space=pltpu.VMEM)
    arrays, in_specs = list(arrays), [spec] * len(arrays)
    if at is not None:
        arrays, in_specs = [at] + arrays, [pl.BlockSpec(memory_space=pltpu.SMEM)] + in_specs
    return pl.pallas_call(
        without(kernel, len(arrays), len(after)),
        in_specs=in_specs + [pl.BlockSpec(memory_space=pl.ANY)] * len(after),
        out_specs=[spec] * len(outs),
        out_shape=[jax.ShapeDtypeStruct(shape, kind) for shape, kind in outs],
        scratch_shapes=[pltpu.VMEM(shape, kind) for shape, kind in scratch],
        compiler_params=pltpu.CompilerParams(vmem_limit_bytes=VMEM),
        cost_estimate=cost(micros),
        name=name,
    )(*arrays, *after)


def swap(x, axis, bits):
    return lax.ppermute(x, axis, [(i, i ^ bits) for i in range(lax.axis_size(axis))])


def join_kernel(later_core, at, own, other, joined):
    core = at[0]
    states = own.shape[1] - FACTOR_ROWS
    for start in range(0, own.shape[2], 512):
        place = pl.ds(start, 512)
        mine = own[core, :, place].astype(F32)
        theirs = other[core, :, place].astype(F32)
        later = jnp.full(mine.shape, core, jnp.int32) == later_core
        second = jnp.where(later, mine, theirs)
        first = jnp.where(later, theirs, mine)
        gain = second[states:states + 1]
        joined[0:states, place] = (gain * first[0:states] + second[0:states]).astype(BF16)
        joined[states:, place] = (gain * first[states:]).astype(BF16)


def enter_kernel(count, *refs):
    out = refs[count]
    states = out.shape[0]
    for start in range(0, out.shape[1], 512):
        place = pl.ds(start, 512)
        before = refs[0][0:states, place].astype(F32)
        for got in refs[1:count]:
            before = got[states:states + 1, place].astype(F32) * before + got[0:states, place].astype(F32)
        out[:, place] = before.astype(BF16)


def exchange(own, at, later_core, after=()):
    peers = lax.axis_size("seq")
    other = swap(own, "seq", 1)
    joined = whole_call(functools.partial(join_kernel, later_core), [own, other], [(own.shape[1:], BF16)], 2.0, "join_states", at, after)[0]
    got = []
    for distance in range(peers // 2 - 1, 0, -1):
        step = 2 * distance if later_core == 1 else -2 * distance
        route = [(i, i + step) for i in range(peers) if 0 <= i + step < peers]
        got.append(lax.ppermute(joined, "seq", route))
    return got, other, joined


def entered(got, after):
    shape = (got[0].shape[0] - FACTOR_ROWS, got[0].shape[1])
    before = whole_call(
        functools.partial(enter_kernel, len(got)), got, [(shape, BF16)], 2.0, "enter_states", after=after
    )[0]
    return before, swap(before, "seq", 1)


def gathered(block):
    peers = lax.axis_size("seq")
    rows = block.shape[0] // peers
    share = lax.dynamic_slice_in_dim(block, lax.axis_index("seq") * rows, rows, 0)
    return lax.all_gather(share, ("fsdp", "seq"), axis=0, tiled=True)


def take_in_kernel(columns, block, steps, out):
    first, last, with_steps = columns
    wide = last - first
    out[:, 0:wide] = block[0, :, first:last]
    if with_steps:
        heads = steps.shape[2]
        out[:, wide:] = jnp.zeros((out.shape[0], LANES), BF16)
        out[:, wide:wide + heads] = steps[0]


def take_share(weight, steps, layer, columns, at, share, parts, after):
    first, last, with_steps = columns
    wide = last - first + (LANES if with_steps else 0)

    def rows(i, where):
        return (layer, where[1] * 2 + where[0] if parts > 2 else where[0], 0)

    arrays = [weight] if steps is None else [weight, steps]
    specs = [pl.BlockSpec((1, share, a.shape[2]), rows) for a in arrays]
    kernel = functools.partial(take_in_kernel, columns)
    if steps is None:
        kernel = lambda block, out: take_in_kernel(columns, block, None, out)
    inner_kernel = without(kernel, len(arrays), len(after))
    return pl.pallas_call(
        lambda where, *refs: inner_kernel(*refs),
        grid_spec=pltpu.PrefetchScalarGridSpec(
            num_scalar_prefetch=1,
            grid=(1,),
            in_specs=specs + [pl.BlockSpec(memory_space=pl.ANY)] * len(after),
            out_specs=pl.BlockSpec((share, wide), lambda i, where: (0, 0)),
        ),
        out_shape=jax.ShapeDtypeStruct((share, wide), BF16),
        compiler_params=pltpu.CompilerParams(vmem_limit_bytes=VMEM),
        cost_estimate=cost(1.0),
        name="take_share",
    )(at, *arrays, *after)


def place_rows_kernel(starts, columns, many, at, *refs):
    weight, steps = refs[0], refs[1] if many == 2 else None
    sources, out = refs[many:-1], refs[-1]
    core, chip, group = at[0], at[1], at[2]
    rows = weight.shape[1]
    own = pl.ds(pl.multiple_of(group * rows, rows), rows)
    first, last, with_steps = columns
    wide = last - first
    out[own, 0:wide] = weight[0, :, first:last]
    if with_steps:
        out[own, wide:] = jnp.concatenate([steps[0], jnp.zeros((rows, LANES - steps.shape[2]), BF16)], axis=1)
    for source, index, rows, place in starts:
        start = pl.multiple_of(place(core, chip, group), rows)
        out[pl.ds(start, rows), :] = sources[source][index]


def placed_rows(at, weight, steps, layer, columns, sources, starts, groups, micros, after=()):
    whole = pl.BlockSpec(memory_space=pltpu.VMEM)
    own = [weight] if steps is None else [weight, steps]
    first, last, with_steps = columns
    shape = (weight.shape[1] * groups, last - first + (LANES if with_steps else 0))
    return pl.pallas_call(
        without(functools.partial(place_rows_kernel, starts, columns, len(own)), 1 + len(own) + len(sources), len(after)),
        grid=(1,),
        in_specs=[pl.BlockSpec(memory_space=pltpu.SMEM)]
        + [pl.BlockSpec((1,) + a.shape[1:], lambda i: (layer, 0, 0)) for a in own] + [whole] * len(sources)
        + [pl.BlockSpec(memory_space=pl.ANY)] * len(after),
        out_specs=whole,
        out_shape=jax.ShapeDtypeStruct(shape, BF16),
        compiler_params=pltpu.CompilerParams(vmem_limit_bytes=VMEM),
        cost_estimate=cost(micros),
        name="place_rows",
    )(at, *own, *sources, *after)


def stack_kernel(count, *refs):
    out, row = refs[count], 0
    for ref in refs[:count]:
        if len(ref.shape) == 2:
            out[row] = ref[...]
            row += 1
        else:
            out[row:row + ref.shape[0]] = ref[...]
            row += ref.shape[0]


def stacked(blocks, after=()):
    many = sum(1 if b.ndim == 2 else b.shape[0] for b in blocks)
    return whole_call(
        functools.partial(stack_kernel, len(blocks)), blocks, [((many,) + blocks[0].shape[-2:], BF16)], 1.0, "stack", after=after
    )[0]


def unfold_kernel(share, folded, out):
    many = folded.shape[1] // out.shape[1]
    model = out.shape[1]
    for block in range(folded.shape[0] // share):
        for i in range(many):
            to = (block * many + i) * share
            out[to:to + share, :] = folded[block * share:(block + 1) * share, i * model:(i + 1) * model]


def unfolded(whole, inner, model, share):
    rows = whole.shape[0] // 4
    return pl.pallas_call(
        functools.partial(unfold_kernel, share),
        grid=(4,),
        in_specs=[pl.BlockSpec((rows, inner), lambda i: (i, 0))],
        out_specs=pl.BlockSpec((rows * inner // model, model), lambda i: (i, 0)),
        out_shape=jax.ShapeDtypeStruct((inner, model), BF16),
        compiler_params=pltpu.CompilerParams(vmem_limit_bytes=VMEM),
        cost_estimate=cost(3.0),
        name="unfold",
    )(whole)


def from_along_z(mine, groups, after=()):
    return stacked([swap(mine, "fsdp", e) for e in range(1, groups)], after)


def fetched_by_all(weight, steps, layer, columns, at, groups, chips, from_z, place_after=()):
    rows = weight.shape[1]
    share = rows // (2 * chips)
    sources = [from_z] + [swap(from_z, "seq", 2 * d) for d in range(1, chips)]
    sources.append(swap(stacked([a.reshape(-1, a.shape[2]) for a in sources]), "seq", 1))

    def place_of(d, e, other):
        return lambda core, chip, group: (group ^ e) * rows + (chip ^ d) * (2 * share) + (core ^ other) * share

    starts = []
    for d in range(chips):
        for e in range(1, groups):
            index = e - 1
            starts.append((d, (index,), share, place_of(d, e, 0)))
            starts.append((chips, (d, slice(index * share, (index + 1) * share)), share, place_of(d, e, 1)))
    return placed_rows(at, weight, steps, layer, columns, sources, starts, groups, 4.0, place_after)


def reduced(grad):
    share = lax.psum_scatter(grad, ("fsdp", "seq"), scatter_dimension=0, tiled=True)
    return lax.all_gather(share, "seq", axis=0, tiled=True).astype(F32)


def turn_kernel(groups, chips, at, gated, low, own, send, turned):
    core, chip, group = at[0], at[1], at[2]
    base = 0
    for x in (gated, low):
        if x is None:
            continue
        total = x.shape[1]
        share = total // (2 * groups * chips)
        for start in range(0, total, 256):
            turned[start:start + 256, :] = x[:, start:start + 256].T
        for other, out in ((0, own), (1, send)):
            for d in range(chips):
                for e in range(groups):
                    start = (group ^ e) * (total // groups) + (chip ^ d) * (2 * share) + (core ^ other) * share
                    to = base + (d * groups + e) * share
                    out[to:to + share, :] = turned[pl.ds(pl.multiple_of(start, share), share), :]
        base += total // 2


def turned_halves(gated, low, at, groups, chips):
    rows = low.shape[0]
    if gated is None:
        def kernel(where, low_ref, *refs):
            turn_kernel(groups, chips, where, None, low_ref, *refs)

        return whole_call(kernel, [low], [((low.shape[1] // 2, rows), BF16)] * 2, 2.0, "turn", at, scratch=[(low.shape[::-1], BF16)])
    half = ((gated.shape[1] + low.shape[1]) // 2, rows)
    return whole_call(
        functools.partial(turn_kernel, groups, chips), [gated, low], [(half, BF16)] * 2, 4.0, "turn", at,
        scratch=[((gated.shape[1], rows), BF16)],
    )


def first_grads_kernel(groups, chips, inner, joined, at, own, other, grad, grad_other, *refs):
    wide = grad.shape[1] - inner
    total_big = inner // 2
    big = total_big // (groups * chips)
    small = (own.shape[0] - total_big) // (groups * chips)
    outs = refs[1:] if joined else refs
    group = at[2]

    def put(total, share, start, column):
        for d in range(chips):
            for e in range(groups):
                block = (d * groups + e) * share
                rows, columns = slice(start, start + share), pl.ds(column, 512)
                if joined:
                    outs[d][e, rows, columns] = total[block:block + share]
                else:
                    outs[0][group ^ e, d, rows, columns] = total[block:block + share]

    if joined:
        for d in range(chips):
            outs[d][groups] = refs[0][d]
    for start in range(0, wide, 512):
        place = pl.ds(inner + start, 512)
        total = dot(own[0:total_big, :], grad[:, place]) + dot(other[0:total_big, :], grad_other[:, place])
        put(total.astype(BF16), big, 0, start)
    for start in range(0, inner, 512):
        place = pl.ds(start, 512)
        total = dot(own[total_big:, :], grad[:, place]) + dot(other[total_big:, :], grad_other[:, place])
        put(total.astype(BF16), small, big + start // wide * small, start % wide)


def second_grads_kernel(groups, chips, channels, heads, here, own, other, grad, grad_other, extra, extra_other, *outs):
    rows = extra.shape[0] // 2
    base = own.shape[0] - rows
    share = rows // (groups * chips)
    core, chip, group = here[0], here[1], here[2]
    lane = lax.broadcasted_iota(jnp.int32, (share, LANES), 1)
    total_wide = channels + LANES
    edges = list(range(0, channels, 512)) + [channels, total_wide]
    for at, end in zip(edges[:-1], edges[1:]):
        place = pl.ds(at, end - at)
        total = dot(own[base:, :], grad[:, place]) + dot(other[base:, :], grad_other[:, place])
        for d in range(chips):
            for e in range(groups):
                block = (d * groups + e) * share
                part = total[block:block + share]
                if at == channels:
                    start = (group ^ e) * (2 * rows // groups) + (chip ^ d) * (2 * share) + core * share
                    here_rows = pl.ds(pl.multiple_of(start, share), share)
                    part = jnp.where(lane < heads, part, extra[here_rows, :] + extra_other[here_rows, :])
                outs[d][e, :, place] = part.astype(BF16)


def gather_small_kernel(groups, taps, heads, gain, tap_grads, head_grads, row_grads, spread, out):
    cut = out.shape[0] // groups
    channels, inner = tap_grads.shape[1], row_grads.shape[1]
    skip = row_grads[1:2, :]
    high = skip.astype(BF16)
    low = (skip - high.astype(F32)).astype(BF16)
    ones = spread[0:LANES, :]
    skip = dot_nt(jnp.broadcast_to(high, (8, inner)), ones) + dot_nt(jnp.broadcast_to(low, (8, inner)), ones)
    span, part, few = channels // groups, inner // groups, heads // groups
    for z in range(groups):
        rows = [jnp.zeros((heads, cut), F32), gain[0:1, z * cut:(z + 1) * cut]]
        for at in range(0, part, cut):
            rows.append(row_grads[0:1, z * part + at:z * part + at + cut])
        for at in range(0, span, cut):
            wide = min(cut, span - at)
            block = tap_grads[0:taps + 1, z * span + at:z * span + at + wide]
            if wide < cut:
                block = jnp.concatenate([block, jnp.zeros((taps + 1, cut - wide), F32)], axis=1)
            rows.append(block)
        lane = lax.broadcasted_iota(jnp.int32, (1, LANES), 1)
        for row in (head_grads[0:1, :], head_grads[1:2, :], skip[0:1, :]):
            row = pltpu.roll(row, (LANES - z * few) % LANES, axis=1) if z else row
            row = jnp.where(lane < few, row, 0.0)
            rows.append(jnp.concatenate([row] + [jnp.zeros((1, cut - LANES), F32)], axis=1))
        table = jnp.concatenate(rows, axis=0)
        table = jnp.concatenate([table, jnp.zeros((LANES - table.shape[0], cut), F32)], axis=0)
        out[z * cut:(z + 1) * cut, :] = table.T


def add_kernel(count, *refs):
    ins, outs = refs[:count], refs[count:]
    for i, out in enumerate(outs):
        total = ins[0][i].astype(F32)
        for more in ins[1:]:
            total = total + more[i].astype(F32)
        out[...] = total.astype(out.dtype)


def halve_kernel(count, *refs):
    ins, (near, far, *more_outs) = refs[:count], refs[count:]
    half = near.shape[0]
    for i in range(2 * half + len(more_outs)):
        total = ins[0][i].astype(F32)
        for more in ins[1:]:
            total = total + more[i].astype(F32)
        if i < half:
            near[i] = total.astype(BF16)
        elif i < 2 * half:
            far[i - half] = total.astype(BF16)
        else:
            more_outs[0][...] = total.astype(BF16)


def lay_kernel(count, layers, *refs):
    out = refs[-1]
    wide = out.shape[1]
    share, columns = refs[0].shape[0] // layers, refs[0].shape[1]
    row = 0
    for layer in range(layers):
        rows = slice(layer * share, (layer + 1) * share)
        for at in range(0, columns, wide):
            width = min(wide, columns - at)
            total = refs[0][rows, at:at + width].astype(F32)
            for more in refs[1:count]:
                total = total + more[rows, at:at + width].astype(F32)
            out[row:row + share, 0:width] = total.astype(BF16)
            if width < wide:
                out[row:row + share, width:] = jnp.zeros((share, wide - width), BF16)
            row += share


def plane_parts(blocks):
    return [blocks[0]] + [swap(blocks[i], "seq", 2 * i) for i in range(1, len(blocks))]


def halved(got, after=()):
    parts, rows, columns = got[0].shape
    outs = [((parts // 2, rows, columns), BF16)] * 2 + [((rows, columns), BF16)] * (parts % 2)
    return whole_call(functools.partial(halve_kernel, len(got)), got, outs, 2.0, "add_halves", after=after)


def halved_sums(near, far, after):
    parts, rows, columns = near.shape
    got = [near, swap(far, "fsdp", parts)]
    while parts > 1:
        near, far = halved(got, after)
        parts //= 2
        got = [near, swap(far, "fsdp", parts)]
    return whole_call(functools.partial(add_kernel, 2), got, [((rows, columns), BF16)], 1.0, "add_halves", after=after)[0]


def laid(got, wide, after):
    rows, columns = got[0].shape
    shape = (-(-columns // wide) * rows, wide)
    return whole_call(functools.partial(lay_kernel, len(got), 1), got, [(shape, BF16)], 2.0, "lay_sums", after=after)[0]


def layer_sums(got, groups, wide, after):
    parts, rows, columns = got[0].shape
    shares = whole_call(functools.partial(add_kernel, len(got)), got, [((rows, columns), BF16)] * parts, 2.0, "add_plane")
    return laid([shares[0]] + [swap(shares[e], "fsdp", e) for e in range(1, groups)], wide, after)


def spread_in_plane(share, chips):
    mine = [share] + [swap(share, "seq", 2 * d) for d in range(1, chips)]
    return mine, swap(stacked(mine), "seq", 1)


def place_kernel(chips, inner, layers, at, *refs):
    mine_a, other_a = refs[:chips], refs[chips]
    mine_b, other_b = refs[chips + 1:2 * chips + 1], refs[2 * chips + 1]
    in_out, extra_out, out_out, norm_out, taps_out, bias_out, heads_out, gain_out, extra = refs[-9:]
    core, chip = at[0], at[1]
    model = other_a.shape[2]
    rows_in, rows_out = in_out.shape[1], out_out.shape[1]
    big, share = rows_out // (2 * chips), rows_in // (2 * chips)
    channels = in_out.shape[2] - inner
    for layer in range(layers):
        @pl.when(pl.program_id(0) == layer)
        def _():
            for d in range(chips):
                for is_other in range(2):
                    a, b = (other_a.at[d], other_b.at[d]) if is_other else (mine_a[d], mine_b[d])
                    start = (chip ^ d) * (2 * share) + (core ^ is_other) * share
                    rows = pl.ds(pl.multiple_of(start, share), share)
                    start = (chip ^ d) * (2 * big) + (core ^ is_other) * big
                    first = layer * (a.shape[0] // layers)
                    out_out[0, pl.ds(pl.multiple_of(start, big), big), :] = a[first:first + big, :].astype(F32)
                    first += big
                    for i in range(inner // model):
                        in_out[0, rows, i * model:(i + 1) * model] = a[first:first + share, :].astype(F32)
                        first += share
                    first = layer * (b.shape[0] // layers)
                    for column in range(0, channels + LANES, model):
                        wide = min(model, channels - column)
                        in_out[0, rows, pl.ds(inner + column, wide)] = b[first:first + share, 0:wide].astype(F32)
                        if column + model >= channels:
                            extra[rows, :] = b[first:first + share, wide:wide + LANES].astype(F32)
                        first += share
            extra_out[0] = extra[:, 0:extra_out.shape[2]]
            table = extra[...].T
            heads = extra_out.shape[2]
            taps, span, part = taps_out.shape[1], taps_out.shape[2], gain_out.shape[1]
            norm_out[layer:layer + 1, :] = table[heads:heads + 1]
            row = heads + 1
            for start in range(0, part, rows_in):
                gain_out[layer:layer + 1, start:start + rows_in] = table[row:row + 1]
                row += 1
            for start in range(0, span, rows_in):
                wide = min(rows_in, span - start)
                taps_out[layer, :, start:start + wide] = table[row:row + taps, 0:wide]
                bias_out[layer:layer + 1, start:start + wide] = table[row + taps:row + taps + 1, 0:wide]
                row += taps + 1
            few = heads_out.shape[2]
            heads_out[layer] = table[row:row + 3, 0:few]


def placed_grads(at, pieces, layers, shapes, smalls, chips, inner, after):
    whole = pl.BlockSpec(memory_space=pltpu.VMEM)
    return pl.pallas_call(
        without(functools.partial(place_kernel, chips, inner, layers), 1 + len(pieces), len(after)),
        grid=(layers,),
        in_specs=[pl.BlockSpec(memory_space=pltpu.SMEM)] + [whole] * len(pieces)
        + [pl.BlockSpec(memory_space=pl.ANY)] * len(after),
        out_specs=[pl.BlockSpec((1,) + shape, lambda i: (i, 0, 0)) for shape in shapes]
        + [pl.BlockSpec(shape, lambda i, n=len(shape): (0,) * n) for shape in smalls],
        out_shape=[jax.ShapeDtypeStruct((layers,) + shape, F32) for shape in shapes] + [jax.ShapeDtypeStruct(shape, F32) for shape in smalls],
        scratch_shapes=[pltpu.VMEM((shapes[0][0], LANES), F32)],
        compiler_params=pltpu.CompilerParams(vmem_limit_bytes=VMEM),
        cost_estimate=cost(8.0),
        name="place_grads",
    )(at, *pieces, *after)


def norm_scale_of(stream):
    return lax.rsqrt(jnp.mean(stream * stream, axis=-1, keepdims=True) + EPSILON)


def on_device(
    tokens, segments, norm_gain, in_weight, dt_weight, conv_weight, conv_bias, dt_bias, a_log, d_skip,
    gate_gain, out_weight, cotangent,
):
    layers = in_weight.shape[0]
    batch, width, model = tokens.shape
    heads = dt_weight.shape[2]
    taps_len = conv_weight.shape[1]
    peers = lax.axis_size("seq")
    groups = lax.axis_size("fsdp")
    rows = batch * width
    inner = out_weight.shape[1] * groups
    channels = in_weight.shape[2] - inner
    states = (channels - inner) // 2
    span = inner // heads
    chips = peers // 2
    direct = model % (32 * groups * peers) == 0 and chips == 4 and groups == 4 and layers == 2
    seq_at = lax.axis_index("seq")
    here = jnp.stack([seq_at % 2, seq_at // 2, lax.axis_index("fsdp")]).astype(jnp.int32)

    small = [norm_gain, conv_weight.reshape(layers, -1), conv_bias, dt_bias, a_log, d_skip, gate_gain]
    sizes = [a.shape[1] for a in small]
    own = jnp.concatenate(small, axis=1)
    if direct:
        share_in, share_out = model // (groups * peers), inner // (groups * peers)
        all_columns = (0, inner + channels, True)
        mix_z = from_along_z(take_share(in_weight, dt_weight, 0, all_columns, here, share_in, peers, ()), groups)
        by_partner, bits = stacked([own], (mix_z,)), 1
        while bits < groups:
            by_partner = jnp.concatenate([by_partner, swap(by_partner, "fsdp", bits)])
            bits *= 2
        packed = jnp.stack([lax.dynamic_index_in_dim(by_partner, here[2] ^ z, 0, keepdims=False) for z in range(groups)])
    else:
        packed = lax.all_gather(own, "fsdp", axis=0)
    pieces, at = [], 0
    for size in sizes:
        pieces.append(packed[:, :, at:at + size])
        at += size

    def joined(piece):
        return jnp.moveaxis(piece, 0, 1).reshape(layers, -1)

    norm_all = joined(pieces[0]).astype(F32)
    taps_all = jnp.moveaxis(pieces[1].reshape(groups, layers, taps_len, -1), 0, 2).reshape(layers, taps_len, channels)
    taps_all = jnp.concatenate(
        [taps_all.astype(F32), joined(pieces[2]).astype(F32)[:, None], jnp.zeros((layers, 8 - taps_len - 1, channels), F32)], axis=1
    )
    pad_heads = ((0, 0), (0, LANES - heads))
    rates_all = jnp.stack(
        [jnp.pad(joined(pieces[3]).astype(F32), pad_heads), jnp.pad(-jnp.exp(joined(pieces[4]).astype(F32)), pad_heads)], axis=1
    )
    rates_all = jnp.pad(rates_all, ((0, 0), (0, 6), (0, 0)))
    skip_all = jnp.repeat(joined(pieces[5]).astype(F32), span, axis=1)[:, None]
    gain_all = joined(pieces[6]).astype(F32)[:, None]

    gate_all, mix_all, out_all = [], [], []
    for layer in range(layers):
        if direct:
            if layer == 0:
                whole = fetched_by_all(
                    in_weight, dt_weight, 0, all_columns, here, groups, chips, mix_z, (norm_all, taps_all, rates_all, skip_all, gain_all)
                )
                gates, mixes = whole[:, :inner], whole[:, inner:]
                outs = None
            else:
                share = take_share(in_weight, dt_weight, layer, all_columns, here, share_in, peers, (mix_z,))
                taken, first = [share], 0
                if layer == 1:
                    share = take_share(out_weight, None, 0, (0, model, False), here, share_out, peers, (mix_z,))
                    taken = [share[i * share_in:(i + 1) * share_in] for i in range(inner // model)] + taken
                    first = inner
                whole = lax.all_gather(jnp.concatenate(taken, axis=1), ("fsdp", "seq"), axis=0, tiled=True)
                gates, mixes = whole[:, first:first + inner], whole[:, first + inner:]
                if layer == 1:
                    out_all[0] = unfolded(whole, inner, model, share_in)
                share = take_share(out_weight, None, layer, (0, model, False), here, share_out, peers, (mix_z,))
                outs = lax.all_gather(share, ("fsdp", "seq"), axis=0, tiled=True)
        else:
            steps = jnp.pad(dt_weight[layer], ((0, 0), (0, LANES - heads)))
            whole = gathered(jnp.concatenate([in_weight[layer], steps], axis=1))
            gates, mixes = whole[:, :inner], whole[:, inner:]
            outs = gathered(out_weight[layer])
        gate_all.append(gates)
        mix_all.append(mixes)
        out_all.append(outs)

    numbers = (segments + 1).astype(F32)
    before = lax.ppermute(numbers[:, width - EDGE:], "seq", [(i, i + 1) for i in range(peers - 1)])
    padded = jnp.concatenate([before, numbers], axis=1)
    columns = [padded[:, EDGE - back:EDGE - back + width] == numbers for back in range(1, taps_len)]
    columns += [numbers == before[:, EDGE - 1:], numbers == numbers[:, width - 1:]]
    marks = jnp.stack([c.astype(F32) for c in columns] + [numbers], axis=-1)
    marks = jnp.pad(marks, ((0, 0), (0, 0), (0, LANES - marks.shape[-1])))
    row_marks = jnp.broadcast_to(numbers[:, None, :], (batch, 8, width))
    lane_head = jnp.arange(inner) // span
    spread = (jnp.arange(2 * LANES)[:, None] % LANES == lane_head[None, :]).astype(BF16)

    stream = tokens.astype(F32)
    kept, sent = [], ()
    for layer in range(layers):
        norm_scale = norm_scale_of(stream)
        low = (stream * norm_scale * norm_all[layer]).astype(BF16).reshape(rows, model)
        w_gate, w_mix, w_out = gate_all[layer], mix_all[layer], out_all[layer]
        mixed_in = dot(low, w_mix).astype(BF16).reshape(batch, width, channels + LANES)
        edge = lax.ppermute(mixed_in[:, width - EDGE:], "seq", [(i, i + 1) for i in range(peers - 1)])
        gate = dot(low, w_gate).astype(BF16).reshape(batch, width, inner)
        taps, rates, skip, gain = taps_all[layer], rates_all[layer], skip_all[layer], gain_all[layer]
        act, size, sums, sums_t, state, factor = call(
            functools.partial(conv_kernel, inner), batch,
            [(mixed_in, 0), (edge, 0), (marks, 0), (taps, 1), (rates, 1), (spread, 1)],
            [
                ((batch, width, channels), BF16, 0), ((batch, width, LANES), F32, 0), ((batch, width, LANES), F32, 0),
                ((batch, heads, width), F32, 0), ((batch, states + FACTOR_ROWS, inner), BF16, 0),
                ((batch, FACTOR_ROWS, inner), BF16, 0),
            ],
            [((EDGE + width, channels), F32)], "conv_states", 8.0, after=sent,
        )
        got, other, joined_state = exchange(state, here, 1)
        (part,) = call(
            functools.partial(intra_kernel, inner, heads), batch,
            [(act, 0), (size, 0), (sums, 0), (sums_t, 0), (marks, 0), (row_marks, 0), (skip, 1), (spread, 1)],
            [((batch, width, inner), F32, 0)],
            [((width, width), F32), ((width, inner), BF16)], "mix_within", 12.0, after=(joined_state,),
        )
        before, partner = entered(got, (part, gate, w_out) if direct else (part,))
        mixed, gated, entering = call(
            functools.partial(post_kernel, inner), batch,
            [
                (part, 0), (act, 0), (before, 1), (partner, 1), (other, 0), (sums, 0), (marks, 0), (gate, 0), (gain, 1), (spread, 1),
            ],
            [((batch, width, inner), BF16, 0), ((batch, width, inner), BF16, 0), ((batch, states, inner), BF16, 0)],
            [((width, inner), F32)], "mix_gate", 6.0, here,
        )
        gated = gated.reshape(rows, inner)
        turned = None
        if direct:
            mine, send = turned_halves(gated, low, here, groups, chips)
            turned = (mine, swap(send, "seq", 1))
            sent = (send,)
        kept.append((turned, stream, norm_scale, low, mixed_in, edge, gate, act, size, sums, sums_t, factor, entering, mixed, gated))
        stream = stream + dot(gated, w_out).reshape(batch, width, model)

    grad_stream = cotangent.astype(F32)
    collected, collected_grads, far_sums, second_shares, waiting = [], [], [], [], []
    started = ()
    for layer in reversed(range(layers)):
        (turned, entry, norm_scale, low, mixed_in, edge, gate, act, size, sums, sums_t, factor, entering, mixed, gated) = kept[layer]
        w_gate, w_mix, w_out = gate_all[layer], mix_all[layer], out_all[layer]
        taps, rates, skip, gain = taps_all[layer], rates_all[layer], skip_all[layer], gain_all[layer]
        grad_low = grad_stream.astype(BF16).reshape(rows, model)
        grad_gated = dot_nt(grad_low, w_out).astype(BF16).reshape(batch, width, inner)
        d_mixed, d_gate, d_state, d_queries, d_sums, row_grads = call(
            functools.partial(gate_back_kernel, inner), batch,
            [
                (grad_gated, 0), (grad_low.reshape(batch, width, model), 0), (factor, 0), (mixed, 0), (gate, 0), (gain, 1), (act, 0),
                (entering, 0), (sums, 0), (marks, 0), (spread, 1),
            ],
            [
                ((batch, width, inner), BF16, 0), ((batch, width, inner + model), BF16, 0),
                ((batch, states + FACTOR_ROWS, inner), BF16, 0), ((batch, width, states), F32, 0), ((batch, width, LANES), F32, 0), ((8, inner), F32, 1),
            ],
            [((width, inner), F32)], "gate_back", 11.0, after=started,
        )
        got, other, joined_state = exchange(d_state, here, 0)
        both = d_gate.reshape(rows, inner + model)
        d_gate = both[:, :inner]
        started, arrived, ordered = (), (), ()
        if direct:
            big, small = inner // (groups * peers), model // (groups * peers)
            mine, theirs = turned
            both_other = swap(both, "seq", 1)
        else:
            out_share = reduced(dot_tn(gated, grad_low).astype(BF16))
        d_stepped, d_pair, d_total = call(
            functools.partial(intra_back_kernel, inner, heads), batch,
            [
                (d_mixed, 0), (act, 0), (size, 0), (sums, 0), (sums_t, 0), (marks, 0), (row_marks, 0), (spread, 1),
                (d_queries, 0), (d_sums, 0),
            ],
            [((batch, width, inner), BF16, 0), ((batch, width, 2 * states), F32, 0), ((batch, width, LANES), F32, 0)],
            [
                ((width, width), F32), ((width, width), F32), ((width, inner), BF16), ((LANES, width), F32), ((width, LANES), F32),
            ], "mix_within_back", 17.0, after=(joined_state,),
        )
        before, partner = entered(got, (d_stepped,))
        if direct and layer > 0:
            (parts,) = whole_call(
                functools.partial(first_grads_kernel, groups, chips, inner, False), [mine, theirs, both, both_other],
                [((groups, chips, big + inner // model * small, model), BF16)], 10.0, "first_grads", here, (before,),
            )
            far_sums.append(lax.psum_scatter(parts, "fsdp", scatter_dimension=0, tiled=True)[0])
            arrived = (parts,)
        if direct and layer == 0:
            first_blocks = whole_call(
                functools.partial(first_grads_kernel, groups, chips, inner, True), [mine, theirs, both, both_other] + far_sums,
                [((groups + 1, big + inner // model * small, model), BF16)] * chips, 10.0, "first_grads", here, (before,),
            )
            arrived = tuple(first_blocks)
            near, far, *passed = halved(plane_parts(first_blocks))
            ordered = (near,)
            gots = []
            for later in waiting:
                blocks = later((first_blocks[0],))
                gots.append(plane_parts(blocks))
                ordered += (blocks[0],)
        d_mixed_in, d_edge, tap_grads, head_grads = call(
            functools.partial(conv_back_kernel, inner), batch,
            [
                (d_stepped, 0), (d_mixed, 0), (act, 0), (mixed_in, 0), (edge, 0), (marks, 0), (taps, 1), (rates, 1),
                (skip, 1), (size, 0), (sums, 0), (spread, 1), (d_pair, 0), (d_total, 0), (before, 1), (partner, 1), (other, 0),
                (entering, 0),
            ],
            [
                ((batch, width, channels + LANES), BF16, 0), ((batch, EDGE, channels), F32, 0),
                ((8, channels), F32, 1), ((8, LANES), F32, 1),
            ],
            [((EDGE + width, channels), F32), ((3, width + 2 * EDGE, 256), F32)], "conv_back", 17.0, here, arrived,
        )
        from_next = lax.ppermute(d_edge.astype(BF16), "seq", [(i + 1, i) for i in range(peers - 1)])
        grad_mixed = with_edges(d_mixed_in, from_next, ordered).reshape(rows, channels + LANES)
        grad_rows = dot_nt(d_gate, w_gate) + dot_nt(grad_mixed, w_mix)
        grad_rows = grad_rows.reshape(batch, width, model)
        scaled = grad_rows * norm_all[layer]
        inward = jnp.mean(scaled * entry, axis=-1, keepdims=True)
        gain_grad = jnp.sum(grad_rows * entry * norm_scale, axis=(0, 1))
        grad_stream = grad_stream + norm_scale * scaled - (norm_scale * norm_scale * norm_scale * inward) * entry
        if direct:
            extra = whole_call(
                functools.partial(gather_small_kernel, groups, taps_len, heads), [gain_grad[None], tap_grads, head_grads, row_grads, spread],
                [((model, LANES), F32)], 3.0, "gather_small",
            )[0]
            operands = [mine, theirs, grad_mixed, swap(grad_mixed, "seq", 1), extra, swap(extra, "seq", 1)]
            kernel = functools.partial(second_grads_kernel, groups, chips, channels, heads)
            outs = [((groups, small, channels + LANES), BF16)] * chips
            if layer > 0:
                waiting.append(functools.partial(whole_call, kernel, operands, outs, 6.0, "second_grads", here))
                started = (operands[3], operands[5])
            else:
                blocks = whole_call(kernel, operands, outs, 6.0, "second_grads", here)
                after = (blocks[0],)
                first_share = stacked([halved_sums(near, far, after)] + passed).reshape(-1, model)
                mine_a, other_a = spread_in_plane(first_share, chips)
                for got in gots:
                    near, far = halved(got, after)
                    second_shares.append(laid([halved_sums(near, far, ())], model, ()))
                second_shares.append(layer_sums(plane_parts(blocks), groups, model, (stream, grad_stream) + tuple(mine_a)))
        else:
            mixed_grad = dot_tn(low, grad_mixed)
            in_share = reduced(jnp.concatenate([dot_tn(low, d_gate).astype(BF16), mixed_grad[:, :channels].astype(BF16)], axis=1))
            dt_share = reduced(mixed_grad[:, channels:].astype(BF16))
            collected_grads.append((in_share, dt_share, out_share))
            small_grads = [
                gain_grad.reshape(groups, -1),
                jnp.moveaxis(tap_grads[:taps_len].reshape(taps_len, groups, -1), 1, 0).reshape(groups, -1),
                tap_grads[taps_len].reshape(groups, -1),
                head_grads[0, :heads].reshape(groups, -1),
                head_grads[1, :heads].reshape(groups, -1),
                jnp.sum(row_grads[1].reshape(heads, span), axis=1).reshape(groups, -1),
                row_grads[0].reshape(groups, -1),
            ]
            collected.append(jnp.concatenate(small_grads, axis=1))
    if direct:
        second_share = stacked(second_shares[::-1]).reshape(-1, model)
        mine_b, other_b = spread_in_plane(second_share, chips)
        shapes = [(model // groups, inner + channels), (model // groups, heads), (inner // groups, model)]
        smalls = [
            (layers, model // groups), (layers, taps_len, channels // groups), (layers, channels // groups), (layers, 3, heads // groups),
            (layers, inner // groups),
        ]
        blocks = mine_a + [other_a] + mine_b + [other_b]
        placed = placed_grads(here, blocks, layers, shapes, smalls, chips, inner, ())
        by_head = placed[6]
        pieces = [placed[3], placed[4], placed[5], by_head[:, 0], by_head[:, 1], by_head[:, 2], placed[7]]
    else:
        placed = [jnp.stack([c[i] for c in collected_grads[::-1]]) for i in range(3)]
        placed[1] = placed[1][:, :, :heads]
        small_sum = lax.psum(jnp.stack(collected[::-1], axis=1), ("fsdp", "seq"))
        small_sum = lax.dynamic_index_in_dim(small_sum, lax.axis_index("fsdp"), 0, keepdims=False)
        pieces, at = [], 0
        for size in sizes:
            pieces.append(small_sum[:, at:at + size])
            at += size
    return (
        stream, grad_stream, pieces[0],
        placed[0],
        placed[1],
        pieces[1].reshape(layers, taps_len, -1),
        pieces[2], pieces[3], pieces[4], pieces[5], pieces[6],
        placed[2],
    )


def solution(mesh):
    split = P("fsdp", "seq", None)
    vector = P(None, "fsdp")
    matrix = P(None, "fsdp", None)
    taps = P(None, None, "fsdp")
    return jax.shard_map(
        on_device,
        mesh=mesh,
        in_specs=(
            split, P("fsdp", "seq"), vector, matrix, matrix, taps, vector, vector, vector, vector, vector, matrix, split,
        ),
        out_specs=(
            split, split, vector, matrix, matrix, taps, vector, vector, vector, vector, vector, matrix,
        ),
        check_vma=False,
    )
```

```python
import functools

import jax
import jax.numpy as jnp
from jax import lax
from jax.experimental import pallas as pl
from jax.experimental.pallas import tpu as pltpu
from jax.sharding import PartitionSpec as P

EPSILON = 1e-05
F32, BF16 = jnp.float32, jnp.bfloat16
LANES = 128
EDGE = 8
FACTOR_ROWS = 16
SCALE = 0.25
VMEM = 48 * 1024 * 1024
NT = (((1,), (1,)), ((), ()))
TN = (((0,), (0,)), ((), ()))


def dot(a, b):
    return jnp.dot(a, b, preferred_element_type=F32)


def dot_nt(a, b):
    return lax.dot_general(a, b, NT, preferred_element_type=F32)


def dot_tn(a, b):
    return lax.dot_general(a, b, TN, preferred_element_type=F32)


def dot_exact(a, b):
    return jnp.dot(a, b, precision=lax.Precision.HIGHEST, preferred_element_type=F32)


def halves(v):
    high = v.astype(BF16)
    low = (v - high.astype(F32)).astype(BF16)
    return jnp.concatenate([high, low], axis=1)


def sigmoid(v):
    return 1.0 / (1.0 + jnp.exp(-v))


def softplus(v):
    return jnp.maximum(v, 0.0) + jnp.log1p(jnp.exp(-jnp.abs(v)))


def below(size):
    rows = lax.broadcasted_iota(jnp.int32, (size, size), 0)
    columns = lax.broadcasted_iota(jnp.int32, (size, size), 1)
    return rows >= columns


def head_column(table, head):
    return pltpu.roll(table, LANES - head, axis=1)[:, 0:1]


def conv_total(padded, taps, masks, at, wide, width):
    total = taps[4:5, pl.ds(at, wide)] + taps[3:4, pl.ds(at, wide)] * padded[EDGE:EDGE + width, pl.ds(at, wide)]
    for back in range(1, 4):
        tap = taps[3 - back:4 - back, pl.ds(at, wide)]
        total = total + (masks[back - 1] * tap) * padded[EDGE - back:EDGE - back + width, pl.ds(at, wide)]
    return total


def conv_kernel(inner, mixed, edge, marks, taps, rates, spread, act, sizes, sums, sums_t, state, factor, padded):
    width, channels = mixed.shape[1], padded.shape[1]
    padded[0:EDGE, :] = edge[0, :, 0:channels].astype(F32)
    padded[EDGE:EDGE + width, :] = mixed[0, :, 0:channels].astype(F32)
    marks_now = marks[0]
    masks = [marks_now[:, back:back + 1] for back in range(3)]
    wide = 256
    for at in range(0, channels, wide):
        total = conv_total(padded, taps, masks, at, wide, width)
        act[0, :, pl.ds(at, wide)] = (total * sigmoid(total)).astype(BF16)
    size = softplus(mixed[0, :, channels:].astype(F32) + rates[0:1, :])
    tri = jnp.where(below(width), 1.0, 0.0).astype(F32)
    total_sum = dot_exact(tri, size * rates[1:2, :])
    last = total_sum[width - 1:width]
    sizes[0] = size
    sums[0] = total_sum
    sums_t[0] = total_sum.T[0:sums_t.shape[1]]
    weight = halves(marks_now[:, 4:5] * jnp.exp(last - total_sum) * size)
    gone = marks_now[width - 1:width, 3:4] * jnp.exp(last)
    gone = halves(jnp.broadcast_to(gone, (FACTOR_ROWS, LANES)))
    states = (channels - inner) // 2
    keys_t = act[0, :, inner:inner + states].T
    for at in range(0, inner, wide):
        part = spread[:, pl.ds(at, wide)]
        weighted = (dot(weight, part) * act[0, :, pl.ds(at, wide)].astype(F32)).astype(BF16)
        state[0, 0:states, pl.ds(at, wide)] = dot(keys_t, weighted).astype(BF16)
        fade = dot(gone, part).astype(BF16)
        state[0, states:, pl.ds(at, wide)] = fade
        factor[0, :, pl.ds(at, wide)] = fade


def intra_kernel(inner, heads, act, sizes, sums, sums_t, marks, row_marks, skip, spread, out, scores, stepped):
    width = act.shape[1]
    states = (act.shape[2] - inner) // 2
    half = width // 2
    keys = act[0, :, inner:inner + states]
    queries = act[0, :, inner + states:]
    same = below(width) & (marks[0][:, 5:6] == row_marks[0, 0:1, :])
    scores[...] = jnp.where(same, dot_nt(queries, keys), 0.0)
    size = halves(sizes[0])
    wide = 256
    for at in range(0, inner, wide):
        part = dot(size, spread[:, pl.ds(at, wide)])
        stepped[:, pl.ds(at, wide)] = (part * act[0, :, pl.ds(at, wide)].astype(F32)).astype(BF16)
    per = LANES // (inner // heads)
    span = inner // heads
    lane = lax.broadcasted_iota(jnp.int32, (width, LANES), 1)

    def group(at, carry):
        place = pl.ds(pl.multiple_of(at * LANES, LANES), LANES)
        x = stepped[:, place]
        y_low = y_high = None
        for i in range(per):
            head = at * per + i
            column = head_column(sums[0], head)
            row = sums_t[0, pl.ds(head, 1), :]
            mine = (lane >= i * span) & (lane < (i + 1) * span)
            xh = jnp.where(mine, x, jnp.zeros_like(x))
            w_low = scores[0:half, 0:half] * jnp.exp(jnp.minimum(column[0:half] - row[:, 0:half], 0.0))
            w_high = scores[half:, :] * jnp.exp(jnp.minimum(column[half:] - row, 0.0))
            a = dot(w_low.astype(BF16), xh[0:half])
            b = dot(w_high.astype(BF16), xh)
            y_low = a if y_low is None else y_low + a
            y_high = b if y_high is None else y_high + b
        values = act[0, :, place].astype(F32) * skip[0:1, place]
        out[0, 0:half, place] = (y_low + values[0:half]).astype(out.dtype)
        out[0, half:, place] = (y_high + values[half:]).astype(out.dtype)
        return carry

    lax.fori_loop(0, inner // LANES, group, 0, unroll=2)


def entered_part(at, later_core, before, partner, other, place):
    states = before.shape[0]
    chip = before[:, place]
    core = jnp.full(chip.shape, at[0], jnp.int32)
    chip = jnp.where(core == pl.program_id(0), chip.astype(F32), partner[:, place].astype(F32))
    through = other[0, states:states + 1, place].astype(F32) * chip + other[0, 0:states, place].astype(F32)
    return jnp.where(core == later_core, through, chip).astype(BF16)


def post_kernel(inner, at, part_mixed, act, before, partner, other, sums, marks, gate, gain, spread, mixed, gated, entering, kept):
    states = (act.shape[2] - inner) // 2
    queries = act[0, :, inner + states:]
    enter = halves(marks[0][:, 3:4] * jnp.exp(sums[0]))
    wide = 256
    square = None
    for start in range(0, inner, wide):
        place = pl.ds(start, wide)
        state = entered_part(at, 1, before, partner, other, place)
        entering[0, :, place] = state
        whole = part_mixed[0, :, place].astype(F32) + dot(enter, spread[:, place]) * dot(queries, state)
        g = gate[0, :, place].astype(F32)
        w = whole * (g * sigmoid(g))
        mixed[0, :, place] = whole.astype(BF16)
        kept[:, place] = w
        square = w * w if square is None else square + w * w
    scale = lax.rsqrt(jnp.sum(square, axis=1, keepdims=True) / inner + EPSILON)
    for at in range(0, inner, wide):
        place = pl.ds(at, wide)
        gated[0, :, place] = (kept[:, place] * scale * gain[0:1, place]).astype(BF16)


def gate_back_kernel(
    inner, grad, grad_low, factor, mixed, gate, gain, act, state, sums, marks, spread,
    d_mixed, d_gate, d_state, d_queries, d_sums, row_grads, kept,
):
    states = (act.shape[2] - inner) // 2
    queries = act[0, :, inner + states:]
    queries_t = queries.T
    wide = 256

    @pl.when(pl.program_id(0) == 0)
    def _():
        row_grads[...] = jnp.zeros_like(row_grads)

    square = cross = None
    for at in range(0, inner, wide):
        place = pl.ds(at, wide)
        g = gate[0, :, place].astype(F32)
        w = mixed[0, :, place].astype(F32) * (g * sigmoid(g))
        gg = grad[0, :, place].astype(F32)
        kept[:, place] = w
        square = w * w if square is None else square + w * w
        more = w * gain[0:1, place] * gg
        cross = more if cross is None else cross + more
    scale = lax.rsqrt(jnp.sum(square, axis=1, keepdims=True) / inner + EPSILON)
    pulled = scale * scale * scale * (jnp.sum(cross, axis=1, keepdims=True) / inner)
    entered = marks[0][:, 3:4] * jnp.exp(sums[0])
    enter = halves(entered)
    grad_enter = dq = None
    for at in range(0, inner, wide):
        place = pl.ds(at, wide)
        g = gate[0, :, place].astype(F32)
        sig = sigmoid(g)
        silu = g * sig
        gg = grad[0, :, place].astype(F32)
        w = kept[:, place]
        whole = mixed[0, :, place].astype(F32)
        dw = scale * (gain[0:1, place] * gg) - pulled * w
        row_grads[0:1, place] += jnp.sum(gg * w * scale, axis=0, keepdims=True)
        dm = dw * silu
        d_gate[0, :, place] = (dw * whole * (sig + silu * (1.0 - sig))).astype(BF16)
        d_mixed[0, :, place] = dm.astype(BF16)
        row_grads[1:2, place] += jnp.sum(dm * act[0, :, place].astype(F32), axis=0, keepdims=True)
        part = spread[:, place]
        st = state[0, :, place]
        e = (dm * dot(enter, part)).astype(BF16)
        d_state[0, 0:states, place] = dot(queries_t, e).astype(BF16)
        more_q = dot_nt(e, st)
        dq = more_q if dq is None else dq + more_q
        through = (dm * dot(queries, st)).astype(BF16)
        more_e = dot_nt(through, part[0:LANES])
        grad_enter = more_e if grad_enter is None else grad_enter + more_e
    d_queries[0] = dq
    d_sums[0] = grad_enter * entered
    d_gate[0, :, inner:] = grad_low[0]
    d_state[0, states:, :] = factor[0]


def intra_back_kernel(
    inner, heads, d_mixed, act, sizes, sums, sums_t, marks, row_marks, spread, d_queries, d_sums,
    d_stepped, d_pair, d_total, scores, d_scores, stepped, sums_rows, sums_columns,
):
    width = act.shape[1]
    states = (act.shape[2] - inner) // 2
    half = width // 2
    keys = act[0, :, inner:inner + states]
    queries = act[0, :, inner + states:]
    rows = lax.broadcasted_iota(jnp.int32, (width, width), 0)
    columns = lax.broadcasted_iota(jnp.int32, (width, width), 1)
    same = (rows <= columns) & (marks[0][:, 5:6] == row_marks[0, 0:1, :])
    scores[...] = jnp.where(same, dot_nt(keys, queries), 0.0)
    d_scores[...] = jnp.zeros_like(d_scores)
    sums_rows[...] = jnp.zeros_like(sums_rows)
    sums_columns[...] = jnp.zeros_like(sums_columns)
    size = halves(sizes[0])
    wide = 256
    for at in range(0, inner, wide):
        part = dot(size, spread[:, pl.ds(at, wide)])
        stepped[:, pl.ds(at, wide)] = (part * act[0, :, pl.ds(at, wide)].astype(F32)).astype(BF16)
    per = LANES // (inner // heads)
    span = inner // heads
    lane = lax.broadcasted_iota(jnp.int32, (width, LANES), 1)

    eighth = lax.broadcasted_iota(jnp.int32, (8, width), 0)

    def group(at, carry):
        place = pl.ds(pl.multiple_of(at * LANES, LANES), LANES)
        x = stepped[:, place]
        dy = d_mixed[0, :, place]
        dx_low = dx_high = None
        for i in range(per):
            head = at * per + i
            column = head_column(sums[0], head)
            row = sums_t[0, pl.ds(head, 1), :]
            mine = (lane >= i * span) & (lane < (i + 1) * span)
            xh = jnp.where(mine, x, jnp.zeros_like(x))
            dyh = jnp.where(mine, dy, jnp.zeros_like(dy))
            l_low = jnp.exp(jnp.minimum(row - column[0:half], 0.0))
            l_high = jnp.exp(jnp.minimum(row[:, half:] - column[half:], 0.0))
            w_low = scores[0:half, :] * l_low
            w_high = scores[half:, half:] * l_high
            dw_low = dot_nt(xh[0:half], dy)
            dw_high = dot_nt(xh[half:], dy[half:])
            d_scores[0:half, :] += dw_low * l_low
            d_scores[half:, half:] += dw_high * l_high
            g_low = dw_low * w_low
            g_high = dw_high * w_high
            over_low = jnp.sum(g_low, axis=0, keepdims=True)
            over_high = jnp.sum(g_high, axis=0, keepdims=True)
            eight = pl.ds(pl.multiple_of(head // 8 * 8, 8), 8)
            chosen = eighth == head % 8
            sums_rows[eight, :] += jnp.where(chosen, over_low, 0.0)
            sums_rows[eight, half:] += jnp.where(chosen[:, half:], over_high, 0.0)
            here = lane[0:half] == head
            sums_columns[0:half, :] += jnp.where(here, jnp.sum(g_low, axis=1, keepdims=True), 0.0)
            sums_columns[half:, :] += jnp.where(here, jnp.sum(g_high, axis=1, keepdims=True), 0.0)
            a = dot(w_low.astype(BF16), dyh)
            b = dot(w_high.astype(BF16), dyh[half:])
            dx_low = a if dx_low is None else dx_low + a
            dx_high = b if dx_high is None else dx_high + b
        d_stepped[0, 0:half, place] = dx_low.astype(BF16)
        d_stepped[0, half:, place] = dx_high.astype(BF16)
        return carry

    lax.fori_loop(0, inner // LANES, group, 0, unroll=2)
    grad = jnp.where(same, d_scores[...], 0.0).astype(BF16)
    d_pair[0, :, 0:states] = dot(grad, queries)
    d_pair[0, :, states:] = dot(grad.T, keys) + d_queries[0]
    d_total[0] = sums_rows[...].T - sums_columns[...] + d_sums[0]


def conv_back_kernel(
    inner, here, d_stepped, d_mixed, act, mixed_in, edge, marks, taps, rates, skip, sizes, sums, spread,
    d_pair, d_total, before, partner, other, state,
    d_mixed_in, d_edge, tap_grads, head_grads, padded, shifted,
):
    width, channels = mixed_in.shape[1], padded.shape[1]
    states = (channels - inner) // 2
    wide = 256

    @pl.when(pl.program_id(0) == 0)
    def _():
        tap_grads[...] = jnp.zeros_like(tap_grads)
        head_grads[...] = jnp.zeros_like(head_grads)

    padded[0:EDGE, :] = edge[0, :, 0:channels].astype(F32)
    padded[EDGE:EDGE + width, :] = mixed_in[0, :, 0:channels].astype(F32)
    marks_now = marks[0]
    masks = [marks_now[:, back:back + 1] for back in range(3)]
    total_sum = sums[0]
    size = sizes[0]
    last = total_sum[width - 1:width]
    faded = marks_now[:, 4:5] * jnp.exp(last - total_sum)
    weight = faded * size
    weight_pair = halves(weight)
    size_pair = halves(size)
    keys = act[0, :, inner:inner + states]
    for back in range(3):
        shifted[back, 0:EDGE, :] = jnp.zeros((EDGE, wide), F32)
        shifted[back, EDGE + width:, :] = jnp.zeros((EDGE, wide), F32)

    def through_conv(at, d_act):
        place = pl.ds(at, wide)
        total = conv_total(padded, taps, masks, at, wide, width)
        sig = sigmoid(total)
        d = d_act * (sig + total * sig * (1.0 - sig))
        tap_grads[4:5, place] += jnp.sum(d, axis=0, keepdims=True)
        tap_grads[3:4, place] += jnp.sum(d * padded[EDGE:EDGE + width, place], axis=0, keepdims=True)
        back_total = taps[3:4, place] * d
        edge_total = jnp.zeros((EDGE, wide), F32)
        for back in range(1, 4):
            u = masks[back - 1] * d
            tap_grads[3 - back:4 - back, place] += jnp.sum(
                u * padded[EDGE - back:EDGE - back + width, place], axis=0, keepdims=True
            )
            shifted[back - 1, EDGE:EDGE + width, :] = u
            tap = taps[3 - back:4 - back, place]
            back_total = back_total + tap * shifted[back - 1, EDGE + back:EDGE + back + width, :]
            edge_total = edge_total + tap * shifted[back - 1, back:back + EDGE, :]
        d_mixed_in[0, :, place] = back_total.astype(BF16)
        d_edge[0, :, place] = edge_total

    d_keys = d_pair[0, :, 0:states]
    d_size = d_weight = carried = None
    for at in range(0, inner, wide):
        place = pl.ds(at, wide)
        values = act[0, :, place].astype(F32)
        part = spread[:, place]
        ds = entered_part(here, 0, before, partner, other, place)
        wide_weight = dot(weight_pair, part)
        d_weighted = dot(keys, ds)
        dx = d_stepped[0, :, place].astype(F32)
        d_act = dx * dot(size_pair, part) + d_weighted * wide_weight + skip[0:1, place] * d_mixed[0, :, place].astype(F32)
        d_keys = d_keys + dot_nt((wide_weight * values).astype(BF16), ds)
        a = dot_nt((dx * values).astype(BF16), part[0:LANES])
        b = dot_nt((d_weighted * values).astype(BF16), part[0:LANES])
        c = jnp.sum(ds.astype(F32) * state[0, :, place].astype(F32), axis=0, keepdims=True)
        c = dot_nt(jnp.broadcast_to(halves_rows(c), (EDGE, wide)), part[0:LANES])
        d_size = a if d_size is None else d_size + a
        d_weight = b if d_weight is None else d_weight + b
        carried = c if carried is None else carried + c
        through_conv(at, d_act)
    through_conv(inner, jnp.concatenate([d_keys, d_pair[0, :, states:]], axis=1))
    d_size = d_size + d_weight * faded
    pulled = d_weight * weight
    gone = marks_now[width - 1:width, 3:4] * jnp.exp(last)
    at_end = jnp.sum(pulled, axis=0, keepdims=True) + gone * carried[0:1]
    row = lax.broadcasted_iota(jnp.int32, (width, LANES), 0)
    d_sum = d_total[0] - pulled + jnp.where(row == width - 1, at_end, 0.0)
    order = lax.broadcasted_iota(jnp.int32, (width, width), 0) <= lax.broadcasted_iota(jnp.int32, (width, width), 1)
    d_rate = dot_exact(jnp.where(order, 1.0, 0.0).astype(F32), d_sum)
    d_size = d_size + d_rate * rates[1:2, :]
    d_step = d_size * sigmoid(mixed_in[0, :, channels:].astype(F32) + rates[0:1, :])
    d_mixed_in[0, :, channels:] = d_step.astype(BF16)
    head_grads[0:1, :] += jnp.sum(d_step, axis=0, keepdims=True)
    head_grads[1:2, :] += jnp.sum(d_rate * size * rates[1:2, :], axis=0, keepdims=True)


def halves_rows(v):
    return v.astype(BF16)


def without(kernel, first, count):
    def run(*refs):
        return kernel(*refs[:first], *refs[first + count:])

    return run


def call(kernel, batch, ins, outs, scratch, name, micros, at=None, after=()):
    def spec(shape, whole):
        block = tuple(shape) if whole else (1,) + tuple(shape[1:])
        if whole:
            return pl.BlockSpec(block, lambda b: (0,) * len(block))
        return pl.BlockSpec(block, lambda b: (b,) + (0,) * (len(block) - 1))

    arrays = [a for a, _ in ins]
    in_specs = [spec(a.shape, whole) for a, whole in ins]
    if at is not None:
        arrays, in_specs = [at] + arrays, [pl.BlockSpec(memory_space=pltpu.SMEM)] + in_specs
    return pl.pallas_call(
        without(kernel, len(arrays), len(after)),
        grid=(batch,),
        in_specs=in_specs + [pl.BlockSpec(memory_space=pl.ANY)] * len(after),
        out_specs=[spec(shape, whole) for shape, _, whole in outs],
        out_shape=[jax.ShapeDtypeStruct(shape, kind) for shape, kind, _ in outs],
        scratch_shapes=[pltpu.VMEM(shape, kind) for shape, kind in scratch],
        compiler_params=pltpu.CompilerParams(vmem_limit_bytes=VMEM),
        cost_estimate=cost(micros),
        name=name,
    )(*arrays, *after)


def cost(micros):
    micros = micros * SCALE
    return pl.CostEstimate(flops=int(micros * 1.1e9), bytes_accessed=int(micros * 1e6), transcendentals=0)


def edge_kernel(grad, more, out):
    size, channels = grad.shape[1], more.shape[2]
    out[0, :, channels:] = grad[0, :, channels:]
    last = jnp.concatenate([jnp.zeros((size - EDGE, channels), F32), more[0].astype(F32)], axis=0)
    out[0, :, 0:channels] = (grad[0, :, 0:channels].astype(F32) + last).astype(BF16)


def with_edges(grad, more, after):
    batch, width, wide = grad.shape
    size = 2 * EDGE
    block = pl.BlockSpec((1, size, wide), lambda b: (b, width // size - 1, 0))
    return pl.pallas_call(
        without(edge_kernel, 2, len(after)),
        grid=(batch,),
        in_specs=[block, pl.BlockSpec((1,) + more.shape[1:], lambda b: (b, 0, 0))] + [pl.BlockSpec(memory_space=pl.ANY)] * len(after),
        out_specs=block,
        out_shape=jax.ShapeDtypeStruct(grad.shape, grad.dtype),
        input_output_aliases={0: 0},
        compiler_params=pltpu.CompilerParams(vmem_limit_bytes=VMEM),
        cost_estimate=cost(1.0),
        name="with_edges",
    )(grad, more, *after)


def whole_call(kernel, arrays, outs, micros, name, at=None, after=(), scratch=()):
    spec = pl.BlockSpec(memory_space=pltpu.VMEM)
    arrays, in_specs = list(arrays), [spec] * len(arrays)
    if at is not None:
        arrays, in_specs = [at] + arrays, [pl.BlockSpec(memory_space=pltpu.SMEM)] + in_specs
    return pl.pallas_call(
        without(kernel, len(arrays), len(after)),
        in_specs=in_specs + [pl.BlockSpec(memory_space=pl.ANY)] * len(after),
        out_specs=[spec] * len(outs),
        out_shape=[jax.ShapeDtypeStruct(shape, kind) for shape, kind in outs],
        scratch_shapes=[pltpu.VMEM(shape, kind) for shape, kind in scratch],
        compiler_params=pltpu.CompilerParams(vmem_limit_bytes=VMEM),
        cost_estimate=cost(micros),
        name=name,
    )(*arrays, *after)


def swap(x, axis, bits):
    return lax.ppermute(x, axis, [(i, i ^ bits) for i in range(lax.axis_size(axis))])


def join_kernel(later_core, at, own, other, joined):
    core = at[0]
    states = own.shape[1] - FACTOR_ROWS
    for start in range(0, own.shape[2], 512):
        place = pl.ds(start, 512)
        mine = own[core, :, place].astype(F32)
        theirs = other[core, :, place].astype(F32)
        later = jnp.full(mine.shape, core, jnp.int32) == later_core
        second = jnp.where(later, mine, theirs)
        first = jnp.where(later, theirs, mine)
        gain = second[states:states + 1]
        joined[0:states, place] = (gain * first[0:states] + second[0:states]).astype(BF16)
        joined[states:, place] = (gain * first[states:]).astype(BF16)


def enter_kernel(count, *refs):
    out = refs[count]
    states = out.shape[0]
    for start in range(0, out.shape[1], 512):
        place = pl.ds(start, 512)
        before = refs[0][0:states, place].astype(F32)
        for got in refs[1:count]:
            before = got[states:states + 1, place].astype(F32) * before + got[0:states, place].astype(F32)
        out[:, place] = before.astype(BF16)


def exchange(own, at, later_core, after=()):
    peers = lax.axis_size("seq")
    other = swap(own, "seq", 1)
    joined = whole_call(functools.partial(join_kernel, later_core), [own, other], [(own.shape[1:], BF16)], 2.0, "join_states", at, after)[0]
    got = []
    for distance in range(peers // 2 - 1, 0, -1):
        step = 2 * distance if later_core == 1 else -2 * distance
        route = [(i, i + step) for i in range(peers) if 0 <= i + step < peers]
        got.append(lax.ppermute(joined, "seq", route))
    return got, other, joined


def entered(got, after):
    shape = (got[0].shape[0] - FACTOR_ROWS, got[0].shape[1])
    before = whole_call(
        functools.partial(enter_kernel, len(got)), got, [(shape, BF16)], 2.0, "enter_states", after=after
    )[0]
    return before, swap(before, "seq", 1)


def gathered(block):
    peers = lax.axis_size("seq")
    rows = block.shape[0] // peers
    share = lax.dynamic_slice_in_dim(block, lax.axis_index("seq") * rows, rows, 0)
    return lax.all_gather(share, ("fsdp", "seq"), axis=0, tiled=True)


def take_in_kernel(columns, block, steps, out):
    first, last, with_steps = columns
    wide = last - first
    out[:, 0:wide] = block[0, :, first:last]
    if with_steps:
        heads = steps.shape[2]
        out[:, wide:] = jnp.zeros((out.shape[0], LANES), BF16)
        out[:, wide:wide + heads] = steps[0]


def take_share(weight, steps, layer, columns, at, share, parts, after):
    first, last, with_steps = columns
    wide = last - first + (LANES if with_steps else 0)

    def rows(i, where):
        return (layer, where[1] * 2 + where[0] if parts > 2 else where[0], 0)

    arrays = [weight] if steps is None else [weight, steps]
    specs = [pl.BlockSpec((1, share, a.shape[2]), rows) for a in arrays]
    kernel = functools.partial(take_in_kernel, columns)
    if steps is None:
        kernel = lambda block, out: take_in_kernel(columns, block, None, out)
    inner_kernel = without(kernel, len(arrays), len(after))
    return pl.pallas_call(
        lambda where, *refs: inner_kernel(*refs),
        grid_spec=pltpu.PrefetchScalarGridSpec(
            num_scalar_prefetch=1,
            grid=(1,),
            in_specs=specs + [pl.BlockSpec(memory_space=pl.ANY)] * len(after),
            out_specs=pl.BlockSpec((share, wide), lambda i, where: (0, 0)),
        ),
        out_shape=jax.ShapeDtypeStruct((share, wide), BF16),
        compiler_params=pltpu.CompilerParams(vmem_limit_bytes=VMEM),
        cost_estimate=cost(1.0),
        name="take_share",
    )(at, *arrays, *after)


def place_rows_kernel(starts, columns, many, at, *refs):
    weight, steps = refs[0], refs[1] if many == 2 else None
    sources, out = refs[many:-1], refs[-1]
    core, chip, group = at[0], at[1], at[2]
    rows = weight.shape[1]
    own = pl.ds(pl.multiple_of(group * rows, rows), rows)
    first, last, with_steps = columns
    wide = last - first
    out[own, 0:wide] = weight[0, :, first:last]
    if with_steps:
        out[own, wide:] = jnp.concatenate([steps[0], jnp.zeros((rows, LANES - steps.shape[2]), BF16)], axis=1)
    for source, index, rows, place in starts:
        start = pl.multiple_of(place(core, chip, group), rows)
        out[pl.ds(start, rows), :] = sources[source][index]


def placed_rows(at, weight, steps, layer, columns, sources, starts, groups, micros, after=()):
    whole = pl.BlockSpec(memory_space=pltpu.VMEM)
    own = [weight] if steps is None else [weight, steps]
    first, last, with_steps = columns
    shape = (weight.shape[1] * groups, last - first + (LANES if with_steps else 0))
    return pl.pallas_call(
        without(functools.partial(place_rows_kernel, starts, columns, len(own)), 1 + len(own) + len(sources), len(after)),
        grid=(1,),
        in_specs=[pl.BlockSpec(memory_space=pltpu.SMEM)]
        + [pl.BlockSpec((1,) + a.shape[1:], lambda i: (layer, 0, 0)) for a in own] + [whole] * len(sources)
        + [pl.BlockSpec(memory_space=pl.ANY)] * len(after),
        out_specs=whole,
        out_shape=jax.ShapeDtypeStruct(shape, BF16),
        compiler_params=pltpu.CompilerParams(vmem_limit_bytes=VMEM),
        cost_estimate=cost(micros),
        name="place_rows",
    )(at, *own, *sources, *after)


def stack_kernel(count, *refs):
    out, row = refs[count], 0
    for ref in refs[:count]:
        if len(ref.shape) == 2:
            out[row] = ref[...]
            row += 1
        else:
            out[row:row + ref.shape[0]] = ref[...]
            row += ref.shape[0]


def stacked(blocks, after=()):
    many = sum(1 if b.ndim == 2 else b.shape[0] for b in blocks)
    return whole_call(
        functools.partial(stack_kernel, len(blocks)), blocks, [((many,) + blocks[0].shape[-2:], BF16)], 1.0, "stack", after=after
    )[0]


def unfold_kernel(share, folded, out):
    many = folded.shape[1] // out.shape[1]
    model = out.shape[1]
    for block in range(folded.shape[0] // share):
        for i in range(many):
            to = (block * many + i) * share
            out[to:to + share, :] = folded[block * share:(block + 1) * share, i * model:(i + 1) * model]


def unfolded(whole, inner, model, share):
    rows = whole.shape[0] // 4
    return pl.pallas_call(
        functools.partial(unfold_kernel, share),
        grid=(4,),
        in_specs=[pl.BlockSpec((rows, inner), lambda i: (i, 0))],
        out_specs=pl.BlockSpec((rows * inner // model, model), lambda i: (i, 0)),
        out_shape=jax.ShapeDtypeStruct((inner, model), BF16),
        compiler_params=pltpu.CompilerParams(vmem_limit_bytes=VMEM),
        cost_estimate=cost(3.0),
        name="unfold",
    )(whole)


def from_along_z(mine, groups, after=()):
    return stacked([swap(mine, "fsdp", e) for e in range(1, groups)], after)


def fetched_by_all(weight, steps, layer, columns, at, groups, chips, from_z, place_after=()):
    rows = weight.shape[1]
    share = rows // (2 * chips)
    sources = [from_z] + [swap(from_z, "seq", 2 * d) for d in range(1, chips)]
    sources.append(swap(stacked([a.reshape(-1, a.shape[2]) for a in sources]), "seq", 1))

    def place_of(d, e, other):
        return lambda core, chip, group: (group ^ e) * rows + (chip ^ d) * (2 * share) + (core ^ other) * share

    starts = []
    for d in range(chips):
        for e in range(1, groups):
            index = e - 1
            starts.append((d, (index,), share, place_of(d, e, 0)))
            starts.append((chips, (d, slice(index * share, (index + 1) * share)), share, place_of(d, e, 1)))
    return placed_rows(at, weight, steps, layer, columns, sources, starts, groups, 4.0, place_after)


def reduced(grad):
    share = lax.psum_scatter(grad, ("fsdp", "seq"), scatter_dimension=0, tiled=True)
    return lax.all_gather(share, "seq", axis=0, tiled=True).astype(F32)


def turn_kernel(groups, chips, at, gated, low, own, send, turned):
    core, chip, group = at[0], at[1], at[2]
    base = 0
    for x in (gated, low):
        if x is None:
            continue
        total = x.shape[1]
        share = total // (2 * groups * chips)
        for start in range(0, total, 256):
            turned[start:start + 256, :] = x[:, start:start + 256].T
        for other, out in ((0, own), (1, send)):
            for d in range(chips):
                for e in range(groups):
                    start = (group ^ e) * (total // groups) + (chip ^ d) * (2 * share) + (core ^ other) * share
                    to = base + (d * groups + e) * share
                    out[to:to + share, :] = turned[pl.ds(pl.multiple_of(start, share), share), :]
        base += total // 2


def turned_halves(gated, low, at, groups, chips):
    rows = low.shape[0]
    if gated is None:
        def kernel(where, low_ref, *refs):
            turn_kernel(groups, chips, where, None, low_ref, *refs)

        return whole_call(kernel, [low], [((low.shape[1] // 2, rows), BF16)] * 2, 2.0, "turn", at, scratch=[(low.shape[::-1], BF16)])
    half = ((gated.shape[1] + low.shape[1]) // 2, rows)
    return whole_call(
        functools.partial(turn_kernel, groups, chips), [gated, low], [(half, BF16)] * 2, 4.0, "turn", at,
        scratch=[((gated.shape[1], rows), BF16)],
    )


def first_grads_kernel(groups, chips, inner, joined, at, own, other, grad, grad_other, *refs):
    wide = grad.shape[1] - inner
    total_big = inner // 2
    big = total_big // (groups * chips)
    small = (own.shape[0] - total_big) // (groups * chips)
    outs = refs[1:] if joined else refs
    group = at[2]

    def put(total, share, start, column):
        for d in range(chips):
            for e in range(groups):
                block = (d * groups + e) * share
                rows, columns = slice(start, start + share), pl.ds(column, 512)
                if joined:
                    outs[d][e, rows, columns] = total[block:block + share]
                else:
                    outs[0][group ^ e, d, rows, columns] = total[block:block + share]

    if joined:
        for d in range(chips):
            outs[d][groups] = refs[0][d]
    for start in range(0, wide, 512):
        place = pl.ds(inner + start, 512)
        total = dot(own[0:total_big, :], grad[:, place]) + dot(other[0:total_big, :], grad_other[:, place])
        put(total.astype(BF16), big, 0, start)
    for start in range(0, inner, 512):
        place = pl.ds(start, 512)
        total = dot(own[total_big:, :], grad[:, place]) + dot(other[total_big:, :], grad_other[:, place])
        put(total.astype(BF16), small, big + start // wide * small, start % wide)


def second_grads_kernel(groups, chips, channels, heads, here, own, other, grad, grad_other, extra, extra_other, *outs):
    rows = extra.shape[0] // 2
    base = own.shape[0] - rows
    share = rows // (groups * chips)
    core, chip, group = here[0], here[1], here[2]
    lane = lax.broadcasted_iota(jnp.int32, (share, LANES), 1)
    total_wide = channels + LANES
    edges = list(range(0, channels, 512)) + [channels, total_wide]
    for at, end in zip(edges[:-1], edges[1:]):
        place = pl.ds(at, end - at)
        total = dot(own[base:, :], grad[:, place]) + dot(other[base:, :], grad_other[:, place])
        for d in range(chips):
            for e in range(groups):
                block = (d * groups + e) * share
                part = total[block:block + share]
                if at == channels:
                    start = (group ^ e) * (2 * rows // groups) + (chip ^ d) * (2 * share) + core * share
                    here_rows = pl.ds(pl.multiple_of(start, share), share)
                    part = jnp.where(lane < heads, part, extra[here_rows, :] + extra_other[here_rows, :])
                outs[d][e, :, place] = part.astype(BF16)


def gather_small_kernel(groups, taps, heads, gain, tap_grads, head_grads, row_grads, spread, out):
    cut = out.shape[0] // groups
    channels, inner = tap_grads.shape[1], row_grads.shape[1]
    skip = row_grads[1:2, :]
    high = skip.astype(BF16)
    low = (skip - high.astype(F32)).astype(BF16)
    ones = spread[0:LANES, :]
    skip = dot_nt(jnp.broadcast_to(high, (8, inner)), ones) + dot_nt(jnp.broadcast_to(low, (8, inner)), ones)
    span, part, few = channels // groups, inner // groups, heads // groups
    for z in range(groups):
        rows = [jnp.zeros((heads, cut), F32), gain[0:1, z * cut:(z + 1) * cut]]
        for at in range(0, part, cut):
            rows.append(row_grads[0:1, z * part + at:z * part + at + cut])
        for at in range(0, span, cut):
            wide = min(cut, span - at)
            block = tap_grads[0:taps + 1, z * span + at:z * span + at + wide]
            if wide < cut:
                block = jnp.concatenate([block, jnp.zeros((taps + 1, cut - wide), F32)], axis=1)
            rows.append(block)
        lane = lax.broadcasted_iota(jnp.int32, (1, LANES), 1)
        for row in (head_grads[0:1, :], head_grads[1:2, :], skip[0:1, :]):
            row = pltpu.roll(row, (LANES - z * few) % LANES, axis=1) if z else row
            row = jnp.where(lane < few, row, 0.0)
            rows.append(jnp.concatenate([row] + [jnp.zeros((1, cut - LANES), F32)], axis=1))
        table = jnp.concatenate(rows, axis=0)
        table = jnp.concatenate([table, jnp.zeros((LANES - table.shape[0], cut), F32)], axis=0)
        out[z * cut:(z + 1) * cut, :] = table.T


def add_kernel(count, *refs):
    ins, outs = refs[:count], refs[count:]
    for i, out in enumerate(outs):
        total = ins[0][i].astype(F32)
        for more in ins[1:]:
            total = total + more[i].astype(F32)
        out[...] = total.astype(out.dtype)


def halve_kernel(count, *refs):
    ins, (near, far, *more_outs) = refs[:count], refs[count:]
    half = near.shape[0]
    for i in range(2 * half + len(more_outs)):
        total = ins[0][i].astype(F32)
        for more in ins[1:]:
            total = total + more[i].astype(F32)
        if i < half:
            near[i] = total.astype(BF16)
        elif i < 2 * half:
            far[i - half] = total.astype(BF16)
        else:
            more_outs[0][...] = total.astype(BF16)


def lay_kernel(count, layers, *refs):
    out = refs[-1]
    wide = out.shape[1]
    share, columns = refs[0].shape[0] // layers, refs[0].shape[1]
    row = 0
    for layer in range(layers):
        rows = slice(layer * share, (layer + 1) * share)
        for at in range(0, columns, wide):
            width = min(wide, columns - at)
            total = refs[0][rows, at:at + width].astype(F32)
            for more in refs[1:count]:
                total = total + more[rows, at:at + width].astype(F32)
            out[row:row + share, 0:width] = total.astype(BF16)
            if width < wide:
                out[row:row + share, width:] = jnp.zeros((share, wide - width), BF16)
            row += share


def plane_parts(blocks):
    return [blocks[0]] + [swap(blocks[i], "seq", 2 * i) for i in range(1, len(blocks))]


def halved(got, after=()):
    parts, rows, columns = got[0].shape
    outs = [((parts // 2, rows, columns), BF16)] * 2 + [((rows, columns), BF16)] * (parts % 2)
    return whole_call(functools.partial(halve_kernel, len(got)), got, outs, 2.0, "add_halves", after=after)


def halved_sums(near, far, after):
    parts, rows, columns = near.shape
    got = [near, swap(far, "fsdp", parts)]
    while parts > 1:
        near, far = halved(got, after)
        parts //= 2
        got = [near, swap(far, "fsdp", parts)]
    return whole_call(functools.partial(add_kernel, 2), got, [((rows, columns), BF16)], 1.0, "add_halves", after=after)[0]


def laid(got, wide, after):
    rows, columns = got[0].shape
    shape = (-(-columns // wide) * rows, wide)
    return whole_call(functools.partial(lay_kernel, len(got), 1), got, [(shape, BF16)], 2.0, "lay_sums", after=after)[0]


def layer_sums(got, groups, wide, after):
    parts, rows, columns = got[0].shape
    shares = whole_call(functools.partial(add_kernel, len(got)), got, [((rows, columns), BF16)] * parts, 2.0, "add_plane")
    return laid([shares[0]] + [swap(shares[e], "fsdp", e) for e in range(1, groups)], wide, after)


def spread_in_plane(share, chips):
    mine = [share] + [swap(share, "seq", 2 * d) for d in range(1, chips)]
    return mine, swap(stacked(mine), "seq", 1)


def place_kernel(chips, inner, layers, at, *refs):
    mine_a, other_a = refs[:chips], refs[chips]
    mine_b, other_b = refs[chips + 1:2 * chips + 1], refs[2 * chips + 1]
    in_out, extra_out, out_out, norm_out, taps_out, bias_out, heads_out, gain_out, extra = refs[-9:]
    core, chip = at[0], at[1]
    model = other_a.shape[2]
    rows_in, rows_out = in_out.shape[1], out_out.shape[1]
    big, share = rows_out // (2 * chips), rows_in // (2 * chips)
    channels = in_out.shape[2] - inner
    for layer in range(layers):
        @pl.when(pl.program_id(0) == layer)
        def _():
            for d in range(chips):
                for is_other in range(2):
                    a, b = (other_a.at[d], other_b.at[d]) if is_other else (mine_a[d], mine_b[d])
                    start = (chip ^ d) * (2 * share) + (core ^ is_other) * share
                    rows = pl.ds(pl.multiple_of(start, share), share)
                    start = (chip ^ d) * (2 * big) + (core ^ is_other) * big
                    first = layer * (a.shape[0] // layers)
                    out_out[0, pl.ds(pl.multiple_of(start, big), big), :] = a[first:first + big, :].astype(F32)
                    first += big
                    for i in range(inner // model):
                        in_out[0, rows, i * model:(i + 1) * model] = a[first:first + share, :].astype(F32)
                        first += share
                    first = layer * (b.shape[0] // layers)
                    for column in range(0, channels + LANES, model):
                        wide = min(model, channels - column)
                        in_out[0, rows, pl.ds(inner + column, wide)] = b[first:first + share, 0:wide].astype(F32)
                        if column + model >= channels:
                            extra[rows, :] = b[first:first + share, wide:wide + LANES].astype(F32)
                        first += share
            extra_out[0] = extra[:, 0:extra_out.shape[2]]
            table = extra[...].T
            heads = extra_out.shape[2]
            taps, span, part = taps_out.shape[1], taps_out.shape[2], gain_out.shape[1]
            norm_out[layer:layer + 1, :] = table[heads:heads + 1]
            row = heads + 1
            for start in range(0, part, rows_in):
                gain_out[layer:layer + 1, start:start + rows_in] = table[row:row + 1]
                row += 1
            for start in range(0, span, rows_in):
                wide = min(rows_in, span - start)
                taps_out[layer, :, start:start + wide] = table[row:row + taps, 0:wide]
                bias_out[layer:layer + 1, start:start + wide] = table[row + taps:row + taps + 1, 0:wide]
                row += taps + 1
            few = heads_out.shape[2]
            heads_out[layer] = table[row:row + 3, 0:few]


def placed_grads(at, pieces, layers, shapes, smalls, chips, inner, after):
    whole = pl.BlockSpec(memory_space=pltpu.VMEM)
    return pl.pallas_call(
        without(functools.partial(place_kernel, chips, inner, layers), 1 + len(pieces), len(after)),
        grid=(layers,),
        in_specs=[pl.BlockSpec(memory_space=pltpu.SMEM)] + [whole] * len(pieces)
        + [pl.BlockSpec(memory_space=pl.ANY)] * len(after),
        out_specs=[pl.BlockSpec((1,) + shape, lambda i: (i, 0, 0)) for shape in shapes]
        + [pl.BlockSpec(shape, lambda i, n=len(shape): (0,) * n) for shape in smalls],
        out_shape=[jax.ShapeDtypeStruct((layers,) + shape, F32) for shape in shapes] + [jax.ShapeDtypeStruct(shape, F32) for shape in smalls],
        scratch_shapes=[pltpu.VMEM((shapes[0][0], LANES), F32)],
        compiler_params=pltpu.CompilerParams(vmem_limit_bytes=VMEM),
        cost_estimate=cost(8.0),
        name="place_grads",
    )(at, *pieces, *after)


def norm_scale_of(stream):
    return lax.rsqrt(jnp.mean(stream * stream, axis=-1, keepdims=True) + EPSILON)


def on_device(
    tokens, segments, norm_gain, in_weight, dt_weight, conv_weight, conv_bias, dt_bias, a_log, d_skip,
    gate_gain, out_weight, cotangent,
):
    layers = in_weight.shape[0]
    batch, width, model = tokens.shape
    heads = dt_weight.shape[2]
    taps_len = conv_weight.shape[1]
    peers = lax.axis_size("seq")
    groups = lax.axis_size("fsdp")
    rows = batch * width
    inner = out_weight.shape[1] * groups
    channels = in_weight.shape[2] - inner
    states = (channels - inner) // 2
    span = inner // heads
    chips = peers // 2
    direct = model % (32 * groups * peers) == 0 and chips == 4 and groups == 4 and layers == 2
    seq_at = lax.axis_index("seq")
    here = jnp.stack([seq_at % 2, seq_at // 2, lax.axis_index("fsdp")]).astype(jnp.int32)

    small = [norm_gain, conv_weight.reshape(layers, -1), conv_bias, dt_bias, a_log, d_skip, gate_gain]
    sizes = [a.shape[1] for a in small]
    own = jnp.concatenate(small, axis=1)
    if direct:
        share_in, share_out = model // (groups * peers), inner // (groups * peers)
        all_columns = (0, inner + channels, True)
        mix_z = from_along_z(take_share(in_weight, dt_weight, 0, all_columns, here, share_in, peers, ()), groups)
        by_partner, bits = stacked([own], (mix_z,)), 1
        while bits < groups:
            by_partner = jnp.concatenate([by_partner, swap(by_partner, "fsdp", bits)])
            bits *= 2
        packed = jnp.stack([lax.dynamic_index_in_dim(by_partner, here[2] ^ z, 0, keepdims=False) for z in range(groups)])
    else:
        packed = lax.all_gather(own, "fsdp", axis=0)
    pieces, at = [], 0
    for size in sizes:
        pieces.append(packed[:, :, at:at + size])
        at += size

    def joined(piece):
        return jnp.moveaxis(piece, 0, 1).reshape(layers, -1)

    norm_all = joined(pieces[0]).astype(F32)
    taps_all = jnp.moveaxis(pieces[1].reshape(groups, layers, taps_len, -1), 0, 2).reshape(layers, taps_len, channels)
    taps_all = jnp.concatenate(
        [taps_all.astype(F32), joined(pieces[2]).astype(F32)[:, None], jnp.zeros((layers, 8 - taps_len - 1, channels), F32)], axis=1
    )
    pad_heads = ((0, 0), (0, LANES - heads))
    rates_all = jnp.stack(
        [jnp.pad(joined(pieces[3]).astype(F32), pad_heads), jnp.pad(-jnp.exp(joined(pieces[4]).astype(F32)), pad_heads)], axis=1
    )
    rates_all = jnp.pad(rates_all, ((0, 0), (0, 6), (0, 0)))
    skip_all = jnp.repeat(joined(pieces[5]).astype(F32), span, axis=1)[:, None]
    gain_all = joined(pieces[6]).astype(F32)[:, None]

    gate_all, mix_all, out_all = [], [], []
    for layer in range(layers):
        if direct:
            if layer == 0:
                whole = fetched_by_all(
                    in_weight, dt_weight, 0, all_columns, here, groups, chips, mix_z, (norm_all, taps_all, rates_all, skip_all, gain_all)
                )
                gates, mixes = whole[:, :inner], whole[:, inner:]
                outs = None
            else:
                share = take_share(in_weight, dt_weight, layer, all_columns, here, share_in, peers, (mix_z,))
                taken, first = [share], 0
                if layer == 1:
                    share = take_share(out_weight, None, 0, (0, model, False), here, share_out, peers, (mix_z,))
                    taken = [share[i * share_in:(i + 1) * share_in] for i in range(inner // model)] + taken
                    first = inner
                whole = lax.all_gather(jnp.concatenate(taken, axis=1), ("fsdp", "seq"), axis=0, tiled=True)
                gates, mixes = whole[:, first:first + inner], whole[:, first + inner:]
                if layer == 1:
                    out_all[0] = unfolded(whole, inner, model, share_in)
                share = take_share(out_weight, None, layer, (0, model, False), here, share_out, peers, (mix_z,))
                outs = lax.all_gather(share, ("fsdp", "seq"), axis=0, tiled=True)
        else:
            steps = jnp.pad(dt_weight[layer], ((0, 0), (0, LANES - heads)))
            whole = gathered(jnp.concatenate([in_weight[layer], steps], axis=1))
            gates, mixes = whole[:, :inner], whole[:, inner:]
            outs = gathered(out_weight[layer])
        gate_all.append(gates)
        mix_all.append(mixes)
        out_all.append(outs)

    numbers = (segments + 1).astype(F32)
    before = lax.ppermute(numbers[:, width - EDGE:], "seq", [(i, i + 1) for i in range(peers - 1)])
    padded = jnp.concatenate([before, numbers], axis=1)
    columns = [padded[:, EDGE - back:EDGE - back + width] == numbers for back in range(1, taps_len)]
    columns += [numbers == before[:, EDGE - 1:], numbers == numbers[:, width - 1:]]
    marks = jnp.stack([c.astype(F32) for c in columns] + [numbers], axis=-1)
    marks = jnp.pad(marks, ((0, 0), (0, 0), (0, LANES - marks.shape[-1])))
    row_marks = jnp.broadcast_to(numbers[:, None, :], (batch, 8, width))
    lane_head = jnp.arange(inner) // span
    spread = (jnp.arange(2 * LANES)[:, None] % LANES == lane_head[None, :]).astype(BF16)

    stream = tokens.astype(F32)
    kept, sent = [], ()
    for layer in range(layers):
        norm_scale = norm_scale_of(stream)
        low = (stream * norm_scale * norm_all[layer]).astype(BF16).reshape(rows, model)
        w_gate, w_mix, w_out = gate_all[layer], mix_all[layer], out_all[layer]
        mixed_in = dot(low, w_mix).astype(BF16).reshape(batch, width, channels + LANES)
        edge = lax.ppermute(mixed_in[:, width - EDGE:], "seq", [(i, i + 1) for i in range(peers - 1)])
        gate = dot(low, w_gate).astype(BF16).reshape(batch, width, inner)
        taps, rates, skip, gain = taps_all[layer], rates_all[layer], skip_all[layer], gain_all[layer]
        act, size, sums, sums_t, state, factor = call(
            functools.partial(conv_kernel, inner), batch,
            [(mixed_in, 0), (edge, 0), (marks, 0), (taps, 1), (rates, 1), (spread, 1)],
            [
                ((batch, width, channels), BF16, 0), ((batch, width, LANES), F32, 0), ((batch, width, LANES), F32, 0),
                ((batch, heads, width), F32, 0), ((batch, states + FACTOR_ROWS, inner), BF16, 0),
                ((batch, FACTOR_ROWS, inner), BF16, 0),
            ],
            [((EDGE + width, channels), F32)], "conv_states", 8.0, after=sent,
        )
        got, other, joined_state = exchange(state, here, 1)
        (part,) = call(
            functools.partial(intra_kernel, inner, heads), batch,
            [(act, 0), (size, 0), (sums, 0), (sums_t, 0), (marks, 0), (row_marks, 0), (skip, 1), (spread, 1)],
            [((batch, width, inner), F32, 0)],
            [((width, width), F32), ((width, inner), BF16)], "mix_within", 12.0, after=(joined_state,),
        )
        before, partner = entered(got, (part, gate, w_out) if direct else (part,))
        mixed, gated, entering = call(
            functools.partial(post_kernel, inner), batch,
            [
                (part, 0), (act, 0), (before, 1), (partner, 1), (other, 0), (sums, 0), (marks, 0), (gate, 0), (gain, 1), (spread, 1),
            ],
            [((batch, width, inner), BF16, 0), ((batch, width, inner), BF16, 0), ((batch, states, inner), BF16, 0)],
            [((width, inner), F32)], "mix_gate", 6.0, here,
        )
        gated = gated.reshape(rows, inner)
        turned = None
        if direct:
            mine, send = turned_halves(gated, low, here, groups, chips)
            turned = (mine, swap(send, "seq", 1))
            sent = (send,)
        kept.append((turned, stream, norm_scale, low, mixed_in, edge, gate, act, size, sums, sums_t, factor, entering, mixed, gated))
        stream = stream + dot(gated, w_out).reshape(batch, width, model)

    grad_stream = cotangent.astype(F32)
    collected, collected_grads, far_sums, second_shares, waiting = [], [], [], [], []
    started = ()
    for layer in reversed(range(layers)):
        (turned, entry, norm_scale, low, mixed_in, edge, gate, act, size, sums, sums_t, factor, entering, mixed, gated) = kept[layer]
        w_gate, w_mix, w_out = gate_all[layer], mix_all[layer], out_all[layer]
        taps, rates, skip, gain = taps_all[layer], rates_all[layer], skip_all[layer], gain_all[layer]
        grad_low = grad_stream.astype(BF16).reshape(rows, model)
        grad_gated = dot_nt(grad_low, w_out).astype(BF16).reshape(batch, width, inner)
        d_mixed, d_gate, d_state, d_queries, d_sums, row_grads = call(
            functools.partial(gate_back_kernel, inner), batch,
            [
                (grad_gated, 0), (grad_low.reshape(batch, width, model), 0), (factor, 0), (mixed, 0), (gate, 0), (gain, 1), (act, 0),
                (entering, 0), (sums, 0), (marks, 0), (spread, 1),
            ],
            [
                ((batch, width, inner), BF16, 0), ((batch, width, inner + model), BF16, 0),
                ((batch, states + FACTOR_ROWS, inner), BF16, 0), ((batch, width, states), F32, 0), ((batch, width, LANES), F32, 0), ((8, inner), F32, 1),
            ],
            [((width, inner), F32)], "gate_back", 11.0, after=started,
        )
        got, other, joined_state = exchange(d_state, here, 0)
        both = d_gate.reshape(rows, inner + model)
        d_gate = both[:, :inner]
        started, arrived, ordered = (), (), ()
        if direct:
            big, small = inner // (groups * peers), model // (groups * peers)
            mine, theirs = turned
            both_other = swap(both, "seq", 1)
        else:
            out_share = reduced(dot_tn(gated, grad_low).astype(BF16))
        d_stepped, d_pair, d_total = call(
            functools.partial(intra_back_kernel, inner, heads), batch,
            [
                (d_mixed, 0), (act, 0), (size, 0), (sums, 0), (sums_t, 0), (marks, 0), (row_marks, 0), (spread, 1),
                (d_queries, 0), (d_sums, 0),
            ],
            [((batch, width, inner), BF16, 0), ((batch, width, 2 * states), F32, 0), ((batch, width, LANES), F32, 0)],
            [
                ((width, width), F32), ((width, width), F32), ((width, inner), BF16), ((LANES, width), F32), ((width, LANES), F32),
            ], "mix_within_back", 17.0, after=(joined_state,),
        )
        filled = (d_stepped,)
        if direct and layer > 0:
            (parts,) = whole_call(
                functools.partial(first_grads_kernel, groups, chips, inner, False), [mine, theirs, both, both_other],
                [((groups, chips, big + inner // model * small, model), BF16)], 10.0, "first_grads", here, (d_stepped,),
            )
            far_sums.append(lax.psum_scatter(parts, "fsdp", scatter_dimension=0, tiled=True)[0])
            filled += (parts,)
        before, partner = entered(got, filled)
        if direct and layer == 0:
            first_blocks = whole_call(
                functools.partial(first_grads_kernel, groups, chips, inner, True), [mine, theirs, both, both_other] + far_sums,
                [((groups + 1, big + inner // model * small, model), BF16)] * chips, 10.0, "first_grads", here, (before,),
            )
            arrived = tuple(first_blocks)
            near, far, *passed = halved(plane_parts(first_blocks))
            ordered = (near,)
            gots = []
            for later in waiting:
                blocks = later((first_blocks[0],))
                gots.append(plane_parts(blocks))
                ordered += (blocks[0],)
        d_mixed_in, d_edge, tap_grads, head_grads = call(
            functools.partial(conv_back_kernel, inner), batch,
            [
                (d_stepped, 0), (d_mixed, 0), (act, 0), (mixed_in, 0), (edge, 0), (marks, 0), (taps, 1), (rates, 1),
                (skip, 1), (size, 0), (sums, 0), (spread, 1), (d_pair, 0), (d_total, 0), (before, 1), (partner, 1), (other, 0),
                (entering, 0),
            ],
            [
                ((batch, width, channels + LANES), BF16, 0), ((batch, EDGE, channels), F32, 0),
                ((8, channels), F32, 1), ((8, LANES), F32, 1),
            ],
            [((EDGE + width, channels), F32), ((3, width + 2 * EDGE, 256), F32)], "conv_back", 17.0, here, arrived,
        )
        from_next = lax.ppermute(d_edge.astype(BF16), "seq", [(i + 1, i) for i in range(peers - 1)])
        grad_mixed = with_edges(d_mixed_in, from_next, ordered).reshape(rows, channels + LANES)
        grad_rows = dot_nt(d_gate, w_gate) + dot_nt(grad_mixed, w_mix)
        grad_rows = grad_rows.reshape(batch, width, model)
        scaled = grad_rows * norm_all[layer]
        inward = jnp.mean(scaled * entry, axis=-1, keepdims=True)
        gain_grad = jnp.sum(grad_rows * entry * norm_scale, axis=(0, 1))
        grad_stream = grad_stream + norm_scale * scaled - (norm_scale * norm_scale * norm_scale * inward) * entry
        if direct:
            extra = whole_call(
                functools.partial(gather_small_kernel, groups, taps_len, heads), [gain_grad[None], tap_grads, head_grads, row_grads, spread],
                [((model, LANES), F32)], 3.0, "gather_small",
            )[0]
            operands = [mine, theirs, grad_mixed, swap(grad_mixed, "seq", 1), extra, swap(extra, "seq", 1)]
            kernel = functools.partial(second_grads_kernel, groups, chips, channels, heads)
            outs = [((groups, small, channels + LANES), BF16)] * chips
            if layer > 0:
                waiting.append(functools.partial(whole_call, kernel, operands, outs, 6.0, "second_grads", here))
                started = (operands[3], operands[5])
            else:
                blocks = whole_call(kernel, operands, outs, 6.0, "second_grads", here)
                after = (blocks[0],)
                first_share = stacked([halved_sums(near, far, after)] + passed).reshape(-1, model)
                mine_a, other_a = spread_in_plane(first_share, chips)
                for got in gots:
                    near, far = halved(got, after)
                    second_shares.append(laid([halved_sums(near, far, ())], model, ()))
                second_shares.append(layer_sums(plane_parts(blocks), groups, model, (stream, grad_stream) + tuple(mine_a)))
        else:
            mixed_grad = dot_tn(low, grad_mixed)
            in_share = reduced(jnp.concatenate([dot_tn(low, d_gate).astype(BF16), mixed_grad[:, :channels].astype(BF16)], axis=1))
            dt_share = reduced(mixed_grad[:, channels:].astype(BF16))
            collected_grads.append((in_share, dt_share, out_share))
            small_grads = [
                gain_grad.reshape(groups, -1),
                jnp.moveaxis(tap_grads[:taps_len].reshape(taps_len, groups, -1), 1, 0).reshape(groups, -1),
                tap_grads[taps_len].reshape(groups, -1),
                head_grads[0, :heads].reshape(groups, -1),
                head_grads[1, :heads].reshape(groups, -1),
                jnp.sum(row_grads[1].reshape(heads, span), axis=1).reshape(groups, -1),
                row_grads[0].reshape(groups, -1),
            ]
            collected.append(jnp.concatenate(small_grads, axis=1))
    if direct:
        second_share = stacked(second_shares[::-1]).reshape(-1, model)
        mine_b, other_b = spread_in_plane(second_share, chips)
        shapes = [(model // groups, inner + channels), (model // groups, heads), (inner // groups, model)]
        smalls = [
            (layers, model // groups), (layers, taps_len, channels // groups), (layers, channels // groups), (layers, 3, heads // groups),
            (layers, inner // groups),
        ]
        blocks = mine_a + [other_a] + mine_b + [other_b]
        placed = placed_grads(here, blocks, layers, shapes, smalls, chips, inner, ())
        by_head = placed[6]
        pieces = [placed[3], placed[4], placed[5], by_head[:, 0], by_head[:, 1], by_head[:, 2], placed[7]]
    else:
        placed = [jnp.stack([c[i] for c in collected_grads[::-1]]) for i in range(3)]
        placed[1] = placed[1][:, :, :heads]
        small_sum = lax.psum(jnp.stack(collected[::-1], axis=1), ("fsdp", "seq"))
        small_sum = lax.dynamic_index_in_dim(small_sum, lax.axis_index("fsdp"), 0, keepdims=False)
        pieces, at = [], 0
        for size in sizes:
            pieces.append(small_sum[:, at:at + size])
            at += size
    return (
        stream, grad_stream, pieces[0],
        placed[0],
        placed[1],
        pieces[1].reshape(layers, taps_len, -1),
        pieces[2], pieces[3], pieces[4], pieces[5], pieces[6],
        placed[2],
    )


def solution(mesh):
    split = P("fsdp", "seq", None)
    vector = P(None, "fsdp")
    matrix = P(None, "fsdp", None)
    taps = P(None, None, "fsdp")
    return jax.shard_map(
        on_device,
        mesh=mesh,
        in_specs=(
            split, P("fsdp", "seq"), vector, matrix, matrix, taps, vector, vector, vector, vector, vector, matrix, split,
        ),
        out_specs=(
            split, split, vector, matrix, matrix, taps, vector, vector, vector, vector, vector, matrix,
        ),
        check_vma=False,
    )
```
